32 devices in a mesh: dp: 8 (over y, x, core), mp: 4 (over z).
Axes of the slice: x: 2, y: 2, z: 4, core: 2. Of those that a mesh axis runs over, the one named last changes fastest.
Arguments:
- tokens: bfloat16 [32768, 512], P(('dp', 'mp')), may hold values from -6 to 6
- cotangent: bfloat16 [32768, 512], P(('dp', 'mp')), may hold values from -13.5 to 13.5
- master: float32 [4, 64, 128, 128], P('mp', 'dp'), may hold values from -0.2165625 to 0.2165625
- moment_one: float32 [4, 64, 128, 128], P('mp', 'dp'), may hold values from -615.46574 to 615.46574
- moment_two: float32 [4, 64, 128, 128], P('mp', 'dp'), may hold values from 838.8608 to 94699.52
- basis_left: float32 [4, 64, 128, 128], P('mp', 'dp'), may hold values from -1 to 1, as said below
- basis_right: float32 [4, 64, 128, 128], P('mp', 'dp'), may hold values from -1 to 1, as said below
- owner: int32 [64], replicated, may hold values from 0 to 7, as said below
- gains: float32 [2, 512], replicated, may hold values from 0.5 to 1.5
- gain_moment_one: float32 [2, 512], replicated, may hold values from -470.65027 to 470.65027
- gain_moment_two: float32 [2, 512], replicated, may hold values from 13844.48 to 55377.92
Outputs:
- block_out: bfloat16 [32768, 512], P(('dp', 'mp'))
- input_grad: float32 [32768, 512], P(('dp', 'mp'))
- moment_one_new: float32 [4, 64, 128, 128], P('mp', 'dp')
- moment_two_new: float32 [4, 64, 128, 128], P('mp', 'dp')
- master_new: float32 [4, 64, 128, 128], P('mp', 'dp')
- master_low: bfloat16 [4, 64, 128, 128], P('mp', 'dp')
- gain_moment_one_new: float32 [2, 512], replicated
- gain_moment_two_new: float32 [2, 512], replicated
- gains_new: float32 [2, 512], replicated
- forget_mean: float32 [], replicated
The draws below stay inside these ranges and needn't reach their ends.
Inputs may be any that keep to these rules, and one draw needn't show every extreme that they name: `owner`: every index of dp appears exactly 64 * 4 / 32 times. `basis_left`: every [128, 128] block is an orthogonal matrix. `basis_right`: every [128, 128] block is an orthogonal matrix.
All inputs are finite; a program needn't handle non-finite values.
Results may differ from the reference program's by a relative error of at most 0.0079.
Values may be sent and summed in bfloat16 or wider, within the bound.
A program may use at most 192 MiB of HBM per device.

```python
import math
import jax
import jax.numpy as jnp
from jax import lax

D = 512
H = 1024
FF = 2048
BLK = 128
STEP = 10
L = 1024
SEQ_DP = 4
TOK_DP = 4096
SEQS = 32
TOKENS = 32768
HM = 256
FM = 512
NBLK = 64


def feature_signs(key):
    picks = jax.random.randint(jax.random.fold_in(key, 11), (D,), 0, 2)
    return (picks * 2 - 1).astype(jnp.float32)


def block_kinds(key):
    owner = jax.random.permutation(jax.random.fold_in(key, 7), NBLK).astype(jnp.int32) % (SEQS // SEQ_DP)
    slot_order = jnp.argsort(owner, stable=True).astype(jnp.int32)
    row_tiles = D // BLK
    col_tiles = (3 * HM + FM) // BLK
    column = slot_order % col_tiles
    low_row = (slot_order - row_tiles * col_tiles) // row_tiles
    upper = jnp.where(column < HM // BLK, 0, jnp.where(column < 2 * HM // BLK, 1, jnp.where(column < 3 * HM // BLK, 2, 3)))
    lower = jnp.where(low_row < HM // BLK, 4, 5)
    kinds = jnp.where(slot_order < row_tiles * col_tiles, upper, lower)
    return (owner, kinds)


def grad_scales(kinds):
    root = math.sqrt(TOKENS)
    table = jnp.array([0.16 * root, 0.16 * root, 0.5 * root, 0.4 * root, 0.8 * root, 0.85 * root], jnp.float32)
    return table[kinds][None, :, None, None]


def rotation_blocks(key):
    model_parts = H // HM
    shape = (model_parts, NBLK)
    half = BLK // 2
    key_one, key_two, key_three = jax.random.split(key, 3)
    first_angle = jax.random.uniform(key_one, shape + (half,), jnp.float32, -math.pi, math.pi)
    second_angle = jax.random.uniform(key_two, shape + (half,), jnp.float32, -math.pi, math.pi)
    index = jnp.arange(BLK)
    scores = jax.random.randint(key_three, shape + (BLK,), 0, 1 << 20) * BLK + index
    mixing = jnp.argsort(scores, axis=-1).astype(jnp.int32)
    pair_of = index // 2
    row_index = index[:, None]
    col_index = index[None, :]
    cos_one = jnp.cos(first_angle)[..., pair_of][..., :, None]
    sin_one = jnp.sin(first_angle)[..., pair_of][..., :, None]
    same_pair = row_index // 2 == col_index // 2
    rotor = jnp.where(row_index == col_index, cos_one, jnp.where(same_pair & (row_index < col_index), -sin_one, jnp.where(same_pair, sin_one, 0.0)))
    partner = index + 1 - 2 * (index % 2)
    mixed_cols = jnp.take_along_axis(rotor, jnp.broadcast_to(mixing[..., None, :], rotor.shape), axis=-1)
    partner_perm = jnp.take_along_axis(mixing, jnp.broadcast_to(partner, mixing.shape), axis=-1)
    partner_cols = jnp.take_along_axis(rotor, jnp.broadcast_to(partner_perm[..., None, :], rotor.shape), axis=-1)
    cos_two = jnp.cos(second_angle)[..., pair_of]
    sin_two = jnp.sin(second_angle)[..., pair_of]
    off_two = jnp.where(index % 2 == 0, sin_two, -sin_two)
    return mixed_cols * cos_two[..., None, :] + partner_cols * off_two[..., None, :]


def draw_owner(key, part):
    owner, _ = block_kinds(key)
    return owner


def draw_tokens(key, part):
    signs = feature_signs(key)
    key = jax.random.fold_in(key, 10)
    base = jax.random.truncated_normal(key, -5.0, 5.0, (TOKENS, D), jnp.float32)
    return (base + signs[None, :]).astype(jnp.bfloat16)


def draw_master(key, part):
    signs = feature_signs(key)
    owner, kinds = block_kinds(key)
    slot_order = jnp.argsort(owner, stable=True).astype(jnp.int32)
    key = jax.random.fold_in(key, 1)
    key_base, key_strength = jax.random.split(key)
    model_parts = H // HM
    table = jnp.array([D ** (-0.5), D ** (-0.5), D ** (-0.5), D ** (-0.5), (H / 3.0) ** (-0.5), (FF / 2.0) ** (-0.5)], jnp.float32)
    base = jax.random.truncated_normal(key_base, -4.0, 4.0, (model_parts, NBLK, BLK, BLK), jnp.float32)
    base = base * table[kinds][None, :, None, None]
    strength = 5.0 * jnp.sqrt(jax.random.uniform(key_strength, (model_parts, HM), jnp.float32))
    row_tiles = D // BLK
    col_tiles = (3 * HM + FM) // BLK
    row_tile = jnp.minimum(slot_order // col_tiles, row_tiles - 1)
    column = slot_order % col_tiles
    first_col = jnp.where(column < HM // BLK, column, column - HM // BLK) * BLK
    col_index = jnp.clip(first_col[:, None] + jnp.arange(BLK)[None, :], 0, HM - 1)
    row_index = row_tile[:, None] * BLK + jnp.arange(BLK)[None, :]
    row_signs = signs[row_index]
    col_strength = strength[:, col_index]
    factor = jnp.where(kinds == 0, 1.0, jnp.where(kinds == 1, -1.0, 0.0)).astype(jnp.float32)
    extra = factor[None, :, None, None] * row_signs[None, :, :, None] * col_strength[:, :, None, :] / float(D)
    return base + extra


def draw_moment_one(key, part):
    _, kinds = block_kinds(key)
    key = jax.random.fold_in(key, 2)
    base = jax.random.truncated_normal(key, -4.0, 4.0, (H // HM, NBLK, BLK, BLK), jnp.float32)
    return base * grad_scales(kinds)


def draw_moment_two(key, part):
    _, kinds = block_kinds(key)
    key = jax.random.fold_in(key, 6)
    factor = jnp.exp(jax.random.uniform(key, (H // HM, NBLK, BLK, BLK), jnp.float32, 0.0, math.log(4.0)))
    scales = grad_scales(kinds)
    return factor * scales * scales


def draw_basis_left(key, part):
    key = jax.random.fold_in(key, 3)
    return rotation_blocks(key)


def draw_basis_right(key, part):
    key = jax.random.fold_in(key, 4)
    return rotation_blocks(key)


def draw_cotangent(key, part):
    key = jax.random.fold_in(key, 5)
    place = jnp.arange(TOKENS)
    outer = (place // TOK_DP).astype(jnp.float32) / max(SEQS // SEQ_DP - 1, 1)
    inner = (place % TOK_DP).astype(jnp.float32) / max(TOK_DP - 1, 1)
    base = jax.random.truncated_normal(key, -5.0, 5.0, (TOKENS, D), jnp.float32)
    scale = (1.0 + 2.0 * outer) * (1.0 + 2.0 * inner) * 0.3
    return (base * scale[:, None]).astype(jnp.bfloat16)


def draw_gain_moment_one(key, part):
    key = jax.random.fold_in(key, 8)
    base = jax.random.truncated_normal(key, -4.0, 4.0, (2, D), jnp.float32)
    return base * (0.65 * math.sqrt(TOKENS))


def draw_gain_moment_two(key, part):
    key = jax.random.fold_in(key, 9)
    factor = jnp.exp(jax.random.uniform(key, (2, D), jnp.float32, 0.0, math.log(4.0)))
    return factor * (0.4225 * TOKENS)


def setup_inputs(seed: int = 0) -> dict:
    key_of = jax.random.split(jax.random.key(seed), 12)
    return {
        "tokens": draw_tokens(jax.random.fold_in(key_of[11], 71), 0),
        "cotangent": draw_cotangent(jax.random.fold_in(key_of[11], 71), 0),
        "master": draw_master(jax.random.fold_in(key_of[11], 71), 0),
        "moment_one": draw_moment_one(jax.random.fold_in(key_of[11], 71), 0),
        "moment_two": draw_moment_two(jax.random.fold_in(key_of[11], 71), 0),
        "basis_left": draw_basis_left(jax.random.fold_in(key_of[11], 71), 0),
        "basis_right": draw_basis_right(jax.random.fold_in(key_of[11], 71), 0),
        "owner": draw_owner(jax.random.fold_in(key_of[11], 71), 0),
        "gains": jnp.clip(1.0 + 0.1 * jax.random.normal(key_of[8], (2, D), jnp.float32), 0.5, 1.5),
        "gain_moment_one": draw_gain_moment_one(jax.random.fold_in(key_of[11], 71), 0),
        "gain_moment_two": draw_gain_moment_two(jax.random.fold_in(key_of[11], 71), 0),
    }


@jax.custom_vjp
def low(v):
    return lax.optimization_barrier(v.astype(jnp.bfloat16)).astype(jnp.float32)

@jax.custom_vjp
def low_back(v):
    return v

def low_keep(v):
    return (low(v), None)

def low_pass(kept, grad):
    return (grad,)

def back_keep(v):
    return (v, None)

def back_low(kept, grad):
    return (low(grad),)
low.defvjp(low_keep, low_pass)
low_back.defvjp(back_keep, back_low)
norm_eps = 1e-05
beta_one = 0.5
beta_two = 0.5
adam_eps = 1e-08
learn_rate = 0.02
gain_rate = 0.1
weight_decay = 0.1
highest = lax.Precision.HIGHEST

def rms_norm(values, gain):
    return values * lax.rsqrt(lax.optimization_barrier(jnp.mean(values * values, axis=-1, keepdims=True)) + norm_eps) * gain

def gate_terms(pre):
    forget = jax.nn.sigmoid(pre[:, 0])
    admit = jax.nn.sigmoid(pre[:, 1])
    total = forget + admit
    return (forget / total, admit / total * pre[:, 2])

def combine_steps(earlier, later):
    return (earlier[0] * later[0], later[0] * earlier[1] + later[1])

def assemble(weight_stack, shard_h, shard_f):
    parts = weight_stack.shape[0]
    row_tiles = D // BLK
    col_tiles = (3 * shard_h + shard_f) // BLK
    low_tiles = (shard_h + shard_f) // BLK
    upper = weight_stack[:, :row_tiles * col_tiles].reshape(parts, row_tiles, col_tiles, BLK, BLK)
    upper = upper.transpose(0, 1, 3, 2, 4).reshape(parts, D, col_tiles * BLK)
    lower = weight_stack[:, row_tiles * col_tiles:].reshape(parts, low_tiles, row_tiles, BLK, BLK)
    lower = lower.transpose(0, 1, 3, 2, 4).reshape(parts, low_tiles * BLK, D)
    w_gate = upper[:, :, :3 * shard_h].reshape(parts, D, 3, shard_h).transpose(1, 2, 0, 3).reshape(D, 3 * parts * shard_h)
    w_up = upper[:, :, 3 * shard_h:].transpose(1, 0, 2).reshape(D, parts * shard_f)
    w_out = lower[:, :shard_h].reshape(parts * shard_h, D)
    w_down = lower[:, shard_h:].reshape(parts * shard_f, D)
    return (w_gate, w_up, w_out, w_down)

def adam_update(first_old, second_old, gradient):
    first_new = beta_one * first_old + (1.0 - beta_one) * gradient
    second_new = beta_two * second_old + (1.0 - beta_two) * gradient * gradient
    first_hat = first_new / (1.0 - beta_one ** STEP)
    second_hat = second_new / (1.0 - beta_two ** STEP)
    return (first_new, second_new, first_hat / (jnp.sqrt(second_hat) + adam_eps))

def soap_update(master, moment_one, moment_two, basis_left, basis_right, grads):
    left_side = jnp.einsum('pkab,pkac->pkbc', basis_left, grads, precision=highest)
    rotated = jnp.einsum('pkbc,pkcd->pkbd', left_side, basis_right, precision=highest)
    first_new, second_new, direction = adam_update(moment_one, moment_two, rotated)
    turned = jnp.einsum('pkab,pkbc->pkac', basis_left, direction, precision=highest)
    turned = jnp.einsum('pkac,pkdc->pkad', turned, basis_right, precision=highest)
    master_new = master - learn_rate * (turned + weight_decay * master)
    return (first_new, second_new, master_new)

def reference(tokens, cotangent, master, moment_one, moment_two, basis_left, basis_right, owner, gains, gain_moment_one, gain_moment_two):
    slot_order = jnp.argsort(owner, stable=True).astype(jnp.int32)
    block_rank = jnp.argsort(slot_order, stable=True).astype(jnp.int32)
    group = math.gcd(SEQS, max(1, 4096 // L))
    groups = SEQS // group

    def forward(tokens_wide, master_wide, gains_wide):
        weights = low(master_wide)
        w_gate, w_up, w_out, w_down = assemble(weights[:, block_rank], HM, FM)

        def block(inputs):
            rows_in, block_index = inputs
            normed_one = low(rms_norm(rows_in, gains_wide[0]))
            pre = low_back(jnp.dot(normed_one, w_gate, precision=highest))
            keep_rate, write_term = gate_terms(pre.reshape(-1, 3, H))
            _, state = lax.associative_scan(combine_steps, (keep_rate.reshape(group, L, H), write_term.reshape(group, L, H)), axis=1)
            state_low = low(state.reshape(-1, H))
            mixed = rows_in + low_back(jnp.dot(state_low, w_out, precision=highest))
            normed_two = low(rms_norm(mixed, gains_wide[1]))
            upward = low_back(jnp.dot(normed_two, w_up, precision=highest))
            act_low = low(jax.nn.gelu(upward, approximate=False))
            result = mixed + low_back(jnp.dot(act_low, w_down, precision=highest))
            place = block_index.astype(jnp.float32) * float(group * L) + jnp.arange(group * L, dtype=jnp.float32) + 1.0
            weighted = jnp.sum(keep_rate * (place / float(TOKENS))[:, None])
            return (result, weighted)
        block_ids = jnp.arange(groups, dtype=jnp.int32)
        results, sums = lax.map(jax.checkpoint(block), (tokens_wide.reshape(groups, group * L, D), block_ids))
        return (results.reshape(SEQS * L, D), jnp.sum(sums))
    tokens_wide = tokens.astype(jnp.float32)
    (result, forget_sum), pull = jax.vjp(forward, tokens_wide, master, gains)
    input_grad, master_grad, gain_grad = pull((cotangent.astype(jnp.float32), jnp.zeros((), jnp.float32)))
    first_new, second_new, master_new = soap_update(master, moment_one, moment_two, basis_left, basis_right, master_grad)
    gain_first, gain_second, gain_direction = adam_update(gain_moment_one, gain_moment_two, gain_grad)
    gains_new = gains - gain_rate * gain_direction
    forget_mean = forget_sum / (H * (TOKENS + 1) / 2.0)
    return (result.astype(jnp.bfloat16), input_grad, first_new, second_new, master_new, master_new.astype(jnp.bfloat16), gain_first, gain_second, gains_new, forget_mean)
```

```python
import functools

import jax
import jax.numpy as jnp
from jax import lax
from jax.experimental import pallas as pl
from jax.experimental.pallas import tpu as pltpu
from jax.sharding import PartitionSpec as P

D = 512
H = 1024
FF = 2048
BLK = 128
STEP = 10
L = 1024

norm_eps = 1e-05
beta_one = 0.5
beta_two = 0.5
adam_eps = 1e-08
learn_rate = 0.02
gain_rate = 0.1
weight_decay = 0.1
highest = lax.Precision.HIGHEST

f32 = jnp.float32
bf16 = jnp.bfloat16
SUB = 8
J = L // SUB
R = 256


def dot(a, b, trans_b=False):
    dims = (((1,), (1,)), ((), ())) if trans_b else (((1,), (0,)), ((), ()))
    return lax.dot_general(a, b, dims, preferred_element_type=f32)


def recip(v):
    return pltpu.reciprocal(v, approx=True)


def sigmoid(v):
    return recip(1.0 + jnp.exp(-v))


def shift_down(v):
    rolled = pltpu.roll(v, 1, 0)
    row = lax.broadcasted_iota(jnp.int32, v.shape, 0)
    return jnp.where(row == 0, 0.0, rolled)


def shift_up(v):
    rolled = pltpu.roll(v, SUB - 1, 0)
    row = lax.broadcasted_iota(jnp.int32, v.shape, 0)
    return jnp.where(row == SUB - 1, 0.0, rolled)


def gelu_terms(x):
    a = jnp.abs(x)
    t = recip(1.0 + a * (0.3275911 * 0.7071067811865476))
    poly = t * (
        0.5 * 0.254829592
        + t
        * (
            0.5 * -0.284496736
            + t * (0.5 * 1.421413741 + t * (0.5 * -1.453152027 + t * (0.5 * 1.061405429)))
        )
    )
    e = jnp.exp(x * x * -0.5)
    tail = poly * e
    cdf = jnp.where(x < 0.0, tail, 1.0 - tail)
    return cdf, x * e * 0.3989422804014327


def compute_kernel(
    tokens,
    cotangent,
    wg,
    wu,
    wo,
    wd,
    gains,
    block_out,
    input_grad,
    gg,
    gu,
    go,
    gd,
    small,
    n1,
    n1t,
    cot,
    cott,
    n2,
    n2t,
    dml,
    dmlt,
    forget,
    admit,
    cand,
    state,
    scan,
    acc_a,
    acc_b,
    mixed,
    act,
    dup,
    dpre,
    fills,
):
    parts, _, hm3 = wg.shape
    hm = hm3 // 3
    fm = wu.shape[2]
    gain_one = gains[0:1, :]
    gain_two = gains[1:2, :]

    def permute_in(src, dst):
        for k in range(D // BLK):
            scan[k] = src[:, k * BLK : (k + 1) * BLK].astype(f32)

        @pl.loop(0, J // 2, unroll=4)
        def _(j):
            for k in range(D // BLK):
                lo = scan[k, pl.ds(2 * j, SUB, stride=J), :]
                hi = scan[k, pl.ds(2 * j + 1, SUB, stride=J), :]
                dst[pl.ds(pl.multiple_of(16 * j, 16), 16), k * BLK : (k + 1) * BLK] = jnp.concatenate([lo, hi], 0).astype(bf16)

    def permute_out(src, dst):
        @pl.loop(0, J, unroll=4)
        def _(j):
            rows = pl.ds(pl.multiple_of(j * SUB, SUB), SUB)
            for k in range(D // BLK):
                scan[k, pl.ds(j, SUB, stride=J), :] = src[rows, k * BLK : (k + 1) * BLK]

        for k in range(D // BLK):
            dst[:, k * BLK : (k + 1) * BLK] = scan[k].astype(dst.dtype)

    def put(first, rows, value):
        for k in range(hm // BLK):
            scan[first + k, rows, :] = value[:, k * BLK : (k + 1) * BLK]

    def take(first, rows):
        return jnp.concatenate([scan[first + k, rows, :] for k in range(hm // BLK)], 1)

    half = hm // BLK

    permute_in(cotangent, cot)
    cott[...] = cot[...].T
    permute_in(tokens, n1)
    mixed[...] = n1[...].astype(f32)

    @pl.loop(0, L // R)
    def _(i):
        rows = pl.ds(pl.multiple_of(i * R, R), R)
        x = mixed[rows, :]
        r = lax.rsqrt(jnp.mean(x * x, axis=-1, keepdims=True) + norm_eps)
        n1[rows, :] = (x * r * gain_one).astype(bf16)

    n1t[...] = n1[...].T

    fills[0] = jnp.zeros((SUB, hm), f32)
    fills[1] = jnp.ones((SUB, hm), f32)
    weigh = fills[0]
    weigh_j = fills[0]
    for m in range(parts):

        @pl.loop(0, L // R)
        def _(i):
            rows = pl.ds(pl.multiple_of(i * R, R), R)
            x = n1[rows, :]
            forget[m, rows, :] = dot(x, wg[m, :, :hm])
            admit[m, rows, :] = dot(x, wg[m, :, hm : 2 * hm])
            cand[m, rows, :] = dot(x, wg[m, :, 2 * hm :])

        def step(j, carry):
            s, p, k_sum, kj_sum = carry
            rows = pl.ds(pl.multiple_of(j * SUB, SUB), SUB)
            f = sigmoid(forget[m, rows, :])
            a = sigmoid(admit[m, rows, :])
            inv = recip(f + a)
            keep = f * inv
            s = keep * s + a * inv * cand[m, rows, :]
            p = keep * p
            forget[m, rows, :] = f
            admit[m, rows, :] = a
            put(0, rows, s)
            put(half, rows, p)
            return s, p, k_sum + keep, kj_sum + keep * j.astype(f32)

        s, p, weigh, weigh_j = lax.fori_loop(
            0,
            J,
            step,
            (fills[0], fills[1], weigh, weigh_j),
            unroll=4,
        )
        enter = fills[0]
        for _ in range(SUB - 1):
            enter = shift_down(s + p * enter)

        @pl.loop(0, J, unroll=4)
        def _(j):
            rows = pl.ds(pl.multiple_of(j * SUB, SUB), SUB)
            state[m, rows, :] = take(0, rows) + take(half, rows) * enter

        @pl.loop(0, L // R)
        def _(i):
            rows = pl.ds(pl.multiple_of(i * R, R), R)
            mixed[rows, :] += dot(state[m, rows, :].astype(bf16), wo[m])

    @pl.loop(0, L // R)
    def _(i):
        rows = pl.ds(pl.multiple_of(i * R, R), R)
        x = mixed[rows, :]
        r = lax.rsqrt(jnp.mean(x * x, axis=-1, keepdims=True) + norm_eps)
        n2[rows, :] = (x * r * gain_two).astype(bf16)
        acc_a[rows, :] = x
        acc_b[rows, :] = jnp.zeros_like(x)

    n2t[...] = n2[...].T

    for m in range(parts):

        @pl.loop(0, L // R)
        def _(i):
            rows = pl.ds(pl.multiple_of(i * R, R), R)
            up = dot(n2[rows, :], wu[m])
            da = dot(cot[rows, :], wd[m], True)
            cdf, xpdf = gelu_terms(up)
            ac = (up * cdf).astype(bf16)
            du = (da * (cdf + xpdf)).astype(bf16)
            act[rows, :] = ac
            dup[rows, :] = du
            acc_a[rows, :] += dot(ac, wd[m])
            acc_b[rows, :] += dot(du, wu[m], True)

        gd[m] = dot(cott[...], act[...]).astype(gd.dtype)
        gu[m] = dot(n2t[...], dup[...]).astype(gu.dtype)

    permute_out(acc_a, block_out)

    gain_sum_two = jnp.zeros((1, D), f32)

    def back_two(i, total):
        rows = pl.ds(pl.multiple_of(i * R, R), R)
        x = mixed[rows, :]
        r = lax.rsqrt(jnp.mean(x * x, axis=-1, keepdims=True) + norm_eps)
        dn = acc_b[rows, :]
        q = dn * gain_two
        d = cot[rows, :].astype(f32) + r * q - r * r * r * x * jnp.mean(q * x, axis=-1, keepdims=True)
        mixed[rows, :] = d
        dml[rows, :] = d.astype(bf16)
        acc_b[rows, :] = jnp.zeros_like(d)
        return total + jnp.sum(dn * x * r, axis=0, keepdims=True)

    gain_sum_two = lax.fori_loop(0, L // R, back_two, gain_sum_two)
    dmlt[...] = dml[...].T

    for m in range(parts):

        @pl.loop(0, L // R)
        def _(i):
            rows = pl.ds(pl.multiple_of(i * R, R), R)
            put(0, rows, dot(dml[rows, :], wo[m], True))

        def step(k, carry):
            u, p, keep_next = carry
            j = J - 1 - k
            rows = pl.ds(pl.multiple_of(j * SUB, SUB), SUB)
            u = take(0, rows) + keep_next * u
            p = keep_next * p
            put(0, rows, u)
            put(half, rows, p)
            f = forget[m, rows, :]
            return u, p, f * recip(f + admit[m, rows, :])

        u, p, keep_first = lax.fori_loop(
            0,
            J,
            step,
            (fills[0], fills[1], fills[1]),
            unroll=4,
        )
        enter = fills[0]
        for _ in range(SUB - 1):
            enter = shift_up(keep_first * (u + p * enter))

        def back(i, before):
            parts_out = []
            for h in range(2):
                rows = pl.ds(pl.multiple_of(i * 2 * SUB + h * SUB, SUB), SUB)
                carried = take(0, rows) + take(half, rows) * enter
                f = forget[m, rows, :]
                a = admit[m, rows, :]
                inv = recip(f + a)
                adm = a * inv
                g = carried * (before - cand[m, rows, :]) * (f * inv * adm)
                parts_out.append((g * (1.0 - f), g * (a - 1.0), carried * adm))
                before = state[m, rows, :]
            both = pl.ds(pl.multiple_of(i * 2 * SUB, 2 * SUB), 2 * SUB)
            for k in range(3):
                dpre[both, k * hm : (k + 1) * hm] = jnp.concatenate(
                    [parts_out[0][k], parts_out[1][k]], 0
                ).astype(bf16)
            return before

        last = state[m, pl.ds(L - SUB, SUB), :]
        lax.fori_loop(0, J // 2, back, shift_down(last), unroll=2)

        gg[m] = dot(n1t[...], dpre[...]).astype(gg.dtype)
        go[m] = dot(dmlt[...], state[m].astype(bf16)).astype(go.dtype)

        @pl.loop(0, L // R)
        def _(i):
            rows = pl.ds(pl.multiple_of(i * R, R), R)
            acc_b[rows, :] += dot(dpre[rows, :], wg[m], True)

    permute_in(tokens, n1)

    def back_one(i, total):
        rows = pl.ds(pl.multiple_of(i * R, R), R)
        x = n1[rows, :].astype(f32)
        r = lax.rsqrt(jnp.mean(x * x, axis=-1, keepdims=True) + norm_eps)
        dn = acc_b[rows, :]
        q = dn * gain_one
        mixed[rows, :] += r * q - r * r * r * x * jnp.mean(q * x, axis=-1, keepdims=True)
        return total + jnp.sum(dn * x * r, axis=0, keepdims=True)

    gain_sum_one = lax.fori_loop(0, L // R, back_one, jnp.zeros((1, D), f32))

    permute_out(mixed, input_grad)

    place = lax.broadcasted_iota(jnp.int32, (SUB, hm), 0).astype(f32) * float(J)
    small[...] = jnp.zeros_like(small)
    small[0:1, :] = gain_sum_one
    small[1:2, :] = gain_sum_two
    small[2:3, :hm] = jnp.sum(weigh, axis=0, keepdims=True)
    small[3:4, :hm] = jnp.sum(weigh_j + weigh * place, axis=0, keepdims=True)


def compute(tokens, cotangent, wg, wu, wo, wd, gains, grad_type):
    parts, _, hm3 = wg.shape
    hm, fm = hm3 // 3, wu.shape[2]
    sds = jax.ShapeDtypeStruct
    vm = pl.BlockSpec(memory_space=pltpu.VMEM)
    return pl.pallas_call(
        compute_kernel,
        out_shape=(
            sds((L, D), bf16),
            sds((L, D), f32),
            sds((parts, D, 3 * hm), grad_type),
            sds((parts, D, fm), grad_type),
            sds((parts, D, hm), grad_type),
            sds((parts, D, fm), grad_type),
            sds((8, D), f32),
        ),
        in_specs=[vm] * 7,
        out_specs=[vm] * 7,
        scratch_shapes=[
            pltpu.VMEM((L, D), bf16),
            pltpu.VMEM((D, L), bf16),
            pltpu.VMEM((L, D), bf16),
            pltpu.VMEM((D, L), bf16),
            pltpu.VMEM((L, D), bf16),
            pltpu.VMEM((D, L), bf16),
            pltpu.VMEM((L, D), bf16),
            pltpu.VMEM((D, L), bf16),
            pltpu.VMEM((parts, L, hm), f32),
            pltpu.VMEM((parts, L, hm), f32),
            pltpu.VMEM((parts, L, hm), f32),
            pltpu.VMEM((parts, L, hm), f32),
            pltpu.VMEM((2 * hm // BLK, L, BLK), f32),
            pltpu.VMEM((L, D), f32),
            pltpu.VMEM((L, D), f32),
            pltpu.VMEM((L, D), f32),
            pltpu.VMEM((L, fm), bf16),
            pltpu.VMEM((L, fm), bf16),
            pltpu.VMEM((L, 3 * hm), bf16),
            pltpu.VMEM((2, SUB, hm), f32),
        ],
        compiler_params=pltpu.CompilerParams(vmem_limit_bytes=63 * 2**20),
        name="block",
    )(tokens, cotangent, wg, wu, wo, wd, gains)


def adam_update(first_old, second_old, gradient):
    first_new = beta_one * first_old + (1.0 - beta_one) * gradient
    second_new = beta_two * second_old + (1.0 - beta_two) * gradient * gradient
    first_hat = first_new / (1.0 - beta_one**STEP)
    second_hat = second_new / (1.0 - beta_two**STEP)
    return (first_new, second_new, first_hat / (jnp.sqrt(second_hat) + adam_eps))


def soap_update(master, moment_one, moment_two, basis_left, basis_right, grads):
    left_side = jnp.einsum("pkab,pkac->pkbc", basis_left, grads, precision=highest)
    rotated = jnp.einsum("pkbc,pkcd->pkbd", left_side, basis_right, precision=highest)
    first_new, second_new, direction = adam_update(moment_one, moment_two, rotated)
    turned = jnp.einsum("pkab,pkbc->pkac", basis_left, direction, precision=highest)
    turned = jnp.einsum("pkac,pkdc->pkad", turned, basis_right, precision=highest)
    master_new = master - learn_rate * (turned + weight_decay * master)
    return (first_new, second_new, master_new)


def on_device(
    tokens,
    cotangent,
    master,
    moment_one,
    moment_two,
    basis_left,
    basis_right,
    owner,
    gains,
    gain_moment_one,
    gain_moment_two,
):
    parts = lax.axis_size("mp")
    data_parts = lax.axis_size("dp")
    hm, fm = H // parts, FF // parts
    token_total = L * data_parts * parts
    row_tiles, cols, lows = D // BLK, (3 * hm + fm) // BLK, (hm + fm) // BLK
    slot_order = jnp.argsort(owner, stable=True)
    block_rank = jnp.argsort(slot_order, stable=True)
    stored = lax.all_gather(master.astype(bf16), "dp", axis=1, tiled=True)
    stored = lax.all_gather(stored, "mp", axis=0, tiled=True)
    stack = stored[:, block_rank]
    upper = stack[:, : row_tiles * cols].reshape(parts, row_tiles, cols, BLK, BLK)
    upper = upper.transpose(0, 1, 3, 2, 4).reshape(parts, D, cols * BLK)
    lower = stack[:, row_tiles * cols :].reshape(parts, lows, row_tiles, BLK, BLK)
    lower = lower.transpose(0, 1, 3, 2, 4).reshape(parts, lows * BLK, D)
    block_out, input_grad, gg, gu, go, gd, small = compute(
        tokens, cotangent, upper[:, :, : 3 * hm], upper[:, :, 3 * hm :], lower[:, :hm], lower[:, hm:], gains, bf16
    )
    upper = jnp.concatenate([gg, gu], axis=2).reshape(parts, row_tiles, BLK, cols, BLK).transpose(0, 1, 3, 2, 4)
    upper = upper.reshape(parts, row_tiles * cols, BLK, BLK)
    lower = jnp.concatenate([go, gd], axis=2).reshape(parts, row_tiles, BLK, lows, BLK).transpose(0, 3, 1, 4, 2)
    lower = lower.reshape(parts, row_tiles * lows, BLK, BLK)
    natural = jnp.concatenate([upper, lower], axis=1).astype(f32)
    owned = lax.psum_scatter(natural[:, slot_order], "dp", scatter_dimension=1, tiled=True)
    owned = lax.psum_scatter(owned, "mp", scatter_dimension=0, tiled=True)
    first_new, second_new, master_new = soap_update(master, moment_one, moment_two, basis_left, basis_right, owned)
    first_row = (lax.axis_index("dp") * parts + lax.axis_index("mp")) * L
    forget_part = (jnp.sum(small[3, :hm]) + (first_row + 1).astype(f32) * jnp.sum(small[2, :hm])) / float(token_total)
    gain_grad, forget_total = lax.psum((small[:2], forget_part), ("dp", "mp"))
    gain_first, gain_second, gain_direction = adam_update(gain_moment_one, gain_moment_two, gain_grad)
    gains_new = gains - gain_rate * gain_direction
    forget_mean = forget_total / (H * (token_total + 1) / 2.0)
    return (
        block_out,
        input_grad,
        first_new,
        second_new,
        master_new,
        master_new.astype(bf16),
        gain_first,
        gain_second,
        gains_new,
        forget_mean,
    )


def solution(mesh):
    rows, blocks = P(("dp", "mp"), None), P("mp", "dp", None, None)
    return jax.shard_map(
        on_device,
        mesh=mesh,
        in_specs=(rows, rows, blocks, blocks, blocks, blocks, blocks, P(), P(), P(), P()),
        out_specs=(rows, rows, blocks, blocks, blocks, blocks, P(), P(), P(), P()),
        check_vma=False,
    )
```

```python
import functools

import jax
import jax.numpy as jnp
from jax import lax
from jax.experimental import pallas as pl
from jax.experimental.pallas import tpu as pltpu
from jax.sharding import PartitionSpec as P

D = 512
H = 1024
FF = 2048
BLK = 128
STEP = 10
L = 1024

norm_eps = 1e-05
beta_one = 0.5
beta_two = 0.5
adam_eps = 1e-08
learn_rate = 0.02
gain_rate = 0.1
weight_decay = 0.1
highest = lax.Precision.HIGHEST

f32 = jnp.float32
bf16 = jnp.bfloat16
SUB = 8
J = L // SUB
R = 256


def dot(a, b, trans_b=False):
    dims = (((1,), (1,)), ((), ())) if trans_b else (((1,), (0,)), ((), ()))
    return lax.dot_general(a, b, dims, preferred_element_type=f32)


def recip(v):
    return pltpu.reciprocal(v, approx=True)


def sigmoid(v):
    return recip(1.0 + jnp.exp(-v))


def shift_down(v):
    rolled = pltpu.roll(v, 1, 0)
    row = lax.broadcasted_iota(jnp.int32, v.shape, 0)
    return jnp.where(row == 0, 0.0, rolled)


def shift_up(v):
    rolled = pltpu.roll(v, SUB - 1, 0)
    row = lax.broadcasted_iota(jnp.int32, v.shape, 0)
    return jnp.where(row == SUB - 1, 0.0, rolled)


def gelu_terms(x):
    a = jnp.abs(x)
    t = recip(1.0 + a * (0.3275911 * 0.7071067811865476))
    poly = t * (
        0.5 * 0.254829592
        + t
        * (
            0.5 * -0.284496736
            + t * (0.5 * 1.421413741 + t * (0.5 * -1.453152027 + t * (0.5 * 1.061405429)))
        )
    )
    e = jnp.exp(x * x * -0.5)
    tail = poly * e
    cdf = jnp.where(x < 0.0, tail, 1.0 - tail)
    return cdf, x * e * 0.3989422804014327


MESH = pl.DeviceIdType.MESH


class Exchange:
    def __init__(self, send, recv):
        self.send, self.recv, self.used, self.open = send, recv, 0, []

    def start(self, src, dst, device):
        k = self.used
        self.used += 1
        copy = pltpu.make_async_remote_copy(
            src_ref=src,
            dst_ref=dst,
            send_sem=self.send.at[k],
            recv_sem=self.recv.at[k],
            device_id=device,
            device_id_type=MESH,
        )
        copy.start()
        self.open.append(copy)
        return copy

    def drain(self):
        for copy in self.open:
            copy.wait_send()
        self.open = []


class Gather:
    def __init__(self, net, master, rank, slots, weights):
        self.net, self.slots, self.weights, self.rank = net, slots, weights, rank
        d, m = lax.axis_index("dp"), lax.axis_index("mp")
        core, col, row = d % 2, (d // 2) % 2, d // 4
        self.me, self.m = d, m
        self.core = d + 1 - 2 * core
        self.plane = [d + 2 - 4 * col, d + 4 - 8 * row, d + 6 - 4 * col - 8 * row]
        self.order = [m, m + 1 - 2 * (m % 2), m + 2 - 4 * (m // 2), 3 - m]
        barrier = pltpu.get_barrier_semaphore()
        for device in [(e, m) for e in [self.core] + self.plane] + [(d, k) for k in self.order[1:]]:
            pl.semaphore_signal(barrier, inc=1, device_id=device, device_id_type=MESH)
        owned = master.shape[0]
        self.owned = owned
        for s in range(owned):
            slots[d * owned + s] = master[s].astype(bf16)
        pl.semaphore_wait(barrier, 7)

    def rows(self, e, first, count):
        return self.slots.at[pl.ds(e * self.owned + first, count)]

    def plane_start(self):
        n, m, (x, y, _) = self.owned, self.m, self.plane
        h = n // 2
        self.first = {}
        for e, first in ((x, 0), (y, h), (x, h), (y, 0)):
            ref = self.rows(self.me, first, h)
            self.first[(e is y, first)] = self.net.start(ref, ref, (e, m))
        ref = self.rows(self.me, 0, n)
        self.sibling = [self.net.start(ref, ref, (self.core, m))]

    def plane_finish(self):
        n, m, (x, y, z) = self.owned, self.m, self.plane
        h = n // 2
        self.first[(False, 0)].wait_recv()
        ref = self.rows(x, 0, h)
        last = [self.net.start(ref, ref, (y, m))]
        self.first[(True, h)].wait_recv()
        ref = self.rows(y, h, h)
        last.append(self.net.start(ref, ref, (x, m)))
        self.first[(False, h)].wait_recv()
        ref = self.rows(x, 0, n)
        self.sibling.append(self.net.start(ref, ref, (self.core, m)))
        self.first[(True, 0)].wait_recv()
        ref = self.rows(y, 0, n)
        self.sibling.append(self.net.start(ref, ref, (self.core, m)))
        for copy in last:
            copy.wait_recv()
        ref = self.rows(z, 0, n)
        self.sibling.append(self.net.start(ref, ref, (self.core, m)))
        for copy in self.sibling:
            copy.wait_recv()

    def place(self, kinds):
        wg, wu, wo, wd = self.weights
        parts, _, hm3 = wg.shape
        row_tiles, gates = D // BLK, hm3 // BLK
        cols, outs = gates + wu.shape[2] // BLK, wo.shape[1] // BLK
        for b in range(self.slots.shape[0]):
            if b < row_tiles * cols:
                r, c = b // cols, b % cols
                kind, ref = (0, wg) if c < gates else (2, wu)
                c -= 0 if c < gates else gates
            else:
                r, c = (b - row_tiles * cols) // row_tiles, (b - row_tiles * cols) % row_tiles
                kind, ref = (1, wo) if r < outs else (3, wd)
                r -= 0 if r < outs else outs
            if kind in kinds:
                ref[self.m, r * BLK : (r + 1) * BLK, c * BLK : (c + 1) * BLK] = self.slots[self.rank[b]]

    def share(self, kind, k, e):
        ref = self.weights[(0, 2, 1, 3)[kind]]
        ref = (self.weights[0], self.weights[2], self.weights[1], self.weights[3])[kind]
        size = ref.shape[1] // 8
        return ref.at[k, pl.ds(pl.multiple_of(e * size, size), size)]

    def along_start(self, kind):
        self.along = getattr(self, "along", {})
        for i in (1, 2, 3):
            ref = self.share(kind, self.m, self.me)
            self.along[kind, i] = self.net.start(ref, ref, (self.me, self.order[i]))

    def spread(self, kind, i):
        self.spreads = getattr(self, "spreads", {})
        self.along[kind, i].wait_recv()
        ref = self.share(kind, self.order[i], self.me)
        self.spreads[kind, i] = (
            [self.net.start(ref, ref, (e, self.m)) for e in self.plane],
            [self.net.start(ref, ref, (self.core, self.m))],
        )

    def pair(self, kind, i):
        across, inside = self.spreads[kind, i]
        for copy, e in zip(across, self.plane):
            copy.wait_recv()
            ref = self.share(kind, self.order[i], e)
            inside.append(self.net.start(ref, ref, (self.core, self.m)))

    def ready(self, kind, i):
        for copy in self.spreads[kind, i][1]:
            copy.wait_recv()


def compute_kernel(linked, *refs):
    if linked:
        tokens, cotangent, master, rank, gains = refs[:5]
        outs = refs[5:12]
        wg, wu, wo, wd, slots, send, recv = refs[12:19]
        scratch = refs[19:]
    else:
        tokens, cotangent, wg, wu, wo, wd, gains = refs[:7]
        outs = refs[7:14]
        scratch = refs[14:]
    block_out, input_grad, gg, gu, go, gd, small = outs
    (n1, n1t, cot, cott, n2, n2t, dml, dmlt, forget, admit, cand, state, scan, acc_a, acc_b, mixed, act, dup, dpre, fills) = scratch
    parts, _, hm3 = wg.shape
    hm = hm3 // 3
    fm = wu.shape[2]
    gain_one = gains[0:1, :]
    gain_two = gains[1:2, :]

    def permute_in(src, dst):
        for k in range(D // BLK):
            scan[k] = src[:, k * BLK : (k + 1) * BLK].astype(f32)

        @pl.loop(0, J // 2, unroll=4)
        def _(j):
            for k in range(D // BLK):
                lo = scan[k, pl.ds(2 * j, SUB, stride=J), :]
                hi = scan[k, pl.ds(2 * j + 1, SUB, stride=J), :]
                dst[pl.ds(pl.multiple_of(16 * j, 16), 16), k * BLK : (k + 1) * BLK] = jnp.concatenate([lo, hi], 0).astype(bf16)

    def permute_out(src, dst):
        @pl.loop(0, J, unroll=4)
        def _(j):
            rows = pl.ds(pl.multiple_of(j * SUB, SUB), SUB)
            for k in range(D // BLK):
                scan[k, pl.ds(j, SUB, stride=J), :] = src[rows, k * BLK : (k + 1) * BLK]

        for k in range(D // BLK):
            dst[:, k * BLK : (k + 1) * BLK] = scan[k].astype(dst.dtype)

    def put(first, rows, value):
        for k in range(hm // BLK):
            scan[first + k, rows, :] = value[:, k * BLK : (k + 1) * BLK]

    def take(first, rows):
        return jnp.concatenate([scan[first + k, rows, :] for k in range(hm // BLK)], 1)

    half = hm // BLK

    if linked:
        net = Exchange(send, recv)
        gather = Gather(net, master, rank, slots, (wg, wu, wo, wd))
        gather.plane_start()
        order = gather.order
    else:
        order = list(range(parts))

    permute_in(cotangent, cot)
    cott[...] = cot[...].T
    permute_in(tokens, n1)
    mixed[...] = n1[...].astype(f32)

    @pl.loop(0, L // R)
    def _(i):
        rows = pl.ds(pl.multiple_of(i * R, R), R)
        x = mixed[rows, :]
        r = lax.rsqrt(jnp.mean(x * x, axis=-1, keepdims=True) + norm_eps)
        n1[rows, :] = (x * r * gain_one).astype(bf16)

    n1t[...] = n1[...].T

    if linked:
        gather.plane_finish()
        gather.place((0,))
        gather.along_start(0)
        gather.place((1, 2, 3))
        for kind in (1, 2, 3):
            gather.along_start(kind)

    fills[0] = jnp.zeros((SUB, hm), f32)
    fills[1] = jnp.ones((SUB, hm), f32)
    weigh = fills[0]
    weigh_j = fills[0]
    for turn, m in enumerate(order):

        if linked and turn:
            gather.ready(0, turn)

        @pl.loop(0, L // R)
        def _(i):
            rows = pl.ds(pl.multiple_of(i * R, R), R)
            x = n1[rows, :]
            forget[m, rows, :] = dot(x, wg[m, :, :hm])
            admit[m, rows, :] = dot(x, wg[m, :, hm : 2 * hm])
            cand[m, rows, :] = dot(x, wg[m, :, 2 * hm :])

        if linked and turn == 0:
            for i in (1, 2, 3):
                gather.spread(0, i)
        if linked and turn == 2:
            gather.pair(0, 3)
        if linked and turn == 1:
            for i in (1, 2, 3):
                gather.spread(1, i)
        if linked and turn == 2:
            for kind, i in ((2, 1), (3, 1), (2, 2), (3, 2), (2, 3), (3, 3)):
                gather.spread(kind, i)
        if linked and turn == 3:
            for i in (1, 2, 3):
                gather.pair(1, i)

        def step(j, carry):
            s, p, k_sum, kj_sum = carry
            rows = pl.ds(pl.multiple_of(j * SUB, SUB), SUB)
            f = sigmoid(forget[m, rows, :])
            a = sigmoid(admit[m, rows, :])
            inv = recip(f + a)
            keep = f * inv
            s = keep * s + a * inv * cand[m, rows, :]
            p = keep * p
            forget[m, rows, :] = f
            admit[m, rows, :] = a
            put(0, rows, s)
            put(half, rows, p)
            return s, p, k_sum + keep, kj_sum + keep * j.astype(f32)

        s, p, weigh, weigh_j = lax.fori_loop(
            0,
            J,
            step,
            (fills[0], fills[1], weigh, weigh_j),
            unroll=4,
        )
        enter = fills[0]
        for _ in range(SUB - 1):
            enter = shift_down(s + p * enter)

        if linked and turn == 0:
            gather.pair(0, 1)
        if linked and turn == 1:
            gather.pair(0, 2)

        @pl.loop(0, J, unroll=4)
        def _(j):
            rows = pl.ds(pl.multiple_of(j * SUB, SUB), SUB)
            state[m, rows, :] = take(0, rows) + take(half, rows) * enter

    if linked:
        for i in (1, 2, 3):
            gather.ready(1, i)
        for kind in (2, 3):
            gather.pair(kind, 1)

    @pl.loop(0, L // R)
    def _(i):
        rows = pl.ds(pl.multiple_of(i * R, R), R)
        x = mixed[rows, :]
        for m in range(parts):
            x += dot(state[m, rows, :].astype(bf16), wo[m])
        mixed[rows, :] = x
        r = lax.rsqrt(jnp.mean(x * x, axis=-1, keepdims=True) + norm_eps)
        n2[rows, :] = (x * r * gain_two).astype(bf16)
        acc_a[rows, :] = x
        acc_b[rows, :] = jnp.zeros_like(x)

    n2t[...] = n2[...].T

    for turn, m in enumerate(order):

        if linked and turn:
            gather.ready(2, turn)
            gather.ready(3, turn)

        @pl.loop(0, L // R)
        def _(i):
            rows = pl.ds(pl.multiple_of(i * R, R), R)
            up = dot(n2[rows, :], wu[m])
            da = dot(cot[rows, :], wd[m], True)
            cdf, xpdf = gelu_terms(up)
            ac = (up * cdf).astype(bf16)
            du = (da * (cdf + xpdf)).astype(bf16)
            act[rows, :] = ac
            dup[rows, :] = du
            acc_a[rows, :] += dot(ac, wd[m])
            acc_b[rows, :] += dot(du, wu[m], True)

        if linked and turn < 2:
            gather.pair(2, turn + 2)
            gather.pair(3, turn + 2)
        gd[m] = dot(cott[...], act[...]).astype(gd.dtype)
        gu[m] = dot(n2t[...], dup[...]).astype(gu.dtype)

    permute_out(acc_a, block_out)

    gain_sum_two = jnp.zeros((1, D), f32)

    def back_two(i, total):
        rows = pl.ds(pl.multiple_of(i * R, R), R)
        x = mixed[rows, :]
        r = lax.rsqrt(jnp.mean(x * x, axis=-1, keepdims=True) + norm_eps)
        dn = acc_b[rows, :]
        q = dn * gain_two
        d = cot[rows, :].astype(f32) + r * q - r * r * r * x * jnp.mean(q * x, axis=-1, keepdims=True)
        mixed[rows, :] = d
        dml[rows, :] = d.astype(bf16)
        acc_b[rows, :] = jnp.zeros_like(d)
        return total + jnp.sum(dn * x * r, axis=0, keepdims=True)

    gain_sum_two = lax.fori_loop(0, L // R, back_two, gain_sum_two)
    dmlt[...] = dml[...].T

    for turn, m in enumerate(order):

        @pl.loop(0, L // R)
        def _(i):
            rows = pl.ds(pl.multiple_of(i * R, R), R)
            put(0, rows, dot(dml[rows, :], wo[m], True))

        def step(k, carry):
            u, p, keep_next = carry
            j = J - 1 - k
            rows = pl.ds(pl.multiple_of(j * SUB, SUB), SUB)
            u = take(0, rows) + keep_next * u
            p = keep_next * p
            put(0, rows, u)
            put(half, rows, p)
            f = forget[m, rows, :]
            return u, p, f * recip(f + admit[m, rows, :])

        u, p, keep_first = lax.fori_loop(
            0,
            J,
            step,
            (fills[0], fills[1], fills[1]),
            unroll=4,
        )
        enter = fills[0]
        for _ in range(SUB - 1):
            enter = shift_up(keep_first * (u + p * enter))

        def back(i, before):
            parts_out = []
            for h in range(2):
                rows = pl.ds(pl.multiple_of(i * 2 * SUB + h * SUB, SUB), SUB)
                carried = take(0, rows) + take(half, rows) * enter
                f = forget[m, rows, :]
                a = admit[m, rows, :]
                inv = recip(f + a)
                adm = a * inv
                g = carried * (before - cand[m, rows, :]) * (f * inv * adm)
                parts_out.append((g * (1.0 - f), g * (a - 1.0), carried * adm))
                before = state[m, rows, :]
            both = pl.ds(pl.multiple_of(i * 2 * SUB, 2 * SUB), 2 * SUB)
            for k in range(3):
                dpre[both, k * hm : (k + 1) * hm] = jnp.concatenate(
                    [parts_out[0][k], parts_out[1][k]], 0
                ).astype(bf16)
            return before

        last = state[m, pl.ds(L - SUB, SUB), :]
        lax.fori_loop(0, J // 2, back, shift_down(last), unroll=2)

        gg[m] = dot(n1t[...], dpre[...]).astype(gg.dtype)
        go[m] = dot(dmlt[...], state[m].astype(bf16)).astype(go.dtype)

        @pl.loop(0, L // R)
        def _(i):
            rows = pl.ds(pl.multiple_of(i * R, R), R)
            acc_b[rows, :] += dot(dpre[rows, :], wg[m], True)

    permute_in(tokens, n1)

    def back_one(i, total):
        rows = pl.ds(pl.multiple_of(i * R, R), R)
        x = n1[rows, :].astype(f32)
        r = lax.rsqrt(jnp.mean(x * x, axis=-1, keepdims=True) + norm_eps)
        dn = acc_b[rows, :]
        q = dn * gain_one
        mixed[rows, :] += r * q - r * r * r * x * jnp.mean(q * x, axis=-1, keepdims=True)
        return total + jnp.sum(dn * x * r, axis=0, keepdims=True)

    gain_sum_one = lax.fori_loop(0, L // R, back_one, jnp.zeros((1, D), f32))

    permute_out(mixed, input_grad)

    place = lax.broadcasted_iota(jnp.int32, (SUB, hm), 0).astype(f32) * float(J)
    small[...] = jnp.zeros_like(small)
    small[0:1, :] = gain_sum_one
    small[1:2, :] = gain_sum_two
    small[2:3, :hm] = jnp.sum(weigh, axis=0, keepdims=True)
    if linked:
        net.drain()
    small[3:4, :hm] = jnp.sum(weigh_j + weigh * place, axis=0, keepdims=True)


def compute(tokens, cotangent, gains, grad_type, weights=None, master=None, rank=None):
    linked = weights is None
    parts = lax.axis_size("mp")
    hm, fm = H // parts, FF // parts
    sds = jax.ShapeDtypeStruct
    vm = pl.BlockSpec(memory_space=pltpu.VMEM)
    if linked:
        args = (tokens, cotangent, master, rank, gains)
        in_specs = [vm, vm, vm, pl.BlockSpec(memory_space=pltpu.SMEM), vm]
        extra = [
            pltpu.VMEM((parts, D, 3 * hm), bf16),
            pltpu.VMEM((parts, D, fm), bf16),
            pltpu.VMEM((parts, hm, D), bf16),
            pltpu.VMEM((parts, fm, D), bf16),
            pltpu.VMEM((rank.shape[0], BLK, BLK), bf16),
            pltpu.SemaphoreType.DMA((128,)),
            pltpu.SemaphoreType.DMA((128,)),
        ]
        params = dict(collective_id=0, has_side_effects=True)
    else:
        args = (tokens, cotangent, *weights, gains)
        in_specs = [vm] * 7
        extra = []
        params = {}
    return pl.pallas_call(
        functools.partial(compute_kernel, linked),
        out_shape=(
            sds((L, D), bf16),
            sds((L, D), f32),
            sds((parts, D, 3 * hm), grad_type),
            sds((parts, D, fm), grad_type),
            sds((parts, D, hm), grad_type),
            sds((parts, D, fm), grad_type),
            sds((8, D), f32),
        ),
        in_specs=in_specs,
        out_specs=[vm] * 7,
        scratch_shapes=extra + [
            pltpu.VMEM((L, D), bf16),
            pltpu.VMEM((D, L), bf16),
            pltpu.VMEM((L, D), bf16),
            pltpu.VMEM((D, L), bf16),
            pltpu.VMEM((L, D), bf16),
            pltpu.VMEM((D, L), bf16),
            pltpu.VMEM((L, D), bf16),
            pltpu.VMEM((D, L), bf16),
            pltpu.VMEM((parts, L, hm), f32),
            pltpu.VMEM((parts, L, hm), f32),
            pltpu.VMEM((parts, L, hm), f32),
            pltpu.VMEM((parts, L, hm), f32),
            pltpu.VMEM((2 * hm // BLK, L, BLK), f32),
            pltpu.VMEM((L, D), f32),
            pltpu.VMEM((L, D), f32),
            pltpu.VMEM((L, D), f32),
            pltpu.VMEM((L, fm), bf16),
            pltpu.VMEM((L, fm), bf16),
            pltpu.VMEM((L, 3 * hm), bf16),
            pltpu.VMEM((2, SUB, hm), f32),
        ],
        compiler_params=pltpu.CompilerParams(vmem_limit_bytes=63 * 2**20, **params),
        name="block",
    )(*args)


def adam_update(first_old, second_old, gradient):
    first_new = beta_one * first_old + (1.0 - beta_one) * gradient
    second_new = beta_two * second_old + (1.0 - beta_two) * gradient * gradient
    first_hat = first_new / (1.0 - beta_one**STEP)
    second_hat = second_new / (1.0 - beta_two**STEP)
    return (first_new, second_new, first_hat / (jnp.sqrt(second_hat) + adam_eps))


def soap_update(master, moment_one, moment_two, basis_left, basis_right, grads):
    left_side = jnp.einsum("pkab,pkac->pkbc", basis_left, grads, precision=highest)
    rotated = jnp.einsum("pkbc,pkcd->pkbd", left_side, basis_right, precision=highest)
    first_new, second_new, direction = adam_update(moment_one, moment_two, rotated)
    turned = jnp.einsum("pkab,pkbc->pkac", basis_left, direction, precision=highest)
    turned = jnp.einsum("pkac,pkdc->pkad", turned, basis_right, precision=highest)
    master_new = master - learn_rate * (turned + weight_decay * master)
    return (first_new, second_new, master_new)


def on_device(
    tokens,
    cotangent,
    master,
    moment_one,
    moment_two,
    basis_left,
    basis_right,
    owner,
    gains,
    gain_moment_one,
    gain_moment_two,
):
    parts = lax.axis_size("mp")
    data_parts = lax.axis_size("dp")
    hm, fm = H // parts, FF // parts
    token_total = L * data_parts * parts
    row_tiles, cols, lows = D // BLK, (3 * hm + fm) // BLK, (hm + fm) // BLK
    number = jnp.arange(owner.shape[0], dtype=jnp.int32)
    ahead = (owner[None, :] < owner[:, None]) | ((owner[None, :] == owner[:, None]) & (number[None, :] < number[:, None]))
    block_rank = jnp.sum(ahead.astype(jnp.int32), axis=1)
    slot_order = jnp.sum(jnp.where(block_rank[None, :] == number[:, None], number[None, :], 0), axis=1)
    if data_parts == 8 and parts == 4:
        outs = compute(tokens, cotangent, gains, bf16, master=master[0], rank=block_rank)
    else:
        stored = lax.all_gather(master.astype(bf16), "dp", axis=1, tiled=True)
        stored = lax.all_gather(stored, "mp", axis=0, tiled=True)
        stack = stored[:, block_rank]
        upper = stack[:, : row_tiles * cols].reshape(parts, row_tiles, cols, BLK, BLK)
        upper = upper.transpose(0, 1, 3, 2, 4).reshape(parts, D, cols * BLK)
        lower = stack[:, row_tiles * cols :].reshape(parts, lows, row_tiles, BLK, BLK)
        lower = lower.transpose(0, 1, 3, 2, 4).reshape(parts, lows * BLK, D)
        weights = (upper[:, :, : 3 * hm], upper[:, :, 3 * hm :], lower[:, :hm], lower[:, hm:])
        outs = compute(tokens, cotangent, gains, bf16, weights=weights)
    block_out, input_grad, gg, gu, go, gd, small = outs
    upper = jnp.concatenate([gg, gu], axis=2).reshape(parts, row_tiles, BLK, cols, BLK).transpose(0, 1, 3, 2, 4)
    upper = upper.reshape(parts, row_tiles * cols, BLK, BLK)
    lower = jnp.concatenate([go, gd], axis=2).reshape(parts, row_tiles, BLK, lows, BLK).transpose(0, 3, 1, 4, 2)
    lower = lower.reshape(parts, row_tiles * lows, BLK, BLK)
    natural = jnp.concatenate([upper, lower], axis=1).astype(f32)
    owned = lax.psum_scatter(natural[:, slot_order], "dp", scatter_dimension=1, tiled=True)
    owned = lax.psum_scatter(owned, "mp", scatter_dimension=0, tiled=True)
    first_new, second_new, master_new = soap_update(master, moment_one, moment_two, basis_left, basis_right, owned)
    first_row = (lax.axis_index("dp") * parts + lax.axis_index("mp")) * L
    forget_part = (jnp.sum(small[3, :hm]) + (first_row + 1).astype(f32) * jnp.sum(small[2, :hm])) / float(token_total)
    gain_grad, forget_total = lax.psum((small[:2], forget_part), ("dp", "mp"))
    gain_first, gain_second, gain_direction = adam_update(gain_moment_one, gain_moment_two, gain_grad)
    gains_new = gains - gain_rate * gain_direction
    forget_mean = forget_total / (H * (token_total + 1) / 2.0)
    return (
        block_out,
        input_grad,
        first_new,
        second_new,
        master_new,
        master_new.astype(bf16),
        gain_first,
        gain_second,
        gains_new,
        forget_mean,
    )


def solution(mesh):
    rows, blocks = P(("dp", "mp"), None), P("mp", "dp", None, None)
    return jax.shard_map(
        on_device,
        mesh=mesh,
        in_specs=(rows, rows, blocks, blocks, blocks, blocks, blocks, P(), P(), P(), P()),
        out_specs=(rows, rows, blocks, blocks, blocks, blocks, P(), P(), P(), P()),
        check_vma=False,
    )
```

```python
import functools

import jax
import jax.numpy as jnp
from jax import lax
from jax.experimental import pallas as pl
from jax.experimental.pallas import tpu as pltpu
from jax.sharding import PartitionSpec as P

D = 512
H = 1024
FF = 2048
BLK = 128
STEP = 10
L = 1024

norm_eps = 1e-05
beta_one = 0.5
beta_two = 0.5
adam_eps = 1e-08
learn_rate = 0.02
gain_rate = 0.1
weight_decay = 0.1
highest = lax.Precision.HIGHEST

f32 = jnp.float32
bf16 = jnp.bfloat16
SUB = 8
J = L // SUB
R = 256


def dot(a, b, trans_b=False):
    dims = (((1,), (1,)), ((), ())) if trans_b else (((1,), (0,)), ((), ()))
    return lax.dot_general(a, b, dims, preferred_element_type=f32)


def recip(v):
    return pltpu.reciprocal(v, approx=True)


def sigmoid(v):
    return recip(1.0 + jnp.exp(-v))


def shift_down(v):
    rolled = pltpu.roll(v, 1, 0)
    row = lax.broadcasted_iota(jnp.int32, v.shape, 0)
    return jnp.where(row == 0, 0.0, rolled)


def shift_up(v):
    rolled = pltpu.roll(v, SUB - 1, 0)
    row = lax.broadcasted_iota(jnp.int32, v.shape, 0)
    return jnp.where(row == SUB - 1, 0.0, rolled)


def gelu_terms(x):
    a = jnp.abs(x)
    t = recip(1.0 + a * (0.3275911 * 0.7071067811865476))
    poly = t * (
        0.5 * 0.254829592
        + t
        * (
            0.5 * -0.284496736
            + t * (0.5 * 1.421413741 + t * (0.5 * -1.453152027 + t * (0.5 * 1.061405429)))
        )
    )
    e = jnp.exp(x * x * -0.5)
    tail = poly * e
    cdf = jnp.where(x < 0.0, tail, 1.0 - tail)
    return cdf, x * e * 0.3989422804014327


MESH = pl.DeviceIdType.MESH


class Exchange:
    def __init__(self, send, recv):
        self.send, self.recv, self.used, self.open = send, recv, 0, []

    def start(self, src, dst, device):
        k = self.used
        self.used += 1
        copy = pltpu.make_async_remote_copy(
            src_ref=src,
            dst_ref=dst,
            send_sem=self.send.at[k],
            recv_sem=self.recv.at[k],
            device_id=device,
            device_id_type=MESH,
        )
        copy.start()
        self.open.append(copy)
        return copy

    def drain(self):
        for copy in self.open:
            copy.wait_send()
        self.open = []


class Gather:
    def __init__(self, net, master, rank, slots, weights):
        self.net, self.slots, self.weights, self.rank = net, slots, weights, rank
        d, m = lax.axis_index("dp"), lax.axis_index("mp")
        core, col, row = d % 2, (d // 2) % 2, d // 4
        self.me, self.m, self.side = d, m, core
        self.core = d + 1 - 2 * core
        self.plane = [d + 2 - 4 * col, d + 4 - 8 * row, d + 6 - 4 * col - 8 * row]
        self.order = [m, m + 1 - 2 * (m % 2), m + 2 - 4 * (m // 2), 3 - m]
        barrier = pltpu.get_barrier_semaphore()
        for device in [(e, m) for e in [self.core] + self.plane] + [(d, k) for k in self.order[1:]]:
            pl.semaphore_signal(barrier, inc=1, device_id=device, device_id_type=MESH)
        owned = master.shape[0]
        self.owned = owned
        for s in range(owned):
            slots[d * owned + s] = master[s].astype(bf16)
        pl.semaphore_wait(barrier, 7)

    def rows(self, e, first, count):
        return self.slots.at[pl.ds(e * self.owned + first, count)]

    def plane_start(self):
        n, m, (x, y, _) = self.owned, self.m, self.plane
        h = n // 2
        self.first = {}
        for e, first in ((x, 0), (y, h), (x, h), (y, 0)):
            ref = self.rows(self.me, first, h)
            self.first[(e is y, first)] = self.net.start(ref, ref, (e, m))
        ref = self.rows(self.me, 0, n)
        self.sibling = [self.net.start(ref, ref, (self.core, m))]

    def plane_finish(self):
        n, m, (x, y, z) = self.owned, self.m, self.plane
        h = n // 2
        self.first[(False, 0)].wait_recv()
        ref = self.rows(x, 0, h)
        last = [self.net.start(ref, ref, (y, m))]
        self.first[(True, h)].wait_recv()
        ref = self.rows(y, h, h)
        last.append(self.net.start(ref, ref, (x, m)))
        self.first[(False, h)].wait_recv()
        ref = self.rows(x, 0, n)
        self.sibling.append(self.net.start(ref, ref, (self.core, m)))
        self.first[(True, 0)].wait_recv()
        ref = self.rows(y, 0, n)
        self.sibling.append(self.net.start(ref, ref, (self.core, m)))
        for copy in last:
            copy.wait_recv()
        ref = self.rows(z, 0, n)
        self.sibling.append(self.net.start(ref, ref, (self.core, m)))
        for copy in self.sibling:
            copy.wait_recv()

    def place(self, kinds):
        wg, wo, wu, wd = self.weights
        parts, _, hm3 = wg.shape
        row_tiles, gates = D // BLK, hm3 // BLK
        cols, outs = gates + wu.shape[2] // BLK, wo.shape[1] // BLK
        for b in range(self.slots.shape[0]):
            if b < row_tiles * cols:
                r, c = b // cols, b % cols
                kind, ref = (0, wg) if c < gates else (2, wu)
                c -= 0 if c < gates else gates
            else:
                r, c = (b - row_tiles * cols) // row_tiles, (b - row_tiles * cols) % row_tiles
                kind, ref = (1, wo) if r < outs else (3, wd)
                r -= 0 if r < outs else outs
            if kind in kinds:
                ref[self.m, r * BLK : (r + 1) * BLK, c * BLK : (c + 1) * BLK] = self.slots[self.rank[b]]

    def share(self, kind, k, e):
        ref = self.weights[kind]
        size = ref.shape[1] // 8
        return ref.at[k, pl.ds(pl.multiple_of(e * size, size), size)]

    def along_start(self, kind):
        self.along = getattr(self, "along", {})
        for i in (1, 2, 3):
            ref = self.share(kind, self.m, self.me)
            self.along[kind, i] = self.net.start(ref, ref, (self.me, self.order[i]))

    def spread(self, kind, i):
        self.spreads = getattr(self, "spreads", {})
        self.along[kind, i].wait_recv()
        ref = self.share(kind, self.order[i], self.me)
        self.spreads[kind, i] = (
            [self.net.start(ref, ref, (e, self.m)) for e in self.plane],
            [self.net.start(ref, ref, (self.core, self.m))],
        )

    def pair(self, kind, i):
        across, inside = self.spreads[kind, i]
        for copy, e in zip(across, self.plane):
            copy.wait_recv()
            ref = self.share(kind, self.order[i], e)
            inside.append(self.net.start(ref, ref, (self.core, self.m)))

    def ready(self, kind, i):
        for copy in self.spreads[kind, i][1]:
            copy.wait_recv()


class Reduce:
    def __init__(self, net, gather, grads, spans, inside, across, along):
        self.net, self.g, self.grads, self.spans = net, gather, grads, spans
        self.inside, self.across, self.along = inside, across, along
        self.size = grads.shape[1] // 8
        self.copies = {}

    def place(self, e):
        return (e % 2) * 4 + e // 2

    def rows(self, first, count):
        return pl.ds(pl.multiple_of(first * self.size, self.size), count * self.size)

    def chip(self, kind, i):
        g, cols = self.g, self.spans[kind]
        src = self.grads.at[g.order[i], self.rows((1 - g.side) * 4, 4), cols]
        dst = self.inside.at[i - 1, :, cols]
        self.copies[0, kind, i] = self.net.start(src, dst, (g.core, g.m))

    def plane(self, kind, i):
        g, cols = self.g, self.spans[kind]
        self.copies[0, kind, i].wait_recv()
        m = g.order[i]
        rows = self.rows(g.side * 4, 4)
        total = self.grads[m, rows, cols].astype(f32) + self.inside[i - 1, :, cols].astype(f32)
        self.grads[m, rows, cols] = total.astype(bf16)
        for k, e in enumerate(g.plane):
            src = self.grads.at[m, self.rows(self.place(e), 1), cols]
            self.copies[1, kind, i, k] = self.net.start(src, self.across.at[i - 1, k, :, cols], (e, g.m))

    def model(self, kind, i):
        g, cols = self.g, self.spans[kind]
        m = g.order[i]
        rows = self.rows(self.place(g.me), 1)
        total = self.grads[m, rows, cols].astype(f32)
        for k in range(3):
            self.copies[1, kind, i, k].wait_recv()
            total += self.across[i - 1, k, :, cols].astype(f32)
        self.grads[m, rows, cols] = total.astype(bf16)
        src = self.grads.at[m, rows, cols]
        self.copies[2, kind, i] = self.net.start(src, self.along.at[i - 1, :, cols], (g.me, m))

    def own(self, kind):
        g, cols = self.g, self.spans[kind]
        rows = self.rows(self.place(g.me), 1)
        total = self.grads[g.m, rows, cols].astype(f32)
        for i in (1, 2, 3):
            self.copies[2, kind, i].wait_recv()
            total += self.along[i - 1, :, cols].astype(f32)
        self.grads[g.m, rows, cols] = total.astype(bf16)

    def into_slots(self, stack, out, slot_order):
        g = self.g
        row_tiles = D // BLK
        gate, outs, ups, downs = self.spans
        cols = (gate.stop - gate.start + ups.stop - ups.start) // BLK
        gates, lows = gate.stop // BLK, (outs.stop - outs.start) // BLK
        for b in range(stack.shape[0]):
            if b < row_tiles * cols:
                r, c = b // cols, b % cols
                first = c * BLK if c < gates else ups.start + (c - gates) * BLK
            else:
                k, r = (b - row_tiles * cols) // row_tiles, (b - row_tiles * cols) % row_tiles
                first = outs.start + k * BLK if k < lows else downs.start + (k - lows) * BLK
            stack[b] = self.grads[g.m, r * BLK : (r + 1) * BLK, first : first + BLK]
        n = stack.shape[0] // 8
        for s in range(stack.shape[0]):
            out[self.place(s // n) * n + s % n] = stack[slot_order[s]]

    def slots_chip(self, out, pair):
        g, n = self.g, out.shape[0] // 8
        self.last = []
        for e in (g.plane[2], g.plane[0], g.plane[1], g.me):
            src = out.at[pl.ds(((1 - g.side) * 4 + e // 2) * n, n)]
            self.last.append(self.net.start(src, pair.at[pl.ds((e // 2) * n, n)], (g.core, g.m)))

    def slots_plane(self, out, pair, far):
        g, n = self.g, out.shape[0] // 8
        self.ends = []
        for copy, e, k in zip(self.last, (g.plane[2], g.plane[0], g.plane[1]), (2, 0, 1)):
            copy.wait_recv()
            rows = pl.ds((g.side * 4 + e // 2) * n, n)
            out[rows] = (out[rows].astype(f32) + pair[pl.ds((e // 2) * n, n)].astype(f32)).astype(bf16)
            self.ends.append(self.net.start(out.at[rows], far.at[k], (e, g.m)))
        self.last[3].wait_recv()

    def slots_end(self, out, pair, far, owned):
        g, n = self.g, out.shape[0] // 8
        total = out[pl.ds((g.side * 4 + g.me // 2) * n, n)].astype(f32)
        total += pair[pl.ds((g.me // 2) * n, n)].astype(f32)
        for copy in self.ends:
            copy.wait_recv()
        for k in range(3):
            total += far[k].astype(f32)
        owned[...] = total


class SmallSum:
    def __init__(self, net, gather, values, along, across, inside):
        self.net, self.g, self.values = net, gather, values
        self.slots = (along, across, inside)
        self.peers = (
            [(gather.me, k) for k in gather.order[1:]],
            [(e, gather.m) for e in gather.plane],
            [(gather.core, gather.m)],
        )
        self.mine = (gather.m, gather.me // 2, gather.side)
        self.open = []

    def send(self, stage):
        slot = self.slots[stage]
        slot[self.mine[stage]] = self.values[...]
        ref = slot.at[self.mine[stage]]
        self.open = [self.net.start(ref, ref, peer) for peer in self.peers[stage]]

    def add(self, stage):
        for copy in self.open:
            copy.wait_recv()
        slot = self.slots[stage]
        total = slot[0]
        for k in range(1, slot.shape[0]):
            total += slot[k]
        self.values[...] = total


def compute_kernel(linked, *refs):
    if linked:
        tokens, cotangent, master, rank, slot_order, gains = refs[:6]
        block_out, input_grad, owned, small = refs[6:10]
        wg, wo, wu, wd, grads, slots, turned, pair, far, inside, across, along, sum_a, sum_b, sum_c, send, recv = refs[10:27]
        scratch = refs[27:]
    else:
        tokens, cotangent, base, wg, wo, wu, wd, gains = refs[:8]
        block_out, input_grad, grads, small = refs[8:12]
        scratch = refs[12:]
    (n1, n1t, cot, cott, n2, n2t, forget, admit, cand, state, scan, acc_a, acc_b, mixed, mid, fills, local) = scratch
    dml, dmlt = n2, n2t
    parts, _, hm3 = wg.shape
    hm = hm3 // 3
    fm = wu.shape[2]
    spans = (slice(0, 3 * hm), slice(3 * hm, 4 * hm), slice(4 * hm, 4 * hm + fm), slice(4 * hm + fm, 4 * hm + 2 * fm))
    gate, outs, ups, downs = spans
    act, dup, dpre = mid.at[:, :fm], mid.at[:, fm:], mid.at[:, : 3 * hm]
    gain_one = gains[0:1, :]
    gain_two = gains[1:2, :]

    fetch_cot = pltpu.make_async_copy(cotangent, cot, local.at[0])
    fetch_tok = pltpu.make_async_copy(tokens, n1, local.at[1])
    fetch_cot.start()
    fetch_tok.start()

    def permute_in(src, dst):
        for k in range(D // BLK):
            scan[k] = src[:, k * BLK : (k + 1) * BLK].astype(f32)

        @pl.loop(0, J // 2, unroll=4)
        def _(j):
            for k in range(D // BLK):
                lo = scan[k, pl.ds(2 * j, SUB, stride=J), :]
                hi = scan[k, pl.ds(2 * j + 1, SUB, stride=J), :]
                dst[pl.ds(pl.multiple_of(16 * j, 16), 16), k * BLK : (k + 1) * BLK] = jnp.concatenate([lo, hi], 0).astype(bf16)

    def permute_out(src, dst):
        @pl.loop(0, J, unroll=4)
        def _(j):
            rows = pl.ds(pl.multiple_of(j * SUB, SUB), SUB)
            for k in range(D // BLK):
                scan[k, pl.ds(j, SUB, stride=J), :] = src[rows, k * BLK : (k + 1) * BLK]

        for k in range(D // BLK):
            dst[:, k * BLK : (k + 1) * BLK] = scan[k].astype(dst.dtype)

    def put(first, rows, value):
        for k in range(hm // BLK):
            scan[first + k, rows, :] = value[:, k * BLK : (k + 1) * BLK]

    def take(first, rows):
        return jnp.concatenate([scan[first + k, rows, :] for k in range(hm // BLK)], 1)

    half = hm // BLK

    if linked:
        net = Exchange(send, recv)
        gather = Gather(net, master, rank, slots, (wg, wo, wu, wd))
        gather.plane_start()
        reduce = Reduce(net, gather, grads, spans, inside, across, along)
        order = gather.order
    else:
        order = list(range(parts))

    fetch_cot.wait()
    permute_in(cot, cot)
    cott[...] = cot[...].T
    fetch_tok.wait()
    permute_in(n1, n1)
    mixed[...] = n1[...].astype(f32)

    @pl.loop(0, L // R)
    def _(i):
        rows = pl.ds(pl.multiple_of(i * R, R), R)
        x = mixed[rows, :]
        r = lax.rsqrt(jnp.mean(x * x, axis=-1, keepdims=True) + norm_eps)
        n1[rows, :] = (x * r * gain_one).astype(bf16)

    n1t[...] = n1[...].T

    if linked:
        gather.plane_finish()
        gather.place((0,))
        gather.along_start(0)
        gather.place((1, 2, 3))
        for kind in (1, 2, 3):
            gather.along_start(kind)

    fills[0] = jnp.zeros((SUB, hm), f32)
    fills[1] = jnp.ones((SUB, hm), f32)
    weigh = fills[0]
    weigh_j = fills[0]
    for turn, m in enumerate(order):

        if linked and turn:
            gather.ready(0, turn)

        @pl.loop(0, L // R)
        def _(i):
            rows = pl.ds(pl.multiple_of(i * R, R), R)
            x = n1[rows, :]
            forget[m, rows, :] = dot(x, wg[m, :, :hm])
            admit[m, rows, :] = dot(x, wg[m, :, hm : 2 * hm])
            cand[m, rows, :] = dot(x, wg[m, :, 2 * hm :])

        if linked and turn == 0:
            for i in (1, 2, 3):
                gather.spread(0, i)
        if linked and turn == 2:
            gather.pair(0, 3)
        if linked and turn == 1:
            for i in (1, 2, 3):
                gather.spread(1, i)
        if linked and turn == 2:
            for kind, i in ((2, 1), (3, 1), (2, 2), (3, 2), (2, 3), (3, 3)):
                gather.spread(kind, i)
        if linked and turn == 3:
            for i in (1, 2, 3):
                gather.pair(1, i)

        def step(j, carry):
            s, p, k_sum, kj_sum = carry
            rows = pl.ds(pl.multiple_of(j * SUB, SUB), SUB)
            f = sigmoid(forget[m, rows, :])
            a = sigmoid(admit[m, rows, :])
            inv = recip(f + a)
            keep = f * inv
            s = keep * s + a * inv * cand[m, rows, :]
            p = keep * p
            forget[m, rows, :] = f
            admit[m, rows, :] = a
            put(0, rows, s)
            put(half, rows, p)
            return s, p, k_sum + keep, kj_sum + keep * j.astype(f32)

        s, p, weigh, weigh_j = lax.fori_loop(
            0,
            J,
            step,
            (fills[0], fills[1], weigh, weigh_j),
            unroll=4,
        )
        enter = fills[0]
        for _ in range(SUB - 1):
            enter = shift_down(s + p * enter)

        if linked and turn == 0:
            gather.pair(0, 1)
        if linked and turn == 1:
            gather.pair(0, 2)

        @pl.loop(0, J, unroll=4)
        def _(j):
            rows = pl.ds(pl.multiple_of(j * SUB, SUB), SUB)
            state[m, rows, :] = take(0, rows) + take(half, rows) * enter

    if linked:
        for i in (1, 2, 3):
            gather.ready(1, i)
        for kind in (2, 3):
            gather.pair(kind, 1)

    @pl.loop(0, L // R)
    def _(i):
        rows = pl.ds(pl.multiple_of(i * R, R), R)
        x = mixed[rows, :]
        for m in range(parts):
            x += dot(state[m, rows, :].astype(bf16), wo[m])
        mixed[rows, :] = x
        r = lax.rsqrt(jnp.mean(x * x, axis=-1, keepdims=True) + norm_eps)
        n2[rows, :] = (x * r * gain_two).astype(bf16)
        acc_a[rows, :] = x
        acc_b[rows, :] = jnp.zeros_like(x)

    n2t[...] = n2[...].T

    for turn, m in enumerate(order):

        if linked and turn:
            gather.ready(2, turn)
            gather.ready(3, turn)

        @pl.loop(0, L // R)
        def _(i):
            rows = pl.ds(pl.multiple_of(i * R, R), R)
            up = dot(n2[rows, :], wu[m])
            da = dot(cot[rows, :], wd[m], True)
            cdf, xpdf = gelu_terms(up)
            ac = (up * cdf).astype(bf16)
            du = (da * (cdf + xpdf)).astype(bf16)
            act[rows, :] = ac
            dup[rows, :] = du
            acc_a[rows, :] += dot(ac, wd[m])
            acc_b[rows, :] += dot(du, wu[m], True)

        if linked and turn < 2:
            gather.pair(2, turn + 2)
            gather.pair(3, turn + 2)
        if linked and turn >= 2:
            reduce.plane(2, turn - 1)
            reduce.plane(3, turn - 1)
        if linked and turn == 3:
            reduce.model(2, 1)
            reduce.model(3, 1)
        grads[m, :, downs] = dot(cott[...], act[...]).astype(bf16)
        grads[m, :, ups] = dot(n2t[...], dup[...]).astype(bf16)
        if linked and turn:
            reduce.chip(2, turn)
            reduce.chip(3, turn)

    permute_out(acc_a, n1)
    push_out = pltpu.make_async_copy(n1, block_out, local.at[0])
    push_out.start()

    if linked:
        for kind in (2, 3):
            reduce.plane(kind, 3)
            reduce.model(kind, 2)

    gain_sum_two = jnp.zeros((1, D), f32)

    def back_two(i, total):
        rows = pl.ds(pl.multiple_of(i * R, R), R)
        x = mixed[rows, :]
        r = lax.rsqrt(jnp.mean(x * x, axis=-1, keepdims=True) + norm_eps)
        dn = acc_b[rows, :]
        q = dn * gain_two
        d = cot[rows, :].astype(f32) + r * q - r * r * r * x * jnp.mean(q * x, axis=-1, keepdims=True)
        mixed[rows, :] = d
        dml[rows, :] = d.astype(bf16)
        acc_b[rows, :] = jnp.zeros_like(d)
        return total + jnp.sum(dn * x * r, axis=0, keepdims=True)

    gain_sum_two = lax.fori_loop(0, L // R, back_two, gain_sum_two)
    dmlt[...] = dml[...].T
    fetch_tok = pltpu.make_async_copy(tokens, cot, local.at[1])
    fetch_tok.start()

    for turn, m in reversed(list(enumerate(order))):

        @pl.loop(0, L // R)
        def _(i):
            rows = pl.ds(pl.multiple_of(i * R, R), R)
            put(0, rows, dot(dml[rows, :], wo[m], True))

        def step(k, carry):
            u, p, keep_next = carry
            j = J - 1 - k
            rows = pl.ds(pl.multiple_of(j * SUB, SUB), SUB)
            u = take(0, rows) + keep_next * u
            p = keep_next * p
            put(0, rows, u)
            put(half, rows, p)
            f = forget[m, rows, :]
            return u, p, f * recip(f + admit[m, rows, :])

        u, p, keep_first = lax.fori_loop(
            0,
            J,
            step,
            (fills[0], fills[1], fills[1]),
            unroll=4,
        )
        enter = fills[0]
        for _ in range(SUB - 1):
            enter = shift_up(keep_first * (u + p * enter))

        def back(i, before):
            parts_out = []
            for h in range(2):
                rows = pl.ds(pl.multiple_of(i * 2 * SUB + h * SUB, SUB), SUB)
                carried = take(0, rows) + take(half, rows) * enter
                f = forget[m, rows, :]
                a = admit[m, rows, :]
                inv = recip(f + a)
                adm = a * inv
                g = carried * (before - cand[m, rows, :]) * (f * inv * adm)
                parts_out.append((g * (1.0 - f), g * (a - 1.0), carried * adm))
                before = state[m, rows, :]
            both = pl.ds(pl.multiple_of(i * 2 * SUB, 2 * SUB), 2 * SUB)
            for k in range(3):
                dpre[both, k * hm : (k + 1) * hm] = jnp.concatenate(
                    [parts_out[0][k], parts_out[1][k]], 0
                ).astype(bf16)
            return before

        last = state[m, pl.ds(L - SUB, SUB), :]
        lax.fori_loop(0, J // 2, back, shift_down(last), unroll=2)

        if linked:
            if turn == 3:
                for kind in (2, 3):
                    reduce.model(kind, 3)
            if turn == 1:
                for kind in (0, 1):
                    reduce.model(kind, 3)
            if turn == 0:
                for kind in (0, 1):
                    reduce.model(kind, 2)
            if turn < 3:
                for kind in (0, 1):
                    reduce.plane(kind, turn + 1)
        grads[m, :, gate] = dot(n1t[...], dpre[...]).astype(bf16)
        grads[m, :, outs] = dot(dmlt[...], state[m].astype(bf16)).astype(bf16)
        if linked and turn:
            for kind in (0, 1):
                reduce.chip(kind, turn)

        @pl.loop(0, L // R)
        def _(i):
            rows = pl.ds(pl.multiple_of(i * R, R), R)
            acc_b[rows, :] += dot(dpre[rows, :], wg[m], True)

    fetch_tok.wait()
    permute_in(cot, cot)

    if linked:
        for kind in (0, 1):
            reduce.model(kind, 1)
        for kind in (2, 3):
            reduce.own(kind)

    def back_one(i, total):
        rows = pl.ds(pl.multiple_of(i * R, R), R)
        x = cot[rows, :].astype(f32)
        r = lax.rsqrt(jnp.mean(x * x, axis=-1, keepdims=True) + norm_eps)
        dn = acc_b[rows, :]
        q = dn * gain_one
        mixed[rows, :] += r * q - r * r * r * x * jnp.mean(q * x, axis=-1, keepdims=True)
        return total + jnp.sum(dn * x * r, axis=0, keepdims=True)

    gain_sum_one = lax.fori_loop(0, L // R, back_one, jnp.zeros((1, D), f32))

    place = lax.broadcasted_iota(jnp.int32, (SUB, hm), 0).astype(f32) * float(J)
    if linked:
        first = ((gather.me * parts + gather.m) * L + 1).astype(f32)
        token_total = float(L * parts * lax.axis_size("dp"))
    else:
        first = base[0]
        token_total = base[1]
    forget_sum = jnp.sum(weigh_j + weigh * (place + first), axis=0, keepdims=True) / token_total
    small[...] = jnp.zeros_like(small)
    small[0:1, :] = gain_sum_one
    small[1:2, :] = gain_sum_two
    small[2:3, :hm] = forget_sum

    if linked:
        tiny = SmallSum(net, gather, small, sum_a, sum_b, sum_c)
        tiny.send(0)
        for kind in (0, 1):
            reduce.own(kind)
        net.drain()
        reduce.into_slots(slots, turned, slot_order)
        reduce.slots_chip(turned, pair)
        tiny.add(0)
        tiny.send(1)
        reduce.slots_plane(turned, pair, far)

    permute_out(mixed, acc_a)
    push_grad = pltpu.make_async_copy(acc_a, input_grad, local.at[2])
    push_grad.start()

    if linked:
        tiny.add(1)
        tiny.send(2)
        reduce.slots_end(turned, pair, far, owned)
        tiny.add(2)
        net.drain()
    push_out.wait()
    push_grad.wait()


def compute(tokens, cotangent, gains, weights=None, base=None, master=None, rank=None, slot_order=None):
    linked = weights is None
    parts = lax.axis_size("mp")
    hm, fm = H // parts, FF // parts
    wide = 4 * hm + 2 * fm
    sds = jax.ShapeDtypeStruct
    vm, sm, hbm = (pl.BlockSpec(memory_space=k) for k in (pltpu.VMEM, pltpu.SMEM, pl.ANY))
    if linked:
        n = rank.shape[0]
        args = (tokens, cotangent, master, rank, slot_order, gains)
        in_specs = [hbm, hbm, vm, sm, sm, vm]
        middle = sds((n // 8, BLK, BLK), f32)
        extra = [
            pltpu.VMEM((parts, D, 3 * hm), bf16),
            pltpu.VMEM((parts, hm, D), bf16),
            pltpu.VMEM((parts, D, fm), bf16),
            pltpu.VMEM((parts, fm, D), bf16),
            pltpu.VMEM((parts, D, wide), bf16),
            pltpu.VMEM((n, BLK, BLK), bf16),
            pltpu.VMEM((n, BLK, BLK), bf16),
            pltpu.VMEM((n // 2, BLK, BLK), bf16),
            pltpu.VMEM((3, n // 8, BLK, BLK), bf16),
            pltpu.VMEM((3, D // 2, wide), bf16),
            pltpu.VMEM((3, 3, D // 8, wide), bf16),
            pltpu.VMEM((3, D // 8, wide), bf16),
            pltpu.VMEM((parts, 8, D), f32),
            pltpu.VMEM((4, 8, D), f32),
            pltpu.VMEM((2, 8, D), f32),
            pltpu.SemaphoreType.DMA((256,)),
            pltpu.SemaphoreType.DMA((256,)),
        ]
        params = dict(collective_id=0, has_side_effects=True)
    else:
        args = (tokens, cotangent, base, *weights, gains)
        in_specs = [hbm, hbm, sm] + [vm] * 5
        middle = sds((parts, D, wide), bf16)
        extra = []
        params = {}
    return pl.pallas_call(
        functools.partial(compute_kernel, linked),
        out_shape=(sds((L, D), bf16), sds((L, D), f32), middle, sds((8, D), f32)),
        in_specs=in_specs,
        out_specs=[hbm, hbm, vm, vm],
        scratch_shapes=extra
        + [pltpu.VMEM(shape, bf16) for shape in ((L, D), (D, L)) * 3]
        + [pltpu.VMEM((parts, L, hm), f32)] * 4
        + [pltpu.VMEM((2 * hm // BLK, L, BLK), f32)]
        + [pltpu.VMEM((L, D), f32)] * 3
        + [
            pltpu.VMEM((L, 2 * fm), bf16),
            pltpu.VMEM((2, SUB, hm), f32),
            pltpu.SemaphoreType.DMA((3,)),
        ],
        compiler_params=pltpu.CompilerParams(vmem_limit_bytes=64 * 2**20 - 2**16, **params),
        name="block",
    )(*args)


def adam_update(first_old, second_old, gradient):
    first_new = beta_one * first_old + (1.0 - beta_one) * gradient
    second_new = beta_two * second_old + (1.0 - beta_two) * gradient * gradient
    first_hat = first_new / (1.0 - beta_one**STEP)
    second_hat = second_new / (1.0 - beta_two**STEP)
    return (first_new, second_new, first_hat / (jnp.sqrt(second_hat) + adam_eps))


def fine_dot(a, b, trans_b=False):
    a_high, b_high = a.astype(bf16), b.astype(bf16)
    a_low, b_low = (a - a_high.astype(f32)).astype(bf16), (b - b_high.astype(f32)).astype(bf16)
    return dot(a_high, b_high, trans_b) + (dot(a_high, b_low, trans_b) + dot(a_low, b_high, trans_b))


def update_kernel(
    low_first,
    token_total,
    low,
    owned,
    master,
    moment_one,
    moment_two,
    basis_left,
    basis_right,
    sums,
    gains,
    gain_moment_one,
    gain_moment_two,
    first_new,
    second_new,
    master_new,
    master_low,
    gain_first,
    gain_second,
    gains_new,
    forget_mean,
):
    for s in range(master.shape[0]):
        grad = owned[s]
        grad = jnp.where(low[s] >= low_first, grad.T, grad)
        left, right = basis_left[s], basis_right[s]
        rotated = fine_dot(fine_dot(left.T, grad), right)
        first, second, direction = adam_update(moment_one[s], moment_two[s], rotated)
        first_new[s] = first
        second_new[s] = second
        turned = fine_dot(fine_dot(left, direction), right, True)
        fresh = master[s] - learn_rate * (turned + weight_decay * master[s])
        master_new[s] = fresh
        master_low[s] = fresh.astype(bf16)
    first, second, direction = adam_update(gain_moment_one[...], gain_moment_two[...], sums[0:2, :])
    gain_first[...] = first
    gain_second[...] = second
    gains_new[...] = gains[...] - gain_rate * direction
    forget_mean[...] = jnp.sum(sums[2:3, :], axis=1, keepdims=True) * (1.0 / (H * (token_total + 1) / 2.0))


def update(low_first, token_total, *args):
    sds = jax.ShapeDtypeStruct
    blocks, gain = args[1].shape, args[8].shape
    vm = pl.BlockSpec(memory_space=pltpu.VMEM)
    return pl.pallas_call(
        functools.partial(update_kernel, low_first, token_total),
        out_shape=[sds(blocks, f32)] * 3 + [sds(blocks, bf16)] + [sds(gain, f32)] * 3 + [sds((1, 1), f32)],
        in_specs=[pl.BlockSpec(memory_space=pltpu.SMEM)] + [vm] * (len(args) - 1),
        out_specs=[vm] * 8,
        compiler_params=pltpu.CompilerParams(vmem_limit_bytes=32 * 2**20),
        name="update",
    )(*args)


def on_device(
    tokens,
    cotangent,
    master,
    moment_one,
    moment_two,
    basis_left,
    basis_right,
    owner,
    gains,
    gain_moment_one,
    gain_moment_two,
):
    parts = lax.axis_size("mp")
    data_parts = lax.axis_size("dp")
    hm, fm = H // parts, FF // parts
    token_total = L * data_parts * parts
    row_tiles, cols, lows = D // BLK, (3 * hm + fm) // BLK, (hm + fm) // BLK
    blocks = owner.shape[0]
    number = jnp.arange(blocks, dtype=jnp.int32)
    ahead = (owner[None, :] < owner[:, None]) | ((owner[None, :] == owner[:, None]) & (number[None, :] < number[:, None]))
    block_rank = jnp.sum(ahead.astype(jnp.int32), axis=1)
    slot_order = jnp.sum(jnp.where(block_rank[None, :] == number[:, None], number[None, :], 0), axis=1)
    if data_parts == 8 and parts == 4:
        block_out, input_grad, owned, sums = compute(
            tokens, cotangent, gains, master=master[0], rank=block_rank, slot_order=slot_order
        )
    else:
        stored = lax.all_gather(master.astype(bf16), "dp", axis=1, tiled=True)
        stored = lax.all_gather(stored, "mp", axis=0, tiled=True)
        stack = stored[:, block_rank]
        upper = stack[:, : row_tiles * cols].reshape(parts, row_tiles, cols, BLK, BLK)
        upper = upper.transpose(0, 1, 3, 2, 4).reshape(parts, D, cols * BLK)
        lower = stack[:, row_tiles * cols :].reshape(parts, lows, row_tiles, BLK, BLK)
        lower = lower.transpose(0, 1, 3, 2, 4).reshape(parts, lows * BLK, D)
        weights = (upper[:, :, : 3 * hm], lower[:, :hm], upper[:, :, 3 * hm :], lower[:, hm:])
        first = ((lax.axis_index("dp") * parts + lax.axis_index("mp")) * L + 1).astype(f32)
        base = jnp.stack([first, jnp.asarray(token_total, f32)])
        block_out, input_grad, grads, sums = compute(tokens, cotangent, gains, weights=weights, base=base)
        upper = jnp.concatenate([grads[:, :, : 3 * hm], grads[:, :, 4 * hm : 4 * hm + fm]], axis=2)
        upper = upper.reshape(parts, row_tiles, BLK, cols, BLK).transpose(0, 1, 3, 2, 4)
        lower = jnp.concatenate([grads[:, :, 3 * hm : 4 * hm], grads[:, :, 4 * hm + fm :]], axis=2)
        lower = lower.reshape(parts, row_tiles, BLK, lows, BLK).transpose(0, 3, 1, 2, 4)
        natural = jnp.concatenate(
            [upper.reshape(parts, -1, BLK, BLK), lower.reshape(parts, -1, BLK, BLK)], axis=1
        ).astype(f32)
        owned = lax.psum_scatter(natural[:, slot_order], "dp", scatter_dimension=1, tiled=True)
        owned = lax.psum_scatter(owned, "mp", scatter_dimension=0, tiled=True)[0]
        sums = lax.psum(sums, ("dp", "mp"))
    mine = lax.dynamic_slice_in_dim(slot_order, lax.axis_index("dp") * master.shape[1], master.shape[1])
    first_new, second_new, master_new, master_low, gain_first, gain_second, gains_new, forget_mean = update(
        row_tiles * cols,
        token_total,
        mine,
        owned,
        master[0],
        moment_one[0],
        moment_two[0],
        basis_left[0],
        basis_right[0],
        sums,
        gains,
        gain_moment_one,
        gain_moment_two,
    )
    return (
        block_out,
        input_grad,
        first_new[None],
        second_new[None],
        master_new[None],
        master_low[None],
        gain_first,
        gain_second,
        gains_new,
        forget_mean[0, 0],
    )


def solution(mesh):
    rows, blocks = P(("dp", "mp"), None), P("mp", "dp", None, None)
    return jax.shard_map(
        on_device,
        mesh=mesh,
        in_specs=(rows, rows, blocks, blocks, blocks, blocks, blocks, P(), P(), P(), P()),
        out_specs=(rows, rows, blocks, blocks, blocks, blocks, P(), P(), P(), P()),
        check_vma=False,
    )
```

```python
import functools

import jax
import jax.numpy as jnp
from jax import lax
from jax.experimental import pallas as pl
from jax.experimental.pallas import tpu as pltpu
from jax.sharding import PartitionSpec as P

D = 512
H = 1024
FF = 2048
BLK = 128
STEP = 10
L = 1024

norm_eps = 1e-05
beta_one = 0.5
beta_two = 0.5
adam_eps = 1e-08
learn_rate = 0.02
gain_rate = 0.1
weight_decay = 0.1
highest = lax.Precision.HIGHEST

f32 = jnp.float32
bf16 = jnp.bfloat16
SUB = 8
J = L // SUB
R = 256


def dot(a, b, trans_b=False):
    dims = (((1,), (1,)), ((), ())) if trans_b else (((1,), (0,)), ((), ()))
    return lax.dot_general(a, b, dims, preferred_element_type=f32)


def recip(v):
    return pltpu.reciprocal(v, approx=True)


def sigmoid(v):
    return recip(1.0 + jnp.exp(-v))


def shift_down(v):
    rolled = pltpu.roll(v, 1, 0)
    row = lax.broadcasted_iota(jnp.int32, v.shape, 0)
    return jnp.where(row == 0, 0.0, rolled)


def shift_up(v):
    rolled = pltpu.roll(v, SUB - 1, 0)
    row = lax.broadcasted_iota(jnp.int32, v.shape, 0)
    return jnp.where(row == SUB - 1, 0.0, rolled)


def gelu_terms(x):
    a = jnp.abs(x)
    t = recip(1.0 + a * (0.3275911 * 0.7071067811865476))
    poly = t * (
        0.5 * 0.254829592
        + t
        * (
            0.5 * -0.284496736
            + t * (0.5 * 1.421413741 + t * (0.5 * -1.453152027 + t * (0.5 * 1.061405429)))
        )
    )
    e = jnp.exp(x * x * -0.5)
    tail = poly * e
    cdf = jnp.where(x < 0.0, tail, 1.0 - tail)
    return cdf, x * e * 0.3989422804014327


MESH = pl.DeviceIdType.MESH


class Exchange:
    def __init__(self, send, recv):
        self.send, self.recv, self.used, self.open = send, recv, 0, []

    def start(self, src, dst, device):
        k = self.used
        self.used += 1
        copy = pltpu.make_async_remote_copy(
            src_ref=src,
            dst_ref=dst,
            send_sem=self.send.at[k],
            recv_sem=self.recv.at[k],
            device_id=device,
            device_id_type=MESH,
        )
        copy.start()
        self.open.append(copy)
        return copy

    def drain(self):
        for copy in self.open:
            copy.wait_send()
        self.open = []


class Gather:
    def __init__(self, net, master, rank, slots, weights):
        self.net, self.slots, self.weights, self.rank = net, slots, weights, rank
        d, m = lax.axis_index("dp"), lax.axis_index("mp")
        core, col, row = d % 2, (d // 2) % 2, d // 4
        self.me, self.m, self.side = d, m, core
        self.core = d + 1 - 2 * core
        self.plane = [d + 2 - 4 * col, d + 4 - 8 * row, d + 6 - 4 * col - 8 * row]
        self.order = [m, m + 1 - 2 * (m % 2), m + 2 - 4 * (m // 2), 3 - m]
        self.along, self.spreads = {}, {}
        barrier = pltpu.get_barrier_semaphore()
        for device in [(e, m) for e in [self.core] + self.plane] + [(d, k) for k in self.order[1:]]:
            pl.semaphore_signal(barrier, inc=1, device_id=device, device_id_type=MESH)
        owned = master.shape[0]
        self.owned = owned
        for s in range(owned):
            slots[d * owned + s] = master[s].astype(bf16)
        pl.semaphore_wait(barrier, 7)

    def rows(self, e, first, count):
        return self.slots.at[pl.ds(e * self.owned + first, count)]

    def plane_start(self):
        n, m, (x, y, _) = self.owned, self.m, self.plane
        h = n // 2
        self.first = {}
        for e, first in ((x, 0), (y, h), (x, h), (y, 0)):
            ref = self.rows(self.me, first, h)
            self.first[(e is y, first)] = self.net.start(ref, ref, (e, m))
        ref = self.rows(self.me, 0, n)
        self.sibling = [self.net.start(ref, ref, (self.core, m))]

    def plane_finish(self):
        n, m, (x, y, z) = self.owned, self.m, self.plane
        h = n // 2
        self.first[(False, 0)].wait_recv()
        ref = self.rows(x, 0, h)
        last = [self.net.start(ref, ref, (y, m))]
        self.first[(True, h)].wait_recv()
        ref = self.rows(y, h, h)
        last.append(self.net.start(ref, ref, (x, m)))
        self.first[(False, h)].wait_recv()
        ref = self.rows(x, 0, n)
        self.sibling.append(self.net.start(ref, ref, (self.core, m)))
        self.first[(True, 0)].wait_recv()
        ref = self.rows(y, 0, n)
        self.sibling.append(self.net.start(ref, ref, (self.core, m)))
        for copy in last:
            copy.wait_recv()
        ref = self.rows(z, 0, n)
        self.sibling.append(self.net.start(ref, ref, (self.core, m)))
        for copy in self.sibling:
            copy.wait_recv()

    def place(self, kinds):
        wg, wo, wu, wd = self.weights
        parts, _, hm3 = wg.shape
        row_tiles, gates = D // BLK, hm3 // BLK
        cols, outs = gates + wu.shape[2] // BLK, wo.shape[1] // BLK
        for b in range(self.slots.shape[0]):
            if b < row_tiles * cols:
                r, c = b // cols, b % cols
                kind, ref = (0, wg) if c < gates else (2, wu)
                c -= 0 if c < gates else gates
            else:
                r, c = (b - row_tiles * cols) // row_tiles, (b - row_tiles * cols) % row_tiles
                kind, ref = (1, wo) if r < outs else (3, wd)
                r -= 0 if r < outs else outs
            if kind in kinds:
                ref[self.m, r * BLK : (r + 1) * BLK, c * BLK : (c + 1) * BLK] = self.slots[self.rank[b]]

    def share(self, kind, k, e):
        ref = self.weights[kind]
        size = ref.shape[1] // 8
        return ref.at[k, pl.ds(pl.multiple_of(e * size, size), size)]

    def along_start(self, kind, i):
        ref = self.share(kind, self.m, self.me)
        self.along[kind, i] = self.net.start(ref, ref, (self.me, self.order[i]))

    def spread(self, kind, i):
        self.along[kind, i].wait_recv()
        ref = self.share(kind, self.order[i], self.me)
        self.spreads[kind, i] = (
            [self.net.start(ref, ref, (e, self.m)) for e in self.plane],
            [self.net.start(ref, ref, (self.core, self.m))],
        )

    def pair(self, kind, i):
        across, inside = self.spreads[kind, i]
        for copy, e in zip(across, self.plane):
            copy.wait_recv()
            ref = self.share(kind, self.order[i], e)
            inside.append(self.net.start(ref, ref, (self.core, self.m)))

    def ready(self, kind, i):
        for copy in self.spreads[kind, i][1]:
            copy.wait_recv()


class Reduce:
    def __init__(self, net, gather, grads, spans, inside, across, along):
        self.net, self.g, self.grads, self.spans = net, gather, grads, spans
        self.inside, self.across, self.along = inside, across, along
        self.size = grads.shape[1] // 8
        self.copies = {}

    def place(self, e):
        return (e % 2) * 4 + e // 2

    def rows(self, first, count):
        return pl.ds(pl.multiple_of(first * self.size, self.size), count * self.size)

    def chip(self, kind, i):
        g, cols = self.g, self.spans[kind]
        src = self.grads.at[g.order[i], self.rows((1 - g.side) * 4, 4), cols]
        dst = self.inside.at[i - 1, :, cols]
        self.copies[0, kind, i] = self.net.start(src, dst, (g.core, g.m))

    def plane(self, kind, i):
        g, cols = self.g, self.spans[kind]
        self.copies[0, kind, i].wait_recv()
        m = g.order[i]
        rows = self.rows(g.side * 4, 4)
        total = self.grads[m, rows, cols].astype(f32) + self.inside[i - 1, :, cols].astype(f32)
        self.grads[m, rows, cols] = total.astype(bf16)
        for k, e in enumerate(g.plane):
            src = self.grads.at[m, self.rows(self.place(e), 1), cols]
            self.copies[1, kind, i, k] = self.net.start(src, self.across.at[i - 1, k, :, cols], (e, g.m))

    def model(self, kind, i):
        g, cols = self.g, self.spans[kind]
        m = g.order[i]
        rows = self.rows(self.place(g.me), 1)
        total = self.grads[m, rows, cols].astype(f32)
        for k in range(3):
            self.copies[1, kind, i, k].wait_recv()
            total += self.across[i - 1, k, :, cols].astype(f32)
        self.grads[m, rows, cols] = total.astype(bf16)
        src = self.grads.at[m, rows, cols]
        self.copies[2, kind, i] = self.net.start(src, self.along.at[i - 1, :, cols], (g.me, m))

    def own(self, kind):
        g, cols = self.g, self.spans[kind]
        rows = self.rows(self.place(g.me), 1)
        total = self.grads[g.m, rows, cols].astype(f32)
        for i in (1, 2, 3):
            self.copies[2, kind, i].wait_recv()
            total += self.along[i - 1, :, cols].astype(f32)
        self.grads[g.m, rows, cols] = total.astype(bf16)

    def into_slots(self, stack, out, slot_order):
        g = self.g
        row_tiles = D // BLK
        gate, outs, ups, downs = self.spans
        cols = (gate.stop - gate.start + ups.stop - ups.start) // BLK
        gates, lows = gate.stop // BLK, (outs.stop - outs.start) // BLK
        for b in range(stack.shape[0]):
            if b < row_tiles * cols:
                r, c = b // cols, b % cols
                first = c * BLK if c < gates else ups.start + (c - gates) * BLK
            else:
                k, r = (b - row_tiles * cols) // row_tiles, (b - row_tiles * cols) % row_tiles
                first = outs.start + k * BLK if k < lows else downs.start + (k - lows) * BLK
            stack[b] = self.grads[g.m, r * BLK : (r + 1) * BLK, first : first + BLK]
        n = stack.shape[0] // 8
        for s in range(stack.shape[0]):
            out[self.place(s // n) * n + s % n] = stack[slot_order[s]]

    def slots_chip(self, out, pair):
        g, n = self.g, out.shape[0] // 8
        self.last = []
        for e in (g.plane[2], g.plane[0], g.plane[1], g.me):
            src = out.at[pl.ds(((1 - g.side) * 4 + e // 2) * n, n)]
            self.last.append(self.net.start(src, pair.at[pl.ds((e // 2) * n, n)], (g.core, g.m)))

    def slots_plane(self, out, pair, far):
        g, n = self.g, out.shape[0] // 8
        h = n // 2
        x, y, z = g.plane
        wait = dict(zip("zxyo", self.last))

        def mine(e, first, count):
            return pl.ds((g.side * 4 + e // 2) * n + first, count)

        def join(e):
            rows = mine(e, 0, n)
            out[rows] = (out[rows].astype(f32) + pair[pl.ds((e // 2) * n, n)].astype(f32)).astype(bf16)

        def send(e, first, slot, to):
            return self.net.start(out.at[mine(e, first, h)], far.at[slot], (to, g.m))

        wait["z"].wait_recv()
        join(z)
        over_x = send(z, 0, 0, x)
        over_y = send(z, h, 1, y)
        wait["x"].wait_recv()
        join(x)
        self.ends = [send(x, 0, 2, x)]
        wait["y"].wait_recv()
        join(y)
        self.ends.append(send(y, h, 3, y))
        over_x.wait_recv()
        rows = mine(y, 0, h)
        out[rows] = (out[rows].astype(f32) + far[0].astype(f32)).astype(bf16)
        self.ends.append(send(y, 0, 4, y))
        over_y.wait_recv()
        rows = mine(x, h, h)
        out[rows] = (out[rows].astype(f32) + far[1].astype(f32)).astype(bf16)
        self.ends.append(send(x, h, 5, x))
        wait["o"].wait_recv()

    def slots_end(self, out, pair, far, owned):
        g, n = self.g, out.shape[0] // 8
        h = n // 2
        for copy in self.ends:
            copy.wait_recv()
        for first, slots in ((0, (2, 4)), (h, (3, 5))):
            total = out[pl.ds((g.side * 4 + g.me // 2) * n + first, h)].astype(f32)
            total += pair[pl.ds((g.me // 2) * n + first, h)].astype(f32)
            for k in slots:
                total += far[k].astype(f32)
            owned[first : first + h] = total


class SmallSum:
    def __init__(self, net, gather, values, along, across, inside):
        self.net, self.g, self.values = net, gather, values
        self.slots = (along, across, inside)
        self.peers = (
            [(gather.me, k) for k in gather.order[1:]],
            [(e, gather.m) for e in gather.plane],
            [(gather.core, gather.m)],
        )
        self.mine = (gather.m, gather.me // 2, gather.side)
        self.open = []

    def send(self, stage):
        slot = self.slots[stage]
        slot[self.mine[stage]] = self.values[...]
        ref = slot.at[self.mine[stage]]
        self.open = [self.net.start(ref, ref, peer) for peer in self.peers[stage]]

    def add(self, stage):
        for copy in self.open:
            copy.wait_recv()
        slot = self.slots[stage]
        total = slot[0]
        for k in range(1, slot.shape[0]):
            total += slot[k]
        self.values[...] = total


def compute_kernel(linked, *refs):
    if linked:
        tokens, cotangent, master, rank, slot_order, gains = refs[:6]
        block_out, input_grad, owned, small = refs[6:10]
        wg, wo, wu, wd, grads, slots, turned, pair, far, inside, across, along, sum_a, sum_b, sum_c, send, recv = refs[10:27]
        scratch = refs[27:]
    else:
        tokens, cotangent, base, wg, wo, wu, wd, gains = refs[:8]
        block_out, input_grad, grads, small = refs[8:12]
        scratch = refs[12:]
    (n1, n1t, cot, cott, n2, n2t, forget, admit, cand, state, scan, acc_a, acc_b, mixed, mid, fills, local) = scratch
    dml, dmlt = n2, n2t
    parts, _, hm3 = wg.shape
    hm = hm3 // 3
    fm = wu.shape[2]
    spans = (slice(0, 3 * hm), slice(3 * hm, 4 * hm), slice(4 * hm, 4 * hm + fm), slice(4 * hm + fm, 4 * hm + 2 * fm))
    gate, outs, ups, downs = spans
    act, dup, dpre = mid.at[:, :fm], mid.at[:, fm:], mid.at[:, : 3 * hm]
    gain_one = gains[0:1, :]
    gain_two = gains[1:2, :]

    fetch_cot = pltpu.make_async_copy(cotangent, cot, local.at[0])
    fetch_tok = pltpu.make_async_copy(tokens, n1, local.at[1])
    fetch_tok.start()
    fetch_cot.start()

    def permute_in(src, dst):
        for k in range(D // BLK):
            scan[k] = src[:, k * BLK : (k + 1) * BLK].astype(f32)

        @pl.loop(0, J // 2, unroll=4)
        def _(j):
            for k in range(D // BLK):
                lo = scan[k, pl.ds(2 * j, SUB, stride=J), :]
                hi = scan[k, pl.ds(2 * j + 1, SUB, stride=J), :]
                dst[pl.ds(pl.multiple_of(16 * j, 16), 16), k * BLK : (k + 1) * BLK] = jnp.concatenate([lo, hi], 0).astype(bf16)

    def permute_out(src, dst):
        @pl.loop(0, J, unroll=4)
        def _(j):
            rows = pl.ds(pl.multiple_of(j * SUB, SUB), SUB)
            for k in range(D // BLK):
                scan[k, pl.ds(j, SUB, stride=J), :] = src[rows, k * BLK : (k + 1) * BLK]

        for k in range(D // BLK):
            dst[:, k * BLK : (k + 1) * BLK] = scan[k].astype(dst.dtype)

    def put(first, rows, value):
        for k in range(hm // BLK):
            scan[first + k, rows, :] = value[:, k * BLK : (k + 1) * BLK]

    def take(first, rows):
        return jnp.concatenate([scan[first + k, rows, :] for k in range(hm // BLK)], 1)

    half = hm // BLK

    if linked:
        net = Exchange(send, recv)
        gather = Gather(net, master, rank, slots, (wg, wo, wu, wd))
        gather.plane_start()
        reduce = Reduce(net, gather, grads, spans, inside, across, along)
        order = gather.order
    else:
        order = list(range(parts))

    fetch_tok.wait()
    permute_in(n1, n1)
    mixed[...] = n1[...].astype(f32)

    @pl.loop(0, L // R)
    def _(i):
        rows = pl.ds(pl.multiple_of(i * R, R), R)
        x = mixed[rows, :]
        r = lax.rsqrt(jnp.mean(x * x, axis=-1, keepdims=True) + norm_eps)
        n1[rows, :] = (x * r * gain_one).astype(bf16)

    n1t[...] = n1[...].T

    if linked:
        gather.plane_finish()
        gather.place((0,))
        for i in (1, 2, 3):
            gather.along_start(0, i)
        gather.place((1, 2, 3))

    fills[0] = jnp.zeros((SUB, hm), f32)
    fills[1] = jnp.ones((SUB, hm), f32)
    weigh = fills[0]
    weigh_j = fills[0]
    for turn, m in enumerate(order):

        if linked and turn:
            gather.ready(0, turn)

        @pl.loop(0, L // R)
        def _(i):
            rows = pl.ds(pl.multiple_of(i * R, R), R)
            x = n1[rows, :]
            forget[m, rows, :] = dot(x, wg[m, :, :hm])
            admit[m, rows, :] = dot(x, wg[m, :, hm : 2 * hm])
            cand[m, rows, :] = dot(x, wg[m, :, 2 * hm :])

        if linked and turn == 0:
            gather.spread(0, 1)
        if linked and turn == 1:
            gather.pair(0, 2)
        if linked and turn == 2:
            for i in (1, 2, 3):
                gather.pair(1, i)

        def step(j, carry):
            s, p, k_sum, kj_sum = carry
            rows = pl.ds(pl.multiple_of(j * SUB, SUB), SUB)
            f = sigmoid(forget[m, rows, :])
            a = sigmoid(admit[m, rows, :])
            inv = recip(f + a)
            keep = f * inv
            s = keep * s + a * inv * cand[m, rows, :]
            p = keep * p
            forget[m, rows, :] = f
            admit[m, rows, :] = a
            put(0, rows, s)
            put(half, rows, p)
            return s, p, k_sum + keep, kj_sum + keep * j.astype(f32)

        s, p, weigh, weigh_j = lax.fori_loop(
            0,
            J,
            step,
            (fills[0], fills[1], weigh, weigh_j),
            unroll=4,
        )
        enter = fills[0]
        for _ in range(SUB - 1):
            enter = shift_down(s + p * enter)

        if linked:
            if turn == 0:
                gather.spread(0, 2)
            if turn == 1:
                gather.pair(0, 3)
                for i in (1, 2, 3):
                    gather.spread(1, i)
            if turn == 2:
                gather.spread(2, 1)
                gather.spread(3, 1)
            if turn == 3:
                gather.pair(2, 1)
                gather.pair(3, 1)
                gather.spread(2, 2)
                gather.spread(3, 2)
            if turn:
                gather.along_start(2, turn)
                gather.along_start(3, turn)

        @pl.loop(0, J, unroll=4)
        def _(j):
            rows = pl.ds(pl.multiple_of(j * SUB, SUB), SUB)
            state[m, rows, :] = take(0, rows) + take(half, rows) * enter

        if turn == 0:
            fetch_cot.wait()
            permute_in(cot, cot)
            if linked:
                gather.pair(0, 1)
                gather.spread(0, 3)
                for i in (1, 2, 3):
                    gather.along_start(1, i)
            cott[...] = cot[...].T

    if linked:
        for i in (1, 2, 3):
            gather.ready(1, i)
        for kind in (2, 3):
            gather.spread(kind, 3)

    @pl.loop(0, L // R)
    def _(i):
        rows = pl.ds(pl.multiple_of(i * R, R), R)
        x = mixed[rows, :]
        for m in range(parts):
            x += dot(state[m, rows, :].astype(bf16), wo[m])
        mixed[rows, :] = x
        r = lax.rsqrt(jnp.mean(x * x, axis=-1, keepdims=True) + norm_eps)
        n2[rows, :] = (x * r * gain_two).astype(bf16)
        acc_a[rows, :] = x
        acc_b[rows, :] = jnp.zeros_like(x)

    n2t[...] = n2[...].T

    for turn, m in enumerate(order):

        if linked and turn:
            gather.ready(2, turn)
            gather.ready(3, turn)

        @pl.loop(0, L // R)
        def _(i):
            rows = pl.ds(pl.multiple_of(i * R, R), R)
            up = dot(n2[rows, :], wu[m])
            da = dot(cot[rows, :], wd[m], True)
            cdf, xpdf = gelu_terms(up)
            ac = (up * cdf).astype(bf16)
            du = (da * (cdf + xpdf)).astype(bf16)
            act[rows, :] = ac
            dup[rows, :] = du
            acc_a[rows, :] += dot(ac, wd[m])
            acc_b[rows, :] += dot(du, wu[m], True)

        if linked and turn < 2:
            gather.pair(2, turn + 2)
            gather.pair(3, turn + 2)
        if linked and turn >= 2:
            reduce.plane(2, turn - 1)
            reduce.plane(3, turn - 1)
        if linked and turn == 3:
            reduce.model(2, 1)
            reduce.model(3, 1)
            net.drain()
        grads[m, :, downs] = dot(cott[...], act[...]).astype(bf16)
        grads[m, :, ups] = dot(n2t[...], dup[...]).astype(bf16)
        if linked and turn:
            reduce.chip(2, turn)
            reduce.chip(3, turn)

    permute_out(acc_a, n1)
    push_out = pltpu.make_async_copy(n1, block_out, local.at[0])
    push_out.start()

    if linked:
        for kind in (2, 3):
            reduce.plane(kind, 3)
            reduce.model(kind, 2)

    gain_sum_two = jnp.zeros((1, D), f32)

    def back_two(i, total):
        rows = pl.ds(pl.multiple_of(i * R, R), R)
        x = mixed[rows, :]
        r = lax.rsqrt(jnp.mean(x * x, axis=-1, keepdims=True) + norm_eps)
        dn = acc_b[rows, :]
        q = dn * gain_two
        d = cot[rows, :].astype(f32) + r * q - r * r * r * x * jnp.mean(q * x, axis=-1, keepdims=True)
        mixed[rows, :] = d
        dml[rows, :] = d.astype(bf16)
        acc_b[rows, :] = jnp.zeros_like(d)
        return total + jnp.sum(dn * x * r, axis=0, keepdims=True)

    gain_sum_two = lax.fori_loop(0, L // R, back_two, gain_sum_two)
    dmlt[...] = dml[...].T
    fetch_tok = pltpu.make_async_copy(tokens, cot, local.at[1])
    fetch_tok.start()

    for turn, m in reversed(list(enumerate(order))):
        grads[m, :, outs] = dot(dmlt[...], state[m].astype(bf16)).astype(bf16)
        if linked and turn:
            reduce.chip(1, turn)

    for turn, m in reversed(list(enumerate(order))):

        @pl.loop(0, L // R)
        def _(i):
            rows = pl.ds(pl.multiple_of(i * R, R), R)
            put(0, rows, dot(dml[rows, :], wo[m], True))

        def step(k, carry):
            u, p, keep_next = carry
            j = J - 1 - k
            rows = pl.ds(pl.multiple_of(j * SUB, SUB), SUB)
            u = take(0, rows) + keep_next * u
            p = keep_next * p
            put(0, rows, u)
            put(half, rows, p)
            f = forget[m, rows, :]
            return u, p, f * recip(f + admit[m, rows, :])

        u, p, keep_first = lax.fori_loop(
            0,
            J,
            step,
            (fills[0], fills[1], fills[1]),
            unroll=4,
        )
        enter = fills[0]
        for _ in range(SUB - 1):
            enter = shift_up(keep_first * (u + p * enter))

        if linked:
            if turn == 3:
                for kind in (2, 3):
                    reduce.model(kind, 3)
                for i in (3, 2, 1):
                    reduce.plane(1, i)
            if turn < 3:
                reduce.plane(0, turn + 1)
            if turn == 2:
                for i in (3, 2, 1):
                    reduce.model(1, i)
            if turn < 2:
                reduce.model(0, turn + 2)
            if turn == 0:
                for kind in (1, 2, 3):
                    reduce.own(kind)

        def back(i, before):
            parts_out = []
            for h in range(2):
                rows = pl.ds(pl.multiple_of(i * 2 * SUB + h * SUB, SUB), SUB)
                carried = take(0, rows) + take(half, rows) * enter
                f = forget[m, rows, :]
                a = admit[m, rows, :]
                inv = recip(f + a)
                adm = a * inv
                g = carried * (before - cand[m, rows, :]) * (f * inv * adm)
                parts_out.append((g * (1.0 - f), g * (a - 1.0), carried * adm))
                before = state[m, rows, :]
            both = pl.ds(pl.multiple_of(i * 2 * SUB, 2 * SUB), 2 * SUB)
            for k in range(3):
                dpre[both, k * hm : (k + 1) * hm] = jnp.concatenate(
                    [parts_out[0][k], parts_out[1][k]], 0
                ).astype(bf16)
            return before

        last = state[m, pl.ds(L - SUB, SUB), :]
        lax.fori_loop(0, J // 2, back, shift_down(last), unroll=2)

        grads[m, :, gate] = dot(n1t[...], dpre[...]).astype(bf16)
        if linked and turn:
            reduce.chip(0, turn)

        @pl.loop(0, L // R)
        def _(i):
            rows = pl.ds(pl.multiple_of(i * R, R), R)
            acc_b[rows, :] += dot(dpre[rows, :], wg[m], True)

    fetch_tok.wait()
    permute_in(cot, cot)

    if linked:
        reduce.model(0, 1)

    def back_one(i, total):
        rows = pl.ds(pl.multiple_of(i * R, R), R)
        x = cot[rows, :].astype(f32)
        r = lax.rsqrt(jnp.mean(x * x, axis=-1, keepdims=True) + norm_eps)
        dn = acc_b[rows, :]
        q = dn * gain_one
        mixed[rows, :] += r * q - r * r * r * x * jnp.mean(q * x, axis=-1, keepdims=True)
        return total + jnp.sum(dn * x * r, axis=0, keepdims=True)

    gain_sum_one = lax.fori_loop(0, L // R, back_one, jnp.zeros((1, D), f32))

    place = lax.broadcasted_iota(jnp.int32, (SUB, hm), 0).astype(f32) * float(J)
    if linked:
        first = ((gather.me * parts + gather.m) * L + 1).astype(f32)
        token_total = float(L * parts * lax.axis_size("dp"))
    else:
        first = base[0]
        token_total = base[1]
    forget_sum = jnp.sum(weigh_j + weigh * (place + first), axis=0, keepdims=True) / token_total
    small[...] = jnp.zeros_like(small)
    small[0:1, :] = gain_sum_one
    small[1:2, :] = gain_sum_two
    small[2:3, :hm] = forget_sum

    if linked:
        tiny = SmallSum(net, gather, small, sum_a, sum_b, sum_c)
        tiny.send(0)
        reduce.own(0)
        reduce.into_slots(slots, turned, slot_order)
        reduce.slots_chip(turned, pair)
        tiny.add(0)
        tiny.send(1)
        reduce.slots_plane(turned, pair, far)

    permute_out(mixed, acc_a)
    push_grad = pltpu.make_async_copy(acc_a, input_grad, local.at[2])
    push_grad.start()

    if linked:
        tiny.add(1)
        tiny.send(2)
        reduce.slots_end(turned, pair, far, owned)
        tiny.add(2)
        net.drain()
    push_out.wait()
    push_grad.wait()


def compute(tokens, cotangent, gains, weights=None, base=None, master=None, rank=None, slot_order=None):
    linked = weights is None
    parts = lax.axis_size("mp")
    hm, fm = H // parts, FF // parts
    wide = 4 * hm + 2 * fm
    sds = jax.ShapeDtypeStruct
    vm, sm, hbm = (pl.BlockSpec(memory_space=k) for k in (pltpu.VMEM, pltpu.SMEM, pl.ANY))
    if linked:
        n = rank.shape[0]
        args = (tokens, cotangent, master, rank, slot_order, gains)
        in_specs = [hbm, hbm, vm, sm, sm, vm]
        middle = sds((n // 8, BLK, BLK), f32)
        extra = [
            pltpu.VMEM((parts, D, 3 * hm), bf16),
            pltpu.VMEM((parts, hm, D), bf16),
            pltpu.VMEM((parts, D, fm), bf16),
            pltpu.VMEM((parts, fm, D), bf16),
            pltpu.VMEM((parts, D, wide), bf16),
            pltpu.VMEM((n, BLK, BLK), bf16),
            pltpu.VMEM((n, BLK, BLK), bf16),
            pltpu.VMEM((n // 2, BLK, BLK), bf16),
            pltpu.VMEM((6, n // 16, BLK, BLK), bf16),
            pltpu.VMEM((3, D // 2, wide), bf16),
            pltpu.VMEM((3, 3, D // 8, wide), bf16),
            pltpu.VMEM((3, D // 8, wide), bf16),
            pltpu.VMEM((parts, 8, D), f32),
            pltpu.VMEM((4, 8, D), f32),
            pltpu.VMEM((2, 8, D), f32),
            pltpu.SemaphoreType.DMA((256,)),
            pltpu.SemaphoreType.DMA((256,)),
        ]
        params = dict(collective_id=0, has_side_effects=True)
    else:
        args = (tokens, cotangent, base, *weights, gains)
        in_specs = [hbm, hbm, sm] + [vm] * 5
        middle = sds((parts, D, wide), bf16)
        extra = []
        params = {}
    return pl.pallas_call(
        functools.partial(compute_kernel, linked),
        out_shape=(sds((L, D), bf16), sds((L, D), f32), middle, sds((8, D), f32)),
        in_specs=in_specs,
        out_specs=[hbm, hbm, vm, vm],
        scratch_shapes=extra
        + [pltpu.VMEM(shape, bf16) for shape in ((L, D), (D, L)) * 3]
        + [pltpu.VMEM((parts, L, hm), f32)] * 4
        + [pltpu.VMEM((2 * hm // BLK, L, BLK), f32)]
        + [pltpu.VMEM((L, D), f32)] * 3
        + [
            pltpu.VMEM((L, 2 * fm), bf16),
            pltpu.VMEM((2, SUB, hm), f32),
            pltpu.SemaphoreType.DMA((3,)),
        ],
        compiler_params=pltpu.CompilerParams(vmem_limit_bytes=64 * 2**20 - 2**16, **params),
        name="block",
    )(*args)


def adam_update(first_old, second_old, gradient):
    first_new = beta_one * first_old + (1.0 - beta_one) * gradient
    second_new = beta_two * second_old + (1.0 - beta_two) * gradient * gradient
    first_hat = first_new / (1.0 - beta_one**STEP)
    second_hat = second_new / (1.0 - beta_two**STEP)
    return (first_new, second_new, first_hat / (jnp.sqrt(second_hat) + adam_eps))


def fine_dot(a, b, trans_b=False):
    a_high, b_high = a.astype(bf16), b.astype(bf16)
    a_low, b_low = (a - a_high.astype(f32)).astype(bf16), (b - b_high.astype(f32)).astype(bf16)
    return dot(a_high, b_high, trans_b) + (dot(a_high, b_low, trans_b) + dot(a_low, b_high, trans_b))


def update_kernel(
    low_first,
    token_total,
    passed,
    low,
    sums,
    gains,
    gain_moment_one,
    gain_moment_two,
    owned,
    master,
    moment_one,
    moment_two,
    basis_left,
    basis_right,
    *refs,
):
    given, refs = refs[:passed], refs[passed:]
    first_new, second_new, master_new, master_low, gain_first, gain_second, gains_new, forget_mean = refs[:8]
    copied, refs = refs[8 : 8 + passed], refs[8 + passed :]
    held, made, made_low, sem_in, sem_out, sem_pass = refs
    count = master.shape[0]
    passing = [pltpu.make_async_copy(src, dst, sem_pass.at[k]) for k, (src, dst) in enumerate(zip(given, copied))]
    sources = (owned, basis_left, basis_right, moment_one, moment_two, master)
    fetch = [
        [pltpu.make_async_copy(src.at[s], held.at[s, k], sem_in.at[s, k]) for k, src in enumerate(sources)]
        for s in range(count)
    ]
    for row in fetch:
        for copy in row:
            copy.start()
    for copy in passing:
        copy.start()
    push = []
    for s in range(count):
        for copy in fetch[s]:
            copy.wait()
        grad = held[s, 0]
        grad = jnp.where(low[s] >= low_first, grad.T, grad)
        left, right = held[s, 1], held[s, 2]
        rotated = fine_dot(fine_dot(left.T, grad), right)
        first, second, direction = adam_update(held[s, 3], held[s, 4], rotated)
        made[s, 0] = first
        made[s, 1] = second
        turned = fine_dot(fine_dot(left, direction), right, True)
        old = held[s, 5]
        fresh = old - learn_rate * (turned + weight_decay * old)
        made[s, 2] = fresh
        made_low[s] = fresh.astype(bf16)
        for k, (src, dst) in enumerate(
            ((made.at[s, 0], first_new), (made.at[s, 1], second_new), (made.at[s, 2], master_new), (made_low.at[s], master_low))
        ):
            copy = pltpu.make_async_copy(src, dst.at[s], sem_out.at[s, k])
            copy.start()
            push.append(copy)
    first, second, direction = adam_update(gain_moment_one[...], gain_moment_two[...], sums[0:2, :])
    gain_first[...] = first
    gain_second[...] = second
    gains_new[...] = gains[...] - gain_rate * direction
    forget_mean[...] = jnp.sum(sums[2:3, :], axis=1, keepdims=True) * (1.0 / (H * (token_total + 1) / 2.0))
    for copy in push + passing:
        copy.wait()


def update(low_first, token_total, small, large, passed):
    sds = jax.ShapeDtypeStruct
    blocks, gain = large[0].shape, small[2].shape
    vm, hbm = pl.BlockSpec(memory_space=pltpu.VMEM), pl.BlockSpec(memory_space=pl.ANY)
    count = blocks[0]
    return pl.pallas_call(
        functools.partial(update_kernel, low_first, token_total, len(passed)),
        out_shape=[sds(blocks, f32)] * 3
        + [sds(blocks, bf16)]
        + [sds(gain, f32)] * 3
        + [sds((1, 1), f32)]
        + [sds(v.shape, v.dtype) for v in passed],
        in_specs=[pl.BlockSpec(memory_space=pltpu.SMEM)] + [vm] * 4 + [hbm] * (len(large) + len(passed)),
        out_specs=[hbm] * 4 + [vm] * 4 + [hbm] * len(passed),
        scratch_shapes=[
            pltpu.VMEM((count, 6, BLK, BLK), f32),
            pltpu.VMEM((count, 3, BLK, BLK), f32),
            pltpu.VMEM((count, BLK, BLK), bf16),
            pltpu.SemaphoreType.DMA((count, 6)),
            pltpu.SemaphoreType.DMA((count, 4)),
            pltpu.SemaphoreType.DMA((max(len(passed), 1),)),
        ],
        compiler_params=pltpu.CompilerParams(vmem_limit_bytes=56 * 2**20),
        name="update",
    )(*small, *large, *passed)


def on_device(
    tokens,
    cotangent,
    master,
    moment_one,
    moment_two,
    basis_left,
    basis_right,
    owner,
    gains,
    gain_moment_one,
    gain_moment_two,
):
    parts = lax.axis_size("mp")
    data_parts = lax.axis_size("dp")
    hm, fm = H // parts, FF // parts
    token_total = L * data_parts * parts
    row_tiles, cols, lows = D // BLK, (3 * hm + fm) // BLK, (hm + fm) // BLK
    blocks = owner.shape[0]
    number = jnp.arange(blocks, dtype=jnp.int32)
    ahead = (owner[None, :] < owner[:, None]) | ((owner[None, :] == owner[:, None]) & (number[None, :] < number[:, None]))
    block_rank = jnp.sum(ahead.astype(jnp.int32), axis=1)
    slot_order = jnp.sum(jnp.where(block_rank[None, :] == number[:, None], number[None, :], 0), axis=1)
    if data_parts == 8 and parts == 4:
        block_out, input_grad, owned, sums = compute(
            tokens, cotangent, gains, master=master[0], rank=block_rank, slot_order=slot_order
        )
    else:
        stored = lax.all_gather(master.astype(bf16), "dp", axis=1, tiled=True)
        stored = lax.all_gather(stored, "mp", axis=0, tiled=True)
        stack = stored[:, block_rank]
        upper = stack[:, : row_tiles * cols].reshape(parts, row_tiles, cols, BLK, BLK)
        upper = upper.transpose(0, 1, 3, 2, 4).reshape(parts, D, cols * BLK)
        lower = stack[:, row_tiles * cols :].reshape(parts, lows, row_tiles, BLK, BLK)
        lower = lower.transpose(0, 1, 3, 2, 4).reshape(parts, lows * BLK, D)
        weights = (upper[:, :, : 3 * hm], lower[:, :hm], upper[:, :, 3 * hm :], lower[:, hm:])
        first = ((lax.axis_index("dp") * parts + lax.axis_index("mp")) * L + 1).astype(f32)
        base = jnp.stack([first, jnp.asarray(token_total, f32)])
        block_out, input_grad, grads, sums = compute(tokens, cotangent, gains, weights=weights, base=base)
        upper = jnp.concatenate([grads[:, :, : 3 * hm], grads[:, :, 4 * hm : 4 * hm + fm]], axis=2)
        upper = upper.reshape(parts, row_tiles, BLK, cols, BLK).transpose(0, 1, 3, 2, 4)
        lower = jnp.concatenate([grads[:, :, 3 * hm : 4 * hm], grads[:, :, 4 * hm + fm :]], axis=2)
        lower = lower.reshape(parts, row_tiles, BLK, lows, BLK).transpose(0, 3, 1, 2, 4)
        natural = jnp.concatenate(
            [upper.reshape(parts, -1, BLK, BLK), lower.reshape(parts, -1, BLK, BLK)], axis=1
        ).astype(f32)
        owned = lax.psum_scatter(natural[:, slot_order], "dp", scatter_dimension=1, tiled=True)
        owned = lax.psum_scatter(owned, "mp", scatter_dimension=0, tiled=True)[0]
        sums = lax.psum(sums, ("dp", "mp"))
    mine = lax.dynamic_slice_in_dim(slot_order, lax.axis_index("dp") * master.shape[1], master.shape[1])
    outs = update(
        row_tiles * cols,
        token_total,
        (mine, sums, gains, gain_moment_one, gain_moment_two),
        (owned, master[0], moment_one[0], moment_two[0], basis_left[0], basis_right[0]),
        (block_out, input_grad),
    )
    first_new, second_new, master_new, master_low, gain_first, gain_second, gains_new, forget_mean = outs[:8]
    block_out, input_grad = outs[8:]
    return (
        block_out,
        input_grad,
        first_new[None],
        second_new[None],
        master_new[None],
        master_low[None],
        gain_first,
        gain_second,
        gains_new,
        forget_mean[0, 0],
    )


def solution(mesh):
    rows, blocks = P(("dp", "mp"), None), P("mp", "dp", None, None)
    return jax.shard_map(
        on_device,
        mesh=mesh,
        in_specs=(rows, rows, blocks, blocks, blocks, blocks, blocks, P(), P(), P(), P()),
        out_specs=(rows, rows, blocks, blocks, blocks, blocks, P(), P(), P(), P()),
        check_vma=False,
    )
```

```python
import functools

import jax
import jax.numpy as jnp
from jax import lax
from jax.experimental import pallas as pl
from jax.experimental.pallas import tpu as pltpu
from jax.sharding import PartitionSpec as P

D = 512
H = 1024
FF = 2048
BLK = 128
STEP = 10
L = 1024

norm_eps = 1e-05
beta_one = 0.5
beta_two = 0.5
adam_eps = 1e-08
learn_rate = 0.02
gain_rate = 0.1
weight_decay = 0.1
highest = lax.Precision.HIGHEST

f32 = jnp.float32
bf16 = jnp.bfloat16
SUB = 8
J = L // SUB
R = 256


def dot(a, b, trans_b=False):
    dims = (((1,), (1,)), ((), ())) if trans_b else (((1,), (0,)), ((), ()))
    return lax.dot_general(a, b, dims, preferred_element_type=f32)


def recip(v):
    return pltpu.reciprocal(v, approx=True)


def sigmoid(v):
    return recip(1.0 + jnp.exp(-v))


def shift_down(v):
    rolled = pltpu.roll(v, 1, 0)
    row = lax.broadcasted_iota(jnp.int32, v.shape, 0)
    return jnp.where(row == 0, 0.0, rolled)


def shift_up(v):
    rolled = pltpu.roll(v, SUB - 1, 0)
    row = lax.broadcasted_iota(jnp.int32, v.shape, 0)
    return jnp.where(row == SUB - 1, 0.0, rolled)


def gelu_terms(x):
    a = jnp.abs(x)
    t = recip(1.0 + a * (0.3275911 * 0.7071067811865476))
    poly = t * (
        0.5 * 0.254829592
        + t
        * (
            0.5 * -0.284496736
            + t * (0.5 * 1.421413741 + t * (0.5 * -1.453152027 + t * (0.5 * 1.061405429)))
        )
    )
    e = jnp.exp(x * x * -0.5)
    tail = poly * e
    cdf = jnp.where(x < 0.0, tail, 1.0 - tail)
    return cdf, x * e * 0.3989422804014327


MESH = pl.DeviceIdType.MESH


class Exchange:
    def __init__(self, send, recv):
        self.send, self.recv, self.used, self.open = send, recv, 0, []

    def start(self, src, dst, device):
        k = self.used
        self.used += 1
        copy = pltpu.make_async_remote_copy(
            src_ref=src,
            dst_ref=dst,
            send_sem=self.send.at[k],
            recv_sem=self.recv.at[k],
            device_id=device,
            device_id_type=MESH,
        )
        copy.start()
        self.open.append(copy)
        return copy

    def drain(self):
        for copy in self.open:
            copy.wait_send()
        self.open = []


class Gather:
    def __init__(self, net, master, rank, slots, pool, weights, free):
        self.net, self.weights, self.rank, self.free = net, weights, rank, free
        self.held = [slots, *pool]
        d, m = lax.axis_index("dp"), lax.axis_index("mp")
        core, col, row = d % 2, (d // 2) % 2, d // 4
        self.me, self.m, self.side = d, m, core
        self.core = d + 1 - 2 * core
        self.plane = [d + 2 - 4 * col, d + 4 - 8 * row, d + 6 - 4 * col - 8 * row]
        self.order = [m, m + 1 - 2 * (m % 2), m + 2 - 4 * (m // 2), 3 - m]
        self.peers = [(e, m) for e in [self.core] + self.plane] + [(d, k) for k in self.order[1:]]
        self.along, self.first, self.last, self.inside = {}, {}, {}, {}
        barrier = pltpu.get_barrier_semaphore()
        for device in self.peers:
            pl.semaphore_signal(barrier, inc=1, device_id=device, device_id_type=MESH)
        self.n = master.shape[0]
        for s in range(self.n):
            slots[d * self.n + s] = master[s].astype(bf16)
        pl.semaphore_wait(barrier, len(self.peers))

    def rows(self, i, e, first, count):
        return self.held[i].at[pl.ds(e * self.n + first, count)]

    def along_start(self, i):
        self.along[i] = self.net.start(
            self.rows(0, self.me, 0, self.n), self.rows(i, self.me, 0, self.n), (self.me, self.order[i])
        )

    def send(self, i, e, first, count, to):
        ref = self.rows(i, e, first, count)
        return self.net.start(ref, ref, (to, self.m))

    def start(self, i):
        if i:
            self.along[i].wait_recv()
        (x, y, _), h = self.plane, self.n // 2
        self.first[i] = [self.send(i, self.me, *job) for job in ((0, h, x), (h, h, y), (h, h, x), (0, h, y))]
        self.inside[i] = [self.send(i, self.me, 0, self.n, self.core)]

    def forward(self, i):
        (x, y, _), h = self.plane, self.n // 2
        self.first[i][0].wait_recv()
        self.last[i] = [self.send(i, x, 0, h, y)]
        self.first[i][1].wait_recv()
        self.last[i].append(self.send(i, y, h, h, x))

    def pair(self, i):
        x, y, z = self.plane
        self.first[i][2].wait_recv()
        self.inside[i].append(self.send(i, x, 0, self.n, self.core))
        self.first[i][3].wait_recv()
        self.inside[i].append(self.send(i, y, 0, self.n, self.core))
        for copy in self.last[i]:
            copy.wait_recv()
        self.inside[i].append(self.send(i, z, 0, self.n, self.core))

    def ready(self, i):
        for copy in self.inside[i]:
            copy.wait_recv()

    def place(self, i):
        wg, wo, wu, wd = self.weights
        row_tiles, gates = D // BLK, wg.shape[2] // BLK
        cols, outs = gates + wu.shape[2] // BLK, wo.shape[1] // BLK
        for b in range(row_tiles * cols + (wo.shape[1] + wd.shape[1]) // BLK * row_tiles):
            if b < row_tiles * cols:
                r, c = b // cols, b % cols
                ref = wg if c < gates else wu
                c -= 0 if c < gates else gates
            else:
                r, c = (b - row_tiles * cols) // row_tiles, (b - row_tiles * cols) % row_tiles
                ref = wo if r < outs else wd
                r -= 0 if r < outs else outs
            block = self.held[i][self.rank[b]]
            ref[self.order[i], r * BLK : (r + 1) * BLK, c * BLK : (c + 1) * BLK] = block

    def done(self):
        for device in self.peers:
            pl.semaphore_signal(self.free, inc=1, device_id=device, device_id_type=MESH)

    def all_done(self):
        pl.semaphore_wait(self.free, len(self.peers))


def stack_places(hm, fm):
    row_tiles, gates, ups, outs = D // BLK, 3 * hm // BLK, fm // BLK, hm // BLK
    cols = gates + ups
    first_down = row_tiles * ups
    first_out = 2 * first_down
    first_gate = first_out + row_tiles * outs
    table = []
    for b in range(row_tiles * (cols + outs + ups)):
        if b < row_tiles * cols:
            r, c = b // cols, b % cols
            table.append(first_gate + r * gates + c if c < gates else r * ups + c - gates)
        else:
            k = b - row_tiles * cols
            table.append(first_out + k if k < row_tiles * outs else first_down + k - row_tiles * outs)
    return ((0, first_out), (first_out, row_tiles * outs), (first_gate, row_tiles * gates)), table


UPDOWN, OUT, GATE = range(3)


class Reduce:
    def __init__(self, net, gather, grads, units, pool):
        self.net, self.g, self.grads, self.units, self.pool = net, gather, grads, units, pool
        self.half = grads.shape[1] // 2
        self.eighth = grads.shape[1] // 8
        self.copies = {}

    def place(self, e):
        return (e % 2) * 4 + e // 2

    def chip(self, unit, i):
        g, (first, count) = self.g, self.units[unit]
        src = self.grads.at[g.order[i], pl.ds(first + (1 - g.side) * (count // 2), count // 2)]
        dst = self.pool[i - 1].at[pl.ds(first // 2, count // 2)]
        self.copies[0, unit, i] = self.net.start(src, dst, (g.core, g.m))

    def plane(self, unit, i):
        g, (first, count) = self.g, self.units[unit]
        n = count // 8
        self.copies[0, unit, i].wait_recv()
        m = g.order[i]
        rows = pl.ds(first + g.side * (count // 2), count // 2)
        total = self.grads[m, rows].astype(f32) + self.pool[i - 1][first // 2 : (first + count) // 2].astype(f32)
        self.grads[m, rows] = total.astype(bf16)
        for k, e in enumerate(g.plane):
            src = self.grads.at[m, pl.ds(first + self.place(e) * n, n)]
            dst = self.pool[i - 1].at[pl.ds(self.half + k * self.eighth + first // 8, n)]
            self.copies[1, unit, i, k] = self.net.start(src, dst, (e, g.m))

    def model(self, unit, i):
        g, (first, count) = self.g, self.units[unit]
        n = count // 8
        m = g.order[i]
        rows = pl.ds(first + self.place(g.me) * n, n)
        total = self.grads[m, rows].astype(f32)
        for k in range(3):
            self.copies[1, unit, i, k].wait_recv()
            total += self.pool[i - 1][pl.ds(self.half + k * self.eighth + first // 8, n)].astype(f32)
        self.grads[m, rows] = total.astype(bf16)
        dst = self.pool[i - 1].at[pl.ds(self.half + 3 * self.eighth + first // 8, n)]
        self.copies[2, unit, i] = self.net.start(self.grads.at[m, rows], dst, (g.me, m))

    def own(self, unit):
        g, (first, count) = self.g, self.units[unit]
        n = count // 8
        rows = pl.ds(first + self.place(g.me) * n, n)
        total = self.grads[g.m, rows].astype(f32)
        for i in (1, 2, 3):
            self.copies[2, unit, i].wait_recv()
            total += self.pool[i - 1][pl.ds(self.half + 3 * self.eighth + first // 8, n)].astype(f32)
        self.grads[g.m, rows] = total.astype(bf16)

    def into_slots(self, out, slot_place):
        n = self.eighth
        for s in range(8 * n):
            out[self.place(s // n) * n + s % n] = self.grads[self.g.m, slot_place[s]]

    def slots_chip(self, out, pair):
        g, n = self.g, out.shape[0] // 8
        self.last = []
        for e in (g.plane[2], g.plane[0], g.plane[1], g.me):
            src = out.at[pl.ds(((1 - g.side) * 4 + e // 2) * n, n)]
            self.last.append(self.net.start(src, pair.at[pl.ds((e // 2) * n, n)], (g.core, g.m)))

    def slots_plane(self, out, pair, far):
        g, n = self.g, out.shape[0] // 8
        h = n // 2
        x, y, z = g.plane
        wait = dict(zip("zxyo", self.last))

        def mine(e, first, count):
            return pl.ds((g.side * 4 + e // 2) * n + first, count)

        def join(e):
            rows = mine(e, 0, n)
            out[rows] = (out[rows].astype(f32) + pair[pl.ds((e // 2) * n, n)].astype(f32)).astype(bf16)

        def send(e, first, slot, to):
            return self.net.start(out.at[mine(e, first, h)], far.at[slot], (to, g.m))

        wait["z"].wait_recv()
        join(z)
        over_x = send(z, 0, 0, x)
        over_y = send(z, h, 1, y)
        wait["x"].wait_recv()
        join(x)
        self.ends = [send(x, 0, 2, x)]
        wait["y"].wait_recv()
        join(y)
        self.ends.append(send(y, h, 3, y))
        over_x.wait_recv()
        rows = mine(y, 0, h)
        out[rows] = (out[rows].astype(f32) + far[0].astype(f32)).astype(bf16)
        self.ends.append(send(y, 0, 4, y))
        over_y.wait_recv()
        rows = mine(x, h, h)
        out[rows] = (out[rows].astype(f32) + far[1].astype(f32)).astype(bf16)
        self.ends.append(send(x, h, 5, x))
        wait["o"].wait_recv()

    def slots_end(self, out, pair, far, owned):
        g, n = self.g, out.shape[0] // 8
        h = n // 2
        for copy in self.ends:
            copy.wait_recv()
        for first, slots in ((0, (2, 4)), (h, (3, 5))):
            total = out[pl.ds((g.side * 4 + g.me // 2) * n + first, h)].astype(f32)
            total += pair[pl.ds((g.me // 2) * n + first, h)].astype(f32)
            for k in slots:
                total += far[k].astype(f32)
            owned[first : first + h] = total


class SmallSum:
    def __init__(self, net, gather, values, along, across, inside):
        self.net, self.g, self.values = net, gather, values
        self.slots = (along, across, inside)
        self.peers = (
            [(gather.me, k) for k in gather.order[1:]],
            [(e, gather.m) for e in gather.plane],
            [(gather.core, gather.m)],
        )
        self.mine = (gather.m, gather.me // 2, gather.side)
        self.open = []

    def send(self, stage):
        slot = self.slots[stage]
        slot[self.mine[stage]] = self.values[...]
        ref = slot.at[self.mine[stage]]
        self.open = [self.net.start(ref, ref, peer) for peer in self.peers[stage]]

    def add(self, stage):
        for copy in self.open:
            copy.wait_recv()
        slot = self.slots[stage]
        total = slot[0]
        for k in range(1, slot.shape[0]):
            total += slot[k]
        self.values[...] = total


def compute_kernel(linked, *refs):
    if linked:
        tokens, cotangent, master, rank, slot_place, gains = refs[:6]
        block_out, input_grad, owned, small = refs[6:10]
        wg, wo, wu, wd, grads, slots, *pool, pair, far, sum_a, sum_b, sum_c, send, recv, free = refs[10:27]
        scratch = refs[27:]
    else:
        tokens, cotangent, base, wg, wo, wu, wd, gains = refs[:8]
        block_out, input_grad, grads, small = refs[8:12]
        scratch = refs[12:]
    (n1, n1t, cot, cott, n2, n2t, forget, admit, cand, state, scan, acc_a, acc_b, mixed, mid, fills, local) = scratch
    dml, dmlt = n2, n2t
    parts, _, hm3 = wg.shape
    hm = hm3 // 3
    fm = wu.shape[2]
    units, _ = stack_places(hm, fm)
    act, dup, dpre = mid.at[:, :fm], mid.at[:, fm:], mid.at[:, : 3 * hm]
    gain_one = gains[0:1, :]
    gain_two = gains[1:2, :]

    fetch_cot = pltpu.make_async_copy(cotangent, cot, local.at[0])
    fetch_tok = pltpu.make_async_copy(tokens, n1, local.at[1])
    fetch_tok.start()
    fetch_cot.start()

    def stack(m, first, value):
        wide = value.shape[1] // BLK
        for r in range(value.shape[0] // BLK):
            for c in range(wide):
                grads[m, first + r * wide + c] = value[r * BLK : (r + 1) * BLK, c * BLK : (c + 1) * BLK].astype(bf16)

    def stack_turned(m, first, value):
        high = value.shape[0] // BLK
        for r in range(high):
            for c in range(value.shape[1] // BLK):
                grads[m, first + c * high + r] = value[r * BLK : (r + 1) * BLK, c * BLK : (c + 1) * BLK].astype(bf16)

    def permute_in(src, dst):
        for k in range(D // BLK):
            scan[k] = src[:, k * BLK : (k + 1) * BLK].astype(f32)

        @pl.loop(0, J // 2, unroll=4)
        def _(j):
            for k in range(D // BLK):
                lo = scan[k, pl.ds(2 * j, SUB, stride=J), :]
                hi = scan[k, pl.ds(2 * j + 1, SUB, stride=J), :]
                dst[pl.ds(pl.multiple_of(16 * j, 16), 16), k * BLK : (k + 1) * BLK] = jnp.concatenate([lo, hi], 0).astype(bf16)

    def permute_out(src, dst):
        @pl.loop(0, J, unroll=4)
        def _(j):
            rows = pl.ds(pl.multiple_of(j * SUB, SUB), SUB)
            for k in range(D // BLK):
                scan[k, pl.ds(j, SUB, stride=J), :] = src[rows, k * BLK : (k + 1) * BLK]

        for k in range(D // BLK):
            dst[:, k * BLK : (k + 1) * BLK] = scan[k].astype(dst.dtype)

    def put(first, rows, value):
        for k in range(hm // BLK):
            scan[first + k, rows, :] = value[:, k * BLK : (k + 1) * BLK]

    def take(first, rows):
        return jnp.concatenate([scan[first + k, rows, :] for k in range(hm // BLK)], 1)

    half = hm // BLK

    if linked:
        net = Exchange(send, recv)
        gather = Gather(net, master, rank, slots, pool, (wg, wo, wu, wd), free)
        gather.start(0)
        gather.along_start(1)
        reduce = Reduce(net, gather, grads, units, pool)
        order = gather.order
    else:
        order = list(range(parts))

    fetch_tok.wait()
    permute_in(n1, n1)
    mixed[...] = n1[...].astype(f32)

    @pl.loop(0, L // R)
    def _(i):
        rows = pl.ds(pl.multiple_of(i * R, R), R)
        x = mixed[rows, :]
        r = lax.rsqrt(jnp.mean(x * x, axis=-1, keepdims=True) + norm_eps)
        n1[rows, :] = (x * r * gain_one).astype(bf16)

    n1t[...] = n1[...].T

    if linked:
        gather.forward(0)
        gather.along_start(2)
        gather.along_start(3)
    fetch_cot.wait()
    permute_in(cot, cot)
    if linked:
        gather.start(1)
        gather.pair(0)
    cott[...] = cot[...].T

    fills[0] = jnp.zeros((SUB, hm), f32)
    fills[1] = jnp.ones((SUB, hm), f32)
    weigh = fills[0]
    weigh_j = fills[0]
    for turn, m in enumerate(order):

        if linked:
            if turn:
                gather.pair(turn)
            gather.ready(turn)
            gather.place(turn)

        @pl.loop(0, L // R)
        def _(i):
            rows = pl.ds(pl.multiple_of(i * R, R), R)
            x = n1[rows, :]
            forget[m, rows, :] = dot(x, wg[m, :, :hm])
            admit[m, rows, :] = dot(x, wg[m, :, hm : 2 * hm])
            cand[m, rows, :] = dot(x, wg[m, :, 2 * hm :])

        if linked and turn < 3:
            gather.forward(turn + 1)
            if turn < 2:
                gather.start(turn + 2)

        def step(j, carry):
            s, p, k_sum, kj_sum = carry
            rows = pl.ds(pl.multiple_of(j * SUB, SUB), SUB)
            f = sigmoid(forget[m, rows, :])
            a = sigmoid(admit[m, rows, :])
            inv = recip(f + a)
            keep = f * inv
            s = keep * s + a * inv * cand[m, rows, :]
            p = keep * p
            forget[m, rows, :] = f
            admit[m, rows, :] = a
            put(0, rows, s)
            put(half, rows, p)
            return s, p, k_sum + keep, kj_sum + keep * j.astype(f32)

        s, p, weigh, weigh_j = lax.fori_loop(
            0,
            J,
            step,
            (fills[0], fills[1], weigh, weigh_j),
            unroll=4,
        )
        enter = fills[0]
        for _ in range(SUB - 1):
            enter = shift_down(s + p * enter)

        @pl.loop(0, J, unroll=4)
        def _(j):
            rows = pl.ds(pl.multiple_of(j * SUB, SUB), SUB)
            state[m, rows, :] = take(0, rows) + take(half, rows) * enter

    if linked:
        net.drain()
        gather.done()

    @pl.loop(0, L // R)
    def _(i):
        rows = pl.ds(pl.multiple_of(i * R, R), R)
        x = mixed[rows, :]
        for m in range(parts):
            x += dot(state[m, rows, :].astype(bf16), wo[m])
        mixed[rows, :] = x
        r = lax.rsqrt(jnp.mean(x * x, axis=-1, keepdims=True) + norm_eps)
        n2[rows, :] = (x * r * gain_two).astype(bf16)
        acc_a[rows, :] = x
        acc_b[rows, :] = jnp.zeros_like(x)

    n2t[...] = n2[...].T

    for turn, m in enumerate(order):

        @pl.loop(0, L // R)
        def _(i):
            rows = pl.ds(pl.multiple_of(i * R, R), R)
            up = dot(n2[rows, :], wu[m])
            da = dot(cot[rows, :], wd[m], True)
            cdf, xpdf = gelu_terms(up)
            ac = (up * cdf).astype(bf16)
            du = (da * (cdf + xpdf)).astype(bf16)
            act[rows, :] = ac
            dup[rows, :] = du
            acc_a[rows, :] += dot(ac, wd[m])
            acc_b[rows, :] += dot(du, wu[m], True)

        if linked and turn >= 2:
            reduce.plane(UPDOWN, turn - 1)
        if linked and turn == 3:
            reduce.model(UPDOWN, 1)
        stack(m, 0, dot(n2t[...], dup[...]))
        stack_turned(m, units[UPDOWN][1] // 2, dot(cott[...], act[...]))
        if linked and turn:
            if turn == 1:
                gather.all_done()
            reduce.chip(UPDOWN, turn)

    permute_out(acc_a, n1)
    push_out = pltpu.make_async_copy(n1, block_out, local.at[0])
    push_out.start()

    if linked:
        reduce.plane(UPDOWN, 3)
        reduce.model(UPDOWN, 2)

    gain_sum_two = jnp.zeros((1, D), f32)

    def back_two(i, total):
        rows = pl.ds(pl.multiple_of(i * R, R), R)
        x = mixed[rows, :]
        r = lax.rsqrt(jnp.mean(x * x, axis=-1, keepdims=True) + norm_eps)
        dn = acc_b[rows, :]
        q = dn * gain_two
        d = cot[rows, :].astype(f32) + r * q - r * r * r * x * jnp.mean(q * x, axis=-1, keepdims=True)
        mixed[rows, :] = d
        dml[rows, :] = d.astype(bf16)
        acc_b[rows, :] = jnp.zeros_like(d)
        return total + jnp.sum(dn * x * r, axis=0, keepdims=True)

    gain_sum_two = lax.fori_loop(0, L // R, back_two, gain_sum_two)
    dmlt[...] = dml[...].T
    fetch_tok = pltpu.make_async_copy(tokens, cot, local.at[1])
    fetch_tok.start()

    for turn, m in reversed(list(enumerate(order))):
        stack_turned(m, units[OUT][0], dot(dmlt[...], state[m].astype(bf16)))
        if linked and turn:
            reduce.chip(OUT, turn)

    for turn, m in reversed(list(enumerate(order))):

        @pl.loop(0, L // R)
        def _(i):
            rows = pl.ds(pl.multiple_of(i * R, R), R)
            put(0, rows, dot(dml[rows, :], wo[m], True))

        def step(k, carry):
            u, p, keep_next = carry
            j = J - 1 - k
            rows = pl.ds(pl.multiple_of(j * SUB, SUB), SUB)
            u = take(0, rows) + keep_next * u
            p = keep_next * p
            put(0, rows, u)
            put(half, rows, p)
            f = forget[m, rows, :]
            return u, p, f * recip(f + admit[m, rows, :])

        u, p, keep_first = lax.fori_loop(
            0,
            J,
            step,
            (fills[0], fills[1], fills[1]),
            unroll=4,
        )
        enter = fills[0]
        for _ in range(SUB - 1):
            enter = shift_up(keep_first * (u + p * enter))

        if linked:
            if turn == 3:
                reduce.model(UPDOWN, 3)
                for i in (3, 2, 1):
                    reduce.plane(OUT, i)
            if turn < 3:
                reduce.plane(GATE, turn + 1)
            if turn == 2:
                for i in (3, 2, 1):
                    reduce.model(OUT, i)
            if turn < 2:
                reduce.model(GATE, turn + 2)
            if turn == 0:
                reduce.own(OUT)
                reduce.own(UPDOWN)

        def back(i, before):
            parts_out = []
            for h in range(2):
                rows = pl.ds(pl.multiple_of(i * 2 * SUB + h * SUB, SUB), SUB)
                carried = take(0, rows) + take(half, rows) * enter
                f = forget[m, rows, :]
                a = admit[m, rows, :]
                inv = recip(f + a)
                adm = a * inv
                g = carried * (before - cand[m, rows, :]) * (f * inv * adm)
                parts_out.append((g * (1.0 - f), g * (a - 1.0), carried * adm))
                before = state[m, rows, :]
            both = pl.ds(pl.multiple_of(i * 2 * SUB, 2 * SUB), 2 * SUB)
            for k in range(3):
                dpre[both, k * hm : (k + 1) * hm] = jnp.concatenate(
                    [parts_out[0][k], parts_out[1][k]], 0
                ).astype(bf16)
            return before

        last = state[m, pl.ds(L - SUB, SUB), :]
        lax.fori_loop(0, J // 2, back, shift_down(last), unroll=2)

        stack(m, units[GATE][0], dot(n1t[...], dpre[...]))
        if linked and turn:
            reduce.chip(GATE, turn)

        @pl.loop(0, L // R)
        def _(i):
            rows = pl.ds(pl.multiple_of(i * R, R), R)
            acc_b[rows, :] += dot(dpre[rows, :], wg[m], True)

    fetch_tok.wait()
    permute_in(cot, cot)

    if linked:
        reduce.model(GATE, 1)

    def back_one(i, total):
        rows = pl.ds(pl.multiple_of(i * R, R), R)
        x = cot[rows, :].astype(f32)
        r = lax.rsqrt(jnp.mean(x * x, axis=-1, keepdims=True) + norm_eps)
        dn = acc_b[rows, :]
        q = dn * gain_one
        mixed[rows, :] += r * q - r * r * r * x * jnp.mean(q * x, axis=-1, keepdims=True)
        return total + jnp.sum(dn * x * r, axis=0, keepdims=True)

    gain_sum_one = lax.fori_loop(0, L // R, back_one, jnp.zeros((1, D), f32))

    place = lax.broadcasted_iota(jnp.int32, (SUB, hm), 0).astype(f32) * float(J)
    if linked:
        first = ((gather.me * parts + gather.m) * L + 1).astype(f32)
        token_total = float(L * parts * lax.axis_size("dp"))
    else:
        first = base[0]
        token_total = base[1]
    forget_sum = jnp.sum(weigh_j + weigh * (place + first), axis=0, keepdims=True) / token_total
    small[...] = jnp.zeros_like(small)
    small[0:1, :] = gain_sum_one
    small[1:2, :] = gain_sum_two
    small[2:3, :hm] = forget_sum

    if linked:
        tiny = SmallSum(net, gather, small, sum_a, sum_b, sum_c)
        tiny.send(0)
        reduce.own(GATE)
        reduce.into_slots(slots, slot_place)
        reduce.slots_chip(slots, pair)
        tiny.add(0)
        tiny.send(1)
        reduce.slots_plane(slots, pair, far)

    permute_out(mixed, acc_a)
    push_grad = pltpu.make_async_copy(acc_a, input_grad, local.at[2])
    push_grad.start()

    if linked:
        tiny.add(1)
        tiny.send(2)
        reduce.slots_end(slots, pair, far, owned)
        tiny.add(2)
        net.drain()
    push_out.wait()
    push_grad.wait()


def compute(tokens, cotangent, gains, weights=None, base=None, master=None, rank=None, slot_place=None):
    linked = weights is None
    parts = lax.axis_size("mp")
    hm, fm = H // parts, FF // parts
    stacked = (parts, D * (4 * hm + 2 * fm) // BLK**2, BLK, BLK)
    sds = jax.ShapeDtypeStruct
    vm, sm, hbm = (pl.BlockSpec(memory_space=k) for k in (pltpu.VMEM, pltpu.SMEM, pl.ANY))
    if linked:
        n = rank.shape[0]
        args = (tokens, cotangent, master, rank, slot_place, gains)
        in_specs = [hbm, hbm, vm, sm, sm, vm]
        middle = sds((n // 8, BLK, BLK), f32)
        extra = [
            pltpu.VMEM((parts, D, 3 * hm), bf16),
            pltpu.VMEM((parts, hm, D), bf16),
            pltpu.VMEM((parts, D, fm), bf16),
            pltpu.VMEM((parts, fm, D), bf16),
            pltpu.VMEM(stacked, bf16),
            pltpu.VMEM((n, BLK, BLK), bf16),
            *[pltpu.VMEM((n, BLK, BLK), bf16) for _ in range(parts - 1)],
            pltpu.VMEM((n // 2, BLK, BLK), bf16),
            pltpu.VMEM((6, n // 16, BLK, BLK), bf16),
            pltpu.VMEM((parts, 8, D), f32),
            pltpu.VMEM((4, 8, D), f32),
            pltpu.VMEM((2, 8, D), f32),
            pltpu.SemaphoreType.DMA((128,)),
            pltpu.SemaphoreType.DMA((128,)),
            pltpu.SemaphoreType.REGULAR,
        ]
        params = dict(collective_id=0, has_side_effects=True)
    else:
        args = (tokens, cotangent, base, *weights, gains)
        in_specs = [hbm, hbm, sm] + [vm] * 5
        middle = sds(stacked, bf16)
        extra = []
        params = {}
    return pl.pallas_call(
        functools.partial(compute_kernel, linked),
        out_shape=(sds((L, D), bf16), sds((L, D), f32), middle, sds((8, D), f32)),
        in_specs=in_specs,
        out_specs=[hbm, hbm, vm, vm],
        scratch_shapes=extra
        + [pltpu.VMEM(shape, bf16) for shape in ((L, D), (D, L)) * 3]
        + [pltpu.VMEM((parts, L, hm), f32)] * 4
        + [pltpu.VMEM((2 * hm // BLK, L, BLK), f32)]
        + [pltpu.VMEM((L, D), f32)] * 3
        + [
            pltpu.VMEM((L, 2 * fm), bf16),
            pltpu.VMEM((2, SUB, hm), f32),
            pltpu.SemaphoreType.DMA((3,)),
        ],
        compiler_params=pltpu.CompilerParams(vmem_limit_bytes=64 * 2**20 - 2**16, **params),
        name="block",
    )(*args)


def adam_update(first_old, second_old, gradient):
    first_new = beta_one * first_old + (1.0 - beta_one) * gradient
    second_new = beta_two * second_old + (1.0 - beta_two) * gradient * gradient
    first_hat = first_new / (1.0 - beta_one**STEP)
    second_hat = second_new / (1.0 - beta_two**STEP)
    return (first_new, second_new, first_hat / (jnp.sqrt(second_hat) + adam_eps))


def fine_dot(a, b, trans_b=False):
    a_high, b_high = a.astype(bf16), b.astype(bf16)
    a_low, b_low = (a - a_high.astype(f32)).astype(bf16), (b - b_high.astype(f32)).astype(bf16)
    return dot(a_high, b_high, trans_b) + (dot(a_high, b_low, trans_b) + dot(a_low, b_high, trans_b))


def update_kernel(
    low_first,
    token_total,
    passed,
    low,
    sums,
    gains,
    gain_moment_one,
    gain_moment_two,
    owned,
    master,
    moment_one,
    moment_two,
    basis_left,
    basis_right,
    *refs,
):
    given, refs = refs[:passed], refs[passed:]
    first_new, second_new, master_new, master_low, gain_first, gain_second, gains_new, forget_mean = refs[:8]
    copied, refs = refs[8 : 8 + passed], refs[8 + passed :]
    held, made, made_low, sem_in, sem_out, sem_pass = refs[:6]
    passage = refs[6:]
    count = master.shape[0]
    enter = [pltpu.make_async_copy(src, via, sem_pass.at[0, k]) for k, (src, via) in enumerate(zip(given, passage))]
    leave = [pltpu.make_async_copy(via, dst, sem_pass.at[1, k]) for k, (via, dst) in enumerate(zip(passage, copied))]
    sources = (owned, basis_left, basis_right, moment_one, moment_two, master)
    fetch = [
        [pltpu.make_async_copy(src.at[s], held.at[s, k], sem_in.at[s, k]) for k, src in enumerate(sources)]
        for s in range(count)
    ]
    for row in fetch:
        for copy in row:
            copy.start()
    for copy in enter:
        copy.start()
    push = []
    for s in range(count):
        for copy in fetch[s]:
            copy.wait()
        if s == min(2, count - 1):
            for come, go in zip(enter, leave):
                come.wait()
                go.start()
        grad = held[s, 0]
        grad = jnp.where(low[s] >= low_first, grad.T, grad)
        left, right = held[s, 1], held[s, 2]
        rotated = fine_dot(fine_dot(left.T, grad), right)
        first, second, direction = adam_update(held[s, 3], held[s, 4], rotated)
        made[s, 0] = first
        made[s, 1] = second
        turned = fine_dot(fine_dot(left, direction), right, True)
        old = held[s, 5]
        fresh = old - learn_rate * (turned + weight_decay * old)
        made[s, 2] = fresh
        made_low[s] = fresh.astype(bf16)
        for k, (src, dst) in enumerate(
            ((made.at[s, 0], first_new), (made.at[s, 1], second_new), (made.at[s, 2], master_new), (made_low.at[s], master_low))
        ):
            copy = pltpu.make_async_copy(src, dst.at[s], sem_out.at[s, k])
            copy.start()
            push.append(copy)
    first, second, direction = adam_update(gain_moment_one[...], gain_moment_two[...], sums[0:2, :])
    gain_first[...] = first
    gain_second[...] = second
    gains_new[...] = gains[...] - gain_rate * direction
    forget_mean[...] = jnp.sum(sums[2:3, :], axis=1, keepdims=True) * (1.0 / (H * (token_total + 1) / 2.0))
    for copy in push + leave:
        copy.wait()


def update(low_first, token_total, small, large, passed):
    sds = jax.ShapeDtypeStruct
    blocks, gain = large[0].shape, small[2].shape
    vm, hbm = pl.BlockSpec(memory_space=pltpu.VMEM), pl.BlockSpec(memory_space=pl.ANY)
    count = blocks[0]
    return pl.pallas_call(
        functools.partial(update_kernel, low_first, token_total, len(passed)),
        out_shape=[sds(blocks, f32)] * 3
        + [sds(blocks, bf16)]
        + [sds(gain, f32)] * 3
        + [sds((1, 1), f32)]
        + [sds(v.shape, v.dtype) for v in passed],
        in_specs=[pl.BlockSpec(memory_space=pltpu.SMEM)] + [vm] * 4 + [hbm] * (len(large) + len(passed)),
        out_specs=[hbm] * 4 + [vm] * 4 + [hbm] * len(passed),
        scratch_shapes=[
            pltpu.VMEM((count, 6, BLK, BLK), f32),
            pltpu.VMEM((count, 3, BLK, BLK), f32),
            pltpu.VMEM((count, BLK, BLK), bf16),
            pltpu.SemaphoreType.DMA((count, 6)),
            pltpu.SemaphoreType.DMA((count, 4)),
            pltpu.SemaphoreType.DMA((2, len(passed))),
        ]
        + [pltpu.VMEM(v.shape, v.dtype) for v in passed],
        compiler_params=pltpu.CompilerParams(vmem_limit_bytes=56 * 2**20),
        name="update",
    )(*small, *large, *passed)


def on_device(
    tokens,
    cotangent,
    master,
    moment_one,
    moment_two,
    basis_left,
    basis_right,
    owner,
    gains,
    gain_moment_one,
    gain_moment_two,
):
    parts = lax.axis_size("mp")
    data_parts = lax.axis_size("dp")
    hm, fm = H // parts, FF // parts
    token_total = L * data_parts * parts
    row_tiles, cols, lows = D // BLK, (3 * hm + fm) // BLK, (hm + fm) // BLK
    blocks = owner.shape[0]
    number = jnp.arange(blocks, dtype=jnp.int32)
    ahead = (owner[None, :] < owner[:, None]) | ((owner[None, :] == owner[:, None]) & (number[None, :] < number[:, None]))
    block_rank = jnp.sum(ahead.astype(jnp.int32), axis=1)
    slot_order = jnp.sum(jnp.where(block_rank[None, :] == number[:, None], number[None, :], 0), axis=1)
    _, table = stack_places(hm, fm)
    table = jnp.asarray(table, jnp.int32)
    slot_place = jnp.sum(jnp.where(block_rank[None, :] == number[:, None], table[None, :], 0), axis=1)
    if data_parts == 8 and parts == 4:
        block_out, input_grad, owned, sums = compute(
            tokens, cotangent, gains, master=master[0], rank=block_rank, slot_place=slot_place
        )
    else:
        stored = lax.all_gather(master.astype(bf16), "dp", axis=1, tiled=True)
        stored = lax.all_gather(stored, "mp", axis=0, tiled=True)
        stack = stored[:, block_rank]
        upper = stack[:, : row_tiles * cols].reshape(parts, row_tiles, cols, BLK, BLK)
        upper = upper.transpose(0, 1, 3, 2, 4).reshape(parts, D, cols * BLK)
        lower = stack[:, row_tiles * cols :].reshape(parts, lows, row_tiles, BLK, BLK)
        lower = lower.transpose(0, 1, 3, 2, 4).reshape(parts, lows * BLK, D)
        weights = (upper[:, :, : 3 * hm], lower[:, :hm], upper[:, :, 3 * hm :], lower[:, hm:])
        first = ((lax.axis_index("dp") * parts + lax.axis_index("mp")) * L + 1).astype(f32)
        base = jnp.stack([first, jnp.asarray(token_total, f32)])
        block_out, input_grad, grads, sums = compute(tokens, cotangent, gains, weights=weights, base=base)
        owned = lax.psum_scatter(grads[:, slot_place].astype(f32), "dp", scatter_dimension=1, tiled=True)
        owned = lax.psum_scatter(owned, "mp", scatter_dimension=0, tiled=True)[0]
        sums = lax.psum(sums, ("dp", "mp"))
    mine = lax.dynamic_slice_in_dim(slot_order, lax.axis_index("dp") * master.shape[1], master.shape[1])
    outs = update(
        row_tiles * cols,
        token_total,
        (mine, sums, gains, gain_moment_one, gain_moment_two),
        (owned, master[0], moment_one[0], moment_two[0], basis_left[0], basis_right[0]),
        (block_out, input_grad),
    )
    first_new, second_new, master_new, master_low, gain_first, gain_second, gains_new, forget_mean = outs[:8]
    block_out, input_grad = outs[8:]
    return (
        block_out,
        input_grad,
        first_new[None],
        second_new[None],
        master_new[None],
        master_low[None],
        gain_first,
        gain_second,
        gains_new,
        forget_mean[0, 0],
    )


def solution(mesh):
    rows, blocks = P(("dp", "mp"), None), P("mp", "dp", None, None)
    return jax.shard_map(
        on_device,
        mesh=mesh,
        in_specs=(rows, rows, blocks, blocks, blocks, blocks, blocks, P(), P(), P(), P()),
        out_specs=(rows, rows, blocks, blocks, blocks, blocks, P(), P(), P(), P()),
        check_vma=False,
    )
```

```python
import functools

import jax
import jax.numpy as jnp
from jax import lax
from jax.experimental import pallas as pl
from jax.experimental.pallas import tpu as pltpu
from jax.sharding import PartitionSpec as P

D = 512
H = 1024
FF = 2048
BLK = 128
STEP = 10
L = 1024

norm_eps = 1e-05
beta_one = 0.5
beta_two = 0.5
adam_eps = 1e-08
learn_rate = 0.02
gain_rate = 0.1
weight_decay = 0.1
highest = lax.Precision.HIGHEST

f32 = jnp.float32
bf16 = jnp.bfloat16
SUB = 8
J = L // SUB
R = 128


def dot(a, b, trans_b=False):
    dims = (((1,), (1,)), ((), ())) if trans_b else (((1,), (0,)), ((), ()))
    return lax.dot_general(a, b, dims, preferred_element_type=f32)


def recip(v):
    return pltpu.reciprocal(v, approx=True)


def sigmoid(v):
    return recip(1.0 + jnp.exp(-v))


def shift_down(v):
    rolled = pltpu.roll(v, 1, 0)
    row = lax.broadcasted_iota(jnp.int32, v.shape, 0)
    return jnp.where(row == 0, 0.0, rolled)


def shift_up(v):
    rolled = pltpu.roll(v, SUB - 1, 0)
    row = lax.broadcasted_iota(jnp.int32, v.shape, 0)
    return jnp.where(row == SUB - 1, 0.0, rolled)


def gelu_terms(x):
    a = jnp.abs(x)
    t = recip(1.0 + a * (0.3275911 * 0.7071067811865476))
    poly = t * (
        0.5 * 0.254829592
        + t
        * (
            0.5 * -0.284496736
            + t * (0.5 * 1.421413741 + t * (0.5 * -1.453152027 + t * (0.5 * 1.061405429)))
        )
    )
    e = jnp.exp(x * x * -0.5)
    tail = poly * e
    cdf = jnp.where(x < 0.0, tail, 1.0 - tail)
    return cdf, x * e * 0.3989422804014327


MESH = pl.DeviceIdType.MESH


class Exchange:
    def __init__(self, send, recv):
        self.send, self.recv, self.used, self.open = send, recv, 0, []

    def start(self, src, dst, device):
        k = self.used
        self.used += 1
        copy = pltpu.make_async_remote_copy(
            src_ref=src,
            dst_ref=dst,
            send_sem=self.send.at[k],
            recv_sem=self.recv.at[k],
            device_id=device,
            device_id_type=MESH,
        )
        copy.start()
        self.open.append(copy)
        return copy

    def drain(self):
        for copy in self.open:
            copy.wait_send()
        self.open = []


class Gather:
    def __init__(self, net, master, rank, slots, pool, weights, free):
        self.net, self.weights, self.rank, self.free = net, weights, rank, free
        self.held = [slots, *pool]
        d, m = lax.axis_index("dp"), lax.axis_index("mp")
        core, col, row = d % 2, (d // 2) % 2, d // 4
        self.me, self.m, self.side = d, m, core
        self.core = d + 1 - 2 * core
        self.plane = [d + 2 - 4 * col, d + 4 - 8 * row, d + 6 - 4 * col - 8 * row]
        self.order = [m, m + 1 - 2 * (m % 2), m + 2 - 4 * (m // 2), 3 - m]
        self.peers = [(e, m) for e in [self.core] + self.plane] + [(d, k) for k in self.order[1:]]
        self.along, self.first, self.last, self.inside = {}, {}, {}, {}
        barrier = pltpu.get_barrier_semaphore()
        for device in self.peers:
            pl.semaphore_signal(barrier, inc=1, device_id=device, device_id_type=MESH)
        self.n = master.shape[0]
        for s in range(self.n):
            slots[d * self.n + s] = master[s].astype(bf16)
        pl.semaphore_wait(barrier, len(self.peers))

    def rows(self, i, e, first, count):
        return self.held[i].at[pl.ds(e * self.n + first, count)]

    def along_start(self, i):
        self.along[i] = self.net.start(
            self.rows(0, self.me, 0, self.n), self.rows(i, self.me, 0, self.n), (self.me, self.order[i])
        )

    def send(self, i, e, first, count, to):
        ref = self.rows(i, e, first, count)
        return self.net.start(ref, ref, (to, self.m))

    def start(self, i):
        if i:
            self.along[i].wait_recv()
        (x, y, _), h = self.plane, self.n // 2
        self.first[i] = [self.send(i, self.me, *job) for job in ((0, h, x), (h, h, y), (h, h, x), (0, h, y))]
        self.inside[i] = [self.send(i, self.me, 0, self.n, self.core)]

    def forward(self, i):
        (x, y, _), h = self.plane, self.n // 2
        self.first[i][0].wait_recv()
        self.last[i] = [self.send(i, x, 0, h, y)]
        self.first[i][1].wait_recv()
        self.last[i].append(self.send(i, y, h, h, x))

    def pair(self, i):
        x, y, z = self.plane
        self.first[i][2].wait_recv()
        self.inside[i].append(self.send(i, x, 0, self.n, self.core))
        self.first[i][3].wait_recv()
        self.inside[i].append(self.send(i, y, 0, self.n, self.core))
        for copy in self.last[i]:
            copy.wait_recv()
        self.inside[i].append(self.send(i, z, 0, self.n, self.core))

    def ready(self, i):
        for copy in self.inside[i]:
            copy.wait_recv()

    def place(self, i):
        wg, wo, wu, wd = self.weights
        row_tiles, gates = D // BLK, wg.shape[2] // BLK
        cols, outs = gates + wu.shape[2] // BLK, wo.shape[1] // BLK
        for b in range(row_tiles * cols + (wo.shape[1] + wd.shape[1]) // BLK * row_tiles):
            if b < row_tiles * cols:
                r, c = b // cols, b % cols
                ref = wg if c < gates else wu
                c -= 0 if c < gates else gates
            else:
                r, c = (b - row_tiles * cols) // row_tiles, (b - row_tiles * cols) % row_tiles
                ref = wo if r < outs else wd
                r -= 0 if r < outs else outs
            block = self.held[i][self.rank[b]]
            ref[self.order[i], r * BLK : (r + 1) * BLK, c * BLK : (c + 1) * BLK] = block

    def done(self):
        for device in self.peers:
            pl.semaphore_signal(self.free, inc=1, device_id=device, device_id_type=MESH)

    def all_done(self):
        pl.semaphore_wait(self.free, len(self.peers))


def stack_places(hm, fm):
    row_tiles, gates, ups, outs = D // BLK, 3 * hm // BLK, fm // BLK, hm // BLK
    cols = gates + ups
    first_down = row_tiles * ups
    first_out = 2 * first_down
    first_gate = first_out + row_tiles * outs
    table = []
    for b in range(row_tiles * (cols + outs + ups)):
        if b < row_tiles * cols:
            r, c = b // cols, b % cols
            table.append(first_gate + r * gates + c if c < gates else r * ups + c - gates)
        else:
            k = b - row_tiles * cols
            table.append(first_out + k if k < row_tiles * outs else first_down + k - row_tiles * outs)
    return ((0, first_out), (first_out, row_tiles * outs), (first_gate, row_tiles * gates)), table


UPDOWN, OUT, GATE = range(3)


class Reduce:
    def __init__(self, net, gather, grads, units, pool):
        self.net, self.g, self.grads, self.units, self.pool = net, gather, grads, units, pool
        self.half = grads.shape[1] // 2
        self.eighth = grads.shape[1] // 8
        self.copies = {}

    def place(self, e):
        return (e % 2) * 4 + e // 2

    def chip(self, unit, i):
        g, (first, count) = self.g, self.units[unit]
        src = self.grads.at[g.order[i], pl.ds(first + (1 - g.side) * (count // 2), count // 2)]
        dst = self.pool[i - 1].at[pl.ds(first // 2, count // 2)]
        self.copies[0, unit, i] = self.net.start(src, dst, (g.core, g.m))

    def spot(self, unit, i, slot, first, count):
        base, total = self.units[unit]
        return self.pool[i - 1].at[pl.ds(self.half + slot * self.eighth + base // 8 + first, count)]

    def parts(self, unit, i):
        n = self.units[unit][1] // 8
        h = (n + i % 2) // 2 if n % 2 else n // 2
        return (0, h), (h, n - h)

    def share(self, unit, i, e, first, count):
        base, total = self.units[unit]
        return self.grads.at[self.g.order[i], pl.ds(base + self.place(e) * (total // 8) + first, count)]

    def send(self, unit, i, e, part, slot, to):
        if part[1]:
            src, dst = self.share(unit, i, e, *part), self.spot(unit, i, slot, *part)
            self.copies[1, unit, i, slot, part] = self.net.start(src, dst, (to, self.g.m))

    def take(self, unit, i, slot, part):
        self.copies[1, unit, i, slot, part].wait_recv()
        return self.spot(unit, i, slot, *part)[...].astype(f32)

    def plane(self, unit, i):
        g, (first, count) = self.g, self.units[unit]
        x, y, z = g.plane
        self.copies[0, unit, i].wait_recv()
        m = g.order[i]
        rows = pl.ds(first + g.side * (count // 2), count // 2)
        total = self.grads[m, rows].astype(f32) + self.pool[i - 1][first // 2 : (first + count) // 2].astype(f32)
        self.grads[m, rows] = total.astype(bf16)
        one, two = self.parts(unit, i)
        self.send(unit, i, z, one, 0, x)
        self.send(unit, i, z, two, 0, y)
        self.send(unit, i, x, one, 1, x)
        self.send(unit, i, y, two, 2, y)

    def turn(self, unit, i):
        x, y, z = self.g.plane
        for part, slot, e in zip(self.parts(unit, i), (2, 1), (y, x)):
            if part[1]:
                ref = self.share(unit, i, e, *part)
                ref[...] = (ref[...].astype(f32) + self.take(unit, i, 0, part)).astype(bf16)
                self.send(unit, i, e, part, slot, e)

    def model(self, unit, i):
        g, (first, count) = self.g, self.units[unit]
        n = count // 8
        for part in self.parts(unit, i):
            if part[1]:
                ref = self.share(unit, i, g.me, *part)
                total = ref[...].astype(f32) + self.take(unit, i, 1, part) + self.take(unit, i, 2, part)
                ref[...] = total.astype(bf16)
        dst = self.pool[i - 1].at[pl.ds(self.half + 3 * self.eighth + first // 8, n)]
        self.copies[2, unit, i] = self.net.start(self.share(unit, i, g.me, 0, n), dst, (g.me, g.order[i]))

    def own(self, unit):
        g, (first, count) = self.g, self.units[unit]
        n = count // 8
        rows = pl.ds(first + self.place(g.me) * n, n)
        total = self.grads[g.m, rows].astype(f32)
        for i in (1, 2, 3):
            self.copies[2, unit, i].wait_recv()
            total += self.pool[i - 1][pl.ds(self.half + 3 * self.eighth + first // 8, n)].astype(f32)
        self.grads[g.m, rows] = total.astype(bf16)

    def into_slots(self, out, slot_place):
        n = self.eighth
        for s in range(8 * n):
            out[self.place(s // n) * n + s % n] = self.grads[self.g.m, slot_place[s]]

    def slots_chip(self, out, pair):
        g, n = self.g, out.shape[0] // 8
        self.last = []
        for e in (g.plane[2], g.plane[0], g.plane[1], g.me):
            src = out.at[pl.ds(((1 - g.side) * 4 + e // 2) * n, n)]
            self.last.append(self.net.start(src, pair.at[pl.ds((e // 2) * n, n)], (g.core, g.m)))

    def slots_plane(self, out, pair, far):
        g, n = self.g, out.shape[0] // 8
        h = n // 2
        x, y, z = g.plane
        wait = dict(zip("zxyo", self.last))

        def mine(e, first, count):
            return pl.ds((g.side * 4 + e // 2) * n + first, count)

        def join(e):
            rows = mine(e, 0, n)
            out[rows] = (out[rows].astype(f32) + pair[pl.ds((e // 2) * n, n)].astype(f32)).astype(bf16)

        def send(e, first, slot, to):
            return self.net.start(out.at[mine(e, first, h)], far.at[slot], (to, g.m))

        wait["z"].wait_recv()
        join(z)
        over_x = send(z, 0, 0, x)
        over_y = send(z, h, 1, y)
        wait["x"].wait_recv()
        join(x)
        self.ends = [send(x, 0, 2, x)]
        wait["y"].wait_recv()
        join(y)
        self.ends.append(send(y, h, 3, y))
        over_x.wait_recv()
        rows = mine(y, 0, h)
        out[rows] = (out[rows].astype(f32) + far[0].astype(f32)).astype(bf16)
        self.ends.append(send(y, 0, 4, y))
        over_y.wait_recv()
        rows = mine(x, h, h)
        out[rows] = (out[rows].astype(f32) + far[1].astype(f32)).astype(bf16)
        self.ends.append(send(x, h, 5, x))
        wait["o"].wait_recv()

    def slots_end(self, out, pair, far, owned):
        g, n = self.g, out.shape[0] // 8
        h = n // 2
        for copy in self.ends:
            copy.wait_recv()
        for first, slots in ((0, (2, 4)), (h, (3, 5))):
            total = out[pl.ds((g.side * 4 + g.me // 2) * n + first, h)].astype(f32)
            total += pair[pl.ds((g.me // 2) * n + first, h)].astype(f32)
            for k in slots:
                total += far[k].astype(f32)
            owned[first : first + h] = total


class SmallSum:
    def __init__(self, net, gather, values, along, across, inside):
        self.net, self.g, self.values = net, gather, values
        self.slots = (along, across, inside)
        self.peers = (
            [(gather.me, k) for k in gather.order[1:]],
            [(e, gather.m) for e in gather.plane],
            [(gather.core, gather.m)],
        )
        self.mine = (gather.m, gather.me // 2, gather.side)
        self.open = []

    def send(self, stage):
        slot = self.slots[stage]
        slot[self.mine[stage]] = self.values[...]
        ref = slot.at[self.mine[stage]]
        self.open = [self.net.start(ref, ref, peer) for peer in self.peers[stage]]

    def add(self, stage):
        for copy in self.open:
            copy.wait_recv()
        slot = self.slots[stage]
        total = slot[0]
        for k in range(1, slot.shape[0]):
            total += slot[k]
        self.values[...] = total


def compute_kernel(linked, *refs):
    if linked:
        tokens, cotangent, master, rank, slot_place, gains = refs[:6]
        block_out, input_grad, owned, small = refs[6:10]
        wg, wo, wu, wd, grads, slots, *pool, pair, far, sum_a, sum_b, sum_c, send, recv, free = refs[10:27]
        scratch = refs[27:]
    else:
        tokens, cotangent, base, wg, wo, wu, wd, gains = refs[:8]
        block_out, input_grad, grads, small = refs[8:12]
        scratch = refs[12:]
    (n1, n1t, cot, cott, n2, n2t, forget, admit, cand, state, scan, acc_a, acc_b, mixed, mid, kept, fills, local) = scratch
    dml, dmlt = n2, n2t
    parts, _, hm3 = wg.shape
    hm = hm3 // 3
    fm = wu.shape[2]
    units, _ = stack_places(hm, fm)
    act, dup, dpre = mid.at[:, :fm], mid.at[:, fm:], mid.at[:, : 3 * hm]
    gain_one = gains[0:1, :]
    gain_two = gains[1:2, :]

    fetch_cot = pltpu.make_async_copy(cotangent, cot, local.at[0])
    fetch_tok = pltpu.make_async_copy(tokens, n1, local.at[1])
    fetch_tok.start()
    fetch_cot.start()

    def stack(m, first, value):
        wide = value.shape[1] // BLK
        for r in range(value.shape[0] // BLK):
            for c in range(wide):
                grads[m, first + r * wide + c] = value[r * BLK : (r + 1) * BLK, c * BLK : (c + 1) * BLK].astype(bf16)

    def stack_turned(m, first, value):
        high = value.shape[0] // BLK
        for r in range(high):
            for c in range(value.shape[1] // BLK):
                grads[m, first + c * high + r] = value[r * BLK : (r + 1) * BLK, c * BLK : (c + 1) * BLK].astype(bf16)

    def permute_in(src, dst):
        for k in range(D // BLK):
            scan[k] = src[:, k * BLK : (k + 1) * BLK].astype(f32)

        @pl.loop(0, J // 2, unroll=4)
        def _(j):
            for k in range(D // BLK):
                lo = scan[k, pl.ds(2 * j, SUB, stride=J), :]
                hi = scan[k, pl.ds(2 * j + 1, SUB, stride=J), :]
                dst[pl.ds(pl.multiple_of(16 * j, 16), 16), k * BLK : (k + 1) * BLK] = jnp.concatenate([lo, hi], 0).astype(bf16)

    def permute_out(src, dst):
        @pl.loop(0, J, unroll=4)
        def _(j):
            rows = pl.ds(pl.multiple_of(j * SUB, SUB), SUB)
            for k in range(D // BLK):
                scan[k, pl.ds(j, SUB, stride=J), :] = src[rows, k * BLK : (k + 1) * BLK]

        for k in range(D // BLK):
            dst[:, k * BLK : (k + 1) * BLK] = scan[k].astype(dst.dtype)

    def put(first, rows, value):
        for k in range(hm // BLK):
            scan[first + k, rows, :] = value[:, k * BLK : (k + 1) * BLK]

    def take(first, rows):
        return jnp.concatenate([scan[first + k, rows, :] for k in range(hm // BLK)], 1)

    half = hm // BLK

    def spread(v):
        return jnp.broadcast_to(v[None], (R // SUB, SUB, hm)).reshape(R, hm)


    if linked:
        net = Exchange(send, recv)
        gather = Gather(net, master, rank, slots, pool, (wg, wo, wu, wd), free)
        gather.start(0)
        gather.along_start(1)
        reduce = Reduce(net, gather, grads, units, pool)
        order = gather.order
    else:
        order = list(range(parts))

    fetch_tok.wait()
    permute_in(n1, n1)
    mixed[...] = n1[...].astype(f32)

    @pl.loop(0, L // R)
    def _(i):
        rows = pl.ds(pl.multiple_of(i * R, R), R)
        x = mixed[rows, :]
        r = lax.rsqrt(jnp.mean(x * x, axis=-1, keepdims=True) + norm_eps)
        n1[rows, :] = (x * r * gain_one).astype(bf16)

    n1t[...] = n1[...].T

    if linked:
        gather.forward(0)
        gather.along_start(2)
        gather.along_start(3)
    fetch_cot.wait()
    permute_in(cot, cot)
    if linked:
        gather.start(1)
        gather.pair(0)
    cott[...] = cot[...].T

    fills[0] = jnp.zeros((SUB, hm), f32)
    fills[1] = jnp.ones((SUB, hm), f32)
    weigh = fills[0]
    weigh_j = fills[0]
    for turn, m in enumerate(order):

        if linked:
            if turn:
                gather.pair(turn)
            gather.ready(turn)
            gather.place(turn)

        forget[m] = dot(n1[...], wg[m, :, :hm])
        admit[m] = dot(n1[...], wg[m, :, hm : 2 * hm])
        cand[m] = dot(n1[...], wg[m, :, 2 * hm :])

        if linked and turn < 3:
            gather.forward(turn + 1)
            if turn < 2:
                gather.start(turn + 2)

        @pl.loop(0, L // R)
        def _(i):
            rows = pl.ds(pl.multiple_of(i * R, R), R)
            f = sigmoid(forget[m, rows, :])
            a = sigmoid(admit[m, rows, :])
            inv = recip(f + a)
            forget[m, rows, :] = f
            admit[m, rows, :] = a
            kept[rows, :] = f * inv
            put(0, rows, a * inv * cand[m, rows, :])

        def step(j, carry):
            s, p, k_sum, kj_sum = carry
            rows = pl.ds(pl.multiple_of(j * SUB, SUB), SUB)
            keep = kept[rows, :]
            s = keep * s + take(0, rows)
            p = keep * p
            put(0, rows, s)
            put(half, rows, p)
            return s, p, k_sum + keep, kj_sum + keep * j.astype(f32)

        s, p, weigh, weigh_j = lax.fori_loop(0, J, step, (fills[0], fills[1], weigh, weigh_j), unroll=16)
        enter = fills[0]
        for _ in range(SUB - 1):
            enter = shift_down(s + p * enter)

        @pl.loop(0, L // R)
        def _(i):
            rows = pl.ds(pl.multiple_of(i * R, R), R)
            state[m, pl.ds(pl.multiple_of(i * R + SUB, SUB), R), :] = take(0, rows) + take(half, rows) * spread(enter)

        state[m, :SUB, :] = shift_down(state[m, L:, :])

    if linked:
        net.drain()
        gather.done()

    for m in range(parts):
        mixed[...] += dot(state[m, SUB:, :].astype(bf16), wo[m])

    @pl.loop(0, L // R)
    def _(i):
        rows = pl.ds(pl.multiple_of(i * R, R), R)
        x = mixed[rows, :]
        r = lax.rsqrt(jnp.mean(x * x, axis=-1, keepdims=True) + norm_eps)
        n2[rows, :] = (x * r * gain_two).astype(bf16)
        acc_a[rows, :] = x
        acc_b[rows, :] = jnp.zeros_like(x)

    n2t[...] = n2[...].T

    for turn, m in enumerate(order):

        for first in range(0, fm, fm // 2):
            units_of = slice(first, first + fm // 2)
            up = dot(n2[...], wu[m, :, units_of])
            da = dot(cot[...], wd[m, units_of, :], True)
            cdf, xpdf = gelu_terms(up)
            act[:, units_of] = (up * cdf).astype(bf16)
            dup[:, units_of] = (da * (cdf + xpdf)).astype(bf16)
        if linked and turn >= 2:
            reduce.plane(UPDOWN, turn - 1)
        acc_a[...] += dot(act[...], wd[m])
        acc_b[...] += dot(dup[...], wu[m], True)
        if linked and turn >= 2:
            reduce.turn(UPDOWN, turn - 1)
        if linked and turn == 3:
            reduce.model(UPDOWN, 1)
        stack(m, 0, dot(n2t[...], dup[...]))
        stack_turned(m, units[UPDOWN][1] // 2, dot(cott[...], act[...]))
        if linked and turn:
            if turn == 1:
                gather.all_done()
            reduce.chip(UPDOWN, turn)

    permute_out(acc_a, n1)
    push_out = pltpu.make_async_copy(n1, block_out, local.at[0])
    push_out.start()

    if linked:
        reduce.plane(UPDOWN, 3)
        reduce.model(UPDOWN, 2)
        reduce.turn(UPDOWN, 3)

    gain_sum_two = jnp.zeros((1, D), f32)

    def back_two(i, total):
        rows = pl.ds(pl.multiple_of(i * R, R), R)
        x = mixed[rows, :]
        r = lax.rsqrt(jnp.mean(x * x, axis=-1, keepdims=True) + norm_eps)
        dn = acc_b[rows, :]
        q = dn * gain_two
        d = cot[rows, :].astype(f32) + r * q - r * r * r * x * jnp.mean(q * x, axis=-1, keepdims=True)
        mixed[rows, :] = d
        dml[rows, :] = d.astype(bf16)
        acc_b[rows, :] = jnp.zeros_like(d)
        return total + jnp.sum(dn * x * r, axis=0, keepdims=True)

    gain_sum_two = lax.fori_loop(0, L // R, back_two, gain_sum_two)
    dmlt[...] = dml[...].T
    fetch_tok = pltpu.make_async_copy(tokens, cot, local.at[1])
    fetch_tok.start()

    for turn, m in reversed(list(enumerate(order))):
        stack_turned(m, units[OUT][0], dot(dmlt[...], state[m, SUB:, :].astype(bf16)))
        if linked and turn:
            reduce.chip(OUT, turn)

    for turn, m in reversed(list(enumerate(order))):

        put(0, slice(None), dot(dml[...], wo[m], True))

        @pl.loop(0, L // R)
        def _(i):
            rows = pl.ds(pl.multiple_of(i * R, R), R)
            f = forget[m, rows, :]
            kept[rows, :] = f * recip(f + admit[m, rows, :])

        def step(k, carry):
            u, p, keep_next = carry
            j = J - 1 - k
            rows = pl.ds(pl.multiple_of(j * SUB, SUB), SUB)
            u = take(0, rows) + keep_next * u
            p = keep_next * p
            put(0, rows, u)
            put(half, rows, p)
            return u, p, kept[rows, :]

        u, p, keep_first = lax.fori_loop(0, J, step, (fills[0], fills[1], fills[1]), unroll=16)
        enter = fills[0]
        for _ in range(SUB - 1):
            enter = shift_up(keep_first * (u + p * enter))

        if linked:
            if turn == 3:
                reduce.model(UPDOWN, 3)
                for i in (3, 2, 1):
                    reduce.plane(OUT, i)
            if turn < 3:
                reduce.plane(GATE, turn + 1)
            if turn < 2:
                reduce.model(GATE, turn + 2)
            if turn == 0:
                reduce.own(OUT)
                reduce.own(UPDOWN)

        @pl.loop(0, L // R)
        def _(i):
            rows = pl.ds(pl.multiple_of(i * R, R), R)
            carried = take(0, rows) + take(half, rows) * spread(enter)
            f = forget[m, rows, :]
            a = admit[m, rows, :]
            adm = a * recip(f + a)
            g = carried * (state[m, rows, :] - cand[m, rows, :]) * (kept[rows, :] * adm)
            dpre[rows, :hm] = (g * (1.0 - f)).astype(bf16)
            dpre[rows, hm : 2 * hm] = (g * (a - 1.0)).astype(bf16)
            dpre[rows, 2 * hm :] = (carried * adm).astype(bf16)

        if linked and turn < 3:
            reduce.turn(GATE, turn + 1)
            if turn == 2:
                for i in (3, 2, 1):
                    reduce.model(OUT, i)
        if linked and turn == 3:
            for i in (3, 2, 1):
                reduce.turn(OUT, i)
        stack(m, units[GATE][0], dot(n1t[...], dpre[...]))
        if linked and turn:
            reduce.chip(GATE, turn)

        acc_b[...] += dot(dpre[...], wg[m], True)

    fetch_tok.wait()
    permute_in(cot, cot)

    if linked:
        reduce.model(GATE, 1)

    def back_one(i, total):
        rows = pl.ds(pl.multiple_of(i * R, R), R)
        x = cot[rows, :].astype(f32)
        r = lax.rsqrt(jnp.mean(x * x, axis=-1, keepdims=True) + norm_eps)
        dn = acc_b[rows, :]
        q = dn * gain_one
        mixed[rows, :] += r * q - r * r * r * x * jnp.mean(q * x, axis=-1, keepdims=True)
        return total + jnp.sum(dn * x * r, axis=0, keepdims=True)

    gain_sum_one = lax.fori_loop(0, L // R, back_one, jnp.zeros((1, D), f32))

    place = lax.broadcasted_iota(jnp.int32, (SUB, hm), 0).astype(f32) * float(J)
    if linked:
        first = ((gather.me * parts + gather.m) * L + 1).astype(f32)
        token_total = float(L * parts * lax.axis_size("dp"))
    else:
        first = base[0]
        token_total = base[1]
    forget_sum = jnp.sum(weigh_j + weigh * (place + first), axis=0, keepdims=True) / token_total
    small[...] = jnp.zeros_like(small)
    small[0:1, :] = gain_sum_one
    small[1:2, :] = gain_sum_two
    small[2:3, :hm] = forget_sum

    if linked:
        tiny = SmallSum(net, gather, small, sum_a, sum_b, sum_c)
        tiny.send(0)
        reduce.own(GATE)
        reduce.into_slots(slots, slot_place)
        reduce.slots_chip(slots, pair)
        tiny.add(0)
        tiny.send(1)
        reduce.slots_plane(slots, pair, far)

    permute_out(mixed, acc_a)
    push_grad = pltpu.make_async_copy(acc_a, input_grad, local.at[2])
    push_grad.start()

    if linked:
        tiny.add(1)
        tiny.send(2)
        reduce.slots_end(slots, pair, far, owned)
        tiny.add(2)
        net.drain()
    push_out.wait()
    push_grad.wait()


def compute(tokens, cotangent, gains, weights=None, base=None, master=None, rank=None, slot_place=None):
    linked = weights is None
    parts = lax.axis_size("mp")
    hm, fm = H // parts, FF // parts
    stacked = (parts, D * (4 * hm + 2 * fm) // BLK**2, BLK, BLK)
    sds = jax.ShapeDtypeStruct
    vm, sm, hbm = (pl.BlockSpec(memory_space=k) for k in (pltpu.VMEM, pltpu.SMEM, pl.ANY))
    if linked:
        n = rank.shape[0]
        args = (tokens, cotangent, master, rank, slot_place, gains)
        in_specs = [hbm, hbm, vm, sm, sm, vm]
        middle = sds((n // 8, BLK, BLK), f32)
        extra = [
            pltpu.VMEM((parts, D, 3 * hm), bf16),
            pltpu.VMEM((parts, hm, D), bf16),
            pltpu.VMEM((parts, D, fm), bf16),
            pltpu.VMEM((parts, fm, D), bf16),
            pltpu.VMEM(stacked, bf16),
            pltpu.VMEM((n, BLK, BLK), bf16),
            *[pltpu.VMEM((n, BLK, BLK), bf16) for _ in range(parts - 1)],
            pltpu.VMEM((n // 2, BLK, BLK), bf16),
            pltpu.VMEM((6, n // 16, BLK, BLK), bf16),
            pltpu.VMEM((parts, 8, D), f32),
            pltpu.VMEM((4, 8, D), f32),
            pltpu.VMEM((2, 8, D), f32),
            pltpu.SemaphoreType.DMA((128,)),
            pltpu.SemaphoreType.DMA((128,)),
            pltpu.SemaphoreType.REGULAR,
        ]
        params = dict(collective_id=0, has_side_effects=True)
    else:
        args = (tokens, cotangent, base, *weights, gains)
        in_specs = [hbm, hbm, sm] + [vm] * 5
        middle = sds(stacked, bf16)
        extra = []
        params = {}
    return pl.pallas_call(
        functools.partial(compute_kernel, linked),
        out_shape=(sds((L, D), bf16), sds((L, D), f32), middle, sds((8, D), f32)),
        in_specs=in_specs,
        out_specs=[hbm, hbm, vm, vm],
        scratch_shapes=extra
        + [pltpu.VMEM(shape, bf16) for shape in ((L, D), (D, L)) * 3]
        + [pltpu.VMEM((parts, L, hm), f32)] * 3
        + [pltpu.VMEM((parts, L + SUB, hm), f32)]
        + [pltpu.VMEM((2 * hm // BLK, L, BLK), f32)]
        + [pltpu.VMEM((L, D), f32)] * 3
        + [
            pltpu.VMEM((L, 2 * fm), bf16),
            pltpu.VMEM((L, hm), f32),
            pltpu.VMEM((2, SUB, hm), f32),
            pltpu.SemaphoreType.DMA((3,)),
        ],
        compiler_params=pltpu.CompilerParams(vmem_limit_bytes=64 * 2**20 - 2**16, **params),
        name="block",
    )(*args)


def adam_update(first_old, second_old, gradient):
    first_new = beta_one * first_old + (1.0 - beta_one) * gradient
    second_new = beta_two * second_old + (1.0 - beta_two) * gradient * gradient
    first_hat = first_new / (1.0 - beta_one**STEP)
    second_hat = second_new / (1.0 - beta_two**STEP)
    return (first_new, second_new, first_hat / (jnp.sqrt(second_hat) + adam_eps))


def fine_dot(a, b, trans_b=False):
    a_high, b_high = a.astype(bf16), b.astype(bf16)
    a_low, b_low = (a - a_high.astype(f32)).astype(bf16), (b - b_high.astype(f32)).astype(bf16)
    return dot(a_high, b_high, trans_b) + (dot(a_high, b_low, trans_b) + dot(a_low, b_high, trans_b))


def update_kernel(
    low_first,
    token_total,
    passed,
    low,
    sums,
    gains,
    gain_moment_one,
    gain_moment_two,
    owned,
    master,
    moment_one,
    moment_two,
    basis_left,
    basis_right,
    *refs,
):
    given, refs = refs[:passed], refs[passed:]
    first_new, second_new, master_new, master_low, gain_first, gain_second, gains_new, forget_mean = refs[:8]
    copied, refs = refs[8 : 8 + passed], refs[8 + passed :]
    held, made, made_low, sem_in, sem_out, sem_pass = refs[:6]
    passage = refs[6:]
    count = master.shape[0]
    enter = [pltpu.make_async_copy(src, via, sem_pass.at[0, k]) for k, (src, via) in enumerate(zip(given, passage))]
    leave = [pltpu.make_async_copy(via, dst, sem_pass.at[1, k]) for k, (via, dst) in enumerate(zip(passage, copied))]
    sources = (owned, basis_left, basis_right, moment_one, moment_two, master)
    fetch = [
        [pltpu.make_async_copy(src.at[s], held.at[s, k], sem_in.at[s, k]) for k, src in enumerate(sources)]
        for s in range(count)
    ]
    for row in fetch:
        for copy in row:
            copy.start()
    for copy in enter:
        copy.start()
    push = []
    for s in range(count):
        for copy in fetch[s]:
            copy.wait()
        if s == min(2, count - 1):
            for come, go in zip(enter, leave):
                come.wait()
                go.start()
        grad = held[s, 0]
        grad = jnp.where(low[s] >= low_first, grad.T, grad)
        left, right = held[s, 1], held[s, 2]
        rotated = fine_dot(fine_dot(left.T, grad), right)
        first, second, direction = adam_update(held[s, 3], held[s, 4], rotated)
        made[s, 0] = first
        made[s, 1] = second
        turned = fine_dot(fine_dot(left, direction), right, True)
        old = held[s, 5]
        fresh = old - learn_rate * (turned + weight_decay * old)
        made[s, 2] = fresh
        made_low[s] = fresh.astype(bf16)
        for k, (src, dst) in enumerate(
            ((made.at[s, 0], first_new), (made.at[s, 1], second_new), (made.at[s, 2], master_new), (made_low.at[s], master_low))
        ):
            copy = pltpu.make_async_copy(src, dst.at[s], sem_out.at[s, k])
            copy.start()
            push.append(copy)
    first, second, direction = adam_update(gain_moment_one[...], gain_moment_two[...], sums[0:2, :])
    gain_first[...] = first
    gain_second[...] = second
    gains_new[...] = gains[...] - gain_rate * direction
    forget_mean[...] = jnp.sum(sums[2:3, :], axis=1, keepdims=True) * (1.0 / (H * (token_total + 1) / 2.0))
    for copy in push + leave:
        copy.wait()


def update(low_first, token_total, small, large, passed):
    sds = jax.ShapeDtypeStruct
    blocks, gain = large[0].shape, small[2].shape
    vm, hbm = pl.BlockSpec(memory_space=pltpu.VMEM), pl.BlockSpec(memory_space=pl.ANY)
    count = blocks[0]
    return pl.pallas_call(
        functools.partial(update_kernel, low_first, token_total, len(passed)),
        out_shape=[sds(blocks, f32)] * 3
        + [sds(blocks, bf16)]
        + [sds(gain, f32)] * 3
        + [sds((1, 1), f32)]
        + [sds(v.shape, v.dtype) for v in passed],
        in_specs=[pl.BlockSpec(memory_space=pltpu.SMEM)] + [vm] * 4 + [hbm] * (len(large) + len(passed)),
        out_specs=[hbm] * 4 + [vm] * 4 + [hbm] * len(passed),
        scratch_shapes=[
            pltpu.VMEM((count, 6, BLK, BLK), f32),
            pltpu.VMEM((count, 3, BLK, BLK), f32),
            pltpu.VMEM((count, BLK, BLK), bf16),
            pltpu.SemaphoreType.DMA((count, 6)),
            pltpu.SemaphoreType.DMA((count, 4)),
            pltpu.SemaphoreType.DMA((2, len(passed))),
        ]
        + [pltpu.VMEM(v.shape, v.dtype) for v in passed],
        compiler_params=pltpu.CompilerParams(vmem_limit_bytes=56 * 2**20),
        name="update",
    )(*small, *large, *passed)


def on_device(
    tokens,
    cotangent,
    master,
    moment_one,
    moment_two,
    basis_left,
    basis_right,
    owner,
    gains,
    gain_moment_one,
    gain_moment_two,
):
    parts = lax.axis_size("mp")
    data_parts = lax.axis_size("dp")
    hm, fm = H // parts, FF // parts
    token_total = L * data_parts * parts
    row_tiles, cols, lows = D // BLK, (3 * hm + fm) // BLK, (hm + fm) // BLK
    blocks = owner.shape[0]
    number = jnp.arange(blocks, dtype=jnp.int32)
    ahead = (owner[None, :] < owner[:, None]) | ((owner[None, :] == owner[:, None]) & (number[None, :] < number[:, None]))
    block_rank = jnp.sum(ahead.astype(jnp.int32), axis=1)
    slot_order = jnp.sum(jnp.where(block_rank[None, :] == number[:, None], number[None, :], 0), axis=1)
    _, table = stack_places(hm, fm)
    table = jnp.asarray(table, jnp.int32)
    slot_place = jnp.sum(jnp.where(block_rank[None, :] == number[:, None], table[None, :], 0), axis=1)
    if data_parts == 8 and parts == 4:
        block_out, input_grad, owned, sums = compute(
            tokens, cotangent, gains, master=master[0], rank=block_rank, slot_place=slot_place
        )
    else:
        stored = lax.all_gather(master.astype(bf16), "dp", axis=1, tiled=True)
        stored = lax.all_gather(stored, "mp", axis=0, tiled=True)
        stack = stored[:, block_rank]
        upper = stack[:, : row_tiles * cols].reshape(parts, row_tiles, cols, BLK, BLK)
        upper = upper.transpose(0, 1, 3, 2, 4).reshape(parts, D, cols * BLK)
        lower = stack[:, row_tiles * cols :].reshape(parts, lows, row_tiles, BLK, BLK)
        lower = lower.transpose(0, 1, 3, 2, 4).reshape(parts, lows * BLK, D)
        weights = (upper[:, :, : 3 * hm], lower[:, :hm], upper[:, :, 3 * hm :], lower[:, hm:])
        first = ((lax.axis_index("dp") * parts + lax.axis_index("mp")) * L + 1).astype(f32)
        base = jnp.stack([first, jnp.asarray(token_total, f32)])
        block_out, input_grad, grads, sums = compute(tokens, cotangent, gains, weights=weights, base=base)
        owned = lax.psum_scatter(grads[:, slot_place].astype(f32), "dp", scatter_dimension=1, tiled=True)
        owned = lax.psum_scatter(owned, "mp", scatter_dimension=0, tiled=True)[0]
        sums = lax.psum(sums, ("dp", "mp"))
    mine = lax.dynamic_slice_in_dim(slot_order, lax.axis_index("dp") * master.shape[1], master.shape[1])
    outs = update(
        row_tiles * cols,
        token_total,
        (mine, sums, gains, gain_moment_one, gain_moment_two),
        (owned, master[0], moment_one[0], moment_two[0], basis_left[0], basis_right[0]),
        (block_out, input_grad),
    )
    first_new, second_new, master_new, master_low, gain_first, gain_second, gains_new, forget_mean = outs[:8]
    block_out, input_grad = outs[8:]
    return (
        block_out,
        input_grad,
        first_new[None],
        second_new[None],
        master_new[None],
        master_low[None],
        gain_first,
        gain_second,
        gains_new,
        forget_mean[0, 0],
    )


def solution(mesh):
    rows, blocks = P(("dp", "mp"), None), P("mp", "dp", None, None)
    return jax.shard_map(
        on_device,
        mesh=mesh,
        in_specs=(rows, rows, blocks, blocks, blocks, blocks, blocks, P(), P(), P(), P()),
        out_specs=(rows, rows, blocks, blocks, blocks, blocks, P(), P(), P(), P()),
        check_vma=False,
    )
```

```python
import functools

import jax
import jax.numpy as jnp
from jax import lax
from jax.experimental import pallas as pl
from jax.experimental.pallas import tpu as pltpu
from jax.sharding import PartitionSpec as P

D = 512
H = 1024
FF = 2048
BLK = 128
STEP = 10
L = 1024

norm_eps = 1e-05
beta_one = 0.5
beta_two = 0.5
adam_eps = 1e-08
learn_rate = 0.02
gain_rate = 0.1
weight_decay = 0.1
highest = lax.Precision.HIGHEST

f32 = jnp.float32
bf16 = jnp.bfloat16
SUB = 8
J = L // SUB
R = 128


def dot(a, b, trans_b=False):
    dims = (((1,), (1,)), ((), ())) if trans_b else (((1,), (0,)), ((), ()))
    return lax.dot_general(a, b, dims, preferred_element_type=f32)


def recip(v):
    return pltpu.reciprocal(v, approx=True)


def sigmoid(v):
    return recip(1.0 + jnp.exp(-v))


def shift_down(v):
    rolled = pltpu.roll(v, 1, 0)
    row = lax.broadcasted_iota(jnp.int32, v.shape, 0)
    return jnp.where(row == 0, 0.0, rolled)


def shift_up(v):
    rolled = pltpu.roll(v, SUB - 1, 0)
    row = lax.broadcasted_iota(jnp.int32, v.shape, 0)
    return jnp.where(row == SUB - 1, 0.0, rolled)


def gelu_terms(x):
    a = jnp.abs(x)
    t = recip(1.0 + a * (0.3275911 * 0.7071067811865476))
    poly = t * (
        0.5 * 0.254829592
        + t
        * (
            0.5 * -0.284496736
            + t * (0.5 * 1.421413741 + t * (0.5 * -1.453152027 + t * (0.5 * 1.061405429)))
        )
    )
    e = jnp.exp(x * x * -0.5)
    tail = poly * e
    cdf = jnp.where(x < 0.0, tail, 1.0 - tail)
    return cdf, x * e * 0.3989422804014327


MESH = pl.DeviceIdType.MESH


class Exchange:
    def __init__(self, send, recv):
        self.send, self.recv, self.used, self.open = send, recv, 0, []

    def start(self, src, dst, device):
        k = self.used
        self.used += 1
        copy = pltpu.make_async_remote_copy(
            src_ref=src,
            dst_ref=dst,
            send_sem=self.send.at[k],
            recv_sem=self.recv.at[k],
            device_id=device,
            device_id_type=MESH,
        )
        copy.start()
        self.open.append(copy)
        return copy

    def drain(self):
        for copy in self.open:
            copy.wait_send()
        self.open = []


class Gather:
    def __init__(self, net, master, rank, slots, pool, weights, free):
        self.net, self.weights, self.rank, self.free = net, weights, rank, free
        self.held = [slots, *pool]
        d, m = lax.axis_index("dp"), lax.axis_index("mp")
        core, col, row = d % 2, (d // 2) % 2, d // 4
        self.me, self.m, self.side = d, m, core
        self.core = d + 1 - 2 * core
        self.plane = [d + 2 - 4 * col, d + 4 - 8 * row, d + 6 - 4 * col - 8 * row]
        self.order = [m, m + 1 - 2 * (m % 2), m + 2 - 4 * (m // 2), 3 - m]
        self.peers = [(e, m) for e in [self.core] + self.plane] + [(d, k) for k in self.order[1:]]
        self.along, self.first, self.last, self.inside = {}, {}, {}, {}
        barrier = pltpu.get_barrier_semaphore()
        for device in self.peers:
            pl.semaphore_signal(barrier, inc=1, device_id=device, device_id_type=MESH)
        self.n = master.shape[0]
        for s in range(self.n):
            slots[d * self.n + s] = master[s].astype(bf16)
        pl.semaphore_wait(barrier, len(self.peers))

    def rows(self, i, e, first, count):
        return self.held[i].at[pl.ds(e * self.n + first, count)]

    def along_start(self, i):
        self.along[i] = self.net.start(
            self.rows(0, self.me, 0, self.n), self.rows(i, self.me, 0, self.n), (self.me, self.order[i])
        )

    def send(self, i, e, first, count, to):
        ref = self.rows(i, e, first, count)
        return self.net.start(ref, ref, (to, self.m))

    def start(self, i):
        if i:
            self.along[i].wait_recv()
        (x, y, _), h = self.plane, self.n // 2
        if i == 1:
            self.first[i] = [self.send(i, self.me, 0, self.n, e) for e in (x, y)]
        else:
            self.first[i] = [self.send(i, self.me, *job) for job in ((0, h, x), (h, h, y), (h, h, x), (0, h, y))]
        self.inside[i] = [self.send(i, self.me, 0, self.n, self.core)]

    def across_start(self):
        z = self.plane[2]
        self.last[1] = [self.net.start(self.rows(0, z, 0, self.n), self.rows(1, z, 0, self.n), (self.me, self.order[1]))]

    def forward(self, i):
        if i == 1:
            return
        (x, y, _), h = self.plane, self.n // 2
        self.first[i][0].wait_recv()
        self.last[i] = [self.send(i, x, 0, h, y)]
        self.first[i][1].wait_recv()
        self.last[i].append(self.send(i, y, h, h, x))

    def pair(self, i):
        x, y, z = self.plane
        self.first[i][-2].wait_recv()
        self.inside[i].append(self.send(i, x, 0, self.n, self.core))
        self.first[i][-1].wait_recv()
        self.inside[i].append(self.send(i, y, 0, self.n, self.core))
        for copy in self.last[i]:
            copy.wait_recv()
        self.inside[i].append(self.send(i, z, 0, self.n, self.core))

    def ready(self, i):
        for copy in self.inside[i]:
            copy.wait_recv()

    def place(self, i):
        wg, wo, wu, wd = self.weights
        row_tiles, gates = D // BLK, wg.shape[2] // BLK
        cols, outs = gates + wu.shape[2] // BLK, wo.shape[1] // BLK
        for b in range(row_tiles * cols + (wo.shape[1] + wd.shape[1]) // BLK * row_tiles):
            if b < row_tiles * cols:
                r, c = b // cols, b % cols
                ref = wg if c < gates else wu
                c -= 0 if c < gates else gates
            else:
                r, c = (b - row_tiles * cols) // row_tiles, (b - row_tiles * cols) % row_tiles
                ref = wo if r < outs else wd
                r -= 0 if r < outs else outs
            block = self.held[i][self.rank[b]]
            ref[self.order[i], r * BLK : (r + 1) * BLK, c * BLK : (c + 1) * BLK] = block

    def done(self):
        for device in self.peers:
            pl.semaphore_signal(self.free, inc=1, device_id=device, device_id_type=MESH)

    def all_done(self):
        pl.semaphore_wait(self.free, len(self.peers))


def stack_places(hm, fm):
    row_tiles, gates, ups, outs = D // BLK, 3 * hm // BLK, fm // BLK, hm // BLK
    cols = gates + ups
    first_down = row_tiles * ups
    first_out = 2 * first_down
    first_gate = first_out + row_tiles * outs
    table = []
    for b in range(row_tiles * (cols + outs + ups)):
        if b < row_tiles * cols:
            r, c = b // cols, b % cols
            table.append(first_gate + r * gates + c if c < gates else r * ups + c - gates)
        else:
            k = b - row_tiles * cols
            table.append(first_out + k if k < row_tiles * outs else first_down + k - row_tiles * outs)
    return ((0, first_out), (first_out, row_tiles * outs), (first_gate, row_tiles * gates)), table


UPDOWN, OUT, GATE = range(3)


class Reduce:
    def __init__(self, net, gather, grads, units, pool):
        self.net, self.g, self.grads, self.units, self.pool = net, gather, grads, units, pool
        self.half = grads.shape[1] // 2
        self.eighth = grads.shape[1] // 8
        self.copies = {}

    def place(self, e):
        return (e % 2) * 4 + e // 2

    def chip(self, unit, i):
        g, (first, count) = self.g, self.units[unit]
        src = self.grads.at[g.order[i], pl.ds(first + (1 - g.side) * (count // 2), count // 2)]
        dst = self.pool[i - 1].at[pl.ds(first // 2, count // 2)]
        self.copies[0, unit, i] = self.net.start(src, dst, (g.core, g.m))

    def spot(self, unit, i, slot, first, count):
        base, total = self.units[unit]
        return self.pool[i - 1].at[pl.ds(self.half + slot * self.eighth + base // 8 + first, count)]

    def parts(self, unit, i):
        n = self.units[unit][1] // 8
        if i == 1:
            return ((0, n),)
        h = (n + i % 2) // 2 if n % 2 else n // 2
        return (0, h), (h, n - h)

    def share(self, unit, i, e, first, count):
        base, total = self.units[unit]
        return self.grads.at[self.g.order[i], pl.ds(base + self.place(e) * (total // 8) + first, count)]

    def send(self, unit, i, e, part, slot, to):
        if part[1]:
            src, dst = self.share(unit, i, e, *part), self.spot(unit, i, slot, *part)
            self.copies[1, unit, i, slot, part] = self.net.start(src, dst, (to, self.g.m))

    def take(self, unit, i, slot, part):
        self.copies[1, unit, i, slot, part].wait_recv()
        return self.spot(unit, i, slot, *part)[...].astype(f32)

    def plane(self, unit, i):
        g, (first, count) = self.g, self.units[unit]
        x, y, z = g.plane
        self.copies[0, unit, i].wait_recv()
        m = g.order[i]
        rows = pl.ds(first + g.side * (count // 2), count // 2)
        total = self.grads[m, rows].astype(f32) + self.pool[i - 1][first // 2 : (first + count) // 2].astype(f32)
        self.grads[m, rows] = total.astype(bf16)
        if i == 1:
            (whole,) = self.parts(unit, i)
            self.send(unit, i, x, whole, 1, x)
            self.send(unit, i, y, whole, 2, y)
            src, dst = self.share(unit, i, z, *whole), self.spot(unit, i, 0, *whole)
            self.copies[3, unit] = self.net.start(src, dst, (g.me, m))
            return
        one, two = self.parts(unit, i)
        self.send(unit, i, z, one, 0, x)
        self.send(unit, i, z, two, 0, y)
        self.send(unit, i, x, one, 1, x)
        self.send(unit, i, y, two, 2, y)

    def turn(self, unit, i):
        if i == 1:
            return
        x, y, z = self.g.plane
        for part, slot, e in zip(self.parts(unit, i), (2, 1), (y, x)):
            if part[1]:
                ref = self.share(unit, i, e, *part)
                ref[...] = (ref[...].astype(f32) + self.take(unit, i, 0, part)).astype(bf16)
                self.send(unit, i, e, part, slot, e)

    def model(self, unit, i):
        g, (first, count) = self.g, self.units[unit]
        n = count // 8
        for part in self.parts(unit, i):
            if part[1]:
                ref = self.share(unit, i, g.me, *part)
                total = ref[...].astype(f32) + self.take(unit, i, 1, part) + self.take(unit, i, 2, part)
                ref[...] = total.astype(bf16)
        dst = self.pool[i - 1].at[pl.ds(self.half + 3 * self.eighth + first // 8, n)]
        self.copies[2, unit, i] = self.net.start(self.share(unit, i, g.me, 0, n), dst, (g.me, g.order[i]))

    def own(self, unit):
        g, (first, count) = self.g, self.units[unit]
        n = count // 8
        rows = pl.ds(first + self.place(g.me) * n, n)
        total = self.grads[g.m, rows].astype(f32)
        for i in (1, 2, 3):
            self.copies[2, unit, i].wait_recv()
            total += self.pool[i - 1][pl.ds(self.half + 3 * self.eighth + first // 8, n)].astype(f32)
        self.grads[g.m, rows] = total.astype(bf16)
        self.copies[3, unit].wait_recv()
        rows = pl.ds(first + self.place(g.plane[2]) * n, n)
        total = self.grads[g.m, rows].astype(f32) + self.spot(unit, 1, 0, 0, n)[...].astype(f32)
        self.grads[g.m, rows] = total.astype(bf16)

    def into_slots(self, out, slot_place, e):
        n = self.eighth
        for k in range(n):
            out[self.place(e) * n + k] = self.grads[self.g.m, slot_place[e * n + k]]

    def slots_chip(self, out, slot_place, pair):
        g, n = self.g, self.eighth
        self.last = []
        targets = (g.plane[2], g.plane[0], g.plane[1], g.me)
        for e in targets:
            other = e + 1 - 2 * g.side
            self.into_slots(out, slot_place, other)
            src = out.at[pl.ds(self.place(other) * n, n)]
            self.last.append(self.net.start(src, pair.at[pl.ds((e // 2) * n, n)], (g.core, g.m)))
        for e in targets:
            self.into_slots(out, slot_place, e)

    def slots_plane(self, out, pair, far):
        g, n = self.g, out.shape[0] // 8
        h = n // 2
        x, y, z = g.plane
        wait = dict(zip("zxyo", self.last))

        def mine(e, first, count):
            return pl.ds((g.side * 4 + e // 2) * n + first, count)

        def join(e):
            rows = mine(e, 0, n)
            out[rows] = (out[rows].astype(f32) + pair[pl.ds((e // 2) * n, n)].astype(f32)).astype(bf16)

        def send(e, first, slot, to):
            return self.net.start(out.at[mine(e, first, h)], far.at[slot], (to, g.m))

        wait["z"].wait_recv()
        join(z)
        over_x = send(z, 0, 0, x)
        over_y = send(z, h, 1, y)
        wait["x"].wait_recv()
        join(x)
        self.ends = [send(x, 0, 2, x)]
        wait["y"].wait_recv()
        join(y)
        self.ends.append(send(y, h, 3, y))
        over_x.wait_recv()
        rows = mine(y, 0, h)
        out[rows] = (out[rows].astype(f32) + far[0].astype(f32)).astype(bf16)
        self.ends.append(send(y, 0, 4, y))
        over_y.wait_recv()
        rows = mine(x, h, h)
        out[rows] = (out[rows].astype(f32) + far[1].astype(f32)).astype(bf16)
        self.ends.append(send(x, h, 5, x))
        wait["o"].wait_recv()

    def slots_end(self, out, pair, far, owned):
        g, n = self.g, out.shape[0] // 8
        h = n // 2
        for copy in self.ends:
            copy.wait_recv()
        for first, slots in ((0, (2, 4)), (h, (3, 5))):
            total = out[pl.ds((g.side * 4 + g.me // 2) * n + first, h)].astype(f32)
            total += pair[pl.ds((g.me // 2) * n + first, h)].astype(f32)
            for k in slots:
                total += far[k].astype(f32)
            owned[first : first + h] = total


class SmallSum:
    def __init__(self, net, gather, values, along, across, inside):
        self.net, self.g, self.values = net, gather, values
        self.slots = (along, across, inside)
        self.peers = (
            [(gather.me, k) for k in gather.order[1:]],
            [(e, gather.m) for e in gather.plane],
            [(gather.core, gather.m)],
        )
        self.mine = (gather.m, gather.me // 2, gather.side)
        self.open = []

    def send(self, stage):
        slot = self.slots[stage]
        slot[self.mine[stage]] = self.values[...]
        ref = slot.at[self.mine[stage]]
        self.open = [self.net.start(ref, ref, peer) for peer in self.peers[stage]]

    def add(self, stage):
        for copy in self.open:
            copy.wait_recv()
        slot = self.slots[stage]
        total = slot[0]
        for k in range(1, slot.shape[0]):
            total += slot[k]
        self.values[...] = total


def compute_kernel(linked, *refs):
    if linked:
        tokens, cotangent, master, rank, slot_place, gains = refs[:6]
        block_out, input_grad, owned, small = refs[6:10]
        wg, wo, wu, wd, grads, slots, *pool, pair, far, sum_a, sum_b, sum_c, send, recv, free = refs[10:27]
        scratch = refs[27:]
    else:
        tokens, cotangent, base, wg, wo, wu, wd, gains = refs[:8]
        block_out, input_grad, grads, small = refs[8:12]
        scratch = refs[12:]
    (n1, n1t, cot, cott, n2, n2t, forget, admit, cand, state, scan, acc_a, acc_b, mixed, mid, kept, fills, local) = scratch
    dml, dmlt = n2, n2t
    parts, _, hm3 = wg.shape
    hm = hm3 // 3
    fm = wu.shape[2]
    units, _ = stack_places(hm, fm)
    act, dup, dpre = mid.at[:, :fm], mid.at[:, fm:], mid.at[:, : 3 * hm]
    gain_one = gains[0:1, :]
    gain_two = gains[1:2, :]

    fetch_cot = pltpu.make_async_copy(cotangent, cot, local.at[0])
    fetch_tok = pltpu.make_async_copy(tokens, n1, local.at[1])
    fetch_tok.start()
    fetch_cot.start()

    def stack(m, first, value):
        wide = value.shape[1] // BLK
        for r in range(value.shape[0] // BLK):
            for c in range(wide):
                grads[m, first + r * wide + c] = value[r * BLK : (r + 1) * BLK, c * BLK : (c + 1) * BLK].astype(bf16)

    def stack_turned(m, first, value):
        high = value.shape[0] // BLK
        for r in range(high):
            for c in range(value.shape[1] // BLK):
                grads[m, first + c * high + r] = value[r * BLK : (r + 1) * BLK, c * BLK : (c + 1) * BLK].astype(bf16)

    def permute_in(src, dst):
        for k in range(D // BLK):
            scan[k] = src[:, k * BLK : (k + 1) * BLK].astype(f32)

        @pl.loop(0, J // 2, unroll=4)
        def _(j):
            for k in range(D // BLK):
                lo = scan[k, pl.ds(2 * j, SUB, stride=J), :]
                hi = scan[k, pl.ds(2 * j + 1, SUB, stride=J), :]
                dst[pl.ds(pl.multiple_of(16 * j, 16), 16), k * BLK : (k + 1) * BLK] = jnp.concatenate([lo, hi], 0).astype(bf16)

    def permute_out(src, dst):
        @pl.loop(0, J, unroll=4)
        def _(j):
            rows = pl.ds(pl.multiple_of(j * SUB, SUB), SUB)
            for k in range(D // BLK):
                scan[k, pl.ds(j, SUB, stride=J), :] = src[rows, k * BLK : (k + 1) * BLK]

        for k in range(D // BLK):
            dst[:, k * BLK : (k + 1) * BLK] = scan[k].astype(dst.dtype)

    def put(first, rows, value):
        for k in range(hm // BLK):
            scan[first + k, rows, :] = value[:, k * BLK : (k + 1) * BLK]

    def take(first, rows):
        return jnp.concatenate([scan[first + k, rows, :] for k in range(hm // BLK)], 1)

    half = hm // BLK

    def spread(v):
        return jnp.broadcast_to(v[None], (R // SUB, SUB, hm)).reshape(R, hm)


    if linked:
        net = Exchange(send, recv)
        gather = Gather(net, master, rank, slots, pool, (wg, wo, wu, wd), free)
        gather.start(0)
        gather.along_start(1)
        reduce = Reduce(net, gather, grads, units, pool)
        order = gather.order
    else:
        order = list(range(parts))

    fetch_tok.wait()
    permute_in(n1, n1)
    mixed[...] = n1[...].astype(f32)

    @pl.loop(0, L // R)
    def _(i):
        rows = pl.ds(pl.multiple_of(i * R, R), R)
        x = mixed[rows, :]
        r = lax.rsqrt(jnp.mean(x * x, axis=-1, keepdims=True) + norm_eps)
        n1[rows, :] = (x * r * gain_one).astype(bf16)

    n1t[...] = n1[...].T

    if linked:
        gather.forward(0)
        gather.along_start(2)
        gather.along_start(3)
    fetch_cot.wait()
    permute_in(cot, cot)
    if linked:
        gather.start(1)
        gather.pair(0)
        gather.across_start()
    cott[...] = cot[...].T

    fills[0] = jnp.zeros((SUB, hm), f32)
    fills[1] = jnp.ones((SUB, hm), f32)
    weigh = fills[0]
    weigh_j = fills[0]
    for turn, m in enumerate(order):

        if linked:
            if turn:
                gather.pair(turn)
            gather.ready(turn)
            gather.place(turn)

        forget[m] = dot(n1[...], wg[m, :, :hm])
        admit[m] = dot(n1[...], wg[m, :, hm : 2 * hm])
        cand[m] = dot(n1[...], wg[m, :, 2 * hm :])

        if linked and turn < 3:
            if turn:
                gather.forward(turn + 1)
            if turn < 2:
                gather.start(turn + 2)

        @pl.loop(0, L // R)
        def _(i):
            rows = pl.ds(pl.multiple_of(i * R, R), R)
            f = sigmoid(forget[m, rows, :])
            a = sigmoid(admit[m, rows, :])
            inv = recip(f + a)
            forget[m, rows, :] = f
            admit[m, rows, :] = a
            kept[rows, :] = f * inv
            put(0, rows, a * inv * cand[m, rows, :])

        def step(j, carry):
            s, p, k_sum, kj_sum = carry
            rows = pl.ds(pl.multiple_of(j * SUB, SUB), SUB)
            keep = kept[rows, :]
            s = keep * s + take(0, rows)
            p = keep * p
            put(0, rows, s)
            put(half, rows, p)
            return s, p, k_sum + keep, kj_sum + keep * j.astype(f32)

        s, p, weigh, weigh_j = lax.fori_loop(0, J, step, (fills[0], fills[1], weigh, weigh_j), unroll=16)
        enter = fills[0]
        for _ in range(SUB - 1):
            enter = shift_down(s + p * enter)

        @pl.loop(0, L // R)
        def _(i):
            rows = pl.ds(pl.multiple_of(i * R, R), R)
            state[m, pl.ds(pl.multiple_of(i * R + SUB, SUB), R), :] = take(0, rows) + take(half, rows) * spread(enter)

        state[m, :SUB, :] = shift_down(state[m, L:, :])

    if linked:
        net.drain()
        gather.done()

    for m in range(parts):
        mixed[...] += dot(state[m, SUB:, :].astype(bf16), wo[m])

    @pl.loop(0, L // R)
    def _(i):
        rows = pl.ds(pl.multiple_of(i * R, R), R)
        x = mixed[rows, :]
        r = lax.rsqrt(jnp.mean(x * x, axis=-1, keepdims=True) + norm_eps)
        n2[rows, :] = (x * r * gain_two).astype(bf16)
        acc_a[rows, :] = x
        acc_b[rows, :] = jnp.zeros_like(x)

    n2t[...] = n2[...].T

    for turn, m in enumerate(order):

        for first in range(0, fm, fm // 2):
            units_of = slice(first, first + fm // 2)
            up = dot(n2[...], wu[m, :, units_of])
            da = dot(cot[...], wd[m, units_of, :], True)
            cdf, xpdf = gelu_terms(up)
            act[:, units_of] = (up * cdf).astype(bf16)
            dup[:, units_of] = (da * (cdf + xpdf)).astype(bf16)
            if linked and first == 0:
                if turn == 2:
                    reduce.plane(UPDOWN, 1)
                if turn == 3:
                    reduce.plane(UPDOWN, 2)
        acc_a[...] += dot(act[...], wd[m])
        acc_b[...] += dot(dup[...], wu[m], True)
        stack(m, 0, dot(n2t[...], dup[...]))
        stack_turned(m, units[UPDOWN][1] // 2, dot(cott[...], act[...]))
        if linked and turn:
            if turn == 1:
                gather.all_done()
            reduce.chip(UPDOWN, turn)

    permute_out(acc_a, n1)
    push_out = pltpu.make_async_copy(n1, block_out, local.at[0])
    push_out.start()

    if linked:
        reduce.model(UPDOWN, 1)
        reduce.turn(UPDOWN, 2)
        reduce.plane(UPDOWN, 3)

    gain_sum_two = jnp.zeros((1, D), f32)

    def back_two(i, total):
        rows = pl.ds(pl.multiple_of(i * R, R), R)
        x = mixed[rows, :]
        r = lax.rsqrt(jnp.mean(x * x, axis=-1, keepdims=True) + norm_eps)
        dn = acc_b[rows, :]
        q = dn * gain_two
        d = cot[rows, :].astype(f32) + r * q - r * r * r * x * jnp.mean(q * x, axis=-1, keepdims=True)
        mixed[rows, :] = d
        dml[rows, :] = d.astype(bf16)
        acc_b[rows, :] = jnp.zeros_like(d)
        return total + jnp.sum(dn * x * r, axis=0, keepdims=True)

    gain_sum_two = lax.fori_loop(0, L // R, back_two, gain_sum_two)
    dmlt[...] = dml[...].T
    fetch_tok = pltpu.make_async_copy(tokens, cot, local.at[1])
    fetch_tok.start()

    for turn, m in reversed(list(enumerate(order))):
        stack_turned(m, units[OUT][0], dot(dmlt[...], state[m, SUB:, :].astype(bf16)))
        if linked and turn:
            reduce.chip(OUT, turn)

    for turn, m in reversed(list(enumerate(order))):

        put(0, slice(None), dot(dml[...], wo[m], True))

        @pl.loop(0, L // R)
        def _(i):
            rows = pl.ds(pl.multiple_of(i * R, R), R)
            f = forget[m, rows, :]
            kept[rows, :] = f * recip(f + admit[m, rows, :])

        def step(k, carry):
            u, p, keep_next = carry
            j = J - 1 - k
            rows = pl.ds(pl.multiple_of(j * SUB, SUB), SUB)
            u = take(0, rows) + keep_next * u
            p = keep_next * p
            put(0, rows, u)
            put(half, rows, p)
            return u, p, kept[rows, :]

        u, p, keep_first = lax.fori_loop(0, J, step, (fills[0], fills[1], fills[1]), unroll=16)
        enter = fills[0]
        for _ in range(SUB - 1):
            enter = shift_up(keep_first * (u + p * enter))

        if linked:
            if turn == 3:
                reduce.turn(UPDOWN, 3)
                reduce.model(UPDOWN, 2)
                for i in (3, 2, 1):
                    reduce.plane(OUT, i)
            if turn == 2:
                reduce.model(UPDOWN, 3)
                for i in (3, 2):
                    reduce.turn(OUT, i)
                reduce.plane(GATE, 3)
            if turn == 1:
                for i in (1, 3, 2):
                    reduce.model(OUT, i)
                reduce.turn(GATE, 3)
                reduce.plane(GATE, 2)
            if turn == 0:
                reduce.plane(GATE, 1)
                reduce.model(GATE, 3)
                reduce.turn(GATE, 2)

        @pl.loop(0, L // R)
        def _(i):
            rows = pl.ds(pl.multiple_of(i * R, R), R)
            carried = take(0, rows) + take(half, rows) * spread(enter)
            f = forget[m, rows, :]
            a = admit[m, rows, :]
            adm = a * recip(f + a)
            g = carried * (state[m, rows, :] - cand[m, rows, :]) * (kept[rows, :] * adm)
            dpre[rows, :hm] = (g * (1.0 - f)).astype(bf16)
            dpre[rows, hm : 2 * hm] = (g * (a - 1.0)).astype(bf16)
            dpre[rows, 2 * hm :] = (carried * adm).astype(bf16)

        stack(m, units[GATE][0], dot(n1t[...], dpre[...]))
        if linked and turn:
            reduce.chip(GATE, turn)

        acc_b[...] += dot(dpre[...], wg[m], True)
        if linked and turn == 0:
            reduce.model(GATE, 1)
            reduce.model(GATE, 2)
            reduce.own(UPDOWN)
            reduce.own(OUT)

    fetch_tok.wait()
    permute_in(cot, cot)

    def back_one(i, total):
        rows = pl.ds(pl.multiple_of(i * R, R), R)
        x = cot[rows, :].astype(f32)
        r = lax.rsqrt(jnp.mean(x * x, axis=-1, keepdims=True) + norm_eps)
        dn = acc_b[rows, :]
        q = dn * gain_one
        mixed[rows, :] += r * q - r * r * r * x * jnp.mean(q * x, axis=-1, keepdims=True)
        return total + jnp.sum(dn * x * r, axis=0, keepdims=True)

    gain_sum_one = lax.fori_loop(0, L // R, back_one, jnp.zeros((1, D), f32))

    place = lax.broadcasted_iota(jnp.int32, (SUB, hm), 0).astype(f32) * float(J)
    if linked:
        first = ((gather.me * parts + gather.m) * L + 1).astype(f32)
        token_total = float(L * parts * lax.axis_size("dp"))
    else:
        first = base[0]
        token_total = base[1]
    forget_sum = jnp.sum(weigh_j + weigh * (place + first), axis=0, keepdims=True) / token_total
    small[...] = jnp.zeros_like(small)
    small[0:1, :] = gain_sum_one
    small[1:2, :] = gain_sum_two
    small[2:3, :hm] = forget_sum
    if linked:
        flat = units[UPDOWN][1] // 2, units[GATE][0]
        count = owned.shape[0]
        flags = []
        for k in range(count):
            spot = slot_place[gather.me * count + k]
            flags.append(jnp.where((spot >= flat[0]) & (spot < flat[1]), 1.0, 0.0).astype(f32))

    if linked:
        tiny = SmallSum(net, gather, small, sum_a, sum_b, sum_c)
        tiny.send(0)
        reduce.own(GATE)
        reduce.slots_chip(slots, slot_place, pair)
        tiny.add(0)
        tiny.send(1)
        reduce.slots_plane(slots, pair, far)

    permute_out(mixed, acc_a)
    push_grad = pltpu.make_async_copy(acc_a, input_grad, local.at[2])
    push_grad.start()

    if linked:
        tiny.add(1)
        tiny.send(2)
        reduce.slots_end(slots, pair, far, owned)
        tiny.add(2)
        for k, flag in enumerate(flags):
            small[3 + k // 4 : 4 + k // 4, (k % 4) * BLK : (k % 4 + 1) * BLK] = jnp.full((1, BLK), flag, f32)
        net.drain()
    push_out.wait()
    push_grad.wait()


def compute(tokens, cotangent, gains, weights=None, base=None, master=None, rank=None, slot_place=None):
    linked = weights is None
    parts = lax.axis_size("mp")
    hm, fm = H // parts, FF // parts
    stacked = (parts, D * (4 * hm + 2 * fm) // BLK**2, BLK, BLK)
    sds = jax.ShapeDtypeStruct
    vm, sm, hbm = (pl.BlockSpec(memory_space=k) for k in (pltpu.VMEM, pltpu.SMEM, pl.ANY))
    if linked:
        n = rank.shape[0]
        args = (tokens, cotangent, master, rank, slot_place, gains)
        in_specs = [hbm, hbm, vm, sm, sm, vm]
        middle = sds((n // 8, BLK, BLK), f32)
        extra = [
            pltpu.VMEM((parts, D, 3 * hm), bf16),
            pltpu.VMEM((parts, hm, D), bf16),
            pltpu.VMEM((parts, D, fm), bf16),
            pltpu.VMEM((parts, fm, D), bf16),
            pltpu.VMEM(stacked, bf16),
            pltpu.VMEM((n, BLK, BLK), bf16),
            *[pltpu.VMEM((n, BLK, BLK), bf16) for _ in range(parts - 1)],
            pltpu.VMEM((n // 2, BLK, BLK), bf16),
            pltpu.VMEM((6, n // 16, BLK, BLK), bf16),
            pltpu.VMEM((parts, 8, D), f32),
            pltpu.VMEM((4, 8, D), f32),
            pltpu.VMEM((2, 8, D), f32),
            pltpu.SemaphoreType.DMA((128,)),
            pltpu.SemaphoreType.DMA((128,)),
            pltpu.SemaphoreType.REGULAR,
        ]
        params = dict(collective_id=0, has_side_effects=True)
    else:
        args = (tokens, cotangent, base, *weights, gains)
        in_specs = [hbm, hbm, sm] + [vm] * 5
        middle = sds(stacked, bf16)
        extra = []
        params = {}
    return pl.pallas_call(
        functools.partial(compute_kernel, linked),
        out_shape=(sds((L, D), bf16), sds((L, D), f32), middle, sds((8, D), f32)),
        in_specs=in_specs,
        out_specs=[hbm, hbm, vm, vm],
        scratch_shapes=extra
        + [pltpu.VMEM(shape, bf16) for shape in ((L, D), (D, L)) * 3]
        + [pltpu.VMEM((parts, L, hm), f32)] * 3
        + [pltpu.VMEM((parts, L + SUB, hm), f32)]
        + [pltpu.VMEM((2 * hm // BLK, L, BLK), f32)]
        + [pltpu.VMEM((L, D), f32)] * 3
        + [
            pltpu.VMEM((L, 2 * fm), bf16),
            pltpu.VMEM((L, hm), f32),
            pltpu.VMEM((2, SUB, hm), f32),
            pltpu.SemaphoreType.DMA((3,)),
        ],
        compiler_params=pltpu.CompilerParams(vmem_limit_bytes=64 * 2**20 - 2**16, **params),
        name="block",
    )(*args)


def adam_update(first_old, second_old, gradient):
    first_new = beta_one * first_old + (1.0 - beta_one) * gradient
    second_new = beta_two * second_old + (1.0 - beta_two) * gradient * gradient
    first_hat = first_new / (1.0 - beta_one**STEP)
    second_hat = second_new / (1.0 - beta_two**STEP)
    return (first_new, second_new, first_hat / (jnp.sqrt(second_hat) + adam_eps))


def fine_dot(a, b, trans_b=False):
    a_high, b_high = a.astype(bf16), b.astype(bf16)
    a_low, b_low = (a - a_high.astype(f32)).astype(bf16), (b - b_high.astype(f32)).astype(bf16)
    return dot(a_high, b_high, trans_b) + (dot(a_high, b_low, trans_b) + dot(a_low, b_high, trans_b))


def update_kernel(token_total, passed, sums, gains, gain_moment_one, gain_moment_two, *refs):
    sources, refs = refs[:6], refs[6:]
    given, refs = refs[:passed], refs[passed:]
    results, refs = refs[:4], refs[4:]
    gain_first, gain_second, gains_new, forget_mean = refs[:4]
    copied, refs = refs[4 : 4 + passed], refs[4 + passed :]
    held, made, made_low, sem_in, sem_out, sem_pass = refs[:6]
    passage = refs[6:]
    count = held.shape[1]
    step = max(count // 2, 1)
    groups = [slice(first, first + step) for first in range(0, count, step)]
    enter = [pltpu.make_async_copy(src, via, sem_pass.at[0, k]) for k, (src, via) in enumerate(zip(given, passage))]
    leave = [pltpu.make_async_copy(via, dst, sem_pass.at[1, k]) for k, (via, dst) in enumerate(zip(passage, copied))]
    fetch = [
        [pltpu.make_async_copy(src.at[group], held.at[k, group], sem_in.at[g, k]) for k, src in enumerate(sources)]
        for g, group in enumerate(groups)
    ]
    for copy in fetch[0]:
        copy.start()
    for copy in enter:
        copy.start()
    for row in fetch[1:]:
        for copy in row:
            copy.start()
    first, second, direction = adam_update(gain_moment_one[...], gain_moment_two[...], sums[0:2, :])
    gain_first[...] = first
    gain_second[...] = second
    gains_new[...] = gains[...] - gain_rate * direction
    forget_mean[...] = jnp.sum(sums[2:3, :], axis=1, keepdims=True) * (1.0 / (H * (token_total + 1) / 2.0))
    push = []
    for g, group in enumerate(groups):
        blocks = range(group.start, group.stop)
        for copy in fetch[g]:
            copy.wait()
        if g == len(groups) - 1:
            for come, go in zip(enter, leave):
                come.wait()
                go.start()
        grads = []
        for s in blocks:
            grad = held[0, s]
            flag = sums[3 + s // 4 : 4 + s // 4, (s % 4) * BLK : (s % 4 + 1) * BLK]
            grads.append(jnp.where(flag > 0.5, grad.T, grad))
        values = [fine_dot(held[1, s].T, grad) for s, grad in zip(blocks, grads)]
        values = [fine_dot(value, held[2, s]) for s, value in zip(blocks, values)]
        for k, s in enumerate(blocks):
            first, second, values[k] = adam_update(held[3, s], held[4, s], values[k])
            made[0, s] = first
            made[1, s] = second
        values = [fine_dot(held[1, s], value) for s, value in zip(blocks, values)]
        values = [fine_dot(value, held[2, s], True) for s, value in zip(blocks, values)]
        for s, value in zip(blocks, values):
            fresh = held[5, s] - learn_rate * (value + weight_decay * held[5, s])
            made[2, s] = fresh
            made_low[s] = fresh.astype(bf16)
        for k, dst in enumerate(results):
            src = made.at[k, group] if k < 3 else made_low.at[group]
            copy = pltpu.make_async_copy(src, dst.at[group], sem_out.at[g, k])
            copy.start()
            push.append(copy)
    for copy in push + leave:
        copy.wait()


def update(token_total, small, large, passed):
    sds = jax.ShapeDtypeStruct
    blocks, gain = large[0].shape, small[1].shape
    vm, hbm = pl.BlockSpec(memory_space=pltpu.VMEM), pl.BlockSpec(memory_space=pl.ANY)
    return pl.pallas_call(
        functools.partial(update_kernel, token_total, len(passed)),
        out_shape=[sds(blocks, f32)] * 3
        + [sds(blocks, bf16)]
        + [sds(gain, f32)] * 3
        + [sds((1, 1), f32)]
        + [sds(v.shape, v.dtype) for v in passed],
        in_specs=[vm] * 4 + [hbm] * (len(large) + len(passed)),
        out_specs=[hbm] * 4 + [vm] * 4 + [hbm] * len(passed),
        scratch_shapes=[
            pltpu.VMEM((6, *blocks), f32),
            pltpu.VMEM((3, *blocks), f32),
            pltpu.VMEM(blocks, bf16),
            pltpu.SemaphoreType.DMA((2, 6)),
            pltpu.SemaphoreType.DMA((2, 4)),
            pltpu.SemaphoreType.DMA((2, len(passed))),
        ]
        + [pltpu.VMEM(v.shape, v.dtype) for v in passed],
        compiler_params=pltpu.CompilerParams(vmem_limit_bytes=56 * 2**20),
        name="update",
    )(*small, *large, *passed)


def on_device(
    tokens,
    cotangent,
    master,
    moment_one,
    moment_two,
    basis_left,
    basis_right,
    owner,
    gains,
    gain_moment_one,
    gain_moment_two,
):
    parts = lax.axis_size("mp")
    data_parts = lax.axis_size("dp")
    hm, fm = H // parts, FF // parts
    token_total = L * data_parts * parts
    row_tiles, cols, lows = D // BLK, (3 * hm + fm) // BLK, (hm + fm) // BLK
    number = jnp.arange(owner.shape[0], dtype=jnp.int32)
    ahead = (owner[None, :] < owner[:, None]) | ((owner[None, :] == owner[:, None]) & (number[None, :] < number[:, None]))
    block_rank = jnp.sum(ahead.astype(jnp.int32), axis=1)
    _, table = stack_places(hm, fm)
    table = jnp.asarray(table, jnp.int32)
    slot_place = jnp.sum(jnp.where(block_rank[None, :] == number[:, None], table[None, :], 0), axis=1)
    if data_parts == 8 and parts == 4:
        block_out, input_grad, owned, sums = compute(
            tokens, cotangent, gains, master=master[0], rank=block_rank, slot_place=slot_place
        )
    else:
        stored = lax.all_gather(master.astype(bf16), "dp", axis=1, tiled=True)
        stored = lax.all_gather(stored, "mp", axis=0, tiled=True)
        stack = stored[:, block_rank]
        upper = stack[:, : row_tiles * cols].reshape(parts, row_tiles, cols, BLK, BLK)
        upper = upper.transpose(0, 1, 3, 2, 4).reshape(parts, D, cols * BLK)
        lower = stack[:, row_tiles * cols :].reshape(parts, lows, row_tiles, BLK, BLK)
        lower = lower.transpose(0, 1, 3, 2, 4).reshape(parts, lows * BLK, D)
        weights = (upper[:, :, : 3 * hm], lower[:, :hm], upper[:, :, 3 * hm :], lower[:, hm:])
        first = ((lax.axis_index("dp") * parts + lax.axis_index("mp")) * L + 1).astype(f32)
        base = jnp.stack([first, jnp.asarray(token_total, f32)])
        block_out, input_grad, grads, sums = compute(tokens, cotangent, gains, weights=weights, base=base)
        owned = lax.psum_scatter(grads[:, slot_place].astype(f32), "dp", scatter_dimension=1, tiled=True)
        owned = lax.psum_scatter(owned, "mp", scatter_dimension=0, tiled=True)[0]
        sums = lax.psum(sums, ("dp", "mp"))
        count = master.shape[1]
        mine = lax.dynamic_slice_in_dim(slot_place, lax.axis_index("dp") * count, count)
        units, _ = stack_places(hm, fm)
        flags = ((mine >= units[UPDOWN][1] // 2) & (mine < units[GATE][0])).astype(f32)
        flags = jnp.pad(jnp.repeat(flags, BLK), (0, (8 - count) * BLK)).reshape(2, 4 * BLK)
        sums = jnp.concatenate([sums[:3], flags, sums[5:]])
    outs = update(
        token_total,
        (sums, gains, gain_moment_one, gain_moment_two),
        (owned, basis_left[0], basis_right[0], moment_one[0], moment_two[0], master[0]),
        (block_out, input_grad),
    )
    first_new, second_new, master_new, master_low, gain_first, gain_second, gains_new, forget_mean = outs[:8]
    block_out, input_grad = outs[8:]
    return (
        block_out,
        input_grad,
        first_new[None],
        second_new[None],
        master_new[None],
        master_low[None],
        gain_first,
        gain_second,
        gains_new,
        forget_mean[0, 0],
    )


def solution(mesh):
    rows, blocks = P(("dp", "mp"), None), P("mp", "dp", None, None)
    return jax.shard_map(
        on_device,
        mesh=mesh,
        in_specs=(rows, rows, blocks, blocks, blocks, blocks, blocks, P(), P(), P(), P()),
        out_specs=(rows, rows, blocks, blocks, blocks, blocks, P(), P(), P(), P()),
        check_vma=False,
    )
```

```python
import functools

import jax
import jax.numpy as jnp
from jax import lax
from jax.experimental import pallas as pl
from jax.experimental.pallas import tpu as pltpu
from jax.sharding import PartitionSpec as P

D = 512
H = 1024
FF = 2048
BLK = 128
STEP = 10
L = 1024

norm_eps = 1e-05
beta_one = 0.5
beta_two = 0.5
adam_eps = 1e-08
learn_rate = 0.02
gain_rate = 0.1
weight_decay = 0.1
highest = lax.Precision.HIGHEST

f32 = jnp.float32
bf16 = jnp.bfloat16
SUB = 8
J = L // SUB
R = 128


def dot(a, b, trans_b=False):
    dims = (((1,), (1,)), ((), ())) if trans_b else (((1,), (0,)), ((), ()))
    return lax.dot_general(a, b, dims, preferred_element_type=f32)


def recip(v):
    return pltpu.reciprocal(v, approx=True)


def sigmoid(v):
    return recip(1.0 + jnp.exp(-v))


def shift_down(v):
    rolled = pltpu.roll(v, 1, 0)
    row = lax.broadcasted_iota(jnp.int32, v.shape, 0)
    return jnp.where(row == 0, 0.0, rolled)


def shift_up(v):
    rolled = pltpu.roll(v, SUB - 1, 0)
    row = lax.broadcasted_iota(jnp.int32, v.shape, 0)
    return jnp.where(row == SUB - 1, 0.0, rolled)


def gelu_terms(x):
    a = jnp.abs(x)
    t = recip(1.0 + a * (0.3275911 * 0.7071067811865476))
    poly = t * (
        0.5 * 0.254829592
        + t
        * (
            0.5 * -0.284496736
            + t * (0.5 * 1.421413741 + t * (0.5 * -1.453152027 + t * (0.5 * 1.061405429)))
        )
    )
    e = jnp.exp(x * x * -0.5)
    tail = poly * e
    cdf = jnp.where(x < 0.0, tail, 1.0 - tail)
    return cdf, x * e * 0.3989422804014327


MESH = pl.DeviceIdType.MESH


class Copy:
    def __init__(self, net, make):
        self.net, self.make = net, make

    def start(self):
        self.net.open.append(self)
        self.make().start()
        return self

    def wait_recv(self):
        self.make().wait_recv()

    def wait_send(self):
        self.make().wait_send()


class Exchange:
    def __init__(self, send, recv):
        self.send, self.recv, self.known, self.used, self.open = send, recv, {}, 0, []

    def copy(self, parts, key=None):
        if key in self.known:
            return self.known[key]
        k = self.used
        self.used += 1

        def make():
            src, dst, device = parts()
            return pltpu.make_async_remote_copy(
                src_ref=src,
                dst_ref=dst,
                send_sem=self.send.at[k],
                recv_sem=self.recv.at[k],
                device_id=device,
                device_id_type=MESH,
            )

        copy = Copy(self, make)
        if key is not None:
            self.known[key] = copy
        return copy

    def start(self, parts):
        return self.copy(parts).start()

    def drain(self):
        for copy in self.open:
            copy.wait_send()
        self.open = []


class Gather:
    def __init__(self, net, master, rank, slots, pool, weights, free):
        self.net, self.weights, self.rank, self.free = net, weights, rank, free
        self.held = [slots, *pool]
        d, m = lax.axis_index("dp"), lax.axis_index("mp")
        core, col, row = d % 2, (d // 2) % 2, d // 4
        self.me, self.m, self.side = d, m, core
        self.core = d + 1 - 2 * core
        self.plane = [d + 2 - 4 * col, d + 4 - 8 * row, d + 6 - 4 * col - 8 * row]
        self.order = [m, m + 1 - 2 * (m % 2), m + 2 - 4 * (m // 2), 3 - m]
        self.peers = [(e, m) for e in [self.core] + self.plane] + [(d, k) for k in self.order[1:]]
        barrier = pltpu.get_barrier_semaphore()
        for device in self.peers:
            pl.semaphore_signal(barrier, inc=1, device_id=device, device_id_type=MESH)
        self.n = master.shape[0]
        for s in range(self.n):
            slots[d * self.n + s] = master[s].astype(bf16)
        pl.semaphore_wait(barrier, len(self.peers))

    def rows(self, i, e, first, count):
        return self.held[i].at[pl.ds(e * self.n + first, count)]

    def along(self, i, e):
        return self.net.copy(
            lambda: (self.rows(0, e, 0, self.n), self.rows(i, e, 0, self.n), (self.me, self.order[i])),
            ("along", i, e is self.me),
        )

    def within(self, key, i, e, first, count, to):
        return self.net.copy(
            lambda: (self.rows(i, e, first, count), self.rows(i, e, first, count), (to, self.m)), (key, i)
        )

    def first(self, i):
        (x, y, _), h = self.plane, self.n // 2
        if i == 1:
            jobs = ((0, self.n, x), (0, self.n, y))
        else:
            jobs = ((0, h, x), (h, h, y), (h, h, x), (0, h, y))
        return [self.within(("first", k), i, self.me, *job) for k, job in enumerate(jobs)]

    def last(self, i):
        x, y, z = self.plane
        if i == 1:
            return [self.along(1, z)]
        h = self.n // 2
        return [self.within("over y", i, x, 0, h, y), self.within("over x", i, y, h, h, x)]

    def inside(self, i):
        return [self.within(("inside", k), i, e, 0, self.n, self.core) for k, e in enumerate([self.me] + self.plane)]

    def along_start(self, i):
        self.along(i, self.me).start()

    def across_start(self):
        self.last(1)[0].start()

    def start(self, i):
        if i:
            self.along(i, self.me).wait_recv()
        for copy in self.first(i):
            copy.start()
        self.inside(i)[0].start()

    def forward(self, i):
        if i == 1:
            return
        for came, copy in zip(self.first(i), self.last(i)):
            came.wait_recv()
            copy.start()

    def pair(self, i):
        for came, copy in zip(self.first(i)[-2:], self.inside(i)[1:3]):
            came.wait_recv()
            copy.start()
        for came in self.last(i):
            came.wait_recv()
        self.inside(i)[3].start()

    def ready(self, i):
        for copy in self.inside(i):
            copy.wait_recv()

    def place(self, i):
        wg, wo, wu, wd = self.weights
        row_tiles, gates = D // BLK, wg.shape[2] // BLK
        cols, outs = gates + wu.shape[2] // BLK, wo.shape[1] // BLK
        for b in range(row_tiles * cols + (wo.shape[1] + wd.shape[1]) // BLK * row_tiles):
            if b < row_tiles * cols:
                r, c = b // cols, b % cols
                ref = wg if c < gates else wu
                c -= 0 if c < gates else gates
            else:
                r, c = (b - row_tiles * cols) // row_tiles, (b - row_tiles * cols) % row_tiles
                ref = wo if r < outs else wd
                r -= 0 if r < outs else outs
            block = self.held[i][self.rank[b]]
            ref[self.order[i], r * BLK : (r + 1) * BLK, c * BLK : (c + 1) * BLK] = block

    def done(self):
        for device in self.peers:
            pl.semaphore_signal(self.free, inc=1, device_id=device, device_id_type=MESH)

    def all_done(self):
        pl.semaphore_wait(self.free, len(self.peers))


def stack_places(hm, fm):
    row_tiles, gates, ups, outs = D // BLK, 3 * hm // BLK, fm // BLK, hm // BLK
    cols = gates + ups
    first_down = row_tiles * ups
    first_out = 2 * first_down
    first_gate = first_out + row_tiles * outs
    table = []
    for b in range(row_tiles * (cols + outs + ups)):
        if b < row_tiles * cols:
            r, c = b // cols, b % cols
            table.append(first_gate + r * gates + c if c < gates else r * ups + c - gates)
        else:
            k = b - row_tiles * cols
            table.append(first_out + k if k < row_tiles * outs else first_down + k - row_tiles * outs)
    return ((0, first_out), (first_out, row_tiles * outs), (first_gate, row_tiles * gates)), table


UPDOWN, OUT, GATE = range(3)


class Reduce:
    def __init__(self, net, gather, grads, units, pool):
        self.net, self.g, self.grads, self.units, self.pool = net, gather, grads, units, pool
        self.half = grads.shape[1] // 2
        self.eighth = grads.shape[1] // 8
        self.copies = {}

    def place(self, e):
        return (e % 2) * 4 + e // 2

    def inside(self, unit, i):
        g, (first, count) = self.g, self.units[unit]
        return self.net.copy(
            lambda: (
                self.grads.at[g.order[i], pl.ds(first + (1 - g.side) * (count // 2), count // 2)],
                self.pool[i - 1].at[pl.ds(first // 2, count // 2)],
                (g.core, g.m),
            ),
            ("chip", unit, i),
        )

    def chip(self, unit, i):
        self.inside(unit, i).start()

    def spot(self, unit, i, slot, first, count):
        base, total = self.units[unit]
        return self.pool[i - 1].at[pl.ds(self.half + slot * self.eighth + base // 8 + first, count)]

    def parts(self, unit, i):
        n = self.units[unit][1] // 8
        if i == 1:
            return ((0, n),)
        h = (n + i % 2) // 2 if n % 2 else n // 2
        return (0, h), (h, n - h)

    def share(self, unit, i, e, first, count):
        base, total = self.units[unit]
        return self.grads.at[self.g.order[i], pl.ds(base + self.place(e) * (total // 8) + first, count)]

    def send(self, unit, i, e, part, slot, to):
        if part[1]:
            self.copies[1, unit, i, slot, part] = self.net.start(
                lambda: (self.share(unit, i, e, *part), self.spot(unit, i, slot, *part), (to, self.g.m))
            )

    def take(self, unit, i, slot, part):
        self.copies[1, unit, i, slot, part].wait_recv()
        return self.spot(unit, i, slot, *part)[...].astype(f32)

    def plane(self, unit, i):
        g, (first, count) = self.g, self.units[unit]
        x, y, z = g.plane
        self.inside(unit, i).wait_recv()
        m = g.order[i]
        start, came = first + g.side * (count // 2), self.pool[i - 1]

        @pl.loop(0, count // 2)
        def _(b):
            total = self.grads[m, start + b].astype(f32) + came[first // 2 + b].astype(f32)
            self.grads[m, start + b] = total.astype(bf16)

        if i == 1:
            (whole,) = self.parts(unit, i)
            self.send(unit, i, x, whole, 1, x)
            self.send(unit, i, y, whole, 2, y)
            self.copies[3, unit] = self.net.start(
                lambda: (self.share(unit, i, z, *whole), self.spot(unit, i, 0, *whole), (g.me, g.order[i]))
            )
            return
        one, two = self.parts(unit, i)
        self.send(unit, i, z, one, 0, x)
        self.send(unit, i, z, two, 0, y)
        self.send(unit, i, x, one, 1, x)
        self.send(unit, i, y, two, 2, y)

    def turn(self, unit, i):
        if i == 1:
            return
        x, y, z = self.g.plane
        for part, slot, e in zip(self.parts(unit, i), (2, 1), (y, x)):
            if part[1]:
                ref = self.share(unit, i, e, *part)
                ref[...] = (ref[...].astype(f32) + self.take(unit, i, 0, part)).astype(bf16)
                self.send(unit, i, e, part, slot, e)

    def model(self, unit, i):
        g, (first, count) = self.g, self.units[unit]
        n = count // 8
        for part in self.parts(unit, i):
            if part[1]:
                ref = self.share(unit, i, g.me, *part)
                total = ref[...].astype(f32) + self.take(unit, i, 1, part) + self.take(unit, i, 2, part)
                ref[...] = total.astype(bf16)
        self.copies[2, unit, i] = self.net.start(
            lambda: (self.share(unit, i, g.me, 0, n), self.spot(unit, i, 3, 0, n), (g.me, g.order[i]))
        )

    def own(self, unit):
        g, (first, count) = self.g, self.units[unit]
        n = count // 8
        rows = pl.ds(first + self.place(g.me) * n, n)
        total = self.grads[g.m, rows].astype(f32)
        for i in (1, 2, 3):
            self.copies[2, unit, i].wait_recv()
            total += self.pool[i - 1][pl.ds(self.half + 3 * self.eighth + first // 8, n)].astype(f32)
        self.grads[g.m, rows] = total.astype(bf16)
        self.copies[3, unit].wait_recv()
        rows = pl.ds(first + self.place(g.plane[2]) * n, n)
        total = self.grads[g.m, rows].astype(f32) + self.spot(unit, 1, 0, 0, n)[...].astype(f32)
        self.grads[g.m, rows] = total.astype(bf16)

    def into_slots(self, out, slot_place, e):
        n = self.eighth
        for k in range(n):
            out[self.place(e) * n + k] = self.grads[self.g.m, slot_place[e * n + k]]

    def slots_chip(self, out, slot_place, pair):
        g, n = self.g, self.eighth
        self.last = []
        targets = (g.plane[2], g.plane[0], g.plane[1], g.me)
        for e in targets:
            other = e + 1 - 2 * g.side
            self.into_slots(out, slot_place, other)
            self.last.append(
                self.net.start(
                    lambda e=e, other=other: (
                        out.at[pl.ds(self.place(other) * n, n)],
                        pair.at[pl.ds((e // 2) * n, n)],
                        (g.core, g.m),
                    )
                )
            )
        for e in targets:
            self.into_slots(out, slot_place, e)

    def slots_plane(self, out, pair, far):
        g, n = self.g, out.shape[0] // 8
        h = n // 2
        x, y, z = g.plane
        wait = dict(zip("zxyo", self.last))

        def mine(e, first, count):
            return pl.ds((g.side * 4 + e // 2) * n + first, count)

        def join(e):
            rows = mine(e, 0, n)
            out[rows] = (out[rows].astype(f32) + pair[pl.ds((e // 2) * n, n)].astype(f32)).astype(bf16)

        def send(e, first, slot, to):
            return self.net.start(lambda: (out.at[mine(e, first, h)], far.at[slot], (to, g.m)))

        wait["z"].wait_recv()
        join(z)
        over_x = send(z, 0, 0, x)
        over_y = send(z, h, 1, y)
        wait["x"].wait_recv()
        join(x)
        self.ends = [send(x, 0, 2, x)]
        wait["y"].wait_recv()
        join(y)
        self.ends.append(send(y, h, 3, y))
        over_x.wait_recv()
        rows = mine(y, 0, h)
        out[rows] = (out[rows].astype(f32) + far[0].astype(f32)).astype(bf16)
        self.ends.append(send(y, 0, 4, y))
        over_y.wait_recv()
        rows = mine(x, h, h)
        out[rows] = (out[rows].astype(f32) + far[1].astype(f32)).astype(bf16)
        self.ends.append(send(x, h, 5, x))
        wait["o"].wait_recv()

    def slots_end(self, out, pair, far, owned):
        g, n = self.g, out.shape[0] // 8
        h = n // 2
        for copy in self.ends:
            copy.wait_recv()
        for first, slots in ((0, (2, 4)), (h, (3, 5))):
            total = out[pl.ds((g.side * 4 + g.me // 2) * n + first, h)].astype(f32)
            total += pair[pl.ds((g.me // 2) * n + first, h)].astype(f32)
            for k in slots:
                total += far[k].astype(f32)
            owned[first : first + h] = total


class SmallSum:
    def __init__(self, net, gather, values, along, across, inside):
        self.net, self.g, self.values = net, gather, values
        self.slots = (along, across, inside)
        self.peers = (
            [(gather.me, k) for k in gather.order[1:]],
            [(e, gather.m) for e in gather.plane],
            [(gather.core, gather.m)],
        )
        self.mine = (gather.m, gather.me // 2, gather.side)
        self.open = []

    def send(self, stage):
        slot = self.slots[stage]
        slot[self.mine[stage]] = self.values[...]
        ref = slot.at[self.mine[stage]]
        self.open = [self.net.start(lambda peer=peer: (ref, ref, peer)) for peer in self.peers[stage]]

    def add(self, stage):
        for copy in self.open:
            copy.wait_recv()
        slot = self.slots[stage]
        total = slot[0]
        for k in range(1, slot.shape[0]):
            total += slot[k]
        self.values[...] = total


def compute_kernel(linked, *refs):
    if linked:
        tokens, cotangent, master, rank, slot_place, gains = refs[:6]
        block_out, input_grad, owned, small = refs[6:10]
        wg, wo, wu, wd, grads, slots, *pool, pair, far, sum_a, sum_b, sum_c, send, recv, free = refs[10:27]
        scratch = refs[27:]
    else:
        tokens, cotangent, base, wg, wo, wu, wd, gains = refs[:8]
        block_out, input_grad, grads, small = refs[8:12]
        scratch = refs[12:]
    (n1, n1t, cot, cott, n2, n2t, forget, admit, cand, state, scan, acc_a, acc_b, mixed, mid, kept, fills, tally, local) = scratch
    dml, dmlt = n2, n2t
    parts, _, hm3 = wg.shape
    hm = hm3 // 3
    fm = wu.shape[2]
    units, _ = stack_places(hm, fm)
    act, dup, dpre = mid.at[:, :fm], mid.at[:, fm:], mid.at[:, : 3 * hm]
    gain_one = gains[0:1, :]
    gain_two = gains[1:2, :]

    fetch_cot = pltpu.make_async_copy(cotangent, cot, local.at[0])
    fetch_tok = pltpu.make_async_copy(tokens, n1, local.at[1])
    fetch_tok.start()
    fetch_cot.start()

    column_halves = (slice(0, D // 2), slice(D // 2, D))

    def stack(m, first, wide, left, value):
        for r in range(value.shape[0] // BLK):
            for c in range(value.shape[1] // BLK):
                grads[m, first + r * wide + left + c] = value[r * BLK : (r + 1) * BLK, c * BLK : (c + 1) * BLK].astype(bf16)

    def stack_turned(m, first, value):
        high = value.shape[0] // BLK
        for r in range(high):
            for c in range(value.shape[1] // BLK):
                grads[m, first + c * high + r] = value[r * BLK : (r + 1) * BLK, c * BLK : (c + 1) * BLK].astype(bf16)

    def permute_in(src, dst):
        for k in range(D // BLK):
            scan[k] = src[:, k * BLK : (k + 1) * BLK].astype(f32)

        @pl.loop(0, J // 2, unroll=4)
        def _(j):
            for k in range(D // BLK):
                lo = scan[k, pl.ds(2 * j, SUB, stride=J), :]
                hi = scan[k, pl.ds(2 * j + 1, SUB, stride=J), :]
                dst[pl.ds(pl.multiple_of(16 * j, 16), 16), k * BLK : (k + 1) * BLK] = jnp.concatenate([lo, hi], 0).astype(bf16)

    def permute_out(src, dst):
        @pl.loop(0, J, unroll=4)
        def _(j):
            rows = pl.ds(pl.multiple_of(j * SUB, SUB), SUB)
            for k in range(D // BLK):
                scan[k, pl.ds(j, SUB, stride=J), :] = src[rows, k * BLK : (k + 1) * BLK]

        for k in range(D // BLK):
            dst[:, k * BLK : (k + 1) * BLK] = scan[k].astype(dst.dtype)

    def put(first, rows, value):
        for k in range(hm // BLK):
            scan[first + k, rows, :] = value[:, k * BLK : (k + 1) * BLK]

    def take(first, rows):
        return jnp.concatenate([scan[first + k, rows, :] for k in range(hm // BLK)], 1)

    half = hm // BLK

    def spread(v):
        return jnp.broadcast_to(v[None], (R // SUB, SUB, hm)).reshape(R, hm)


    if linked:
        net = Exchange(send, recv)
        gather = Gather(net, master, rank, slots, pool, (wg, wo, wu, wd), free)
        gather.start(0)
        gather.along_start(1)
        reduce = Reduce(net, gather, grads, units, pool)

    def of_turn(t):
        if not linked:
            return t
        high, low = gather.m // 2, gather.m % 2
        t_high, t_low = t // 2, t % 2
        return 2 * (high + t_high - 2 * high * t_high) + low + t_low - 2 * low * t_low

    fetch_tok.wait()
    permute_in(n1, n1)
    mixed[...] = n1[...].astype(f32)

    @pl.loop(0, L // R)
    def _(i):
        rows = pl.ds(pl.multiple_of(i * R, R), R)
        x = mixed[rows, :]
        r = lax.rsqrt(jnp.mean(x * x, axis=-1, keepdims=True) + norm_eps)
        n1[rows, :] = (x * r * gain_one).astype(bf16)

    n1t[...] = n1[...].T

    if linked:
        gather.forward(0)
        gather.along_start(2)
        gather.along_start(3)
    fetch_cot.wait()
    permute_in(cot, cot)
    if linked:
        gather.start(1)
        gather.pair(0)
        gather.across_start()
    cott[...] = cot[...].T

    fills[0] = jnp.zeros((SUB, hm), f32)
    fills[1] = jnp.ones((SUB, hm), f32)
    tally[0] = fills[0]
    tally[1] = fills[0]

    @pl.loop(0, parts)
    def _(turn):
        m = of_turn(turn)
        if linked:
            for k in range(parts):

                @pl.when(turn == k)
                def _():
                    if k:
                        gather.pair(k)
                    gather.ready(k)
                    gather.place(k)

        forget[m] = dot(n1[...], wg[m, :, :hm])
        admit[m] = dot(n1[...], wg[m, :, hm : 2 * hm])
        cand[m] = dot(n1[...], wg[m, :, 2 * hm :])

        if linked:
            for k in range(parts - 1):

                @pl.when(turn == k)
                def _():
                    if k:
                        gather.forward(k + 1)
                    if k < 2:
                        gather.start(k + 2)

        @pl.loop(0, L // R)
        def _(i):
            rows = pl.ds(pl.multiple_of(i * R, R), R)
            f = sigmoid(forget[m, rows, :])
            a = sigmoid(admit[m, rows, :])
            inv = recip(f + a)
            forget[m, rows, :] = f
            admit[m, rows, :] = a
            kept[rows, :] = f * inv
            put(0, rows, a * inv * cand[m, rows, :])

        def step(j, carry):
            s, p, k_sum, kj_sum = carry
            rows = pl.ds(pl.multiple_of(j * SUB, SUB), SUB)
            keep = kept[rows, :]
            s = keep * s + take(0, rows)
            p = keep * p
            put(0, rows, s)
            put(half, rows, p)
            return s, p, k_sum + keep, kj_sum + keep * j.astype(f32)

        s, p, k_sum, kj_sum = lax.fori_loop(0, J, step, (fills[0], fills[1], fills[0], fills[0]), unroll=16)
        tally[0] += k_sum
        tally[1] += kj_sum
        enter = fills[0]
        for _ in range(SUB - 1):
            enter = shift_down(s + p * enter)

        @pl.loop(0, L // R)
        def _(i):
            rows = pl.ds(pl.multiple_of(i * R, R), R)
            state[m, pl.ds(pl.multiple_of(i * R + SUB, SUB), R), :] = take(0, rows) + take(half, rows) * spread(enter)

        state[m, :SUB, :] = shift_down(state[m, L:, :])

    if linked:
        net.drain()
        gather.done()

    @pl.loop(0, parts)
    def _(m):
        for cols in column_halves:
            mixed[:, cols] += dot(state[m, SUB:, :].astype(bf16), wo[m, :, cols])

    @pl.loop(0, L // R)
    def _(i):
        rows = pl.ds(pl.multiple_of(i * R, R), R)
        x = mixed[rows, :]
        r = lax.rsqrt(jnp.mean(x * x, axis=-1, keepdims=True) + norm_eps)
        n2[rows, :] = (x * r * gain_two).astype(bf16)
        acc_a[rows, :] = x
        acc_b[rows, :] = jnp.zeros_like(x)

    n2t[...] = n2[...].T

    @pl.loop(0, parts)
    def _(turn):
        m = of_turn(turn)
        for first in range(0, fm, fm // 2):
            units_of = slice(first, first + fm // 2)
            up = dot(n2[...], wu[m, :, units_of])
            da = dot(cot[...], wd[m, units_of, :], True)
            cdf, xpdf = gelu_terms(up)
            act[:, units_of] = (up * cdf).astype(bf16)
            dup[:, units_of] = (da * (cdf + xpdf)).astype(bf16)
            if linked and first == 0:
                for k in (2, 3):

                    @pl.when(turn == k)
                    def _():
                        reduce.plane(UPDOWN, k - 1)

        for cols in column_halves:
            acc_a[:, cols] += dot(act[...], wd[m, :, cols])
        for cols in column_halves:
            acc_b[:, cols] += dot(dup[...], wu[m, cols, :], True)
        for c in range(0, fm, fm // 2):
            part = slice(c, c + fm // 2)
            stack(m, 0, fm // BLK, c // BLK, dot(n2t[...], dup[:, part]))
        for c in range(0, fm, fm // 2):
            part = slice(c, c + fm // 2)
            stack_turned(m, units[UPDOWN][1] // 2 + c // BLK * (D // BLK), dot(cott[...], act[:, part]))
        if linked:
            for k in (1, 2, 3):

                @pl.when(turn == k)
                def _():
                    if k == 1:
                        gather.all_done()
                    reduce.chip(UPDOWN, k)

    permute_out(acc_a, n1)
    push_out = pltpu.make_async_copy(n1, block_out, local.at[0])
    push_out.start()

    if linked:
        reduce.model(UPDOWN, 1)
        reduce.turn(UPDOWN, 2)
        reduce.plane(UPDOWN, 3)

    gain_sum_two = jnp.zeros((1, D), f32)

    def back_two(i, total):
        rows = pl.ds(pl.multiple_of(i * R, R), R)
        x = mixed[rows, :]
        r = lax.rsqrt(jnp.mean(x * x, axis=-1, keepdims=True) + norm_eps)
        dn = acc_b[rows, :]
        q = dn * gain_two
        d = cot[rows, :].astype(f32) + r * q - r * r * r * x * jnp.mean(q * x, axis=-1, keepdims=True)
        mixed[rows, :] = d
        dml[rows, :] = d.astype(bf16)
        acc_b[rows, :] = jnp.zeros_like(d)
        return total + jnp.sum(dn * x * r, axis=0, keepdims=True)

    gain_sum_two = lax.fori_loop(0, L // R, back_two, gain_sum_two)
    dmlt[...] = dml[...].T
    fetch_tok = pltpu.make_async_copy(tokens, cot, local.at[1])
    fetch_tok.start()

    @pl.loop(0, parts)
    def _(m):
        stack_turned(m, units[OUT][0], dot(dmlt[...], state[m, SUB:, :].astype(bf16)))

    if linked:
        for i in (3, 2, 1):
            reduce.chip(OUT, i)

    @pl.loop(0, parts)
    def _(back_turn):
        turn = parts - 1 - back_turn
        m = of_turn(turn)
        put(0, slice(None), dot(dml[...], wo[m], True))

        @pl.loop(0, L // R)
        def _(i):
            rows = pl.ds(pl.multiple_of(i * R, R), R)
            f = forget[m, rows, :]
            kept[rows, :] = f * recip(f + admit[m, rows, :])

        def step(k, carry):
            u, p, keep_next = carry
            j = J - 1 - k
            rows = pl.ds(pl.multiple_of(j * SUB, SUB), SUB)
            u = take(0, rows) + keep_next * u
            p = keep_next * p
            put(0, rows, u)
            put(half, rows, p)
            return u, p, kept[rows, :]

        u, p, keep_first = lax.fori_loop(0, J, step, (fills[0], fills[1], fills[1]), unroll=16)
        enter = fills[0]
        for _ in range(SUB - 1):
            enter = shift_up(keep_first * (u + p * enter))

        if linked:

            @pl.when(turn == 3)
            def _():
                reduce.turn(UPDOWN, 3)
                reduce.model(UPDOWN, 2)
                for i in (3, 2, 1):
                    reduce.plane(OUT, i)

            @pl.when(turn == 2)
            def _():
                reduce.model(UPDOWN, 3)
                for i in (3, 2):
                    reduce.turn(OUT, i)
                reduce.plane(GATE, 3)

            @pl.when(turn == 1)
            def _():
                for i in (1, 3, 2):
                    reduce.model(OUT, i)
                reduce.turn(GATE, 3)
                reduce.plane(GATE, 2)

            @pl.when(turn == 0)
            def _():
                reduce.plane(GATE, 1)
                reduce.model(GATE, 3)
                reduce.turn(GATE, 2)

        @pl.loop(0, L // R)
        def _(i):
            rows = pl.ds(pl.multiple_of(i * R, R), R)
            carried = take(0, rows) + take(half, rows) * spread(enter)
            f = forget[m, rows, :]
            a = admit[m, rows, :]
            adm = a * recip(f + a)
            g = carried * (state[m, rows, :] - cand[m, rows, :]) * (kept[rows, :] * adm)
            dpre[rows, :hm] = (g * (1.0 - f)).astype(bf16)
            dpre[rows, hm : 2 * hm] = (g * (a - 1.0)).astype(bf16)
            dpre[rows, 2 * hm :] = (carried * adm).astype(bf16)

        for k in range(3):
            stack(m, units[GATE][0], 3 * hm // BLK, k * hm // BLK, dot(n1t[...], dpre[:, k * hm : (k + 1) * hm]))
        if linked:
            for k in (3, 2, 1):

                @pl.when(turn == k)
                def _():
                    reduce.chip(GATE, k)

        for cols in column_halves:
            acc_b[:, cols] += dot(dpre[...], wg[m, cols, :], True)

    if linked:
        reduce.model(GATE, 1)
        reduce.model(GATE, 2)
        reduce.own(UPDOWN)
        reduce.own(OUT)

    fetch_tok.wait()
    permute_in(cot, cot)

    def back_one(i, total):
        rows = pl.ds(pl.multiple_of(i * R, R), R)
        x = cot[rows, :].astype(f32)
        r = lax.rsqrt(jnp.mean(x * x, axis=-1, keepdims=True) + norm_eps)
        dn = acc_b[rows, :]
        q = dn * gain_one
        mixed[rows, :] += r * q - r * r * r * x * jnp.mean(q * x, axis=-1, keepdims=True)
        return total + jnp.sum(dn * x * r, axis=0, keepdims=True)

    gain_sum_one = lax.fori_loop(0, L // R, back_one, jnp.zeros((1, D), f32))

    place = lax.broadcasted_iota(jnp.int32, (SUB, hm), 0).astype(f32) * float(J)
    if linked:
        first = ((gather.me * parts + gather.m) * L + 1).astype(f32)
        token_total = float(L * parts * lax.axis_size("dp"))
    else:
        first = base[0]
        token_total = base[1]
    forget_sum = jnp.sum(tally[1] + tally[0] * (place + first), axis=0, keepdims=True) / token_total
    small[...] = jnp.zeros_like(small)
    small[0:1, :] = gain_sum_one
    small[1:2, :] = gain_sum_two
    small[2:3, :hm] = forget_sum
    if linked:
        flat = units[UPDOWN][1] // 2, units[GATE][0]
        count = owned.shape[0]
        flags = []
        for k in range(count):
            spot = slot_place[gather.me * count + k]
            flags.append(jnp.where((spot >= flat[0]) & (spot < flat[1]), 1.0, 0.0).astype(f32))

    if linked:
        tiny = SmallSum(net, gather, small, sum_a, sum_b, sum_c)
        tiny.send(0)
        reduce.own(GATE)
        reduce.slots_chip(slots, slot_place, pair)
        tiny.add(0)
        tiny.send(1)
        reduce.slots_plane(slots, pair, far)

    permute_out(mixed, acc_a)
    push_grad = pltpu.make_async_copy(acc_a, input_grad, local.at[2])
    push_grad.start()

    if linked:
        tiny.add(1)
        tiny.send(2)
        reduce.slots_end(slots, pair, far, owned)
        tiny.add(2)
        for k, flag in enumerate(flags):
            small[3 + k // 4 : 4 + k // 4, (k % 4) * BLK : (k % 4 + 1) * BLK] = jnp.full((1, BLK), flag, f32)
        net.drain()
    push_out.wait()
    push_grad.wait()


def compute(tokens, cotangent, gains, weights=None, base=None, master=None, rank=None, slot_place=None):
    linked = weights is None
    parts = lax.axis_size("mp")
    hm, fm = H // parts, FF // parts
    stacked = (parts, D * (4 * hm + 2 * fm) // BLK**2, BLK, BLK)
    sds = jax.ShapeDtypeStruct
    vm, sm, hbm = (pl.BlockSpec(memory_space=k) for k in (pltpu.VMEM, pltpu.SMEM, pl.ANY))
    if linked:
        n = rank.shape[0]
        args = (tokens, cotangent, master, rank, slot_place, gains)
        in_specs = [hbm, hbm, vm, sm, sm, vm]
        middle = sds((n // 8, BLK, BLK), f32)
        extra = [
            pltpu.VMEM((parts, D, 3 * hm), bf16),
            pltpu.VMEM((parts, hm, D), bf16),
            pltpu.VMEM((parts, D, fm), bf16),
            pltpu.VMEM((parts, fm, D), bf16),
            pltpu.VMEM(stacked, bf16),
            pltpu.VMEM((n, BLK, BLK), bf16),
            *[pltpu.VMEM((n, BLK, BLK), bf16) for _ in range(parts - 1)],
            pltpu.VMEM((n // 2, BLK, BLK), bf16),
            pltpu.VMEM((6, n // 16, BLK, BLK), bf16),
            pltpu.VMEM((parts, 8, D), f32),
            pltpu.VMEM((4, 8, D), f32),
            pltpu.VMEM((2, 8, D), f32),
            pltpu.SemaphoreType.DMA((128,)),
            pltpu.SemaphoreType.DMA((128,)),
            pltpu.SemaphoreType.REGULAR,
        ]
        params = dict(collective_id=0, has_side_effects=True)
    else:
        args = (tokens, cotangent, base, *weights, gains)
        in_specs = [hbm, hbm, sm] + [vm] * 5
        middle = sds(stacked, bf16)
        extra = []
        params = {}
    return pl.pallas_call(
        functools.partial(compute_kernel, linked),
        out_shape=(sds((L, D), bf16), sds((L, D), f32), middle, sds((8, D), f32)),
        in_specs=in_specs,
        out_specs=[hbm, hbm, vm, vm],
        scratch_shapes=extra
        + [pltpu.VMEM(shape, bf16) for shape in ((L, D), (D, L)) * 3]
        + [pltpu.VMEM((parts, L, hm), f32)] * 3
        + [pltpu.VMEM((parts, L + SUB, hm), f32)]
        + [pltpu.VMEM((2 * hm // BLK, L, BLK), f32)]
        + [pltpu.VMEM((L, D), f32)] * 3
        + [
            pltpu.VMEM((L, 2 * fm), bf16),
            pltpu.VMEM((L, hm), f32),
            pltpu.VMEM((2, SUB, hm), f32),
            pltpu.VMEM((2, SUB, hm), f32),
            pltpu.SemaphoreType.DMA((3,)),
        ],
        compiler_params=pltpu.CompilerParams(vmem_limit_bytes=64 * 2**20 - 2**16, **params),
        name="block",
    )(*args)


def adam_update(first_old, second_old, gradient):
    first_new = beta_one * first_old + (1.0 - beta_one) * gradient
    second_new = beta_two * second_old + (1.0 - beta_two) * gradient * gradient
    first_hat = first_new / (1.0 - beta_one**STEP)
    second_hat = second_new / (1.0 - beta_two**STEP)
    return (first_new, second_new, first_hat / (jnp.sqrt(second_hat) + adam_eps))


def fine_dot(a, b, trans_b=False):
    a_high, b_high = a.astype(bf16), b.astype(bf16)
    a_low, b_low = (a - a_high.astype(f32)).astype(bf16), (b - b_high.astype(f32)).astype(bf16)
    return dot(a_high, b_high, trans_b) + (dot(a_high, b_low, trans_b) + dot(a_low, b_high, trans_b))


def update_kernel(token_total, passed, sums, gains, gain_moment_one, gain_moment_two, *refs):
    sources, refs = refs[:6], refs[6:]
    given, refs = refs[:passed], refs[passed:]
    results, refs = refs[:4], refs[4:]
    gain_first, gain_second, gains_new, forget_mean = refs[:4]
    copied, refs = refs[4 : 4 + passed], refs[4 + passed :]
    held, made, made_low, sem_in, sem_out, sem_pass = refs[:6]
    passage = refs[6:]
    count = held.shape[1]
    step = max(count // 2, 1)
    groups = [slice(first, first + step) for first in range(0, count, step)]
    enter = [pltpu.make_async_copy(src, via, sem_pass.at[0, k]) for k, (src, via) in enumerate(zip(given, passage))]
    leave = [pltpu.make_async_copy(via, dst, sem_pass.at[1, k]) for k, (via, dst) in enumerate(zip(passage, copied))]
    fetch = [
        [pltpu.make_async_copy(src.at[group], held.at[k, group], sem_in.at[g, k]) for k, src in enumerate(sources)]
        for g, group in enumerate(groups)
    ]
    for copy in fetch[0]:
        copy.start()
    for copy in enter:
        copy.start()
    for row in fetch[1:]:
        for copy in row:
            copy.start()
    first, second, direction = adam_update(gain_moment_one[...], gain_moment_two[...], sums[0:2, :])
    gain_first[...] = first
    gain_second[...] = second
    gains_new[...] = gains[...] - gain_rate * direction
    forget_mean[...] = jnp.sum(sums[2:3, :], axis=1, keepdims=True) * (1.0 / (H * (token_total + 1) / 2.0))
    push = []
    for g, group in enumerate(groups):
        blocks = range(group.start, group.stop)
        for copy in fetch[g]:
            copy.wait()
        if g == len(groups) - 1:
            for come, go in zip(enter, leave):
                come.wait()
                go.start()
        grads = []
        for s in blocks:
            grad = held[0, s]
            flag = sums[3 + s // 4 : 4 + s // 4, (s % 4) * BLK : (s % 4 + 1) * BLK]
            grads.append(jnp.where(flag > 0.5, grad.T, grad))
        values = [fine_dot(held[1, s].T, grad) for s, grad in zip(blocks, grads)]
        values = [fine_dot(value, held[2, s]) for s, value in zip(blocks, values)]
        for k, s in enumerate(blocks):
            first, second, values[k] = adam_update(held[3, s], held[4, s], values[k])
            made[0, s] = first
            made[1, s] = second
        values = [fine_dot(held[1, s], value) for s, value in zip(blocks, values)]
        values = [fine_dot(value, held[2, s], True) for s, value in zip(blocks, values)]
        for s, value in zip(blocks, values):
            fresh = held[5, s] - learn_rate * (value + weight_decay * held[5, s])
            made[2, s] = fresh
            made_low[s] = fresh.astype(bf16)
        for k, dst in enumerate(results):
            src = made.at[k, group] if k < 3 else made_low.at[group]
            copy = pltpu.make_async_copy(src, dst.at[group], sem_out.at[g, k])
            copy.start()
            push.append(copy)
    for copy in push + leave:
        copy.wait()


def update(token_total, small, large, passed):
    sds = jax.ShapeDtypeStruct
    blocks, gain = large[0].shape, small[1].shape
    vm, hbm = pl.BlockSpec(memory_space=pltpu.VMEM), pl.BlockSpec(memory_space=pl.ANY)
    return pl.pallas_call(
        functools.partial(update_kernel, token_total, len(passed)),
        out_shape=[sds(blocks, f32)] * 3
        + [sds(blocks, bf16)]
        + [sds(gain, f32)] * 3
        + [sds((1, 1), f32)]
        + [sds(v.shape, v.dtype) for v in passed],
        in_specs=[vm] * 4 + [hbm] * (len(large) + len(passed)),
        out_specs=[hbm] * 4 + [vm] * 4 + [hbm] * len(passed),
        scratch_shapes=[
            pltpu.VMEM((6, *blocks), f32),
            pltpu.VMEM((3, *blocks), f32),
            pltpu.VMEM(blocks, bf16),
            pltpu.SemaphoreType.DMA((2, 6)),
            pltpu.SemaphoreType.DMA((2, 4)),
            pltpu.SemaphoreType.DMA((2, len(passed))),
        ]
        + [pltpu.VMEM(v.shape, v.dtype) for v in passed],
        compiler_params=pltpu.CompilerParams(vmem_limit_bytes=56 * 2**20),
        name="update",
    )(*small, *large, *passed)


def on_device(
    tokens,
    cotangent,
    master,
    moment_one,
    moment_two,
    basis_left,
    basis_right,
    owner,
    gains,
    gain_moment_one,
    gain_moment_two,
):
    parts = lax.axis_size("mp")
    data_parts = lax.axis_size("dp")
    hm, fm = H // parts, FF // parts
    token_total = L * data_parts * parts
    row_tiles, cols, lows = D // BLK, (3 * hm + fm) // BLK, (hm + fm) // BLK
    number = jnp.arange(owner.shape[0], dtype=jnp.int32)
    ahead = (owner[None, :] < owner[:, None]) | ((owner[None, :] == owner[:, None]) & (number[None, :] < number[:, None]))
    block_rank = jnp.sum(ahead.astype(jnp.int32), axis=1)
    _, table = stack_places(hm, fm)
    table = jnp.asarray(table, jnp.int32)
    slot_place = jnp.sum(jnp.where(block_rank[None, :] == number[:, None], table[None, :], 0), axis=1)
    if data_parts == 8 and parts == 4:
        block_out, input_grad, owned, sums = compute(
            tokens, cotangent, gains, master=master[0], rank=block_rank, slot_place=slot_place
        )
    else:
        stored = lax.all_gather(master.astype(bf16), "dp", axis=1, tiled=True)
        stored = lax.all_gather(stored, "mp", axis=0, tiled=True)
        stack = stored[:, block_rank]
        upper = stack[:, : row_tiles * cols].reshape(parts, row_tiles, cols, BLK, BLK)
        upper = upper.transpose(0, 1, 3, 2, 4).reshape(parts, D, cols * BLK)
        lower = stack[:, row_tiles * cols :].reshape(parts, lows, row_tiles, BLK, BLK)
        lower = lower.transpose(0, 1, 3, 2, 4).reshape(parts, lows * BLK, D)
        weights = (upper[:, :, : 3 * hm], lower[:, :hm], upper[:, :, 3 * hm :], lower[:, hm:])
        first = ((lax.axis_index("dp") * parts + lax.axis_index("mp")) * L + 1).astype(f32)
        base = jnp.stack([first, jnp.asarray(token_total, f32)])
        block_out, input_grad, grads, sums = compute(tokens, cotangent, gains, weights=weights, base=base)
        owned = lax.psum_scatter(grads[:, slot_place].astype(f32), "dp", scatter_dimension=1, tiled=True)
        owned = lax.psum_scatter(owned, "mp", scatter_dimension=0, tiled=True)[0]
        sums = lax.psum(sums, ("dp", "mp"))
        count = master.shape[1]
        mine = lax.dynamic_slice_in_dim(slot_place, lax.axis_index("dp") * count, count)
        units, _ = stack_places(hm, fm)
        flags = ((mine >= units[UPDOWN][1] // 2) & (mine < units[GATE][0])).astype(f32)
        flags = jnp.pad(jnp.repeat(flags, BLK), (0, (8 - count) * BLK)).reshape(2, 4 * BLK)
        sums = jnp.concatenate([sums[:3], flags, sums[5:]])
    outs = update(
        token_total,
        (sums, gains, gain_moment_one, gain_moment_two),
        (owned, basis_left[0], basis_right[0], moment_one[0], moment_two[0], master[0]),
        (block_out, input_grad),
    )
    first_new, second_new, master_new, master_low, gain_first, gain_second, gains_new, forget_mean = outs[:8]
    block_out, input_grad = outs[8:]
    return (
        block_out,
        input_grad,
        first_new[None],
        second_new[None],
        master_new[None],
        master_low[None],
        gain_first,
        gain_second,
        gains_new,
        forget_mean[0, 0],
    )


def solution(mesh):
    rows, blocks = P(("dp", "mp"), None), P("mp", "dp", None, None)
    return jax.shard_map(
        on_device,
        mesh=mesh,
        in_specs=(rows, rows, blocks, blocks, blocks, blocks, blocks, P(), P(), P(), P()),
        out_specs=(rows, rows, blocks, blocks, blocks, blocks, P(), P(), P(), P()),
        check_vma=False,
    )
```

```python
import functools

import jax
import jax.numpy as jnp
from jax import lax
from jax.experimental import pallas as pl
from jax.experimental.pallas import tpu as pltpu
from jax.sharding import PartitionSpec as P

D = 512
H = 1024
FF = 2048
BLK = 128
STEP = 10
L = 1024

norm_eps = 1e-05
beta_one = 0.5
beta_two = 0.5
adam_eps = 1e-08
learn_rate = 0.02
gain_rate = 0.1
weight_decay = 0.1
highest = lax.Precision.HIGHEST

f32 = jnp.float32
bf16 = jnp.bfloat16
SUB = 8
J = L // SUB
R = 128


def dot(a, b, trans_b=False):
    dims = (((1,), (1,)), ((), ())) if trans_b else (((1,), (0,)), ((), ()))
    return lax.dot_general(a, b, dims, preferred_element_type=f32)


def recip(v):
    return pltpu.reciprocal(v, approx=True)


def sigmoid(v):
    return recip(1.0 + jnp.exp(-v))


def shift_down(v):
    rolled = pltpu.roll(v, 1, 0)
    row = lax.broadcasted_iota(jnp.int32, v.shape, 0)
    return jnp.where(row == 0, 0.0, rolled)


def shift_up(v):
    rolled = pltpu.roll(v, SUB - 1, 0)
    row = lax.broadcasted_iota(jnp.int32, v.shape, 0)
    return jnp.where(row == SUB - 1, 0.0, rolled)


def gelu_terms(x):
    a = jnp.abs(x)
    t = recip(1.0 + a * (0.3275911 * 0.7071067811865476))
    poly = t * (
        0.5 * 0.254829592
        + t
        * (
            0.5 * -0.284496736
            + t * (0.5 * 1.421413741 + t * (0.5 * -1.453152027 + t * (0.5 * 1.061405429)))
        )
    )
    e = jnp.exp(x * x * -0.5)
    tail = poly * e
    cdf = jnp.where(x < 0.0, tail, 1.0 - tail)
    return cdf, x * e * 0.3989422804014327


MESH = pl.DeviceIdType.MESH


class Copy:
    def __init__(self, net, make):
        self.net, self.make = net, make

    def start(self):
        self.net.open.append(self)
        self.make().start()
        return self

    def wait_recv(self):
        self.make().wait_recv()

    def wait_send(self):
        self.make().wait_send()


class Exchange:
    def __init__(self, send, recv):
        self.send, self.recv, self.known, self.used, self.open = send, recv, {}, 0, []

    def copy(self, parts, key=None):
        if key in self.known:
            return self.known[key]
        k = self.used
        self.used += 1

        def make():
            src, dst, device = parts()
            return pltpu.make_async_remote_copy(
                src_ref=src,
                dst_ref=dst,
                send_sem=self.send.at[k],
                recv_sem=self.recv.at[k],
                device_id=device,
                device_id_type=MESH,
            )

        copy = Copy(self, make)
        if key is not None:
            self.known[key] = copy
        return copy

    def start(self, parts):
        return self.copy(parts).start()

    def drain(self):
        for copy in self.open:
            copy.wait_send()
        self.open = []


class Gather:
    def __init__(self, net, master, rank, slots, pool, weights, free):
        self.net, self.weights, self.rank, self.free = net, weights, rank, free
        self.held = [slots, *pool]
        d, m = lax.axis_index("dp"), lax.axis_index("mp")
        core, col, row = d % 2, (d // 2) % 2, d // 4
        self.me, self.m, self.side = d, m, core
        self.core = d + 1 - 2 * core
        self.plane = [d + 2 - 4 * col, d + 4 - 8 * row, d + 6 - 4 * col - 8 * row]
        self.order = [m, m + 1 - 2 * (m % 2), m + 2 - 4 * (m // 2), 3 - m]
        self.peers = [(e, m) for e in [self.core] + self.plane] + [(d, k) for k in self.order[1:]]
        barrier = pltpu.get_barrier_semaphore()
        for device in self.peers:
            pl.semaphore_signal(barrier, inc=1, device_id=device, device_id_type=MESH)
        self.n = master.shape[0]
        for s in range(self.n):
            slots[d * self.n + s] = master[s].astype(bf16)
        pl.semaphore_wait(barrier, len(self.peers))

    def rows(self, i, e, first, count):
        return self.held[i].at[pl.ds(e * self.n + first, count)]

    def along(self, i, e):
        return self.net.copy(
            lambda: (self.rows(0, e, 0, self.n), self.rows(i, e, 0, self.n), (self.me, self.order[i])),
            ("along", i, e is self.me),
        )

    def within(self, key, i, e, first, count, to):
        return self.net.copy(
            lambda: (self.rows(i, e, first, count), self.rows(i, e, first, count), (to, self.m)), (key, i)
        )

    def first(self, i):
        (x, y, _), h = self.plane, self.n // 2
        if i == 1:
            jobs = ((0, self.n, x), (0, self.n, y))
        else:
            jobs = ((0, h, x), (h, h, y), (h, h, x), (0, h, y))
        return [self.within(("first", k), i, self.me, *job) for k, job in enumerate(jobs)]

    def last(self, i):
        x, y, z = self.plane
        if i == 1:
            return [self.along(1, z)]
        h = self.n // 2
        return [self.within("over y", i, x, 0, h, y), self.within("over x", i, y, h, h, x)]

    def inside(self, i):
        return [self.within(("inside", k), i, e, 0, self.n, self.core) for k, e in enumerate([self.me] + self.plane)]

    def along_start(self, i):
        self.along(i, self.me).start()

    def across_start(self):
        self.last(1)[0].start()

    def start(self, i):
        if i:
            self.along(i, self.me).wait_recv()
        for copy in self.first(i):
            copy.start()
        self.inside(i)[0].start()

    def forward(self, i):
        if i == 1:
            return
        for came, copy in zip(self.first(i), self.last(i)):
            came.wait_recv()
            copy.start()

    def pair(self, i):
        for came, copy in zip(self.first(i)[-2:], self.inside(i)[1:3]):
            came.wait_recv()
            copy.start()
        for came in self.last(i):
            came.wait_recv()
        self.inside(i)[3].start()

    def ready(self, i):
        for copy in self.inside(i):
            copy.wait_recv()

    def place(self, i):
        wg, wo, wu, wd = self.weights
        row_tiles, gates = D // BLK, wg.shape[2] // BLK
        cols, outs = gates + wu.shape[2] // BLK, wo.shape[1] // BLK
        for b in range(row_tiles * cols + (wo.shape[1] + wd.shape[1]) // BLK * row_tiles):
            if b < row_tiles * cols:
                r, c = b // cols, b % cols
                ref = wg if c < gates else wu
                c -= 0 if c < gates else gates
            else:
                r, c = (b - row_tiles * cols) // row_tiles, (b - row_tiles * cols) % row_tiles
                ref = wo if r < outs else wd
                r -= 0 if r < outs else outs
            block = self.held[i][self.rank[b]]
            ref[self.order[i], r * BLK : (r + 1) * BLK, c * BLK : (c + 1) * BLK] = block

    def done(self):
        for device in self.peers:
            pl.semaphore_signal(self.free, inc=1, device_id=device, device_id_type=MESH)

    def all_done(self):
        pl.semaphore_wait(self.free, len(self.peers))


def stack_places(hm, fm):
    row_tiles, gates, ups, outs = D // BLK, 3 * hm // BLK, fm // BLK, hm // BLK
    cols = gates + ups
    first_down = row_tiles * ups
    first_out = 2 * first_down
    first_gate = first_out + row_tiles * outs
    table = []
    for b in range(row_tiles * (cols + outs + ups)):
        if b < row_tiles * cols:
            r, c = b // cols, b % cols
            table.append(first_gate + r * gates + c if c < gates else r * ups + c - gates)
        else:
            k = b - row_tiles * cols
            table.append(first_out + k if k < row_tiles * outs else first_down + k - row_tiles * outs)
    return ((0, first_out), (first_out, row_tiles * outs), (first_gate, row_tiles * gates)), table


UPDOWN, OUT, GATE = range(3)


class Reduce:
    def __init__(self, net, gather, grads, units, pool):
        self.net, self.g, self.grads, self.units, self.pool = net, gather, grads, units, pool
        self.half = grads.shape[1] // 2
        self.eighth = grads.shape[1] // 8

    def place(self, e):
        return (e % 2) * 4 + e // 2

    def inside(self, unit, i):
        g, (first, count) = self.g, self.units[unit]
        return self.net.copy(
            lambda: (
                self.grads.at[g.order[i], pl.ds(first + (1 - g.side) * (count // 2), count // 2)],
                self.pool[i - 1].at[pl.ds(first // 2, count // 2)],
                (g.core, g.m),
            ),
            ("chip", unit, i),
        )

    def chip(self, unit, i):
        self.inside(unit, i).start()

    def spot(self, unit, i, slot, first, count):
        base, total = self.units[unit]
        return self.pool[i - 1].at[pl.ds(self.half + slot * self.eighth + base // 8 + first, count)]

    def parts(self, unit, i):
        n = self.units[unit][1] // 8
        if i == 1:
            return ((0, n),)
        h = (n + i % 2) // 2 if n % 2 else n // 2
        return (0, h), (h, n - h)

    def share(self, unit, i, e, first, count):
        base, total = self.units[unit]
        return self.grads.at[self.g.order[i], pl.ds(base + self.place(e) * (total // 8) + first, count)]

    def over(self, unit, i, slot, part):
        x, y, z = self.g.plane
        e = (z, x, y)[slot]
        to = (x if part == self.parts(unit, i)[0] else y, x, y)[slot]
        return self.net.copy(
            lambda: (self.share(unit, i, e, *part), self.spot(unit, i, slot, *part), (to, self.g.m)),
            ("over", unit, i, slot, part),
        )

    def send(self, unit, i, slot, part):
        if part[1]:
            self.over(unit, i, slot, part).start()

    def take(self, unit, i, slot, part):
        self.over(unit, i, slot, part).wait_recv()
        return self.spot(unit, i, slot, *part)[...].astype(f32)

    def model_copy(self, unit, i):
        n = self.units[unit][1] // 8
        return self.net.copy(
            lambda: (self.share(unit, i, self.g.me, 0, n), self.spot(unit, i, 3, 0, n), (self.g.me, self.g.order[i])),
            ("model", unit, i),
        )

    def aside(self, unit):
        part = (0, self.units[unit][1] // 8)
        return self.net.copy(
            lambda: (
                self.share(unit, 1, self.g.plane[2], *part),
                self.spot(unit, 1, 0, *part),
                (self.g.me, self.g.order[1]),
            ),
            ("aside", unit),
        )

    def plane(self, unit, i):
        g, (first, count) = self.g, self.units[unit]
        x, y, z = g.plane
        self.inside(unit, i).wait_recv()
        m = g.order[i]
        start, came = first + g.side * (count // 2), self.pool[i - 1]

        @pl.loop(0, count // 2)
        def _(b):
            total = self.grads[m, start + b].astype(f32) + came[first // 2 + b].astype(f32)
            self.grads[m, start + b] = total.astype(bf16)

        if i == 1:
            (whole,) = self.parts(unit, i)
            self.send(unit, i, 1, whole)
            self.send(unit, i, 2, whole)
            self.aside(unit).start()
            return
        one, two = self.parts(unit, i)
        self.send(unit, i, 0, one)
        self.send(unit, i, 0, two)
        self.send(unit, i, 1, one)
        self.send(unit, i, 2, two)

    def turn(self, unit, i):
        if i == 1:
            return
        x, y, _ = self.g.plane
        for part, slot, e in zip(self.parts(unit, i), (2, 1), (y, x)):
            if part[1]:
                ref = self.share(unit, i, e, *part)
                ref[...] = (ref[...].astype(f32) + self.take(unit, i, 0, part)).astype(bf16)
                self.send(unit, i, slot, part)

    def model(self, unit, i):
        g, (first, count) = self.g, self.units[unit]
        n = count // 8
        for part in self.parts(unit, i):
            if part[1]:
                ref = self.share(unit, i, g.me, *part)
                total = ref[...].astype(f32) + self.take(unit, i, 1, part) + self.take(unit, i, 2, part)
                ref[...] = total.astype(bf16)
        self.model_copy(unit, i).start()

    def own(self, unit):
        g, (first, count) = self.g, self.units[unit]
        n = count // 8
        rows = pl.ds(first + self.place(g.me) * n, n)
        total = self.grads[g.m, rows].astype(f32)
        for i in (1, 2, 3):
            self.model_copy(unit, i).wait_recv()
            total += self.pool[i - 1][pl.ds(self.half + 3 * self.eighth + first // 8, n)].astype(f32)
        self.grads[g.m, rows] = total.astype(bf16)
        self.aside(unit).wait_recv()
        rows = pl.ds(first + self.place(g.plane[2]) * n, n)
        total = self.grads[g.m, rows].astype(f32) + self.spot(unit, 1, 0, 0, n)[...].astype(f32)
        self.grads[g.m, rows] = total.astype(bf16)

    def into_slots(self, out, slot_place, e):
        n = self.eighth
        for k in range(n):
            out[self.place(e) * n + k] = self.grads[self.g.m, slot_place[e * n + k]]

    def slots_chip(self, out, slot_place, pair):
        g, n = self.g, self.eighth
        self.last = []
        targets = (g.plane[2], g.plane[0], g.plane[1], g.me)
        for e in targets:
            other = e + 1 - 2 * g.side
            self.into_slots(out, slot_place, other)
            self.last.append(
                self.net.start(
                    lambda e=e, other=other: (
                        out.at[pl.ds(self.place(other) * n, n)],
                        pair.at[pl.ds((e // 2) * n, n)],
                        (g.core, g.m),
                    )
                )
            )
        for e in targets:
            self.into_slots(out, slot_place, e)

    def slots_plane(self, out, pair, far):
        g, n = self.g, out.shape[0] // 8
        h = n // 2
        x, y, z = g.plane
        wait = dict(zip("zxyo", self.last))

        def mine(e, first, count):
            return pl.ds((g.side * 4 + e // 2) * n + first, count)

        def join(e):
            rows = mine(e, 0, n)
            out[rows] = (out[rows].astype(f32) + pair[pl.ds((e // 2) * n, n)].astype(f32)).astype(bf16)

        def send(e, first, slot, to):
            return self.net.start(lambda: (out.at[mine(e, first, h)], far.at[slot], (to, g.m)))

        wait["z"].wait_recv()
        join(z)
        over_x = send(z, 0, 0, x)
        over_y = send(z, h, 1, y)
        wait["x"].wait_recv()
        join(x)
        self.ends = [send(x, 0, 2, x)]
        wait["y"].wait_recv()
        join(y)
        self.ends.append(send(y, h, 3, y))
        over_x.wait_recv()
        rows = mine(y, 0, h)
        out[rows] = (out[rows].astype(f32) + far[0].astype(f32)).astype(bf16)
        self.ends.append(send(y, 0, 4, y))
        over_y.wait_recv()
        rows = mine(x, h, h)
        out[rows] = (out[rows].astype(f32) + far[1].astype(f32)).astype(bf16)
        self.ends.append(send(x, h, 5, x))
        wait["o"].wait_recv()

    def slots_end(self, out, pair, far, owned):
        g, n = self.g, out.shape[0] // 8
        h = n // 2
        for copy in self.ends:
            copy.wait_recv()
        for first, slots in ((0, (2, 4)), (h, (3, 5))):
            total = out[pl.ds((g.side * 4 + g.me // 2) * n + first, h)].astype(f32)
            total += pair[pl.ds((g.me // 2) * n + first, h)].astype(f32)
            for k in slots:
                total += far[k].astype(f32)
            owned[first : first + h] = total


class SmallSum:
    def __init__(self, net, gather, values, along, across, inside):
        self.net, self.g, self.values = net, gather, values
        self.slots = (along, across, inside)
        self.peers = (
            [(gather.me, k) for k in gather.order[1:]],
            [(e, gather.m) for e in gather.plane],
            [(gather.core, gather.m)],
        )
        self.mine = (gather.m, gather.me // 2, gather.side)
        self.open = []

    def send(self, stage):
        slot = self.slots[stage]
        slot[self.mine[stage]] = self.values[...]
        ref = slot.at[self.mine[stage]]
        self.open = [self.net.start(lambda peer=peer: (ref, ref, peer)) for peer in self.peers[stage]]

    def add(self, stage):
        for copy in self.open:
            copy.wait_recv()
        slot = self.slots[stage]
        total = slot[0]
        for k in range(1, slot.shape[0]):
            total += slot[k]
        self.values[...] = total


def compute_kernel(linked, *refs):
    if linked:
        tokens, cotangent, master, rank, slot_place, gains = refs[:6]
        block_out, input_grad, owned, small = refs[6:10]
        wg, wo, wu, wd, grads, slots, *pool, pair, far, sum_a, sum_b, sum_c, send, recv, free = refs[10:27]
        scratch = refs[27:]
    else:
        tokens, cotangent, base, wg, wo, wu, wd, gains = refs[:8]
        block_out, input_grad, grads, small = refs[8:12]
        scratch = refs[12:]
    (n1, n1t, cot, cott, n2, n2t, forget, admit, cand, state, scan, acc_a, acc_b, mixed, mid, kept, fills, tally, local) = scratch
    dml, dmlt = n2, n2t
    parts, _, hm3 = wg.shape
    hm = hm3 // 3
    fm = wu.shape[2]
    units, _ = stack_places(hm, fm)
    act, dup, dpre = mid.at[:, :fm], mid.at[:, fm:], mid.at[:, : 3 * hm]
    gain_one = gains[0:1, :]
    gain_two = gains[1:2, :]

    fetch_cot = pltpu.make_async_copy(cotangent, cot, local.at[0])
    fetch_tok = pltpu.make_async_copy(tokens, n1, local.at[1])
    fetch_tok.start()
    fetch_cot.start()

    column_halves = (slice(0, D // 2), slice(D // 2, D))

    def stack(m, first, wide, left, value):
        for r in range(value.shape[0] // BLK):
            for c in range(value.shape[1] // BLK):
                grads[m, first + r * wide + left + c] = value[r * BLK : (r + 1) * BLK, c * BLK : (c + 1) * BLK].astype(bf16)

    def stack_turned(m, first, value):
        high = value.shape[0] // BLK
        for r in range(high):
            for c in range(value.shape[1] // BLK):
                grads[m, first + c * high + r] = value[r * BLK : (r + 1) * BLK, c * BLK : (c + 1) * BLK].astype(bf16)

    def permute_in(src, dst):
        for k in range(D // BLK):
            scan[k] = src[:, k * BLK : (k + 1) * BLK].astype(f32)

        @pl.loop(0, J // 2, unroll=4)
        def _(j):
            for k in range(D // BLK):
                lo = scan[k, pl.ds(2 * j, SUB, stride=J), :]
                hi = scan[k, pl.ds(2 * j + 1, SUB, stride=J), :]
                dst[pl.ds(pl.multiple_of(16 * j, 16), 16), k * BLK : (k + 1) * BLK] = jnp.concatenate([lo, hi], 0).astype(bf16)

    def permute_out(src, dst):
        @pl.loop(0, J, unroll=4)
        def _(j):
            rows = pl.ds(pl.multiple_of(j * SUB, SUB), SUB)
            for k in range(D // BLK):
                scan[k, pl.ds(j, SUB, stride=J), :] = src[rows, k * BLK : (k + 1) * BLK]

        for k in range(D // BLK):
            dst[:, k * BLK : (k + 1) * BLK] = scan[k].astype(dst.dtype)

    def put(first, rows, value):
        for k in range(hm // BLK):
            scan[first + k, rows, :] = value[:, k * BLK : (k + 1) * BLK]

    def take(first, rows):
        return jnp.concatenate([scan[first + k, rows, :] for k in range(hm // BLK)], 1)

    half = hm // BLK

    def spread(v):
        return jnp.broadcast_to(v[None], (R // SUB, SUB, hm)).reshape(R, hm)


    if linked:
        net = Exchange(send, recv)
        gather = Gather(net, master, rank, slots, pool, (wg, wo, wu, wd), free)
        gather.start(0)
        gather.along_start(1)
        gather.along_start(2)
        reduce = Reduce(net, gather, grads, units, pool)

    def of_turn(t):
        if not linked:
            return t
        high, low = gather.m // 2, gather.m % 2
        t_high, t_low = t // 2, t % 2
        return 2 * (high + t_high - 2 * high * t_high) + low + t_low - 2 * low * t_low

    fetch_tok.wait()
    permute_in(n1, n1)
    mixed[...] = n1[...].astype(f32)

    @pl.loop(0, L // R)
    def _(i):
        rows = pl.ds(pl.multiple_of(i * R, R), R)
        x = mixed[rows, :]
        r = lax.rsqrt(jnp.mean(x * x, axis=-1, keepdims=True) + norm_eps)
        n1[rows, :] = (x * r * gain_one).astype(bf16)

    n1t[...] = n1[...].T

    if linked:
        gather.forward(0)
        gather.along_start(3)
    fetch_cot.wait()
    permute_in(cot, cot)
    if linked:
        gather.start(1)
        gather.pair(0)
        gather.across_start()
        gather.start(2)
    cott[...] = cot[...].T

    fills[0] = jnp.zeros((SUB, hm), f32)
    fills[1] = jnp.ones((SUB, hm), f32)
    tally[0] = fills[0]
    tally[1] = fills[0]

    @pl.loop(0, parts)
    def _(turn):
        m = of_turn(turn)
        if linked:
            for k in range(parts):

                @pl.when(turn == k)
                def _():
                    if k:
                        gather.pair(k)
                    gather.ready(k)
                    gather.place(k)

        forget[m] = dot(n1[...], wg[m, :, :hm])
        admit[m] = dot(n1[...], wg[m, :, hm : 2 * hm])
        cand[m] = dot(n1[...], wg[m, :, 2 * hm :])

        if linked:
            for k in range(parts - 1):

                @pl.when(turn == k)
                def _():
                    if k == 0:
                        gather.forward(2)
                    if k == 1:
                        gather.start(3)
                    if k == 2:
                        gather.forward(3)

        @pl.loop(0, L // R)
        def _(i):
            rows = pl.ds(pl.multiple_of(i * R, R), R)
            f = sigmoid(forget[m, rows, :])
            a = sigmoid(admit[m, rows, :])
            inv = recip(f + a)
            forget[m, rows, :] = f
            admit[m, rows, :] = a
            kept[rows, :] = f * inv
            put(0, rows, a * inv * cand[m, rows, :])

        def step(j, carry):
            s, p, k_sum, kj_sum = carry
            rows = pl.ds(pl.multiple_of(j * SUB, SUB), SUB)
            keep = kept[rows, :]
            s = keep * s + take(0, rows)
            p = keep * p
            put(0, rows, s)
            put(half, rows, p)
            return s, p, k_sum + keep, kj_sum + keep * j.astype(f32)

        s, p, k_sum, kj_sum = lax.fori_loop(0, J, step, (fills[0], fills[1], fills[0], fills[0]), unroll=16)
        tally[0] += k_sum
        tally[1] += kj_sum
        enter = fills[0]
        for _ in range(SUB - 1):
            enter = shift_down(s + p * enter)

        @pl.loop(0, L // R)
        def _(i):
            rows = pl.ds(pl.multiple_of(i * R, R), R)
            state[m, pl.ds(pl.multiple_of(i * R + SUB, SUB), R), :] = take(0, rows) + take(half, rows) * spread(enter)

        state[m, :SUB, :] = shift_down(state[m, L:, :])

    if linked:
        net.drain()
        gather.done()

    @pl.loop(0, parts)
    def _(m):
        for cols in column_halves:
            mixed[:, cols] += dot(state[m, SUB:, :].astype(bf16), wo[m, :, cols])

    @pl.loop(0, L // R)
    def _(i):
        rows = pl.ds(pl.multiple_of(i * R, R), R)
        x = mixed[rows, :]
        r = lax.rsqrt(jnp.mean(x * x, axis=-1, keepdims=True) + norm_eps)
        n2[rows, :] = (x * r * gain_two).astype(bf16)
        acc_a[rows, :] = x
        acc_b[rows, :] = jnp.zeros_like(x)

    n2t[...] = n2[...].T

    @pl.loop(0, parts)
    def _(turn):
        m = of_turn(turn)
        for first in range(0, fm, fm // 2):
            units_of = slice(first, first + fm // 2)
            up = dot(n2[...], wu[m, :, units_of])
            da = dot(cot[...], wd[m, units_of, :], True)
            cdf, xpdf = gelu_terms(up)
            act[:, units_of] = (up * cdf).astype(bf16)
            dup[:, units_of] = (da * (cdf + xpdf)).astype(bf16)
        for cols in column_halves:
            acc_a[:, cols] += dot(act[...], wd[m, :, cols])
        for cols in column_halves:
            acc_b[:, cols] += dot(dup[...], wu[m, cols, :], True)
        if linked:
            for k in (2, 3):

                @pl.when(turn == k)
                def _():
                    reduce.plane(UPDOWN, k - 1)
                    if k == 3:
                        reduce.model(UPDOWN, 1)

        for c in range(0, fm, fm // 2):
            part = slice(c, c + fm // 2)
            stack(m, 0, fm // BLK, c // BLK, dot(n2t[...], dup[:, part]))
        for c in range(0, fm, fm // 2):
            part = slice(c, c + fm // 2)
            stack_turned(m, units[UPDOWN][1] // 2 + c // BLK * (D // BLK), dot(cott[...], act[:, part]))
        if linked:
            for k in (1, 2, 3):

                @pl.when(turn == k)
                def _():
                    if k == 1:
                        gather.all_done()
                    reduce.chip(UPDOWN, k)

    permute_out(acc_a, n1)
    push_out = pltpu.make_async_copy(n1, block_out, local.at[0])
    push_out.start()

    if linked:
        reduce.plane(UPDOWN, 3)

    gain_sum_two = jnp.zeros((1, D), f32)

    def back_two(i, total):
        rows = pl.ds(pl.multiple_of(i * R, R), R)
        x = mixed[rows, :]
        r = lax.rsqrt(jnp.mean(x * x, axis=-1, keepdims=True) + norm_eps)
        dn = acc_b[rows, :]
        q = dn * gain_two
        d = cot[rows, :].astype(f32) + r * q - r * r * r * x * jnp.mean(q * x, axis=-1, keepdims=True)
        mixed[rows, :] = d
        dml[rows, :] = d.astype(bf16)
        acc_b[rows, :] = jnp.zeros_like(d)
        return total + jnp.sum(dn * x * r, axis=0, keepdims=True)

    gain_sum_two = lax.fori_loop(0, L // R, back_two, gain_sum_two)
    if linked:
        reduce.turn(UPDOWN, 2)
    dmlt[...] = dml[...].T
    fetch_tok = pltpu.make_async_copy(tokens, cot, local.at[1])
    fetch_tok.start()

    @pl.loop(0, parts)
    def _(m):
        stack_turned(m, units[OUT][0], dot(dmlt[...], state[m, SUB:, :].astype(bf16)))

    if linked:
        for i in (3, 2, 1):
            reduce.chip(OUT, i)

    @pl.loop(0, parts)
    def _(back_turn):
        turn = parts - 1 - back_turn
        m = of_turn(turn)
        put(0, slice(None), dot(dml[...], wo[m], True))

        @pl.loop(0, L // R)
        def _(i):
            rows = pl.ds(pl.multiple_of(i * R, R), R)
            f = forget[m, rows, :]
            kept[rows, :] = f * recip(f + admit[m, rows, :])

        def step(k, carry):
            u, p, keep_next = carry
            j = J - 1 - k
            rows = pl.ds(pl.multiple_of(j * SUB, SUB), SUB)
            u = take(0, rows) + keep_next * u
            p = keep_next * p
            put(0, rows, u)
            put(half, rows, p)
            return u, p, kept[rows, :]

        u, p, keep_first = lax.fori_loop(0, J, step, (fills[0], fills[1], fills[1]), unroll=16)
        enter = fills[0]
        for _ in range(SUB - 1):
            enter = shift_up(keep_first * (u + p * enter))

        if linked:

            @pl.when(turn == 3)
            def _():
                for i in (3, 2, 1):
                    reduce.plane(OUT, i)

            @pl.when(turn == 0)
            def _():
                reduce.plane(GATE, 1)

        @pl.loop(0, L // R)
        def _(i):
            rows = pl.ds(pl.multiple_of(i * R, R), R)
            carried = take(0, rows) + take(half, rows) * spread(enter)
            f = forget[m, rows, :]
            a = admit[m, rows, :]
            adm = a * recip(f + a)
            g = carried * (state[m, rows, :] - cand[m, rows, :]) * (kept[rows, :] * adm)
            dpre[rows, :hm] = (g * (1.0 - f)).astype(bf16)
            dpre[rows, hm : 2 * hm] = (g * (a - 1.0)).astype(bf16)
            dpre[rows, 2 * hm :] = (carried * adm).astype(bf16)

        if linked:

            @pl.when(turn == 3)
            def _():
                reduce.turn(UPDOWN, 3)
                reduce.model(UPDOWN, 2)

            @pl.when(turn == 2)
            def _():
                reduce.plane(GATE, 3)
                for i in (3, 2):
                    reduce.turn(OUT, i)
                reduce.model(UPDOWN, 3)

            @pl.when(turn == 1)
            def _():
                reduce.plane(GATE, 2)
                for i in (1, 3, 2):
                    reduce.model(OUT, i)

            @pl.when(turn == 0)
            def _():
                reduce.turn(GATE, 2)
                reduce.model(GATE, 3)

        for k in range(3):
            stack(m, units[GATE][0], 3 * hm // BLK, k * hm // BLK, dot(n1t[...], dpre[:, k * hm : (k + 1) * hm]))
        if linked:
            for k in (3, 2, 1):

                @pl.when(turn == k)
                def _():
                    reduce.chip(GATE, k)
                    if k == 1:
                        reduce.turn(GATE, 3)

        for cols in column_halves:
            acc_b[:, cols] += dot(dpre[...], wg[m, cols, :], True)

    if linked:
        reduce.own(UPDOWN)
        reduce.own(OUT)

    fetch_tok.wait()
    permute_in(cot, cot)
    if linked:
        reduce.model(GATE, 1)
        reduce.model(GATE, 2)

    def back_one(i, total):
        rows = pl.ds(pl.multiple_of(i * R, R), R)
        x = cot[rows, :].astype(f32)
        r = lax.rsqrt(jnp.mean(x * x, axis=-1, keepdims=True) + norm_eps)
        dn = acc_b[rows, :]
        q = dn * gain_one
        mixed[rows, :] += r * q - r * r * r * x * jnp.mean(q * x, axis=-1, keepdims=True)
        return total + jnp.sum(dn * x * r, axis=0, keepdims=True)

    gain_sum_one = lax.fori_loop(0, L // R, back_one, jnp.zeros((1, D), f32))

    place = lax.broadcasted_iota(jnp.int32, (SUB, hm), 0).astype(f32) * float(J)
    if linked:
        first = ((gather.me * parts + gather.m) * L + 1).astype(f32)
        token_total = float(L * parts * lax.axis_size("dp"))
    else:
        first = base[0]
        token_total = base[1]
    forget_sum = jnp.sum(tally[1] + tally[0] * (place + first), axis=0, keepdims=True) / token_total
    small[...] = jnp.zeros_like(small)
    small[0:1, :] = gain_sum_one
    small[1:2, :] = gain_sum_two
    small[2:3, :hm] = forget_sum
    if linked:
        flat = units[UPDOWN][1] // 2, units[GATE][0]
        count = owned.shape[0]
        flags = []
        for k in range(count):
            spot = slot_place[gather.me * count + k]
            flags.append(jnp.where((spot >= flat[0]) & (spot < flat[1]), 1.0, 0.0).astype(f32))

    if linked:
        tiny = SmallSum(net, gather, small, sum_a, sum_b, sum_c)
        tiny.send(0)
        reduce.own(GATE)
        reduce.slots_chip(slots, slot_place, pair)
        tiny.add(0)
        tiny.send(1)
        reduce.slots_plane(slots, pair, far)

    permute_out(mixed, acc_a)
    push_grad = pltpu.make_async_copy(acc_a, input_grad, local.at[2])
    push_grad.start()

    if linked:
        tiny.add(1)
        tiny.send(2)
        reduce.slots_end(slots, pair, far, owned)
        tiny.add(2)
        for k, flag in enumerate(flags):
            small[3 + k // 4 : 4 + k // 4, (k % 4) * BLK : (k % 4 + 1) * BLK] = jnp.full((1, BLK), flag, f32)
        net.drain()
    push_out.wait()
    push_grad.wait()


def compute(tokens, cotangent, gains, weights=None, base=None, master=None, rank=None, slot_place=None):
    linked = weights is None
    parts = lax.axis_size("mp")
    hm, fm = H // parts, FF // parts
    stacked = (parts, D * (4 * hm + 2 * fm) // BLK**2, BLK, BLK)
    sds = jax.ShapeDtypeStruct
    vm, sm, hbm = (pl.BlockSpec(memory_space=k) for k in (pltpu.VMEM, pltpu.SMEM, pl.ANY))
    if linked:
        n = rank.shape[0]
        args = (tokens, cotangent, master, rank, slot_place, gains)
        in_specs = [hbm, hbm, vm, sm, sm, vm]
        middle = sds((n // 8, BLK, BLK), f32)
        extra = [
            pltpu.VMEM((parts, D, 3 * hm), bf16),
            pltpu.VMEM((parts, hm, D), bf16),
            pltpu.VMEM((parts, D, fm), bf16),
            pltpu.VMEM((parts, fm, D), bf16),
            pltpu.VMEM(stacked, bf16),
            pltpu.VMEM((n, BLK, BLK), bf16),
            *[pltpu.VMEM((n, BLK, BLK), bf16) for _ in range(parts - 1)],
            pltpu.VMEM((n // 2, BLK, BLK), bf16),
            pltpu.VMEM((6, n // 16, BLK, BLK), bf16),
            pltpu.VMEM((parts, 8, D), f32),
            pltpu.VMEM((4, 8, D), f32),
            pltpu.VMEM((2, 8, D), f32),
            pltpu.SemaphoreType.DMA((128,)),
            pltpu.SemaphoreType.DMA((128,)),
            pltpu.SemaphoreType.REGULAR,
        ]
        params = dict(collective_id=0, has_side_effects=True)
    else:
        args = (tokens, cotangent, base, *weights, gains)
        in_specs = [hbm, hbm, sm] + [vm] * 5
        middle = sds(stacked, bf16)
        extra = []
        params = {}
    return pl.pallas_call(
        functools.partial(compute_kernel, linked),
        out_shape=(sds((L, D), bf16), sds((L, D), f32), middle, sds((8, D), f32)),
        in_specs=in_specs,
        out_specs=[hbm, hbm, vm, vm],
        scratch_shapes=extra
        + [pltpu.VMEM(shape, bf16) for shape in ((L, D), (D, L)) * 3]
        + [pltpu.VMEM((parts, L, hm), f32)] * 3
        + [pltpu.VMEM((parts, L + SUB, hm), f32)]
        + [pltpu.VMEM((2 * hm // BLK, L, BLK), f32)]
        + [pltpu.VMEM((L, D), f32)] * 3
        + [
            pltpu.VMEM((L, 2 * fm), bf16),
            pltpu.VMEM((L, hm), f32),
            pltpu.VMEM((2, SUB, hm), f32),
            pltpu.VMEM((2, SUB, hm), f32),
            pltpu.SemaphoreType.DMA((3,)),
        ],
        compiler_params=pltpu.CompilerParams(vmem_limit_bytes=64 * 2**20 - 2**16, **params),
        name="block",
    )(*args)


def adam_update(first_old, second_old, gradient):
    first_new = beta_one * first_old + (1.0 - beta_one) * gradient
    second_new = beta_two * second_old + (1.0 - beta_two) * gradient * gradient
    first_hat = first_new / (1.0 - beta_one**STEP)
    second_hat = second_new / (1.0 - beta_two**STEP)
    return (first_new, second_new, first_hat / (jnp.sqrt(second_hat) + adam_eps))


def fine_dot(a, b, trans_b=False):
    a_high, b_high = a.astype(bf16), b.astype(bf16)
    a_low, b_low = (a - a_high.astype(f32)).astype(bf16), (b - b_high.astype(f32)).astype(bf16)
    return dot(a_high, b_high, trans_b) + (dot(a_high, b_low, trans_b) + dot(a_low, b_high, trans_b))


def update_kernel(token_total, passed, sums, gains, gain_moment_one, gain_moment_two, *refs):
    sources, refs = refs[:6], refs[6:]
    given, refs = refs[:passed], refs[passed:]
    results, refs = refs[:4], refs[4:]
    gain_first, gain_second, gains_new, forget_mean = refs[:4]
    copied, refs = refs[4 : 4 + passed], refs[4 + passed :]
    held, made, made_low, sem_in, sem_out, sem_pass = refs[:6]
    passage = refs[6:]
    count = held.shape[1]
    step = max(count // 2, 1)
    groups = [slice(first, first + step) for first in range(0, count, step)]
    enter = [pltpu.make_async_copy(src, via, sem_pass.at[0, k]) for k, (src, via) in enumerate(zip(given, passage))]
    leave = [pltpu.make_async_copy(via, dst, sem_pass.at[1, k]) for k, (via, dst) in enumerate(zip(passage, copied))]
    fetch = [
        [pltpu.make_async_copy(src.at[group], held.at[k, group], sem_in.at[g, k]) for k, src in enumerate(sources)]
        for g, group in enumerate(groups)
    ]
    for copy in fetch[0]:
        copy.start()
    for copy in enter:
        copy.start()
    for row in fetch[1:]:
        for copy in row:
            copy.start()
    first, second, direction = adam_update(gain_moment_one[...], gain_moment_two[...], sums[0:2, :])
    gain_first[...] = first
    gain_second[...] = second
    gains_new[...] = gains[...] - gain_rate * direction
    forget_mean[...] = jnp.sum(sums[2:3, :], axis=1, keepdims=True) * (1.0 / (H * (token_total + 1) / 2.0))
    push = []
    for g, group in enumerate(groups):
        blocks = range(group.start, group.stop)
        for copy in fetch[g]:
            copy.wait()
        if g == len(groups) - 1:
            for come, go in zip(enter, leave):
                come.wait()
                go.start()
        grads = []
        for s in blocks:
            grad = held[0, s]
            flag = sums[3 + s // 4 : 4 + s // 4, (s % 4) * BLK : (s % 4 + 1) * BLK]
            grads.append(jnp.where(flag > 0.5, grad.T, grad))
        values = [fine_dot(held[1, s].T, grad) for s, grad in zip(blocks, grads)]
        values = [fine_dot(value, held[2, s]) for s, value in zip(blocks, values)]
        for k, s in enumerate(blocks):
            first, second, values[k] = adam_update(held[3, s], held[4, s], values[k])
            made[0, s] = first
            made[1, s] = second
        values = [fine_dot(held[1, s], value) for s, value in zip(blocks, values)]
        values = [fine_dot(value, held[2, s], True) for s, value in zip(blocks, values)]
        for s, value in zip(blocks, values):
            fresh = held[5, s] - learn_rate * (value + weight_decay * held[5, s])
            made[2, s] = fresh
            made_low[s] = fresh.astype(bf16)
        for k, dst in enumerate(results):
            src = made.at[k, group] if k < 3 else made_low.at[group]
            copy = pltpu.make_async_copy(src, dst.at[group], sem_out.at[g, k])
            copy.start()
            push.append(copy)
    for copy in push + leave:
        copy.wait()


def update(token_total, small, large, passed):
    sds = jax.ShapeDtypeStruct
    blocks, gain = large[0].shape, small[1].shape
    vm, hbm = pl.BlockSpec(memory_space=pltpu.VMEM), pl.BlockSpec(memory_space=pl.ANY)
    return pl.pallas_call(
        functools.partial(update_kernel, token_total, len(passed)),
        out_shape=[sds(blocks, f32)] * 3
        + [sds(blocks, bf16)]
        + [sds(gain, f32)] * 3
        + [sds((1, 1), f32)]
        + [sds(v.shape, v.dtype) for v in passed],
        in_specs=[vm] * 4 + [hbm] * (len(large) + len(passed)),
        out_specs=[hbm] * 4 + [vm] * 4 + [hbm] * len(passed),
        scratch_shapes=[
            pltpu.VMEM((6, *blocks), f32),
            pltpu.VMEM((3, *blocks), f32),
            pltpu.VMEM(blocks, bf16),
            pltpu.SemaphoreType.DMA((2, 6)),
            pltpu.SemaphoreType.DMA((2, 4)),
            pltpu.SemaphoreType.DMA((2, len(passed))),
        ]
        + [pltpu.VMEM(v.shape, v.dtype) for v in passed],
        compiler_params=pltpu.CompilerParams(vmem_limit_bytes=56 * 2**20),
        name="update",
    )(*small, *large, *passed)


def on_device(
    tokens,
    cotangent,
    master,
    moment_one,
    moment_two,
    basis_left,
    basis_right,
    owner,
    gains,
    gain_moment_one,
    gain_moment_two,
):
    parts = lax.axis_size("mp")
    data_parts = lax.axis_size("dp")
    hm, fm = H // parts, FF // parts
    token_total = L * data_parts * parts
    row_tiles, cols, lows = D // BLK, (3 * hm + fm) // BLK, (hm + fm) // BLK
    number = jnp.arange(owner.shape[0], dtype=jnp.int32)
    ahead = (owner[None, :] < owner[:, None]) | ((owner[None, :] == owner[:, None]) & (number[None, :] < number[:, None]))
    block_rank = jnp.sum(ahead.astype(jnp.int32), axis=1)
    _, table = stack_places(hm, fm)
    table = jnp.asarray(table, jnp.int32)
    slot_place = jnp.sum(jnp.where(block_rank[None, :] == number[:, None], table[None, :], 0), axis=1)
    if data_parts == 8 and parts == 4:
        block_out, input_grad, owned, sums = compute(
            tokens, cotangent, gains, master=master[0], rank=block_rank, slot_place=slot_place
        )
    else:
        stored = lax.all_gather(master.astype(bf16), "dp", axis=1, tiled=True)
        stored = lax.all_gather(stored, "mp", axis=0, tiled=True)
        stack = stored[:, block_rank]
        upper = stack[:, : row_tiles * cols].reshape(parts, row_tiles, cols, BLK, BLK)
        upper = upper.transpose(0, 1, 3, 2, 4).reshape(parts, D, cols * BLK)
        lower = stack[:, row_tiles * cols :].reshape(parts, lows, row_tiles, BLK, BLK)
        lower = lower.transpose(0, 1, 3, 2, 4).reshape(parts, lows * BLK, D)
        weights = (upper[:, :, : 3 * hm], lower[:, :hm], upper[:, :, 3 * hm :], lower[:, hm:])
        first = ((lax.axis_index("dp") * parts + lax.axis_index("mp")) * L + 1).astype(f32)
        base = jnp.stack([first, jnp.asarray(token_total, f32)])
        block_out, input_grad, grads, sums = compute(tokens, cotangent, gains, weights=weights, base=base)
        owned = lax.psum_scatter(grads[:, slot_place].astype(f32), "dp", scatter_dimension=1, tiled=True)
        owned = lax.psum_scatter(owned, "mp", scatter_dimension=0, tiled=True)[0]
        sums = lax.psum(sums, ("dp", "mp"))
        count = master.shape[1]
        mine = lax.dynamic_slice_in_dim(slot_place, lax.axis_index("dp") * count, count)
        units, _ = stack_places(hm, fm)
        flags = ((mine >= units[UPDOWN][1] // 2) & (mine < units[GATE][0])).astype(f32)
        flags = jnp.pad(jnp.repeat(flags, BLK), (0, (8 - count) * BLK)).reshape(2, 4 * BLK)
        sums = jnp.concatenate([sums[:3], flags, sums[5:]])
    outs = update(
        token_total,
        (sums, gains, gain_moment_one, gain_moment_two),
        (owned, basis_left[0], basis_right[0], moment_one[0], moment_two[0], master[0]),
        (block_out, input_grad),
    )
    first_new, second_new, master_new, master_low, gain_first, gain_second, gains_new, forget_mean = outs[:8]
    block_out, input_grad = outs[8:]
    return (
        block_out,
        input_grad,
        first_new[None],
        second_new[None],
        master_new[None],
        master_low[None],
        gain_first,
        gain_second,
        gains_new,
        forget_mean[0, 0],
    )


def solution(mesh):
    rows, blocks = P(("dp", "mp"), None), P("mp", "dp", None, None)
    return jax.shard_map(
        on_device,
        mesh=mesh,
        in_specs=(rows, rows, blocks, blocks, blocks, blocks, blocks, P(), P(), P(), P()),
        out_specs=(rows, rows, blocks, blocks, blocks, blocks, P(), P(), P(), P()),
        check_vma=False,
    )
```

```python
import functools

import jax
import jax.numpy as jnp
from jax import lax
from jax.experimental import pallas as pl
from jax.experimental.pallas import tpu as pltpu
from jax.sharding import PartitionSpec as P

D = 512
H = 1024
FF = 2048
BLK = 128
STEP = 10
L = 1024

norm_eps = 1e-05
beta_one = 0.5
beta_two = 0.5
adam_eps = 1e-08
learn_rate = 0.02
gain_rate = 0.1
weight_decay = 0.1
highest = lax.Precision.HIGHEST

f32 = jnp.float32
bf16 = jnp.bfloat16
SUB = 8
J = L // SUB
R = 128


def dot(a, b, trans_b=False):
    dims = (((1,), (1,)), ((), ())) if trans_b else (((1,), (0,)), ((), ()))
    return lax.dot_general(a, b, dims, preferred_element_type=f32)


def recip(v):
    return pltpu.reciprocal(v, approx=True)


def sigmoid(v):
    return recip(1.0 + jnp.exp(-v))


def shift_down(v):
    rolled = pltpu.roll(v, 1, 0)
    row = lax.broadcasted_iota(jnp.int32, v.shape, 0)
    return jnp.where(row == 0, 0.0, rolled)


def shift_up(v):
    rolled = pltpu.roll(v, SUB - 1, 0)
    row = lax.broadcasted_iota(jnp.int32, v.shape, 0)
    return jnp.where(row == SUB - 1, 0.0, rolled)


def gelu_terms(x):
    a = jnp.abs(x)
    t = recip(1.0 + a * (0.3275911 * 0.7071067811865476))
    poly = t * (
        0.5 * 0.254829592
        + t
        * (
            0.5 * -0.284496736
            + t * (0.5 * 1.421413741 + t * (0.5 * -1.453152027 + t * (0.5 * 1.061405429)))
        )
    )
    e = jnp.exp(x * x * -0.5)
    tail = poly * e
    cdf = jnp.where(x < 0.0, tail, 1.0 - tail)
    return cdf, x * e * 0.3989422804014327


MESH = pl.DeviceIdType.MESH


class Copy:
    def __init__(self, net, make):
        self.net, self.make = net, make

    def start(self):
        self.net.open.append(self)
        self.make().start()
        return self

    def wait_recv(self):
        self.make().wait_recv()

    def wait_send(self):
        self.make().wait_send()


class Exchange:
    def __init__(self, send, recv):
        self.send, self.recv, self.known, self.used, self.open = send, recv, {}, 0, []

    def copy(self, parts, key=None):
        if key in self.known:
            return self.known[key]
        k = self.used
        self.used += 1

        def make():
            src, dst, device = parts()
            return pltpu.make_async_remote_copy(
                src_ref=src,
                dst_ref=dst,
                send_sem=self.send.at[k],
                recv_sem=self.recv.at[k],
                device_id=device,
                device_id_type=MESH,
            )

        copy = Copy(self, make)
        if key is not None:
            self.known[key] = copy
        return copy

    def start(self, parts):
        return self.copy(parts).start()

    def drain(self):
        for copy in self.open:
            copy.wait_send()
        self.open = []


class Gather:
    def __init__(self, net, fetch, master, slots, pool, weights, free):
        self.net, self.weights, self.free = net, weights, free
        self.held = [slots, *pool]
        d, m = lax.axis_index("dp"), lax.axis_index("mp")
        core, col, row = d % 2, (d // 2) % 2, d // 4
        self.me, self.m, self.side = d, m, core
        self.core = d + 1 - 2 * core
        self.plane = [d + 2 - 4 * col, d + 4 - 8 * row, d + 6 - 4 * col - 8 * row]
        self.order = [m, m + 1 - 2 * (m % 2), m + 2 - 4 * (m // 2), 3 - m]
        self.peers = [(e, m) for e in [self.core] + self.plane] + [(d, k) for k in self.order[1:]]
        barrier = pltpu.get_barrier_semaphore()
        for device in self.peers:
            pl.semaphore_signal(barrier, inc=1, device_id=device, device_id_type=MESH)
        self.n = master.shape[0]
        fetch.wait()
        for s in range(self.n):
            slots[d * self.n + s] = master[s].astype(bf16)
        pl.semaphore_wait(barrier, len(self.peers))

    def rows(self, i, e, first, count):
        return self.held[i].at[pl.ds(e * self.n + first, count)]

    def along(self, i, e):
        return self.net.copy(
            lambda: (self.rows(0, e, 0, self.n), self.rows(i, e, 0, self.n), (self.me, self.order[i])),
            ("along", i, e is self.me),
        )

    def within(self, key, i, e, first, count, to):
        return self.net.copy(
            lambda: (self.rows(i, e, first, count), self.rows(i, e, first, count), (to, self.m)), (key, i)
        )

    def first(self, i):
        (x, y, _), h = self.plane, self.n // 2
        if i == 1:
            jobs = ((0, self.n, x), (0, self.n, y))
        else:
            jobs = ((0, h, x), (h, h, y), (h, h, x), (0, h, y))
        return [self.within(("first", k), i, self.me, *job) for k, job in enumerate(jobs)]

    def last(self, i):
        x, y, z = self.plane
        if i == 1:
            return [self.along(1, z)]
        h = self.n // 2
        return [self.within("over y", i, x, 0, h, y), self.within("over x", i, y, h, h, x)]

    def inside(self, i):
        return [self.within(("inside", k), i, e, 0, self.n, self.core) for k, e in enumerate([self.me] + self.plane)]

    def along_start(self, i):
        self.along(i, self.me).start()

    def across_start(self):
        self.last(1)[0].start()

    def start(self, i):
        if i:
            self.along(i, self.me).wait_recv()
        for copy in self.first(i):
            copy.start()
        self.inside(i)[0].start()

    def forward(self, i):
        if i == 1:
            return
        for came, copy in zip(self.first(i), self.last(i)):
            came.wait_recv()
            copy.start()

    def pair(self, i):
        for came, copy in zip(self.first(i)[-2:], self.inside(i)[1:3]):
            came.wait_recv()
            copy.start()
        for came in self.last(i):
            came.wait_recv()
        self.inside(i)[3].start()

    def ready(self, i):
        for copy in self.inside(i):
            copy.wait_recv()

    def place(self, i, rank):
        wg, wo, wu, wd = self.weights
        row_tiles, gates = D // BLK, wg.shape[2] // BLK
        cols, outs = gates + wu.shape[2] // BLK, wo.shape[1] // BLK
        for b in range(row_tiles * cols + (wo.shape[1] + wd.shape[1]) // BLK * row_tiles):
            if b < row_tiles * cols:
                r, c = b // cols, b % cols
                ref = wg if c < gates else wu
                c -= 0 if c < gates else gates
            else:
                r, c = (b - row_tiles * cols) // row_tiles, (b - row_tiles * cols) % row_tiles
                ref = wo if r < outs else wd
                r -= 0 if r < outs else outs
            block = self.held[i][rank[0, b]]
            ref[self.order[i], r * BLK : (r + 1) * BLK, c * BLK : (c + 1) * BLK] = block

    def done(self):
        for device in self.peers:
            pl.semaphore_signal(self.free, inc=1, device_id=device, device_id_type=MESH)

    def all_done(self):
        pl.semaphore_wait(self.free, len(self.peers))


def stack_places(hm, fm):
    row_tiles, gates, ups, outs = D // BLK, 3 * hm // BLK, fm // BLK, hm // BLK
    cols = gates + ups
    first_down = row_tiles * ups
    first_out = 2 * first_down
    first_gate = first_out + row_tiles * outs
    table = []
    for b in range(row_tiles * (cols + outs + ups)):
        if b < row_tiles * cols:
            r, c = b // cols, b % cols
            table.append(first_gate + r * gates + c if c < gates else r * ups + c - gates)
        else:
            k = b - row_tiles * cols
            table.append(first_out + k if k < row_tiles * outs else first_down + k - row_tiles * outs)
    return ((0, first_out), (first_out, row_tiles * outs), (first_gate, row_tiles * gates)), table


UPDOWN, OUT, GATE = range(3)


class Reduce:
    def __init__(self, net, gather, grads, units, pool):
        self.net, self.g, self.grads, self.units, self.pool = net, gather, grads, units, pool
        self.half = grads.shape[1] // 2
        self.eighth = grads.shape[1] // 8

    def place(self, e):
        return (e % 2) * 4 + e // 2

    def inside(self, unit, i):
        g, (first, count) = self.g, self.units[unit]
        return self.net.copy(
            lambda: (
                self.grads.at[g.order[i], pl.ds(first + (1 - g.side) * (count // 2), count // 2)],
                self.pool[i - 1].at[pl.ds(first // 2, count // 2)],
                (g.core, g.m),
            ),
            ("chip", unit, i),
        )

    def chip(self, unit, i):
        self.inside(unit, i).start()

    def spot(self, unit, i, slot, first, count):
        base, total = self.units[unit]
        return self.pool[i - 1].at[pl.ds(self.half + slot * self.eighth + base // 8 + first, count)]

    def parts(self, unit, i):
        n = self.units[unit][1] // 8
        if i == 1:
            return ((0, n),)
        h = (n + i % 2) // 2 if n % 2 else n // 2
        return (0, h), (h, n - h)

    def share(self, unit, i, e, first, count):
        base, total = self.units[unit]
        return self.grads.at[self.g.order[i], pl.ds(base + self.place(e) * (total // 8) + first, count)]

    def over(self, unit, i, slot, part):
        x, y, z = self.g.plane
        e = (z, x, y)[slot]
        to = (x if part == self.parts(unit, i)[0] else y, x, y)[slot]
        return self.net.copy(
            lambda: (self.share(unit, i, e, *part), self.spot(unit, i, slot, *part), (to, self.g.m)),
            ("over", unit, i, slot, part),
        )

    def send(self, unit, i, slot, part):
        if part[1]:
            self.over(unit, i, slot, part).start()

    def take(self, unit, i, slot, part):
        self.over(unit, i, slot, part).wait_recv()
        return self.spot(unit, i, slot, *part)[...].astype(f32)

    def model_copy(self, unit, i):
        n = self.units[unit][1] // 8
        return self.net.copy(
            lambda: (self.share(unit, i, self.g.me, 0, n), self.spot(unit, i, 3, 0, n), (self.g.me, self.g.order[i])),
            ("model", unit, i),
        )

    def aside(self, unit):
        part = (0, self.units[unit][1] // 8)
        return self.net.copy(
            lambda: (
                self.share(unit, 1, self.g.plane[2], *part),
                self.spot(unit, 1, 0, *part),
                (self.g.me, self.g.order[1]),
            ),
            ("aside", unit),
        )

    def plane(self, unit, i):
        g, (first, count) = self.g, self.units[unit]
        x, y, z = g.plane
        self.inside(unit, i).wait_recv()
        m = g.order[i]
        start, came = first + g.side * (count // 2), self.pool[i - 1]

        @pl.loop(0, count // 2)
        def _(b):
            total = self.grads[m, start + b].astype(f32) + came[first // 2 + b].astype(f32)
            self.grads[m, start + b] = total.astype(bf16)

        if i == 1:
            (whole,) = self.parts(unit, i)
            self.send(unit, i, 1, whole)
            self.send(unit, i, 2, whole)
            self.aside(unit).start()
            return
        one, two = self.parts(unit, i)
        self.send(unit, i, 0, one)
        self.send(unit, i, 0, two)
        self.send(unit, i, 1, one)
        self.send(unit, i, 2, two)

    def turn(self, unit, i):
        if i == 1:
            return
        x, y, _ = self.g.plane
        for part, slot, e in zip(self.parts(unit, i), (2, 1), (y, x)):
            if part[1]:
                ref = self.share(unit, i, e, *part)
                ref[...] = (ref[...].astype(f32) + self.take(unit, i, 0, part)).astype(bf16)
                self.send(unit, i, slot, part)

    def model(self, unit, i):
        g, (first, count) = self.g, self.units[unit]
        n = count // 8
        for part in self.parts(unit, i):
            if part[1]:
                ref = self.share(unit, i, g.me, *part)
                total = ref[...].astype(f32) + self.take(unit, i, 1, part) + self.take(unit, i, 2, part)
                ref[...] = total.astype(bf16)
        self.model_copy(unit, i).start()

    def own(self, unit):
        g, (first, count) = self.g, self.units[unit]
        n = count // 8
        rows = pl.ds(first + self.place(g.me) * n, n)
        total = self.grads[g.m, rows].astype(f32)
        for i in (1, 2, 3):
            self.model_copy(unit, i).wait_recv()
            total += self.pool[i - 1][pl.ds(self.half + 3 * self.eighth + first // 8, n)].astype(f32)
        self.grads[g.m, rows] = total.astype(bf16)
        self.aside(unit).wait_recv()
        rows = pl.ds(first + self.place(g.plane[2]) * n, n)
        total = self.grads[g.m, rows].astype(f32) + self.spot(unit, 1, 0, 0, n)[...].astype(f32)
        self.grads[g.m, rows] = total.astype(bf16)

    def into_slots(self, out, slot_place, e):
        n = self.eighth
        for k in range(n):
            out[self.place(e) * n + k] = self.grads[self.g.m, slot_place[0, e * n + k]]

    def slots_chip(self, out, slot_place, pair):
        g, n = self.g, self.eighth
        self.last = []
        targets = (g.plane[2], g.plane[0], g.plane[1], g.me)
        for e in targets:
            other = e + 1 - 2 * g.side
            self.into_slots(out, slot_place, other)
            self.last.append(
                self.net.start(
                    lambda e=e, other=other: (
                        out.at[pl.ds(self.place(other) * n, n)],
                        pair.at[pl.ds((e // 2) * n, n)],
                        (g.core, g.m),
                    )
                )
            )
        for e in targets:
            self.into_slots(out, slot_place, e)

    def slots_plane(self, out, pair, far):
        g, n = self.g, out.shape[0] // 8
        h = n // 2
        x, y, z = g.plane
        wait = dict(zip("zxyo", self.last))

        def mine(e, first, count):
            return pl.ds((g.side * 4 + e // 2) * n + first, count)

        def join(e):
            rows = mine(e, 0, n)
            out[rows] = (out[rows].astype(f32) + pair[pl.ds((e // 2) * n, n)].astype(f32)).astype(bf16)

        def send(e, first, slot, to):
            return self.net.start(lambda: (out.at[mine(e, first, h)], far.at[slot], (to, g.m)))

        wait["z"].wait_recv()
        join(z)
        over_x = send(z, 0, 0, x)
        over_y = send(z, h, 1, y)
        wait["x"].wait_recv()
        join(x)
        self.ends = [send(x, 0, 2, x)]
        wait["y"].wait_recv()
        join(y)
        self.ends.append(send(y, h, 3, y))
        over_x.wait_recv()
        rows = mine(y, 0, h)
        out[rows] = (out[rows].astype(f32) + far[0].astype(f32)).astype(bf16)
        self.ends.append(send(y, 0, 4, y))
        over_y.wait_recv()
        rows = mine(x, h, h)
        out[rows] = (out[rows].astype(f32) + far[1].astype(f32)).astype(bf16)
        self.ends.append(send(x, h, 5, x))
        wait["o"].wait_recv()

    def slots_end(self, out, pair, far, owned):
        g, n = self.g, out.shape[0] // 8
        h = n // 2
        for copy in self.ends:
            copy.wait_recv()
        for first, slots in ((0, (2, 4)), (h, (3, 5))):
            total = out[pl.ds((g.side * 4 + g.me // 2) * n + first, h)].astype(f32)
            total += pair[pl.ds((g.me // 2) * n + first, h)].astype(f32)
            for k in slots:
                total += far[k].astype(f32)
            owned[first : first + h] = total


class SmallSum:
    def __init__(self, net, gather, values, along, across, inside):
        self.net, self.g, self.values = net, gather, values
        self.slots = (along, across, inside)
        self.peers = (
            [(gather.me, k) for k in gather.order[1:]],
            [(e, gather.m) for e in gather.plane],
            [(gather.core, gather.m)],
        )
        self.mine = (gather.m, gather.me // 2, gather.side)
        self.open = []

    def send(self, stage):
        slot = self.slots[stage]
        slot[self.mine[stage]] = self.values[...]
        ref = slot.at[self.mine[stage]]
        self.open = [self.net.start(lambda peer=peer: (ref, ref, peer)) for peer in self.peers[stage]]

    def add(self, stage):
        for copy in self.open:
            copy.wait_recv()
        slot = self.slots[stage]
        total = slot[0]
        for k in range(1, slot.shape[0]):
            total += slot[k]
        self.values[...] = total


def number_blocks(owner, table, vector, rank, slot_place, sem):
    lane = lax.broadcasted_iota(jnp.int32, vector.shape, 1)
    count = owner.shape[0]
    owners = jnp.zeros_like(lane)
    for b in range(count):
        owners = jnp.where(lane == b, owner[b], owners)
    ranks = jnp.zeros_like(lane)
    for b in range(count):
        ahead = (owner[b] < owners) | ((owner[b] == owners) & (lane > b))
        ranks += jnp.where(ahead, 1, 0)
    vector[...] = ranks
    copy = pltpu.make_async_copy(vector, rank, sem)
    copy.start()
    copy.wait()
    places = jnp.zeros_like(lane)
    for b in range(count):
        places = jnp.where(lane == rank[0, b], table[b], places)
    vector[...] = places
    copy = pltpu.make_async_copy(vector, slot_place, sem)
    copy.start()
    copy.wait()


def compute_kernel(linked, *refs):
    if linked:
        tokens, cotangent, master, owner, gains = refs[:5]
        block_out, input_grad, owned, small = refs[5:9]
        wg, wo, wu, wd, grads, slots, *pool, pair, far, sum_a, sum_b, sum_c, vector, rank, slot_place, send, recv, free = refs[9:29]
        scratch = refs[29:]
    else:
        tokens, cotangent, base, wg, wo, wu, wd, gains = refs[:8]
        block_out, input_grad, grads, small = refs[8:12]
        scratch = refs[12:]
    (n1, n1t, cot, cott, n2, n2t, forget, admit, cand, state, scan, acc_a, acc_b, mixed, mid, kept, fills, tally, local) = scratch
    dml, dmlt = n2, n2t
    parts, _, hm3 = wg.shape
    hm = hm3 // 3
    fm = wu.shape[2]
    units, table = stack_places(hm, fm)
    act, dup, dpre = mid.at[:, :fm], mid.at[:, fm:], mid.at[:, : 3 * hm]
    gain_one = gains[0:1, :]
    gain_two = gains[1:2, :]

    if linked:
        fetch_master = pltpu.make_async_copy(master, owned, local.at[2])
        fetch_master.start()
    fetch_cot = pltpu.make_async_copy(cotangent, cot, local.at[0])
    fetch_tok = pltpu.make_async_copy(tokens, n1, local.at[1])
    fetch_tok.start()
    fetch_cot.start()

    column_halves = (slice(0, D // 2), slice(D // 2, D))

    def stack(m, first, wide, left, value):
        for r in range(value.shape[0] // BLK):
            for c in range(value.shape[1] // BLK):
                grads[m, first + r * wide + left + c] = value[r * BLK : (r + 1) * BLK, c * BLK : (c + 1) * BLK].astype(bf16)

    def stack_turned(m, first, value):
        high = value.shape[0] // BLK
        for r in range(high):
            for c in range(value.shape[1] // BLK):
                grads[m, first + c * high + r] = value[r * BLK : (r + 1) * BLK, c * BLK : (c + 1) * BLK].astype(bf16)

    def permute_in(src, dst):
        for k in range(D // BLK):
            scan[k] = src[:, k * BLK : (k + 1) * BLK].astype(f32)

        @pl.loop(0, J // 2, unroll=4)
        def _(j):
            for k in range(D // BLK):
                lo = scan[k, pl.ds(2 * j, SUB, stride=J), :]
                hi = scan[k, pl.ds(2 * j + 1, SUB, stride=J), :]
                dst[pl.ds(pl.multiple_of(16 * j, 16), 16), k * BLK : (k + 1) * BLK] = jnp.concatenate([lo, hi], 0).astype(bf16)

    def permute_out(src, dst):
        @pl.loop(0, J, unroll=4)
        def _(j):
            rows = pl.ds(pl.multiple_of(j * SUB, SUB), SUB)
            for k in range(D // BLK):
                scan[k, pl.ds(j, SUB, stride=J), :] = src[rows, k * BLK : (k + 1) * BLK]

        for k in range(D // BLK):
            dst[:, k * BLK : (k + 1) * BLK] = scan[k].astype(dst.dtype)

    def put(first, rows, value):
        for k in range(hm // BLK):
            scan[first + k, rows, :] = value[:, k * BLK : (k + 1) * BLK]

    def take(first, rows):
        return jnp.concatenate([scan[first + k, rows, :] for k in range(hm // BLK)], 1)

    half = hm // BLK

    def spread(v):
        return jnp.broadcast_to(v[None], (R // SUB, SUB, hm)).reshape(R, hm)


    if linked:
        net = Exchange(send, recv)
        gather = Gather(net, fetch_master, owned, slots, pool, (wg, wo, wu, wd), free)
        gather.start(0)
        gather.along_start(1)
        gather.along_start(2)
        reduce = Reduce(net, gather, grads, units, pool)

    def of_turn(t):
        if not linked:
            return t
        high, low = gather.m // 2, gather.m % 2
        t_high, t_low = t // 2, t % 2
        return 2 * (high + t_high - 2 * high * t_high) + low + t_low - 2 * low * t_low

    fetch_tok.wait()
    permute_in(n1, n1)
    mixed[...] = n1[...].astype(f32)

    @pl.loop(0, L // R)
    def _(i):
        rows = pl.ds(pl.multiple_of(i * R, R), R)
        x = mixed[rows, :]
        r = lax.rsqrt(jnp.mean(x * x, axis=-1, keepdims=True) + norm_eps)
        n1[rows, :] = (x * r * gain_one).astype(bf16)

    n1t[...] = n1[...].T

    if linked:
        gather.forward(0)
        gather.along_start(3)
        number_blocks(owner, table, vector, rank, slot_place, local.at[2])
    fetch_cot.wait()
    permute_in(cot, cot)
    if linked:
        gather.start(1)
        gather.pair(0)
        gather.across_start()
        gather.start(2)
    cott[...] = cot[...].T

    fills[0] = jnp.zeros((SUB, hm), f32)
    fills[1] = jnp.ones((SUB, hm), f32)
    tally[0] = fills[0]
    tally[1] = fills[0]

    @pl.loop(0, parts)
    def _(turn):
        m = of_turn(turn)
        if linked:
            for k in range(parts):

                @pl.when(turn == k)
                def _():
                    if k:
                        gather.pair(k)
                    gather.ready(k)
                    gather.place(k, rank)

        forget[m] = dot(n1[...], wg[m, :, :hm])
        admit[m] = dot(n1[...], wg[m, :, hm : 2 * hm])
        cand[m] = dot(n1[...], wg[m, :, 2 * hm :])

        if linked:
            for k in range(parts - 1):

                @pl.when(turn == k)
                def _():
                    if k == 0:
                        gather.forward(2)
                    if k == 1:
                        gather.start(3)
                    if k == 2:
                        gather.forward(3)

        @pl.loop(0, L // R)
        def _(i):
            rows = pl.ds(pl.multiple_of(i * R, R), R)
            f = sigmoid(forget[m, rows, :])
            a = sigmoid(admit[m, rows, :])
            inv = recip(f + a)
            forget[m, rows, :] = f
            admit[m, rows, :] = a
            kept[rows, :] = f * inv
            put(0, rows, a * inv * cand[m, rows, :])

        def step(j, carry):
            s, p, k_sum, kj_sum = carry
            rows = pl.ds(pl.multiple_of(j * SUB, SUB), SUB)
            keep = kept[rows, :]
            s = keep * s + take(0, rows)
            p = keep * p
            put(0, rows, s)
            put(half, rows, p)
            return s, p, k_sum + keep, kj_sum + keep * j.astype(f32)

        s, p, k_sum, kj_sum = lax.fori_loop(0, J, step, (fills[0], fills[1], fills[0], fills[0]), unroll=16)
        tally[0] += k_sum
        tally[1] += kj_sum
        enter = fills[0]
        for _ in range(SUB - 1):
            enter = shift_down(s + p * enter)

        @pl.loop(0, L // R)
        def _(i):
            rows = pl.ds(pl.multiple_of(i * R, R), R)
            state[m, pl.ds(pl.multiple_of(i * R + SUB, SUB), R), :] = take(0, rows) + take(half, rows) * spread(enter)

        state[m, :SUB, :] = shift_down(state[m, L:, :])
        for cols in column_halves:
            mixed[:, cols] += dot(state[m, SUB:, :].astype(bf16), wo[m, :, cols])

    if linked:
        net.drain()
        gather.done()

    @pl.loop(0, L // R)
    def _(i):
        rows = pl.ds(pl.multiple_of(i * R, R), R)
        x = mixed[rows, :]
        r = lax.rsqrt(jnp.mean(x * x, axis=-1, keepdims=True) + norm_eps)
        n2[rows, :] = (x * r * gain_two).astype(bf16)
        acc_a[rows, :] = x
        acc_b[rows, :] = jnp.zeros_like(x)

    n2t[...] = n2[...].T

    @pl.loop(0, parts)
    def _(turn):
        m = of_turn(turn)
        for first in range(0, fm, fm // 2):
            units_of = slice(first, first + fm // 2)
            up = dot(n2[...], wu[m, :, units_of])
            da = dot(cot[...], wd[m, units_of, :], True)
            cdf, xpdf = gelu_terms(up)
            act[:, units_of] = (up * cdf).astype(bf16)
            dup[:, units_of] = (da * (cdf + xpdf)).astype(bf16)
        for cols in column_halves:
            acc_a[:, cols] += dot(act[...], wd[m, :, cols])
        for cols in column_halves:
            acc_b[:, cols] += dot(dup[...], wu[m, cols, :], True)
        if linked:
            for k in (2, 3):

                @pl.when(turn == k)
                def _():
                    reduce.plane(UPDOWN, k - 1)
                    if k == 3:
                        reduce.model(UPDOWN, 1)

        for c in range(0, fm, fm // 2):
            part = slice(c, c + fm // 2)
            stack(m, 0, fm // BLK, c // BLK, dot(n2t[...], dup[:, part]))
        for c in range(0, fm, fm // 2):
            part = slice(c, c + fm // 2)
            stack_turned(m, units[UPDOWN][1] // 2 + c // BLK * (D // BLK), dot(cott[...], act[:, part]))
        if linked:
            for k in (1, 2, 3):

                @pl.when(turn == k)
                def _():
                    if k == 1:
                        gather.all_done()
                    reduce.chip(UPDOWN, k)

    gain_sum_two = jnp.zeros((1, D), f32)

    def back_two(i, total):
        rows = pl.ds(pl.multiple_of(i * R, R), R)
        x = mixed[rows, :]
        r = lax.rsqrt(jnp.mean(x * x, axis=-1, keepdims=True) + norm_eps)
        dn = acc_b[rows, :]
        q = dn * gain_two
        d = cot[rows, :].astype(f32) + r * q - r * r * r * x * jnp.mean(q * x, axis=-1, keepdims=True)
        mixed[rows, :] = d
        dml[rows, :] = d.astype(bf16)
        acc_b[rows, :] = jnp.zeros_like(d)
        return total + jnp.sum(dn * x * r, axis=0, keepdims=True)

    gain_sum_two = lax.fori_loop(0, L // R, back_two, gain_sum_two)
    if linked:
        reduce.plane(UPDOWN, 3)
    dmlt[...] = dml[...].T
    fetch_tok = pltpu.make_async_copy(tokens, cot, local.at[1])
    fetch_tok.start()

    @pl.loop(0, parts)
    def _(m):
        stack_turned(m, units[OUT][0], dot(dmlt[...], state[m, SUB:, :].astype(bf16)))

    if linked:
        for i in (3, 2, 1):
            reduce.chip(OUT, i)

    @pl.loop(0, parts)
    def _(back_turn):
        turn = parts - 1 - back_turn
        m = of_turn(turn)
        put(0, slice(None), dot(dml[...], wo[m], True))

        @pl.loop(0, L // R)
        def _(i):
            rows = pl.ds(pl.multiple_of(i * R, R), R)
            f = forget[m, rows, :]
            kept[rows, :] = f * recip(f + admit[m, rows, :])

        def step(k, carry):
            u, p, keep_next = carry
            j = J - 1 - k
            rows = pl.ds(pl.multiple_of(j * SUB, SUB), SUB)
            u = take(0, rows) + keep_next * u
            p = keep_next * p
            put(0, rows, u)
            put(half, rows, p)
            return u, p, kept[rows, :]

        u, p, keep_first = lax.fori_loop(0, J, step, (fills[0], fills[1], fills[1]), unroll=16)
        enter = fills[0]
        for _ in range(SUB - 1):
            enter = shift_up(keep_first * (u + p * enter))

        if linked:

            @pl.when(turn == 3)
            def _():
                reduce.turn(UPDOWN, 2)
                for i in (3, 2, 1):
                    reduce.plane(OUT, i)

            @pl.when(turn == 0)
            def _():
                reduce.plane(GATE, 1)

        @pl.loop(0, L // R)
        def _(i):
            rows = pl.ds(pl.multiple_of(i * R, R), R)
            carried = take(0, rows) + take(half, rows) * spread(enter)
            f = forget[m, rows, :]
            a = admit[m, rows, :]
            adm = a * recip(f + a)
            g = carried * (state[m, rows, :] - cand[m, rows, :]) * (kept[rows, :] * adm)
            dpre[rows, :hm] = (g * (1.0 - f)).astype(bf16)
            dpre[rows, hm : 2 * hm] = (g * (a - 1.0)).astype(bf16)
            dpre[rows, 2 * hm :] = (carried * adm).astype(bf16)

        if linked:

            @pl.when(turn == 3)
            def _():
                reduce.turn(UPDOWN, 3)

            @pl.when(turn == 2)
            def _():
                reduce.plane(GATE, 3)
                for i in (3, 2):
                    reduce.turn(OUT, i)
                reduce.model(UPDOWN, 3)
                reduce.model(UPDOWN, 2)

            @pl.when(turn == 1)
            def _():
                reduce.plane(GATE, 2)
                for i in (1, 3, 2):
                    reduce.model(OUT, i)

            @pl.when(turn == 0)
            def _():
                reduce.turn(GATE, 2)
                reduce.model(GATE, 3)

        for k in range(3):
            stack(m, units[GATE][0], 3 * hm // BLK, k * hm // BLK, dot(n1t[...], dpre[:, k * hm : (k + 1) * hm]))
        if linked:
            for k in (3, 2, 1):

                @pl.when(turn == k)
                def _():
                    reduce.chip(GATE, k)
                    if k == 1:
                        reduce.turn(GATE, 3)

        for cols in column_halves:
            acc_b[:, cols] += dot(dpre[...], wg[m, cols, :], True)

    if linked:
        reduce.own(UPDOWN)
        reduce.own(OUT)

    fetch_tok.wait()
    permute_in(cot, cot)
    if linked:
        reduce.model(GATE, 1)
        reduce.model(GATE, 2)

    def back_one(i, total):
        rows = pl.ds(pl.multiple_of(i * R, R), R)
        x = cot[rows, :].astype(f32)
        r = lax.rsqrt(jnp.mean(x * x, axis=-1, keepdims=True) + norm_eps)
        dn = acc_b[rows, :]
        q = dn * gain_one
        mixed[rows, :] += r * q - r * r * r * x * jnp.mean(q * x, axis=-1, keepdims=True)
        return total + jnp.sum(dn * x * r, axis=0, keepdims=True)

    gain_sum_one = lax.fori_loop(0, L // R, back_one, jnp.zeros((1, D), f32))

    permute_out(acc_a, n1)
    push_out = pltpu.make_async_copy(n1, block_out, local.at[0])
    push_out.start()

    place = lax.broadcasted_iota(jnp.int32, (SUB, hm), 0).astype(f32) * float(J)
    if linked:
        first = ((gather.me * parts + gather.m) * L + 1).astype(f32)
        token_total = float(L * parts * lax.axis_size("dp"))
    else:
        first = base[0]
        token_total = base[1]
    forget_sum = jnp.sum(tally[1] + tally[0] * (place + first), axis=0, keepdims=True) / token_total
    small[...] = jnp.zeros_like(small)
    small[0:1, :] = gain_sum_one
    small[1:2, :] = gain_sum_two
    small[2:3, :hm] = forget_sum
    if linked:
        flat = units[UPDOWN][1] // 2, units[GATE][0]
        count = owned.shape[0]
        flags = []
        for k in range(count):
            spot = slot_place[0, gather.me * count + k]
            flags.append(jnp.where((spot >= flat[0]) & (spot < flat[1]), 1.0, 0.0).astype(f32))

    if linked:
        tiny = SmallSum(net, gather, small, sum_a, sum_b, sum_c)
        tiny.send(0)
        reduce.own(GATE)
        reduce.slots_chip(slots, slot_place, pair)
        tiny.add(0)
        tiny.send(1)
        reduce.slots_plane(slots, pair, far)

    permute_out(mixed, acc_a)
    push_grad = pltpu.make_async_copy(acc_a, input_grad, local.at[2])
    push_grad.start()

    if linked:
        tiny.add(1)
        tiny.send(2)
        reduce.slots_end(slots, pair, far, owned)
        tiny.add(2)
        for k, flag in enumerate(flags):
            small[3 + k // 4 : 4 + k // 4, (k % 4) * BLK : (k % 4 + 1) * BLK] = jnp.full((1, BLK), flag, f32)
        net.drain()
    push_out.wait()
    push_grad.wait()


def compute(tokens, cotangent, gains, weights=None, base=None, master=None, owner=None):
    linked = weights is None
    parts = lax.axis_size("mp")
    hm, fm = H // parts, FF // parts
    stacked = (parts, D * (4 * hm + 2 * fm) // BLK**2, BLK, BLK)
    sds = jax.ShapeDtypeStruct
    vm, sm, hbm = (pl.BlockSpec(memory_space=k) for k in (pltpu.VMEM, pltpu.SMEM, pl.ANY))
    if linked:
        n = owner.shape[0]
        args = (tokens, cotangent, master, owner, gains)
        in_specs = [hbm, hbm, hbm, sm, vm]
        middle = sds((n // 8, BLK, BLK), f32)
        extra = [
            pltpu.VMEM((parts, D, 3 * hm), bf16),
            pltpu.VMEM((parts, hm, D), bf16),
            pltpu.VMEM((parts, D, fm), bf16),
            pltpu.VMEM((parts, fm, D), bf16),
            pltpu.VMEM(stacked, bf16),
            pltpu.VMEM((n, BLK, BLK), bf16),
            *[pltpu.VMEM((n, BLK, BLK), bf16) for _ in range(parts - 1)],
            pltpu.VMEM((n // 2, BLK, BLK), bf16),
            pltpu.VMEM((6, n // 16, BLK, BLK), bf16),
            pltpu.VMEM((parts, 8, D), f32),
            pltpu.VMEM((4, 8, D), f32),
            pltpu.VMEM((2, 8, D), f32),
            pltpu.VMEM((8, BLK), jnp.int32),
            pltpu.SMEM((8, BLK), jnp.int32),
            pltpu.SMEM((8, BLK), jnp.int32),
            pltpu.SemaphoreType.DMA((128,)),
            pltpu.SemaphoreType.DMA((128,)),
            pltpu.SemaphoreType.REGULAR,
        ]
        params = dict(collective_id=0, has_side_effects=True)
    else:
        args = (tokens, cotangent, base, *weights, gains)
        in_specs = [hbm, hbm, sm] + [vm] * 5
        middle = sds(stacked, bf16)
        extra = []
        params = {}
    return pl.pallas_call(
        functools.partial(compute_kernel, linked),
        out_shape=(sds((L, D), bf16), sds((L, D), f32), middle, sds((8, D), f32)),
        in_specs=in_specs,
        out_specs=[hbm, hbm, vm, vm],
        scratch_shapes=extra
        + [pltpu.VMEM(shape, bf16) for shape in ((L, D), (D, L)) * 3]
        + [pltpu.VMEM((parts, L, hm), f32)] * 3
        + [pltpu.VMEM((parts, L + SUB, hm), f32)]
        + [pltpu.VMEM((2 * hm // BLK, L, BLK), f32)]
        + [pltpu.VMEM((L, D), f32)] * 3
        + [
            pltpu.VMEM((L, 2 * fm), bf16),
            pltpu.VMEM((L, hm), f32),
            pltpu.VMEM((2, SUB, hm), f32),
            pltpu.VMEM((2, SUB, hm), f32),
            pltpu.SemaphoreType.DMA((3,)),
        ],
        compiler_params=pltpu.CompilerParams(vmem_limit_bytes=64 * 2**20 - 2**16, **params),
        name="block",
    )(*args)


def adam_update(first_old, second_old, gradient):
    first_new = beta_one * first_old + (1.0 - beta_one) * gradient
    second_new = beta_two * second_old + (1.0 - beta_two) * gradient * gradient
    first_hat = first_new / (1.0 - beta_one**STEP)
    second_hat = second_new / (1.0 - beta_two**STEP)
    return (first_new, second_new, first_hat / (jnp.sqrt(second_hat) + adam_eps))


def fine_dot(a, b, trans_b=False):
    a_high, b_high = a.astype(bf16), b.astype(bf16)
    a_low, b_low = (a - a_high.astype(f32)).astype(bf16), (b - b_high.astype(f32)).astype(bf16)
    return dot(a_high, b_high, trans_b) + (dot(a_high, b_low, trans_b) + dot(a_low, b_high, trans_b))


def update_kernel(token_total, passed, sums, gains, gain_moment_one, gain_moment_two, *refs):
    sources, refs = refs[:6], refs[6:]
    given, refs = refs[:passed], refs[passed:]
    results, refs = refs[:4], refs[4:]
    gain_first, gain_second, gains_new, forget_mean = refs[:4]
    copied, refs = refs[4 : 4 + passed], refs[4 + passed :]
    held, made, made_low, sem_in, sem_out, sem_pass = refs[:6]
    passage = refs[6:]
    count = held.shape[1]
    step = max(count // 2, 1)
    groups = [slice(first, first + step) for first in range(0, count, step)]
    enter = [pltpu.make_async_copy(src, via, sem_pass.at[0, k]) for k, (src, via) in enumerate(zip(given, passage))]
    leave = [pltpu.make_async_copy(via, dst, sem_pass.at[1, k]) for k, (via, dst) in enumerate(zip(passage, copied))]
    fetch = [
        [pltpu.make_async_copy(src.at[group], held.at[k, group], sem_in.at[g, k]) for k, src in enumerate(sources)]
        for g, group in enumerate(groups)
    ]
    for copy in fetch[0]:
        copy.start()
    for copy in enter:
        copy.start()
    for row in fetch[1:]:
        for copy in row:
            copy.start()
    first, second, direction = adam_update(gain_moment_one[...], gain_moment_two[...], sums[0:2, :])
    gain_first[...] = first
    gain_second[...] = second
    gains_new[...] = gains[...] - gain_rate * direction
    forget_mean[...] = jnp.sum(sums[2:3, :], axis=1, keepdims=True) * (1.0 / (H * (token_total + 1) / 2.0))
    push = []
    for g, group in enumerate(groups):
        blocks = range(group.start, group.stop)
        for copy in fetch[g]:
            copy.wait()
        if g == len(groups) - 1:
            for come, go in zip(enter, leave):
                come.wait()
                go.start()
        grads = []
        for s in blocks:
            grad = held[0, s]
            flag = sums[3 + s // 4 : 4 + s // 4, (s % 4) * BLK : (s % 4 + 1) * BLK]
            grads.append(jnp.where(flag > 0.5, grad.T, grad))
        values = [fine_dot(held[1, s].T, grad) for s, grad in zip(blocks, grads)]
        values = [fine_dot(value, held[2, s]) for s, value in zip(blocks, values)]
        for k, s in enumerate(blocks):
            first, second, values[k] = adam_update(held[3, s], held[4, s], values[k])
            made[0, s] = first
            made[1, s] = second
        values = [fine_dot(held[1, s], value) for s, value in zip(blocks, values)]
        values = [fine_dot(value, held[2, s], True) for s, value in zip(blocks, values)]
        for s, value in zip(blocks, values):
            fresh = held[5, s] - learn_rate * (value + weight_decay * held[5, s])
            made[2, s] = fresh
            made_low[s] = fresh.astype(bf16)
        for k, dst in enumerate(results):
            src = made.at[k, group] if k < 3 else made_low.at[group]
            copy = pltpu.make_async_copy(src, dst.at[group], sem_out.at[g, k])
            copy.start()
            push.append(copy)
    for copy in push + leave:
        copy.wait()


def update(token_total, small, large, passed):
    sds = jax.ShapeDtypeStruct
    blocks, gain = large[0].shape, small[1].shape
    vm, hbm = pl.BlockSpec(memory_space=pltpu.VMEM), pl.BlockSpec(memory_space=pl.ANY)
    return pl.pallas_call(
        functools.partial(update_kernel, token_total, len(passed)),
        out_shape=[sds(blocks, f32)] * 3
        + [sds(blocks, bf16)]
        + [sds(gain, f32)] * 3
        + [sds((1, 1), f32)]
        + [sds(v.shape, v.dtype) for v in passed],
        in_specs=[vm] * 4 + [hbm] * (len(large) + len(passed)),
        out_specs=[hbm] * 4 + [vm] * 4 + [hbm] * len(passed),
        scratch_shapes=[
            pltpu.VMEM((6, *blocks), f32),
            pltpu.VMEM((3, *blocks), f32),
            pltpu.VMEM(blocks, bf16),
            pltpu.SemaphoreType.DMA((2, 6)),
            pltpu.SemaphoreType.DMA((2, 4)),
            pltpu.SemaphoreType.DMA((2, len(passed))),
        ]
        + [pltpu.VMEM(v.shape, v.dtype) for v in passed],
        compiler_params=pltpu.CompilerParams(vmem_limit_bytes=56 * 2**20),
        name="update",
    )(*small, *large, *passed)


def on_device(
    tokens,
    cotangent,
    master,
    moment_one,
    moment_two,
    basis_left,
    basis_right,
    owner,
    gains,
    gain_moment_one,
    gain_moment_two,
):
    parts = lax.axis_size("mp")
    data_parts = lax.axis_size("dp")
    hm, fm = H // parts, FF // parts
    token_total = L * data_parts * parts
    row_tiles, cols, lows = D // BLK, (3 * hm + fm) // BLK, (hm + fm) // BLK
    if data_parts == 8 and parts == 4:
        block_out, input_grad, owned, sums = compute(tokens, cotangent, gains, master=master[0], owner=owner)
    else:
        number = jnp.arange(owner.shape[0], dtype=jnp.int32)
        ahead = (owner[None, :] < owner[:, None]) | ((owner[None, :] == owner[:, None]) & (number[None, :] < number[:, None]))
        block_rank = jnp.sum(ahead.astype(jnp.int32), axis=1)
        _, table = stack_places(hm, fm)
        table = jnp.asarray(table, jnp.int32)
        slot_place = jnp.sum(jnp.where(block_rank[None, :] == number[:, None], table[None, :], 0), axis=1)
        stored = lax.all_gather(master.astype(bf16), "dp", axis=1, tiled=True)
        stored = lax.all_gather(stored, "mp", axis=0, tiled=True)
        stack = stored[:, block_rank]
        upper = stack[:, : row_tiles * cols].reshape(parts, row_tiles, cols, BLK, BLK)
        upper = upper.transpose(0, 1, 3, 2, 4).reshape(parts, D, cols * BLK)
        lower = stack[:, row_tiles * cols :].reshape(parts, lows, row_tiles, BLK, BLK)
        lower = lower.transpose(0, 1, 3, 2, 4).reshape(parts, lows * BLK, D)
        weights = (upper[:, :, : 3 * hm], lower[:, :hm], upper[:, :, 3 * hm :], lower[:, hm:])
        first = ((lax.axis_index("dp") * parts + lax.axis_index("mp")) * L + 1).astype(f32)
        base = jnp.stack([first, jnp.asarray(token_total, f32)])
        block_out, input_grad, grads, sums = compute(tokens, cotangent, gains, weights=weights, base=base)
        owned = lax.psum_scatter(grads[:, slot_place].astype(f32), "dp", scatter_dimension=1, tiled=True)
        owned = lax.psum_scatter(owned, "mp", scatter_dimension=0, tiled=True)[0]
        sums = lax.psum(sums, ("dp", "mp"))
        count = master.shape[1]
        mine = lax.dynamic_slice_in_dim(slot_place, lax.axis_index("dp") * count, count)
        units, _ = stack_places(hm, fm)
        flags = ((mine >= units[UPDOWN][1] // 2) & (mine < units[GATE][0])).astype(f32)
        flags = jnp.pad(jnp.repeat(flags, BLK), (0, (8 - count) * BLK)).reshape(2, 4 * BLK)
        sums = jnp.concatenate([sums[:3], flags, sums[5:]])
    outs = update(
        token_total,
        (sums, gains, gain_moment_one, gain_moment_two),
        (owned, basis_left[0], basis_right[0], moment_one[0], moment_two[0], master[0]),
        (block_out, input_grad),
    )
    first_new, second_new, master_new, master_low, gain_first, gain_second, gains_new, forget_mean = outs[:8]
    block_out, input_grad = outs[8:]
    return (
        block_out,
        input_grad,
        first_new[None],
        second_new[None],
        master_new[None],
        master_low[None],
        gain_first,
        gain_second,
        gains_new,
        forget_mean[0, 0],
    )


def solution(mesh):
    rows, blocks = P(("dp", "mp"), None), P("mp", "dp", None, None)
    return jax.shard_map(
        on_device,
        mesh=mesh,
        in_specs=(rows, rows, blocks, blocks, blocks, blocks, blocks, P(), P(), P(), P()),
        out_specs=(rows, rows, blocks, blocks, blocks, blocks, P(), P(), P(), P()),
        check_vma=False,
    )
```

```python
import functools

import jax
import jax.numpy as jnp
from jax import lax
from jax.experimental import pallas as pl
from jax.experimental.pallas import tpu as pltpu
from jax.sharding import PartitionSpec as P

D = 512
H = 1024
FF = 2048
BLK = 128
STEP = 10
L = 1024

norm_eps = 1e-05
beta_one = 0.5
beta_two = 0.5
adam_eps = 1e-08
learn_rate = 0.02
gain_rate = 0.1
weight_decay = 0.1
highest = lax.Precision.HIGHEST

f32 = jnp.float32
bf16 = jnp.bfloat16
SUB = 8
J = L // SUB
R = 256


def dot(a, b, trans_b=False):
    dims = (((1,), (1,)), ((), ())) if trans_b else (((1,), (0,)), ((), ()))
    return lax.dot_general(a, b, dims, preferred_element_type=f32)


def recip(v):
    return pltpu.reciprocal(v, approx=True)


def sigmoid(v):
    return recip(1.0 + jnp.exp(-v))


def shift_down(v):
    rolled = pltpu.roll(v, 1, 0)
    row = lax.broadcasted_iota(jnp.int32, v.shape, 0)
    return jnp.where(row == 0, 0.0, rolled)


def shift_up(v):
    rolled = pltpu.roll(v, SUB - 1, 0)
    row = lax.broadcasted_iota(jnp.int32, v.shape, 0)
    return jnp.where(row == SUB - 1, 0.0, rolled)


def gelu_terms(x):
    a = jnp.abs(x)
    t = recip(1.0 + a * (0.3275911 * 0.7071067811865476))
    poly = t * (
        0.5 * 0.254829592
        + t
        * (
            0.5 * -0.284496736
            + t * (0.5 * 1.421413741 + t * (0.5 * -1.453152027 + t * (0.5 * 1.061405429)))
        )
    )
    e = jnp.exp(x * x * -0.5)
    tail = poly * e
    cdf = jnp.where(x < 0.0, tail, 1.0 - tail)
    return cdf, x * e * 0.3989422804014327


MESH = pl.DeviceIdType.MESH


class Copy:
    def __init__(self, net, make):
        self.net, self.make = net, make

    def start(self):
        self.net.open.append(self)
        self.make().start()
        return self

    def wait_recv(self):
        self.make().wait_recv()

    def wait_send(self):
        self.make().wait_send()


class Exchange:
    def __init__(self, send, recv):
        self.send, self.recv, self.known, self.used, self.open = send, recv, {}, 0, []

    def copy(self, parts, key=None):
        if key in self.known:
            return self.known[key]
        k = self.used
        self.used += 1

        def make():
            src, dst, device = parts()
            return pltpu.make_async_remote_copy(
                src_ref=src,
                dst_ref=dst,
                send_sem=self.send.at[k],
                recv_sem=self.recv.at[k],
                device_id=device,
                device_id_type=MESH,
            )

        copy = Copy(self, make)
        if key is not None:
            self.known[key] = copy
        return copy

    def start(self, parts):
        return self.copy(parts).start()

    def drain(self):
        for copy in self.open:
            copy.wait_send()
        self.open = []


class Gather:
    def __init__(self, net, fetch, master, slots, pool, weights, free):
        self.net, self.weights, self.free = net, weights, free
        self.held = [slots, *pool]
        d, m = lax.axis_index("dp"), lax.axis_index("mp")
        core, col, row = d % 2, (d // 2) % 2, d // 4
        self.me, self.m, self.side = d, m, core
        self.core = d + 1 - 2 * core
        self.plane = [d + 2 - 4 * col, d + 4 - 8 * row, d + 6 - 4 * col - 8 * row]
        self.order = [m, m + 1 - 2 * (m % 2), m + 2 - 4 * (m // 2), 3 - m]
        self.peers = [(e, m) for e in [self.core] + self.plane] + [(d, k) for k in self.order[1:]]
        barrier = pltpu.get_barrier_semaphore()
        for device in self.peers:
            pl.semaphore_signal(barrier, inc=1, device_id=device, device_id_type=MESH)
        self.n = master.shape[0]
        fetch.wait()
        for s in range(self.n):
            slots[d * self.n + s] = master[s].astype(bf16)
        pl.semaphore_wait(barrier, len(self.peers))

    def rows(self, i, e, first, count):
        return self.held[i].at[pl.ds(e * self.n + first, count)]

    def along(self, i, e):
        return self.net.copy(
            lambda: (self.rows(0, e, 0, self.n), self.rows(i, e, 0, self.n), (self.me, self.order[i])),
            ("along", i, e is self.me),
        )

    def within(self, key, i, e, first, count, to):
        return self.net.copy(
            lambda: (self.rows(i, e, first, count), self.rows(i, e, first, count), (to, self.m)), (key, i)
        )

    def first(self, i):
        (x, y, _), h = self.plane, self.n // 2
        if i == 1:
            jobs = ((0, self.n, x), (0, self.n, y))
        else:
            jobs = ((0, h, x), (h, h, y), (h, h, x), (0, h, y))
        return [self.within(("first", k), i, self.me, *job) for k, job in enumerate(jobs)]

    def last(self, i):
        x, y, z = self.plane
        if i == 1:
            return [self.along(1, z)]
        h = self.n // 2
        return [self.within("over y", i, x, 0, h, y), self.within("over x", i, y, h, h, x)]

    def inside(self, i):
        return [self.within(("inside", k), i, e, 0, self.n, self.core) for k, e in enumerate([self.me] + self.plane)]

    def along_start(self, i):
        self.along(i, self.me).start()

    def across_start(self):
        self.last(1)[0].start()

    def start(self, i):
        if i:
            self.along(i, self.me).wait_recv()
        for copy in self.first(i):
            copy.start()
        self.inside(i)[0].start()

    def forward(self, i):
        if i == 1:
            return
        for came, copy in zip(self.first(i), self.last(i)):
            came.wait_recv()
            copy.start()

    def pair(self, i):
        for came, copy in zip(self.first(i)[-2:], self.inside(i)[1:3]):
            came.wait_recv()
            copy.start()
        for came in self.last(i):
            came.wait_recv()
        self.inside(i)[3].start()

    def ready(self, i):
        for copy in self.inside(i):
            copy.wait_recv()

    def place(self, i, rank):
        wg, wo, wu, wd = self.weights
        row_tiles, gates = D // BLK, wg.shape[2] // BLK
        cols, outs = gates + wu.shape[2] // BLK, wo.shape[1] // BLK
        for b in range(row_tiles * cols + (wo.shape[1] + wd.shape[1]) // BLK * row_tiles):
            if b < row_tiles * cols:
                r, c = b // cols, b % cols
                ref = wg if c < gates else wu
                c -= 0 if c < gates else gates
            else:
                r, c = (b - row_tiles * cols) // row_tiles, (b - row_tiles * cols) % row_tiles
                ref = wo if r < outs else wd
                r -= 0 if r < outs else outs
            block = self.held[i][rank[0, b]]
            ref[self.order[i], r * BLK : (r + 1) * BLK, c * BLK : (c + 1) * BLK] = block

    def done(self):
        for device in self.peers:
            pl.semaphore_signal(self.free, inc=1, device_id=device, device_id_type=MESH)

    def all_done(self):
        pl.semaphore_wait(self.free, len(self.peers))


def stack_places(hm, fm):
    row_tiles, gates, ups, outs = D // BLK, 3 * hm // BLK, fm // BLK, hm // BLK
    cols = gates + ups
    first_down = row_tiles * ups
    first_out = 2 * first_down
    first_gate = first_out + row_tiles * outs
    table = []
    for b in range(row_tiles * (cols + outs + ups)):
        if b < row_tiles * cols:
            r, c = b // cols, b % cols
            table.append(first_gate + r * gates + c if c < gates else r * ups + c - gates)
        else:
            k = b - row_tiles * cols
            table.append(first_out + k if k < row_tiles * outs else first_down + k - row_tiles * outs)
    return ((0, first_out), (first_out, row_tiles * outs), (first_gate, row_tiles * gates)), table


UPDOWN, OUT, GATE = range(3)


class Reduce:
    def __init__(self, net, gather, grads, units, pool):
        self.net, self.g, self.grads, self.units, self.pool = net, gather, grads, units, pool
        self.half = grads.shape[1] // 2
        self.eighth = grads.shape[1] // 8

    def place(self, e):
        return (e % 2) * 4 + e // 2

    def inside(self, unit, i):
        g, (first, count) = self.g, self.units[unit]
        return self.net.copy(
            lambda: (
                self.grads.at[g.order[i], pl.ds(first + (1 - g.side) * (count // 2), count // 2)],
                self.pool[i - 1].at[pl.ds(first // 2, count // 2)],
                (g.core, g.m),
            ),
            ("chip", unit, i),
        )

    def chip(self, unit, i):
        self.inside(unit, i).start()

    def spot(self, unit, i, slot, first, count):
        base, total = self.units[unit]
        return self.pool[i - 1].at[pl.ds(self.half + slot * self.eighth + base // 8 + first, count)]

    def parts(self, unit, i):
        n = self.units[unit][1] // 8
        if i == 1:
            return ((0, n),)
        h = (n + i % 2) // 2 if n % 2 else n // 2
        return (0, h), (h, n - h)

    def share(self, unit, i, e, first, count):
        base, total = self.units[unit]
        return self.grads.at[self.g.order[i], pl.ds(base + self.place(e) * (total // 8) + first, count)]

    def over(self, unit, i, slot, part):
        x, y, z = self.g.plane
        e = (z, x, y)[slot]
        to = (x if part == self.parts(unit, i)[0] else y, x, y)[slot]
        return self.net.copy(
            lambda: (self.share(unit, i, e, *part), self.spot(unit, i, slot, *part), (to, self.g.m)),
            ("over", unit, i, slot, part),
        )

    def send(self, unit, i, slot, part):
        if part[1]:
            self.over(unit, i, slot, part).start()

    def take(self, unit, i, slot, part):
        self.over(unit, i, slot, part).wait_recv()
        return self.spot(unit, i, slot, *part)[...].astype(f32)

    def model_copy(self, unit, i):
        n = self.units[unit][1] // 8
        return self.net.copy(
            lambda: (self.share(unit, i, self.g.me, 0, n), self.spot(unit, i, 3, 0, n), (self.g.me, self.g.order[i])),
            ("model", unit, i),
        )

    def aside(self, unit):
        part = (0, self.units[unit][1] // 8)
        return self.net.copy(
            lambda: (
                self.share(unit, 1, self.g.plane[2], *part),
                self.spot(unit, 1, 0, *part),
                (self.g.me, self.g.order[1]),
            ),
            ("aside", unit),
        )

    def plane(self, unit, i):
        g, (first, count) = self.g, self.units[unit]
        x, y, z = g.plane
        self.inside(unit, i).wait_recv()
        m = g.order[i]
        start, came = first + g.side * (count // 2), self.pool[i - 1]

        @pl.loop(0, count // 2)
        def _(b):
            total = self.grads[m, start + b].astype(f32) + came[first // 2 + b].astype(f32)
            self.grads[m, start + b] = total.astype(bf16)

        if i == 1:
            (whole,) = self.parts(unit, i)
            self.send(unit, i, 1, whole)
            self.send(unit, i, 2, whole)
            self.aside(unit).start()
            return
        one, two = self.parts(unit, i)
        self.send(unit, i, 0, one)
        self.send(unit, i, 0, two)
        self.send(unit, i, 1, one)
        self.send(unit, i, 2, two)

    def turn(self, unit, i):
        if i == 1:
            return
        x, y, _ = self.g.plane
        for part, slot, e in zip(self.parts(unit, i), (2, 1), (y, x)):
            if part[1]:
                ref = self.share(unit, i, e, *part)
                ref[...] = (ref[...].astype(f32) + self.take(unit, i, 0, part)).astype(bf16)
                self.send(unit, i, slot, part)

    def model(self, unit, i):
        g, (first, count) = self.g, self.units[unit]
        n = count // 8
        for part in self.parts(unit, i):
            if part[1]:
                ref = self.share(unit, i, g.me, *part)
                total = ref[...].astype(f32) + self.take(unit, i, 1, part) + self.take(unit, i, 2, part)
                ref[...] = total.astype(bf16)
        self.model_copy(unit, i).start()

    def own(self, unit):
        g, (first, count) = self.g, self.units[unit]
        n = count // 8
        rows = pl.ds(first + self.place(g.me) * n, n)
        total = self.grads[g.m, rows].astype(f32)
        for i in (1, 2, 3):
            self.model_copy(unit, i).wait_recv()
            total += self.pool[i - 1][pl.ds(self.half + 3 * self.eighth + first // 8, n)].astype(f32)
        self.grads[g.m, rows] = total.astype(bf16)
        self.aside(unit).wait_recv()
        rows = pl.ds(first + self.place(g.plane[2]) * n, n)
        total = self.grads[g.m, rows].astype(f32) + self.spot(unit, 1, 0, 0, n)[...].astype(f32)
        self.grads[g.m, rows] = total.astype(bf16)

    def into_slots(self, out, slot_place, e):
        n = self.eighth
        for k in range(n):
            out[self.place(e) * n + k] = self.grads[self.g.m, slot_place[0, e * n + k]]

    def slots_chip(self, out, slot_place, pair):
        g, n = self.g, self.eighth
        self.last = []
        targets = (g.plane[2], g.plane[0], g.plane[1], g.me)
        for e in targets:
            other = e + 1 - 2 * g.side
            self.into_slots(out, slot_place, other)
            self.last.append(
                self.net.start(
                    lambda e=e, other=other: (
                        out.at[pl.ds(self.place(other) * n, n)],
                        pair.at[pl.ds((e // 2) * n, n)],
                        (g.core, g.m),
                    )
                )
            )
        for e in targets:
            self.into_slots(out, slot_place, e)

    def slots_plane(self, out, pair, far):
        g, n = self.g, out.shape[0] // 8
        h = n // 2
        x, y, z = g.plane
        wait = dict(zip("zxyo", self.last))

        def mine(e, first, count):
            return pl.ds((g.side * 4 + e // 2) * n + first, count)

        def join(e):
            rows = mine(e, 0, n)
            out[rows] = (out[rows].astype(f32) + pair[pl.ds((e // 2) * n, n)].astype(f32)).astype(bf16)

        def send(e, first, slot, to):
            return self.net.start(lambda: (out.at[mine(e, first, h)], far.at[slot], (to, g.m)))

        wait["z"].wait_recv()
        join(z)
        over_x = send(z, 0, 0, x)
        over_y = send(z, h, 1, y)
        wait["x"].wait_recv()
        join(x)
        self.ends = [send(x, 0, 2, x)]
        wait["y"].wait_recv()
        join(y)
        self.ends.append(send(y, h, 3, y))
        over_x.wait_recv()
        rows = mine(y, 0, h)
        out[rows] = (out[rows].astype(f32) + far[0].astype(f32)).astype(bf16)
        self.ends.append(send(y, 0, 4, y))
        over_y.wait_recv()
        rows = mine(x, h, h)
        out[rows] = (out[rows].astype(f32) + far[1].astype(f32)).astype(bf16)
        self.ends.append(send(x, h, 5, x))
        wait["o"].wait_recv()

    def slots_end(self, out, pair, far, owned):
        g, n = self.g, out.shape[0] // 8
        h = n // 2
        for copy in self.ends:
            copy.wait_recv()
        for first, slots in ((0, (2, 4)), (h, (3, 5))):
            total = out[pl.ds((g.side * 4 + g.me // 2) * n + first, h)].astype(f32)
            total += pair[pl.ds((g.me // 2) * n + first, h)].astype(f32)
            for k in slots:
                total += far[k].astype(f32)
            owned[first : first + h] = total


class SmallSum:
    def __init__(self, net, gather, values, along, across, inside):
        self.net, self.g, self.values = net, gather, values
        self.slots = (along, across, inside)
        self.peers = (
            [(gather.me, k) for k in gather.order[1:]],
            [(e, gather.m) for e in gather.plane],
            [(gather.core, gather.m)],
        )
        self.mine = (gather.m, gather.me // 2, gather.side)
        self.open = []

    def send(self, stage):
        slot = self.slots[stage]
        slot[self.mine[stage]] = self.values[...]
        ref = slot.at[self.mine[stage]]
        self.open = [self.net.start(lambda peer=peer: (ref, ref, peer)) for peer in self.peers[stage]]

    def add(self, stage):
        for copy in self.open:
            copy.wait_recv()
        slot = self.slots[stage]
        total = slot[0]
        for k in range(1, slot.shape[0]):
            total += slot[k]
        self.values[...] = total


def number_blocks(owner, table, vector, rank, slot_place, sem):
    lane = lax.broadcasted_iota(jnp.int32, vector.shape, 1)
    count = owner.shape[0]
    owners = jnp.zeros_like(lane)
    for b in range(count):
        owners = jnp.where(lane == b, owner[b], owners)
    ranks = jnp.zeros_like(lane)
    for b in range(count):
        ahead = (owner[b] < owners) | ((owner[b] == owners) & (lane > b))
        ranks += jnp.where(ahead, 1, 0)
    vector[...] = ranks
    copy = pltpu.make_async_copy(vector, rank, sem)
    copy.start()
    copy.wait()
    places = jnp.zeros_like(lane)
    for b in range(count):
        places = jnp.where(lane == rank[0, b], table[b], places)
    vector[...] = places
    copy = pltpu.make_async_copy(vector, slot_place, sem)
    copy.start()
    copy.wait()


def compute_kernel(linked, *refs):
    if linked:
        tokens, cotangent, master, owner, gains = refs[:5]
        block_out, input_grad, owned, small = refs[5:9]
        wg, wo, wu, wd, grads, slots, *pool, pair, far, sum_a, sum_b, sum_c, vector, rank, slot_place, send, recv, free = refs[9:29]
        scratch = refs[29:]
    else:
        tokens, cotangent, base, wg, wo, wu, wd, gains = refs[:8]
        block_out, input_grad, grads, small = refs[8:12]
        scratch = refs[12:]
    (n1, n1t, cot, cott, n2, n2t, forget, admit, cand, state, scan, acc_a, acc_b, mixed, mid, kept, fills, tally, local) = scratch
    dml, dmlt = n2, n2t
    parts, _, hm3 = wg.shape
    hm = hm3 // 3
    fm = wu.shape[2]
    units, table = stack_places(hm, fm)
    act, dup, dpre = mid.at[:, :fm], mid.at[:, fm:], mid.at[:, : 3 * hm]
    gain_one = gains[0:1, :]
    gain_two = gains[1:2, :]

    if linked:
        fetch_master = pltpu.make_async_copy(master, owned, local.at[2])
        fetch_master.start()
    fetch_cot = pltpu.make_async_copy(cotangent, cot, local.at[0])
    fetch_tok = pltpu.make_async_copy(tokens, n1, local.at[1])
    fetch_tok.start()
    fetch_cot.start()

    column_halves = (slice(0, D // 2), slice(D // 2, D))

    def stack(m, first, wide, left, value):
        for r in range(value.shape[0] // BLK):
            for c in range(value.shape[1] // BLK):
                grads[m, first + r * wide + left + c] = value[r * BLK : (r + 1) * BLK, c * BLK : (c + 1) * BLK].astype(bf16)

    def stack_turned(m, first, value):
        high = value.shape[0] // BLK
        for r in range(high):
            for c in range(value.shape[1] // BLK):
                grads[m, first + c * high + r] = value[r * BLK : (r + 1) * BLK, c * BLK : (c + 1) * BLK].astype(bf16)

    def permute_in(src, dst):
        for k in range(D // BLK):
            scan[k] = src[:, k * BLK : (k + 1) * BLK].astype(f32)

        @pl.loop(0, J // 2, unroll=4)
        def _(j):
            for k in range(D // BLK):
                lo = scan[k, pl.ds(2 * j, SUB, stride=J), :]
                hi = scan[k, pl.ds(2 * j + 1, SUB, stride=J), :]
                dst[pl.ds(pl.multiple_of(16 * j, 16), 16), k * BLK : (k + 1) * BLK] = jnp.concatenate([lo, hi], 0).astype(bf16)

    def permute_out(src, dst):
        @pl.loop(0, J, unroll=4)
        def _(j):
            rows = pl.ds(pl.multiple_of(j * SUB, SUB), SUB)
            for k in range(D // BLK):
                scan[k, pl.ds(j, SUB, stride=J), :] = src[rows, k * BLK : (k + 1) * BLK]

        for k in range(D // BLK):
            dst[:, k * BLK : (k + 1) * BLK] = scan[k].astype(dst.dtype)

    def put(first, rows, value):
        for k in range(hm // BLK):
            scan[first + k, rows, :] = value[:, k * BLK : (k + 1) * BLK]

    def take(first, rows):
        return jnp.concatenate([scan[first + k, rows, :] for k in range(hm // BLK)], 1)

    half = hm // BLK

    def spread(v):
        return jnp.broadcast_to(v[None], (R // SUB, SUB, hm)).reshape(R, hm)


    if linked:
        net = Exchange(send, recv)
        gather = Gather(net, fetch_master, owned, slots, pool, (wg, wo, wu, wd), free)
        gather.start(0)
        gather.along_start(1)
        gather.along_start(2)
        reduce = Reduce(net, gather, grads, units, pool)

    def of_turn(t):
        if not linked:
            return t
        high, low = gather.m // 2, gather.m % 2
        t_high, t_low = t // 2, t % 2
        return 2 * (high + t_high - 2 * high * t_high) + low + t_low - 2 * low * t_low

    fetch_tok.wait()
    permute_in(n1, n1)
    mixed[...] = n1[...].astype(f32)

    @pl.loop(0, L // R)
    def _(i):
        rows = pl.ds(pl.multiple_of(i * R, R), R)
        x = mixed[rows, :]
        r = lax.rsqrt(jnp.mean(x * x, axis=-1, keepdims=True) + norm_eps)
        n1[rows, :] = (x * r * gain_one).astype(bf16)

    n1t[...] = n1[...].T

    if linked:
        gather.forward(0)
        gather.along_start(3)
        number_blocks(owner, table, vector, rank, slot_place, local.at[2])
    fetch_cot.wait()
    permute_in(cot, cot)
    if linked:
        gather.start(1)
        gather.pair(0)
        gather.across_start()
        gather.start(2)
    cott[...] = cot[...].T

    fills[0] = jnp.zeros((SUB, hm), f32)
    fills[1] = jnp.ones((SUB, hm), f32)
    tally[0] = fills[0]
    tally[1] = fills[0]

    @pl.loop(0, parts)
    def _(turn):
        m = of_turn(turn)
        if linked:
            for k in range(parts):

                @pl.when(turn == k)
                def _():
                    if k:
                        gather.pair(k)
                    gather.ready(k)
                    gather.place(k, rank)

        forget[m] = dot(n1[...], wg[m, :, :hm])
        admit[m] = dot(n1[...], wg[m, :, hm : 2 * hm])
        cand[m] = dot(n1[...], wg[m, :, 2 * hm :])

        if linked:
            for k in range(parts - 1):

                @pl.when(turn == k)
                def _():
                    if k == 0:
                        gather.forward(2)
                    if k == 1:
                        gather.start(3)
                    if k == 2:
                        gather.forward(3)

        @pl.loop(0, L // R)
        def _(i):
            rows = pl.ds(pl.multiple_of(i * R, R), R)
            f = sigmoid(forget[m, rows, :])
            a = sigmoid(admit[m, rows, :])
            inv = recip(f + a)
            forget[m, rows, :] = f
            admit[m, rows, :] = a
            kept[rows, :] = f * inv
            put(0, rows, a * inv * cand[m, rows, :])

        def step(j, carry):
            s, p, k_sum, kj_sum = carry
            rows = pl.ds(pl.multiple_of(j * SUB, SUB), SUB)
            keep = kept[rows, :]
            s = keep * s + take(0, rows)
            p = keep * p
            put(0, rows, s)
            put(half, rows, p)
            return s, p, k_sum + keep, kj_sum + keep * j.astype(f32)

        s, p, k_sum, kj_sum = lax.fori_loop(0, J, step, (fills[0], fills[1], fills[0], fills[0]), unroll=16)
        tally[0] += k_sum
        tally[1] += kj_sum
        enter = fills[0]
        for _ in range(SUB - 1):
            enter = shift_down(s + p * enter)

        @pl.loop(0, L // R)
        def _(i):
            rows = pl.ds(pl.multiple_of(i * R, R), R)
            state[m, pl.ds(pl.multiple_of(i * R + SUB, SUB), R), :] = take(0, rows) + take(half, rows) * spread(enter)

        state[m, :SUB, :] = shift_down(state[m, L:, :])
        for cols in column_halves:
            mixed[:, cols] += dot(state[m, SUB:, :].astype(bf16), wo[m, :, cols])

    if linked:
        net.drain()
        gather.done()

    @pl.loop(0, L // R)
    def _(i):
        rows = pl.ds(pl.multiple_of(i * R, R), R)
        x = mixed[rows, :]
        r = lax.rsqrt(jnp.mean(x * x, axis=-1, keepdims=True) + norm_eps)
        n2[rows, :] = (x * r * gain_two).astype(bf16)
        acc_a[rows, :] = x
        acc_b[rows, :] = jnp.zeros_like(x)

    n2t[...] = n2[...].T

    @pl.loop(0, parts)
    def _(turn):
        m = of_turn(turn)
        for first in range(0, fm, fm // 2):
            units_of = slice(first, first + fm // 2)
            up = dot(n2[...], wu[m, :, units_of])
            da = dot(cot[...], wd[m, units_of, :], True)
            cdf, xpdf = gelu_terms(up)
            act[:, units_of] = (up * cdf).astype(bf16)
            dup[:, units_of] = (da * (cdf + xpdf)).astype(bf16)
        for cols in column_halves:
            acc_a[:, cols] += dot(act[...], wd[m, :, cols])
        for cols in column_halves:
            acc_b[:, cols] += dot(dup[...], wu[m, cols, :], True)
        for c in range(0, fm, fm // 2):
            part = slice(c, c + fm // 2)
            stack(m, 0, fm // BLK, c // BLK, dot(n2t[...], dup[:, part]))
        for c in range(0, fm, fm // 2):
            part = slice(c, c + fm // 2)
            stack_turned(m, units[UPDOWN][1] // 2 + c // BLK * (D // BLK), dot(cott[...], act[:, part]))
        if linked:
            for k in (1, 2, 3):

                @pl.when(turn == k)
                def _():
                    if k == 1:
                        gather.all_done()
                    reduce.chip(UPDOWN, k)
                    if k > 1:
                        reduce.plane(UPDOWN, k - 1)
                    if k == 3:
                        reduce.model(UPDOWN, 1)

    gain_sum_two = jnp.zeros((1, D), f32)

    def back_two(i, total):
        rows = pl.ds(pl.multiple_of(i * R, R), R)
        x = mixed[rows, :]
        r = lax.rsqrt(jnp.mean(x * x, axis=-1, keepdims=True) + norm_eps)
        dn = acc_b[rows, :]
        q = dn * gain_two
        d = cot[rows, :].astype(f32) + r * q - r * r * r * x * jnp.mean(q * x, axis=-1, keepdims=True)
        mixed[rows, :] = d
        dml[rows, :] = d.astype(bf16)
        acc_b[rows, :] = jnp.zeros_like(d)
        return total + jnp.sum(dn * x * r, axis=0, keepdims=True)

    gain_sum_two = lax.fori_loop(0, L // R, back_two, gain_sum_two)
    if linked:
        reduce.plane(UPDOWN, 3)
    dmlt[...] = dml[...].T
    fetch_tok = pltpu.make_async_copy(tokens, cot, local.at[1])
    fetch_tok.start()

    @pl.loop(0, parts)
    def _(m):
        stack_turned(m, units[OUT][0], dot(dmlt[...], state[m, SUB:, :].astype(bf16)))

    if linked:
        for i in (3, 2, 1):
            reduce.chip(OUT, i)

    def keeps(m, rows):
        f = forget[m, rows, :]
        kept[rows, :] = f * recip(f + admit[m, rows, :])

    def state_grads(m):
        put(0, slice(None), dot(dml[...], wo[m], True))

    state_grads(of_turn(parts - 1))

    @pl.loop(0, L // R)
    def _(i):
        keeps(of_turn(parts - 1), pl.ds(pl.multiple_of(i * R, R), R))

    @pl.loop(0, parts)
    def _(back_turn):
        turn = parts - 1 - back_turn
        m = of_turn(turn)
        m_next = of_turn((turn + parts - 1) % parts)

        def step(k, carry):
            u, p, keep_next = carry
            j = J - 1 - k
            rows = pl.ds(pl.multiple_of(j * SUB, SUB), SUB)
            u = take(0, rows) + keep_next * u
            p = keep_next * p
            put(0, rows, u)
            put(half, rows, p)
            return u, p, kept[rows, :]

        u, p, keep_first = lax.fori_loop(0, J, step, (fills[0], fills[1], fills[1]), unroll=16)
        enter = fills[0]
        for _ in range(SUB - 1):
            enter = shift_up(keep_first * (u + p * enter))

        if linked:

            @pl.when(turn == 3)
            def _():
                reduce.turn(UPDOWN, 2)
                for i in (3, 2, 1):
                    reduce.plane(OUT, i)

            @pl.when(turn == 0)
            def _():
                reduce.plane(GATE, 1)

        @pl.loop(0, L // R)
        def _(i):
            rows = pl.ds(pl.multiple_of(i * R, R), R)
            carried = take(0, rows) + take(half, rows) * spread(enter)
            f = forget[m, rows, :]
            a = admit[m, rows, :]
            adm = a * recip(f + a)
            g = carried * (state[m, rows, :] - cand[m, rows, :]) * (kept[rows, :] * adm)
            dpre[rows, :hm] = (g * (1.0 - f)).astype(bf16)
            dpre[rows, hm : 2 * hm] = (g * (a - 1.0)).astype(bf16)
            dpre[rows, 2 * hm :] = (carried * adm).astype(bf16)
            keeps(m_next, rows)

        if linked:

            @pl.when(turn == 3)
            def _():
                reduce.turn(UPDOWN, 3)

            @pl.when(turn == 2)
            def _():
                reduce.plane(GATE, 3)
                for i in (3, 2):
                    reduce.turn(OUT, i)
                reduce.model(UPDOWN, 3)
                reduce.model(UPDOWN, 2)

            @pl.when(turn == 1)
            def _():
                reduce.plane(GATE, 2)
                for i in (1, 3, 2):
                    reduce.model(OUT, i)

            @pl.when(turn == 0)
            def _():
                reduce.turn(GATE, 2)
                reduce.model(GATE, 3)

        for k in range(3):
            stack(m, units[GATE][0], 3 * hm // BLK, k * hm // BLK, dot(n1t[...], dpre[:, k * hm : (k + 1) * hm]))
        for cols in column_halves:
            acc_b[:, cols] += dot(dpre[...], wg[m, cols, :], True)
        state_grads(m_next)
        if linked:
            for k in (3, 2, 1):

                @pl.when(turn == k)
                def _():
                    reduce.chip(GATE, k)
                    if k == 1:
                        reduce.turn(GATE, 3)

    if linked:
        reduce.own(UPDOWN)
        reduce.own(OUT)

    fetch_tok.wait()
    permute_in(cot, cot)
    if linked:
        reduce.model(GATE, 1)
        reduce.model(GATE, 2)

    def back_one(i, total):
        rows = pl.ds(pl.multiple_of(i * R, R), R)
        x = cot[rows, :].astype(f32)
        r = lax.rsqrt(jnp.mean(x * x, axis=-1, keepdims=True) + norm_eps)
        dn = acc_b[rows, :]
        q = dn * gain_one
        mixed[rows, :] += r * q - r * r * r * x * jnp.mean(q * x, axis=-1, keepdims=True)
        return total + jnp.sum(dn * x * r, axis=0, keepdims=True)

    gain_sum_one = lax.fori_loop(0, L // R, back_one, jnp.zeros((1, D), f32))

    permute_out(acc_a, n1)
    push_out = pltpu.make_async_copy(n1, block_out, local.at[0])
    push_out.start()

    place = lax.broadcasted_iota(jnp.int32, (SUB, hm), 0).astype(f32) * float(J)
    if linked:
        first = ((gather.me * parts + gather.m) * L + 1).astype(f32)
        token_total = float(L * parts * lax.axis_size("dp"))
    else:
        first = base[0]
        token_total = base[1]
    forget_sum = jnp.sum(tally[1] + tally[0] * (place + first), axis=0, keepdims=True) / token_total
    small[...] = jnp.zeros_like(small)
    small[0:1, :] = gain_sum_one
    small[1:2, :] = gain_sum_two
    small[2:3, :hm] = forget_sum
    if linked:
        flat = units[UPDOWN][1] // 2, units[GATE][0]
        count = owned.shape[0]
        flags = []
        for k in range(count):
            spot = slot_place[0, gather.me * count + k]
            flags.append(jnp.where((spot >= flat[0]) & (spot < flat[1]), 1.0, 0.0).astype(f32))

    if linked:
        tiny = SmallSum(net, gather, small, sum_a, sum_b, sum_c)
        tiny.send(0)
        reduce.own(GATE)
        reduce.slots_chip(slots, slot_place, pair)
        tiny.add(0)
        tiny.send(1)
        reduce.slots_plane(slots, pair, far)

    permute_out(mixed, acc_a)
    push_grad = pltpu.make_async_copy(acc_a, input_grad, local.at[2])
    push_grad.start()

    if linked:
        tiny.add(1)
        tiny.send(2)
        reduce.slots_end(slots, pair, far, owned)
        tiny.add(2)
        for k, flag in enumerate(flags):
            small[3 + k // 4 : 4 + k // 4, (k % 4) * BLK : (k % 4 + 1) * BLK] = jnp.full((1, BLK), flag, f32)
        net.drain()
    push_out.wait()
    push_grad.wait()


def compute(tokens, cotangent, gains, weights=None, base=None, master=None, owner=None):
    linked = weights is None
    parts = lax.axis_size("mp")
    hm, fm = H // parts, FF // parts
    stacked = (parts, D * (4 * hm + 2 * fm) // BLK**2, BLK, BLK)
    sds = jax.ShapeDtypeStruct
    vm, sm, hbm = (pl.BlockSpec(memory_space=k) for k in (pltpu.VMEM, pltpu.SMEM, pl.ANY))
    if linked:
        n = owner.shape[0]
        args = (tokens, cotangent, master, owner, gains)
        in_specs = [hbm, hbm, hbm, sm, vm]
        middle = sds((n // 8, BLK, BLK), f32)
        extra = [
            pltpu.VMEM((parts, D, 3 * hm), bf16),
            pltpu.VMEM((parts, hm, D), bf16),
            pltpu.VMEM((parts, D, fm), bf16),
            pltpu.VMEM((parts, fm, D), bf16),
            pltpu.VMEM(stacked, bf16),
            pltpu.VMEM((n, BLK, BLK), bf16),
            *[pltpu.VMEM((n, BLK, BLK), bf16) for _ in range(parts - 1)],
            pltpu.VMEM((n // 2, BLK, BLK), bf16),
            pltpu.VMEM((6, n // 16, BLK, BLK), bf16),
            pltpu.VMEM((parts, 8, D), f32),
            pltpu.VMEM((4, 8, D), f32),
            pltpu.VMEM((2, 8, D), f32),
            pltpu.VMEM((8, BLK), jnp.int32),
            pltpu.SMEM((8, BLK), jnp.int32),
            pltpu.SMEM((8, BLK), jnp.int32),
            pltpu.SemaphoreType.DMA((128,)),
            pltpu.SemaphoreType.DMA((128,)),
            pltpu.SemaphoreType.REGULAR,
        ]
        params = dict(collective_id=0, has_side_effects=True)
    else:
        args = (tokens, cotangent, base, *weights, gains)
        in_specs = [hbm, hbm, sm] + [vm] * 5
        middle = sds(stacked, bf16)
        extra = []
        params = {}
    return pl.pallas_call(
        functools.partial(compute_kernel, linked),
        out_shape=(sds((L, D), bf16), sds((L, D), f32), middle, sds((8, D), f32)),
        in_specs=in_specs,
        out_specs=[hbm, hbm, vm, vm],
        scratch_shapes=extra
        + [pltpu.VMEM(shape, bf16) for shape in ((L, D), (D, L)) * 3]
        + [pltpu.VMEM((parts, L, hm), f32)] * 3
        + [pltpu.VMEM((parts, L + SUB, hm), f32)]
        + [pltpu.VMEM((2 * hm // BLK, L, BLK), f32)]
        + [pltpu.VMEM((L, D), f32)] * 3
        + [
            pltpu.VMEM((L, 2 * fm), bf16),
            pltpu.VMEM((L, hm), f32),
            pltpu.VMEM((2, SUB, hm), f32),
            pltpu.VMEM((2, SUB, hm), f32),
            pltpu.SemaphoreType.DMA((3,)),
        ],
        compiler_params=pltpu.CompilerParams(vmem_limit_bytes=64 * 2**20 - 2**16, **params),
        name="block",
    )(*args)


def adam_update(first_old, second_old, gradient):
    first_new = beta_one * first_old + (1.0 - beta_one) * gradient
    second_new = beta_two * second_old + (1.0 - beta_two) * gradient * gradient
    first_hat = first_new / (1.0 - beta_one**STEP)
    second_hat = second_new / (1.0 - beta_two**STEP)
    return (first_new, second_new, first_hat / (jnp.sqrt(second_hat) + adam_eps))


def fine_dot(a, b, trans_b=False):
    a_high, b_high = a.astype(bf16), b.astype(bf16)
    a_low, b_low = (a - a_high.astype(f32)).astype(bf16), (b - b_high.astype(f32)).astype(bf16)
    return dot(a_high, b_high, trans_b) + (dot(a_high, b_low, trans_b) + dot(a_low, b_high, trans_b))


def update_kernel(token_total, passed, sums, gains, gain_moment_one, gain_moment_two, *refs):
    sources, refs = refs[:6], refs[6:]
    given, refs = refs[:passed], refs[passed:]
    results, refs = refs[:4], refs[4:]
    gain_first, gain_second, gains_new, forget_mean = refs[:4]
    copied, refs = refs[4 : 4 + passed], refs[4 + passed :]
    held, made, made_low, sem_in, sem_out, sem_pass = refs[:6]
    passage = refs[6:]
    count = held.shape[1]
    step = max(count // 2, 1)
    groups = [slice(first, first + step) for first in range(0, count, step)]
    enter = [pltpu.make_async_copy(src, via, sem_pass.at[0, k]) for k, (src, via) in enumerate(zip(given, passage))]
    leave = [pltpu.make_async_copy(via, dst, sem_pass.at[1, k]) for k, (via, dst) in enumerate(zip(passage, copied))]
    fetch = [
        [pltpu.make_async_copy(src.at[group], held.at[k, group], sem_in.at[g, k]) for k, src in enumerate(sources)]
        for g, group in enumerate(groups)
    ]
    for copy in fetch[0]:
        copy.start()
    for copy in enter:
        copy.start()
    for row in fetch[1:]:
        for copy in row:
            copy.start()
    first, second, direction = adam_update(gain_moment_one[...], gain_moment_two[...], sums[0:2, :])
    gain_first[...] = first
    gain_second[...] = second
    gains_new[...] = gains[...] - gain_rate * direction
    forget_mean[...] = jnp.sum(sums[2:3, :], axis=1, keepdims=True) * (1.0 / (H * (token_total + 1) / 2.0))
    push = []
    for g, group in enumerate(groups):
        blocks = range(group.start, group.stop)
        for copy in fetch[g]:
            copy.wait()
        if g == len(groups) - 1:
            for come, go in zip(enter, leave):
                come.wait()
                go.start()
        grads = []
        for s in blocks:
            grad = held[0, s]
            flag = sums[3 + s // 4 : 4 + s // 4, (s % 4) * BLK : (s % 4 + 1) * BLK]
            grads.append(jnp.where(flag > 0.5, grad.T, grad))
        values = [fine_dot(held[1, s].T, grad) for s, grad in zip(blocks, grads)]
        values = [fine_dot(value, held[2, s]) for s, value in zip(blocks, values)]
        for k, s in enumerate(blocks):
            first, second, values[k] = adam_update(held[3, s], held[4, s], values[k])
            made[0, s] = first
            made[1, s] = second
        values = [fine_dot(held[1, s], value) for s, value in zip(blocks, values)]
        values = [fine_dot(value, held[2, s], True) for s, value in zip(blocks, values)]
        for s, value in zip(blocks, values):
            fresh = held[5, s] - learn_rate * (value + weight_decay * held[5, s])
            made[2, s] = fresh
            made_low[s] = fresh.astype(bf16)
        for k, dst in enumerate(results):
            src = made.at[k, group] if k < 3 else made_low.at[group]
            copy = pltpu.make_async_copy(src, dst.at[group], sem_out.at[g, k])
            copy.start()
            push.append(copy)
    for copy in push + leave:
        copy.wait()


def update(token_total, small, large, passed):
    sds = jax.ShapeDtypeStruct
    blocks, gain = large[0].shape, small[1].shape
    vm, hbm = pl.BlockSpec(memory_space=pltpu.VMEM), pl.BlockSpec(memory_space=pl.ANY)
    return pl.pallas_call(
        functools.partial(update_kernel, token_total, len(passed)),
        out_shape=[sds(blocks, f32)] * 3
        + [sds(blocks, bf16)]
        + [sds(gain, f32)] * 3
        + [sds((1, 1), f32)]
        + [sds(v.shape, v.dtype) for v in passed],
        in_specs=[vm] * 4 + [hbm] * (len(large) + len(passed)),
        out_specs=[hbm] * 4 + [vm] * 4 + [hbm] * len(passed),
        scratch_shapes=[
            pltpu.VMEM((6, *blocks), f32),
            pltpu.VMEM((3, *blocks), f32),
            pltpu.VMEM(blocks, bf16),
            pltpu.SemaphoreType.DMA((2, 6)),
            pltpu.SemaphoreType.DMA((2, 4)),
            pltpu.SemaphoreType.DMA((2, len(passed))),
        ]
        + [pltpu.VMEM(v.shape, v.dtype) for v in passed],
        compiler_params=pltpu.CompilerParams(vmem_limit_bytes=56 * 2**20),
        name="update",
    )(*small, *large, *passed)


def on_device(
    tokens,
    cotangent,
    master,
    moment_one,
    moment_two,
    basis_left,
    basis_right,
    owner,
    gains,
    gain_moment_one,
    gain_moment_two,
):
    parts = lax.axis_size("mp")
    data_parts = lax.axis_size("dp")
    hm, fm = H // parts, FF // parts
    token_total = L * data_parts * parts
    row_tiles, cols, lows = D // BLK, (3 * hm + fm) // BLK, (hm + fm) // BLK
    if data_parts == 8 and parts == 4:
        block_out, input_grad, owned, sums = compute(tokens, cotangent, gains, master=master[0], owner=owner)
    else:
        number = jnp.arange(owner.shape[0], dtype=jnp.int32)
        ahead = (owner[None, :] < owner[:, None]) | ((owner[None, :] == owner[:, None]) & (number[None, :] < number[:, None]))
        block_rank = jnp.sum(ahead.astype(jnp.int32), axis=1)
        _, table = stack_places(hm, fm)
        table = jnp.asarray(table, jnp.int32)
        slot_place = jnp.sum(jnp.where(block_rank[None, :] == number[:, None], table[None, :], 0), axis=1)
        stored = lax.all_gather(master.astype(bf16), "dp", axis=1, tiled=True)
        stored = lax.all_gather(stored, "mp", axis=0, tiled=True)
        stack = stored[:, block_rank]
        upper = stack[:, : row_tiles * cols].reshape(parts, row_tiles, cols, BLK, BLK)
        upper = upper.transpose(0, 1, 3, 2, 4).reshape(parts, D, cols * BLK)
        lower = stack[:, row_tiles * cols :].reshape(parts, lows, row_tiles, BLK, BLK)
        lower = lower.transpose(0, 1, 3, 2, 4).reshape(parts, lows * BLK, D)
        weights = (upper[:, :, : 3 * hm], lower[:, :hm], upper[:, :, 3 * hm :], lower[:, hm:])
        first = ((lax.axis_index("dp") * parts + lax.axis_index("mp")) * L + 1).astype(f32)
        base = jnp.stack([first, jnp.asarray(token_total, f32)])
        block_out, input_grad, grads, sums = compute(tokens, cotangent, gains, weights=weights, base=base)
        owned = lax.psum_scatter(grads[:, slot_place].astype(f32), "dp", scatter_dimension=1, tiled=True)
        owned = lax.psum_scatter(owned, "mp", scatter_dimension=0, tiled=True)[0]
        sums = lax.psum(sums, ("dp", "mp"))
        count = master.shape[1]
        mine = lax.dynamic_slice_in_dim(slot_place, lax.axis_index("dp") * count, count)
        units, _ = stack_places(hm, fm)
        flags = ((mine >= units[UPDOWN][1] // 2) & (mine < units[GATE][0])).astype(f32)
        flags = jnp.pad(jnp.repeat(flags, BLK), (0, (8 - count) * BLK)).reshape(2, 4 * BLK)
        sums = jnp.concatenate([sums[:3], flags, sums[5:]])
    outs = update(
        token_total,
        (sums, gains, gain_moment_one, gain_moment_two),
        (owned, basis_left[0], basis_right[0], moment_one[0], moment_two[0], master[0]),
        (block_out, input_grad),
    )
    first_new, second_new, master_new, master_low, gain_first, gain_second, gains_new, forget_mean = outs[:8]
    block_out, input_grad = outs[8:]
    return (
        block_out,
        input_grad,
        first_new[None],
        second_new[None],
        master_new[None],
        master_low[None],
        gain_first,
        gain_second,
        gains_new,
        forget_mean[0, 0],
    )


def solution(mesh):
    rows, blocks = P(("dp", "mp"), None), P("mp", "dp", None, None)
    return jax.shard_map(
        on_device,
        mesh=mesh,
        in_specs=(rows, rows, blocks, blocks, blocks, blocks, blocks, P(), P(), P(), P()),
        out_specs=(rows, rows, blocks, blocks, blocks, blocks, P(), P(), P(), P()),
        check_vma=False,
    )
```

```python
import functools

import jax
import jax.numpy as jnp
from jax import lax
from jax.experimental import pallas as pl
from jax.experimental.pallas import tpu as pltpu
from jax.sharding import PartitionSpec as P

D = 512
H = 1024
FF = 2048
BLK = 128
STEP = 10
L = 1024

norm_eps = 1e-05
beta_one = 0.5
beta_two = 0.5
adam_eps = 1e-08
learn_rate = 0.02
gain_rate = 0.1
weight_decay = 0.1
highest = lax.Precision.HIGHEST

f32 = jnp.float32
bf16 = jnp.bfloat16
SUB = 8
J = L // SUB
R = 256


def dot(a, b, trans_b=False):
    dims = (((1,), (1,)), ((), ())) if trans_b else (((1,), (0,)), ((), ()))
    return lax.dot_general(a, b, dims, preferred_element_type=f32)


def recip(v):
    return pltpu.reciprocal(v, approx=True)


def sigmoid(v):
    return recip(1.0 + jnp.exp(-v))


def shift_down(v):
    rolled = pltpu.roll(v, 1, 0)
    row = lax.broadcasted_iota(jnp.int32, v.shape, 0)
    return jnp.where(row == 0, 0.0, rolled)


def shift_up(v):
    rolled = pltpu.roll(v, SUB - 1, 0)
    row = lax.broadcasted_iota(jnp.int32, v.shape, 0)
    return jnp.where(row == SUB - 1, 0.0, rolled)


def gelu_terms(x):
    a = jnp.abs(x)
    t = recip(1.0 + a * (0.3275911 * 0.7071067811865476))
    poly = t * (
        0.5 * 0.254829592
        + t
        * (
            0.5 * -0.284496736
            + t * (0.5 * 1.421413741 + t * (0.5 * -1.453152027 + t * (0.5 * 1.061405429)))
        )
    )
    e = jnp.exp(x * x * -0.5)
    tail = poly * e
    cdf = jnp.where(x < 0.0, tail, 1.0 - tail)
    return cdf, x * e * 0.3989422804014327


MESH = pl.DeviceIdType.MESH


class Copy:
    def __init__(self, net, make):
        self.net, self.make = net, make

    def start(self):
        self.net.open.append(self)
        self.make().start()
        return self

    def wait_recv(self):
        self.make().wait_recv()

    def wait_send(self):
        self.make().wait_send()


class Exchange:
    def __init__(self, send, recv):
        self.send, self.recv, self.known, self.used, self.open = send, recv, {}, 0, []

    def copy(self, parts, key=None):
        if key in self.known:
            return self.known[key]
        k = self.used
        self.used += 1

        def make():
            src, dst, device = parts()
            return pltpu.make_async_remote_copy(
                src_ref=src,
                dst_ref=dst,
                send_sem=self.send.at[k],
                recv_sem=self.recv.at[k],
                device_id=device,
                device_id_type=MESH,
            )

        copy = Copy(self, make)
        if key is not None:
            self.known[key] = copy
        return copy

    def start(self, parts):
        return self.copy(parts).start()

    def drain(self):
        for copy in self.open:
            copy.wait_send()
        self.open = []


class Gather:
    def __init__(self, net, fetch, master, slots, pool, weights, free):
        self.net, self.weights, self.free = net, weights, free
        self.held = [slots, *pool]
        d, m = lax.axis_index("dp"), lax.axis_index("mp")
        core, col, row = d % 2, (d // 2) % 2, d // 4
        self.me, self.m, self.side = d, m, core
        self.core = d + 1 - 2 * core
        self.plane = [d + 2 - 4 * col, d + 4 - 8 * row, d + 6 - 4 * col - 8 * row]
        self.order = [m, m + 1 - 2 * (m % 2), m + 2 - 4 * (m // 2), 3 - m]
        self.peers = [(e, m) for e in [self.core] + self.plane] + [(d, k) for k in self.order[1:]]
        barrier = pltpu.get_barrier_semaphore()
        for device in self.peers:
            pl.semaphore_signal(barrier, inc=1, device_id=device, device_id_type=MESH)
        self.n = master.shape[0]
        fetch.wait()
        for s in range(self.n):
            slots[d * self.n + s] = master[s].astype(bf16)
        pl.semaphore_wait(barrier, len(self.peers))

    def rows(self, i, e, first, count):
        return self.held[i].at[pl.ds(e * self.n + first, count)]

    def along(self, i, e):
        return self.net.copy(
            lambda: (self.rows(0, e, 0, self.n), self.rows(i, e, 0, self.n), (self.me, self.order[i])),
            ("along", i, e is self.me),
        )

    def within(self, key, i, e, first, count, to):
        return self.net.copy(
            lambda: (self.rows(i, e, first, count), self.rows(i, e, first, count), (to, self.m)), (key, i)
        )

    def first(self, i):
        (x, y, _), h = self.plane, self.n // 2
        if i == 1:
            jobs = ((0, self.n, x), (0, self.n, y))
        else:
            jobs = ((0, h, x), (h, h, y), (h, h, x), (0, h, y))
        return [self.within(("first", k), i, self.me, *job) for k, job in enumerate(jobs)]

    def last(self, i):
        x, y, z = self.plane
        if i == 1:
            return [self.along(1, z)]
        h = self.n // 2
        return [self.within("over y", i, x, 0, h, y), self.within("over x", i, y, h, h, x)]

    def inside(self, i):
        return [self.within(("inside", k), i, e, 0, self.n, self.core) for k, e in enumerate([self.me] + self.plane)]

    def along_start(self, i):
        self.along(i, self.me).start()

    def across_start(self):
        self.last(1)[0].start()

    def start(self, i):
        if i:
            self.along(i, self.me).wait_recv()
        for copy in self.first(i):
            copy.start()
        self.inside(i)[0].start()

    def forward(self, i):
        if i == 1:
            return
        for came, copy in zip(self.first(i), self.last(i)):
            came.wait_recv()
            copy.start()

    def pair(self, i):
        for came, copy in zip(self.first(i)[-2:], self.inside(i)[1:3]):
            came.wait_recv()
            copy.start()
        for came in self.last(i):
            came.wait_recv()
        self.inside(i)[3].start()

    def ready(self, i):
        for copy in self.inside(i):
            copy.wait_recv()

    def place(self, i, rank):
        wg, wo, wu, wd = self.weights
        row_tiles, gates = D // BLK, wg.shape[2] // BLK
        cols, outs = gates + wu.shape[2] // BLK, wo.shape[1] // BLK
        for b in range(row_tiles * cols + (wo.shape[1] + wd.shape[1]) // BLK * row_tiles):
            if b < row_tiles * cols:
                r, c = b // cols, b % cols
                ref = wg if c < gates else wu
                c -= 0 if c < gates else gates
            else:
                r, c = (b - row_tiles * cols) // row_tiles, (b - row_tiles * cols) % row_tiles
                ref = wo if r < outs else wd
                r -= 0 if r < outs else outs
            block = self.held[i][rank[0, b]]
            ref[self.order[i], r * BLK : (r + 1) * BLK, c * BLK : (c + 1) * BLK] = block

    def done(self):
        for device in self.peers:
            pl.semaphore_signal(self.free, inc=1, device_id=device, device_id_type=MESH)

    def all_done(self):
        pl.semaphore_wait(self.free, len(self.peers))


def stack_places(hm, fm):
    row_tiles, gates, ups, outs = D // BLK, 3 * hm // BLK, fm // BLK, hm // BLK
    cols = gates + ups
    first_down = row_tiles * ups
    first_out = 2 * first_down
    first_gate = first_out + row_tiles * outs
    table = []
    for b in range(row_tiles * (cols + outs + ups)):
        if b < row_tiles * cols:
            r, c = b // cols, b % cols
            table.append(first_gate + r * gates + c if c < gates else r * ups + c - gates)
        else:
            k = b - row_tiles * cols
            table.append(first_out + k if k < row_tiles * outs else first_down + k - row_tiles * outs)
    return ((0, first_out), (first_out, row_tiles * outs), (first_gate, row_tiles * gates)), table


UPDOWN, OUT, GATE = range(3)


class Reduce:
    def __init__(self, net, gather, grads, units, pool):
        self.net, self.g, self.grads, self.units, self.pool = net, gather, grads, units, pool
        self.half = grads.shape[1] // 2
        self.eighth = grads.shape[1] // 8

    def place(self, e):
        return (e % 2) * 4 + e // 2

    def inside(self, unit, i):
        g, (first, count) = self.g, self.units[unit]
        return self.net.copy(
            lambda: (
                self.grads.at[g.order[i], pl.ds(first + (1 - g.side) * (count // 2), count // 2)],
                self.pool[i - 1].at[pl.ds(first // 2, count // 2)],
                (g.core, g.m),
            ),
            ("chip", unit, i),
        )

    def chip(self, unit, i):
        self.inside(unit, i).start()

    def spot(self, unit, i, slot, first, count):
        base, total = self.units[unit]
        return self.pool[i - 1].at[pl.ds(self.half + slot * self.eighth + base // 8 + first, count)]

    def parts(self, unit, i):
        n = self.units[unit][1] // 8
        if i == 1:
            return ((0, n),)
        h = (n + i % 2) // 2 if n % 2 else n // 2
        return (0, h), (h, n - h)

    def share(self, unit, i, e, first, count):
        base, total = self.units[unit]
        return self.grads.at[self.g.order[i], pl.ds(base + self.place(e) * (total // 8) + first, count)]

    def over(self, unit, i, slot, part):
        x, y, z = self.g.plane
        e = (z, x, y)[slot]
        to = (x if part == self.parts(unit, i)[0] else y, x, y)[slot]
        return self.net.copy(
            lambda: (self.share(unit, i, e, *part), self.spot(unit, i, slot, *part), (to, self.g.m)),
            ("over", unit, i, slot, part),
        )

    def send(self, unit, i, slot, part):
        if part[1]:
            self.over(unit, i, slot, part).start()

    def take(self, unit, i, slot, part):
        self.over(unit, i, slot, part).wait_recv()
        return self.spot(unit, i, slot, *part)[...].astype(f32)

    def model_copy(self, unit, i):
        n = self.units[unit][1] // 8
        return self.net.copy(
            lambda: (self.share(unit, i, self.g.me, 0, n), self.spot(unit, i, 3, 0, n), (self.g.me, self.g.order[i])),
            ("model", unit, i),
        )

    def aside(self, unit):
        part = (0, self.units[unit][1] // 8)
        return self.net.copy(
            lambda: (
                self.share(unit, 1, self.g.plane[2], *part),
                self.spot(unit, 1, 0, *part),
                (self.g.me, self.g.order[1]),
            ),
            ("aside", unit),
        )

    def plane(self, unit, i):
        g, (first, count) = self.g, self.units[unit]
        x, y, z = g.plane
        self.inside(unit, i).wait_recv()
        m = g.order[i]
        start, came = first + g.side * (count // 2), self.pool[i - 1]

        @pl.loop(0, count // 2)
        def _(b):
            total = self.grads[m, start + b].astype(f32) + came[first // 2 + b].astype(f32)
            self.grads[m, start + b] = total.astype(bf16)

        if i == 1:
            (whole,) = self.parts(unit, i)
            self.send(unit, i, 1, whole)
            self.send(unit, i, 2, whole)
            self.aside(unit).start()
            return
        one, two = self.parts(unit, i)
        self.send(unit, i, 0, one)
        self.send(unit, i, 0, two)
        self.send(unit, i, 1, one)
        self.send(unit, i, 2, two)

    def turn(self, unit, i):
        if i == 1:
            return
        x, y, _ = self.g.plane
        for part, slot, e in zip(self.parts(unit, i), (2, 1), (y, x)):
            if part[1]:
                ref = self.share(unit, i, e, *part)
                ref[...] = (ref[...].astype(f32) + self.take(unit, i, 0, part)).astype(bf16)
                self.send(unit, i, slot, part)

    def model(self, unit, i):
        g, (first, count) = self.g, self.units[unit]
        n = count // 8
        for part in self.parts(unit, i):
            if part[1]:
                ref = self.share(unit, i, g.me, *part)
                total = ref[...].astype(f32) + self.take(unit, i, 1, part) + self.take(unit, i, 2, part)
                ref[...] = total.astype(bf16)
        self.model_copy(unit, i).start()

    def own(self, unit):
        g, (first, count) = self.g, self.units[unit]
        n = count // 8
        rows = pl.ds(first + self.place(g.me) * n, n)
        total = self.grads[g.m, rows].astype(f32)
        for i in (1, 2, 3):
            self.model_copy(unit, i).wait_recv()
            total += self.pool[i - 1][pl.ds(self.half + 3 * self.eighth + first // 8, n)].astype(f32)
        self.grads[g.m, rows] = total.astype(bf16)
        self.aside(unit).wait_recv()
        rows = pl.ds(first + self.place(g.plane[2]) * n, n)
        total = self.grads[g.m, rows].astype(f32) + self.spot(unit, 1, 0, 0, n)[...].astype(f32)
        self.grads[g.m, rows] = total.astype(bf16)

    def into_slots(self, out, slot_place, e):
        n = self.eighth
        for k in range(n):
            out[self.place(e) * n + k] = self.grads[self.g.m, slot_place[0, e * n + k]]

    def slots_chip(self, out, slot_place, pair):
        g, n = self.g, self.eighth
        self.last = []
        targets = (g.plane[2], g.plane[0], g.plane[1], g.me)
        for e in targets:
            other = e + 1 - 2 * g.side
            self.into_slots(out, slot_place, other)
            self.last.append(
                self.net.start(
                    lambda e=e, other=other: (
                        out.at[pl.ds(self.place(other) * n, n)],
                        pair.at[pl.ds((e // 2) * n, n)],
                        (g.core, g.m),
                    )
                )
            )
        for e in targets:
            self.into_slots(out, slot_place, e)

    def slots_plane(self, out, pair, far):
        g, n = self.g, out.shape[0] // 8
        h = n // 2
        x, y, z = g.plane
        wait = dict(zip("zxyo", self.last))

        def mine(e, first, count):
            return pl.ds((g.side * 4 + e // 2) * n + first, count)

        def join(e):
            rows = mine(e, 0, n)
            out[rows] = (out[rows].astype(f32) + pair[pl.ds((e // 2) * n, n)].astype(f32)).astype(bf16)

        def send(e, first, slot, to):
            return self.net.start(lambda: (out.at[mine(e, first, h)], far.at[slot], (to, g.m)))

        wait["z"].wait_recv()
        join(z)
        over_x = send(z, 0, 0, x)
        over_y = send(z, h, 1, y)
        wait["x"].wait_recv()
        join(x)
        self.ends = [send(x, 0, 2, x)]
        wait["y"].wait_recv()
        join(y)
        self.ends.append(send(y, h, 3, y))
        over_x.wait_recv()
        rows = mine(y, 0, h)
        out[rows] = (out[rows].astype(f32) + far[0].astype(f32)).astype(bf16)
        self.ends.append(send(y, 0, 4, y))
        over_y.wait_recv()
        rows = mine(x, h, h)
        out[rows] = (out[rows].astype(f32) + far[1].astype(f32)).astype(bf16)
        self.ends.append(send(x, h, 5, x))
        wait["o"].wait_recv()

    def slots_end(self, out, pair, far, owned):
        g, n = self.g, out.shape[0] // 8
        h = n // 2
        for copy in self.ends:
            copy.wait_recv()
        for first, slots in ((0, (2, 4)), (h, (3, 5))):
            total = out[pl.ds((g.side * 4 + g.me // 2) * n + first, h)].astype(f32)
            total += pair[pl.ds((g.me // 2) * n + first, h)].astype(f32)
            for k in slots:
                total += far[k].astype(f32)
            owned[first : first + h] = total


class SmallSum:
    def __init__(self, net, gather, values, along, across, inside):
        self.net, self.g, self.values = net, gather, values
        self.slots = (along, across, inside)
        self.peers = (
            [(gather.me, k) for k in gather.order[1:]],
            [(e, gather.m) for e in gather.plane],
            [(gather.core, gather.m)],
        )
        self.mine = (gather.m, gather.me // 2, gather.side)
        self.open = []

    def send(self, stage):
        slot = self.slots[stage]
        slot[self.mine[stage]] = self.values[...]
        ref = slot.at[self.mine[stage]]
        self.open = [self.net.start(lambda peer=peer: (ref, ref, peer)) for peer in self.peers[stage]]

    def add(self, stage):
        for copy in self.open:
            copy.wait_recv()
        slot = self.slots[stage]
        total = slot[0]
        for k in range(1, slot.shape[0]):
            total += slot[k]
        self.values[...] = total


def number_blocks(owner, table, vector, rank, slot_place, sem):
    lane = lax.broadcasted_iota(jnp.int32, vector.shape, 1)
    count = owner.shape[0]
    owners = jnp.zeros_like(lane)
    for b in range(count):
        owners = jnp.where(lane == b, owner[b], owners)
    ranks = jnp.zeros_like(lane)
    for b in range(count):
        ahead = (owner[b] < owners) | ((owner[b] == owners) & (lane > b))
        ranks += jnp.where(ahead, 1, 0)
    vector[...] = ranks
    copy = pltpu.make_async_copy(vector, rank, sem)
    copy.start()
    copy.wait()
    places = jnp.zeros_like(lane)
    for b in range(count):
        places = jnp.where(lane == rank[0, b], table[b], places)
    vector[...] = places
    copy = pltpu.make_async_copy(vector, slot_place, sem)
    copy.start()
    copy.wait()


def compute_kernel(linked, *refs):
    if linked:
        tokens, cotangent, master, owner, gains = refs[:5]
        block_out, input_grad, owned, small = refs[5:9]
        wg, wo, wu, wd, grads, slots, *pool, pair, far, sum_a, sum_b, sum_c, vector, rank, slot_place, send, recv, free = refs[9:29]
        scratch = refs[29:]
    else:
        tokens, cotangent, base, wg, wo, wu, wd, gains = refs[:8]
        block_out, input_grad, grads, small = refs[8:12]
        scratch = refs[12:]
    (n1, n1t, cot, cott, n2, n2t, forget, admit, cand, state, scan, acc_a, acc_b, mixed, mid, kept, fills, tally, local) = scratch
    dml, dmlt = n2, n2t
    parts, _, hm3 = wg.shape
    hm = hm3 // 3
    fm = wu.shape[2]
    units, table = stack_places(hm, fm)
    act, dup, dpre = mid.at[:, :fm], mid.at[:, fm:], mid.at[:, : 3 * hm]
    gain_one = gains[0:1, :]
    gain_two = gains[1:2, :]

    if linked:
        fetch_master = pltpu.make_async_copy(master, owned, local.at[2])
        fetch_master.start()
    fetch_cot = pltpu.make_async_copy(cotangent, cot, local.at[0])
    fetch_tok = pltpu.make_async_copy(tokens, n1, local.at[1])
    fetch_tok.start()
    fetch_cot.start()

    column_halves = (slice(0, D // 2), slice(D // 2, D))

    def stack(m, first, wide, left, value):
        for r in range(value.shape[0] // BLK):
            for c in range(value.shape[1] // BLK):
                grads[m, first + r * wide + left + c] = value[r * BLK : (r + 1) * BLK, c * BLK : (c + 1) * BLK].astype(bf16)

    def stack_turned(m, first, value):
        high = value.shape[0] // BLK
        for r in range(high):
            for c in range(value.shape[1] // BLK):
                grads[m, first + c * high + r] = value[r * BLK : (r + 1) * BLK, c * BLK : (c + 1) * BLK].astype(bf16)

    def permute_in(src, dst):
        for k in range(D // BLK):
            scan[k] = src[:, k * BLK : (k + 1) * BLK].astype(f32)

        @pl.loop(0, J // 2, unroll=4)
        def _(j):
            for k in range(D // BLK):
                lo = scan[k, pl.ds(2 * j, SUB, stride=J), :]
                hi = scan[k, pl.ds(2 * j + 1, SUB, stride=J), :]
                dst[pl.ds(pl.multiple_of(16 * j, 16), 16), k * BLK : (k + 1) * BLK] = jnp.concatenate([lo, hi], 0).astype(bf16)

    def permute_out(src, dst):
        @pl.loop(0, J, unroll=4)
        def _(j):
            rows = pl.ds(pl.multiple_of(j * SUB, SUB), SUB)
            for k in range(D // BLK):
                scan[k, pl.ds(j, SUB, stride=J), :] = src[rows, k * BLK : (k + 1) * BLK]

        for k in range(D // BLK):
            dst[:, k * BLK : (k + 1) * BLK] = scan[k].astype(dst.dtype)

    def put(first, rows, value):
        for k in range(hm // BLK):
            scan[first + k, rows, :] = value[:, k * BLK : (k + 1) * BLK]

    def take(first, rows):
        return jnp.concatenate([scan[first + k, rows, :] for k in range(hm // BLK)], 1)

    half = hm // BLK

    def spread(v):
        return jnp.broadcast_to(v[None], (R // SUB, SUB, hm)).reshape(R, hm)


    if linked:
        net = Exchange(send, recv)
        gather = Gather(net, fetch_master, owned, slots, pool, (wg, wo, wu, wd), free)
        gather.start(0)
        gather.along_start(1)
        gather.along_start(2)
        reduce = Reduce(net, gather, grads, units, pool)

    def of_turn(t):
        if not linked:
            return t
        high, low = gather.m // 2, gather.m % 2
        t_high, t_low = t // 2, t % 2
        return 2 * (high + t_high - 2 * high * t_high) + low + t_low - 2 * low * t_low

    fetch_tok.wait()
    permute_in(n1, n1)
    mixed[...] = n1[...].astype(f32)

    @pl.loop(0, L // R)
    def _(i):
        rows = pl.ds(pl.multiple_of(i * R, R), R)
        x = mixed[rows, :]
        r = lax.rsqrt(jnp.mean(x * x, axis=-1, keepdims=True) + norm_eps)
        n1[rows, :] = (x * r * gain_one).astype(bf16)

    n1t[...] = n1[...].T

    if linked:
        gather.forward(0)
        gather.along_start(3)
        number_blocks(owner, table, vector, rank, slot_place, local.at[2])
    fetch_cot.wait()
    permute_in(cot, cot)
    if linked:
        gather.start(1)
        gather.pair(0)
        gather.across_start()
        gather.start(2)
    cott[...] = cot[...].T

    fills[0] = jnp.zeros((SUB, hm), f32)
    fills[1] = jnp.ones((SUB, hm), f32)
    tally[0] = fills[0]
    tally[1] = fills[0]

    @pl.loop(0, parts)
    def _(turn):
        m = of_turn(turn)
        if linked:
            for k in range(parts):

                @pl.when(turn == k)
                def _():
                    if k > 1:
                        gather.pair(k)
                    gather.ready(k)
                    gather.place(k, rank)

        forget[m] = dot(n1[...], wg[m, :, :hm])
        admit[m] = dot(n1[...], wg[m, :, hm : 2 * hm])
        cand[m] = dot(n1[...], wg[m, :, 2 * hm :])

        if linked:

            @pl.when(turn == 2)
            def _():
                gather.forward(3)

        @pl.loop(0, L // R)
        def _(i):
            rows = pl.ds(pl.multiple_of(i * R, R), R)
            f = sigmoid(forget[m, rows, :])
            a = sigmoid(admit[m, rows, :])
            inv = recip(f + a)
            forget[m, rows, :] = f
            admit[m, rows, :] = a
            kept[rows, :] = f * inv
            put(0, rows, a * inv * cand[m, rows, :])

        def step(j, carry):
            s, p, k_sum, kj_sum = carry
            rows = pl.ds(pl.multiple_of(j * SUB, SUB), SUB)
            keep = kept[rows, :]
            s = keep * s + take(0, rows)
            p = keep * p
            put(0, rows, s)
            put(half, rows, p)
            return s, p, k_sum + keep, kj_sum + keep * j.astype(f32)

        s, p, k_sum, kj_sum = lax.fori_loop(0, J, step, (fills[0], fills[1], fills[0], fills[0]), unroll=16)
        tally[0] += k_sum
        tally[1] += kj_sum
        enter = fills[0]
        for _ in range(SUB - 1):
            enter = shift_down(s + p * enter)

        @pl.loop(0, L // R)
        def _(i):
            rows = pl.ds(pl.multiple_of(i * R, R), R)
            state[m, pl.ds(pl.multiple_of(i * R + SUB, SUB), R), :] = take(0, rows) + take(half, rows) * spread(enter)

        state[m, :SUB, :] = shift_down(state[m, L:, :])
        for cols in column_halves:
            mixed[:, cols] += dot(state[m, SUB:, :].astype(bf16), wo[m, :, cols])
        if linked:

            @pl.when(turn == 0)
            def _():
                gather.pair(1)
                gather.forward(2)
                gather.start(3)

    if linked:
        net.drain()
        gather.done()

    @pl.loop(0, L // R)
    def _(i):
        rows = pl.ds(pl.multiple_of(i * R, R), R)
        x = mixed[rows, :]
        r = lax.rsqrt(jnp.mean(x * x, axis=-1, keepdims=True) + norm_eps)
        n2[rows, :] = (x * r * gain_two).astype(bf16)
        acc_a[rows, :] = x
        acc_b[rows, :] = jnp.zeros_like(x)

    n2t[...] = n2[...].T

    @pl.loop(0, parts)
    def _(turn):
        m = of_turn((2 * (turn // 2 + turn % 2 - 2 * (turn // 2) * (turn % 2)) + turn // 2) if linked else turn)
        for first in range(0, fm, fm // 2):
            units_of = slice(first, first + fm // 2)
            up = dot(n2[...], wu[m, :, units_of])
            da = dot(cot[...], wd[m, units_of, :], True)
            cdf, xpdf = gelu_terms(up)
            act[:, units_of] = (up * cdf).astype(bf16)
            dup[:, units_of] = (da * (cdf + xpdf)).astype(bf16)
            if linked and first == 0:

                @pl.when(turn == 2)
                def _():
                    reduce.plane(UPDOWN, 2)

                @pl.when(turn == 3)
                def _():
                    reduce.plane(UPDOWN, 3)
                    reduce.model(UPDOWN, 2)

        for cols in column_halves:
            acc_a[:, cols] += dot(act[...], wd[m, :, cols])
        for cols in column_halves:
            acc_b[:, cols] += dot(dup[...], wu[m, cols, :], True)
        for c in range(0, fm, fm // 2):
            part = slice(c, c + fm // 2)
            stack(m, 0, fm // BLK, c // BLK, dot(n2t[...], dup[:, part]))
        for c in range(0, fm, fm // 2):
            part = slice(c, c + fm // 2)
            stack_turned(m, units[UPDOWN][1] // 2 + c // BLK * (D // BLK), dot(cott[...], act[:, part]))
        if linked:

            @pl.when(turn == 1)
            def _():
                gather.all_done()
                reduce.chip(UPDOWN, 2)

            @pl.when(turn == 2)
            def _():
                reduce.chip(UPDOWN, 3)
                reduce.turn(UPDOWN, 2)

            @pl.when(turn == 3)
            def _():
                reduce.chip(UPDOWN, 1)
                reduce.turn(UPDOWN, 3)

    gain_sum_two = jnp.zeros((1, D), f32)

    def back_two(i, total):
        rows = pl.ds(pl.multiple_of(i * R, R), R)
        x = mixed[rows, :]
        r = lax.rsqrt(jnp.mean(x * x, axis=-1, keepdims=True) + norm_eps)
        dn = acc_b[rows, :]
        q = dn * gain_two
        d = cot[rows, :].astype(f32) + r * q - r * r * r * x * jnp.mean(q * x, axis=-1, keepdims=True)
        mixed[rows, :] = d
        dml[rows, :] = d.astype(bf16)
        acc_b[rows, :] = jnp.zeros_like(d)
        return total + jnp.sum(dn * x * r, axis=0, keepdims=True)

    gain_sum_two = lax.fori_loop(0, L // R, back_two, gain_sum_two)
    if linked:
        reduce.plane(UPDOWN, 1)
        reduce.model(UPDOWN, 3)
    dmlt[...] = dml[...].T
    fetch_tok = pltpu.make_async_copy(tokens, cot, local.at[1])
    fetch_tok.start()

    @pl.loop(0, parts)
    def _(m):
        stack_turned(m, units[OUT][0], dot(dmlt[...], state[m, SUB:, :].astype(bf16)))

    if linked:
        for i in (3, 2, 1):
            reduce.chip(OUT, i)

    def keeps(m, rows):
        f = forget[m, rows, :]
        kept[rows, :] = f * recip(f + admit[m, rows, :])

    def state_grads(m):
        put(0, slice(None), dot(dml[...], wo[m], True))

    state_grads(of_turn(parts - 1))

    @pl.loop(0, L // R)
    def _(i):
        keeps(of_turn(parts - 1), pl.ds(pl.multiple_of(i * R, R), R))

    @pl.loop(0, parts)
    def _(back_turn):
        turn = parts - 1 - back_turn
        m = of_turn(turn)
        m_next = of_turn((turn + parts - 1) % parts)

        def step(k, carry):
            u, p, keep_next = carry
            j = J - 1 - k
            rows = pl.ds(pl.multiple_of(j * SUB, SUB), SUB)
            u = take(0, rows) + keep_next * u
            p = keep_next * p
            put(0, rows, u)
            put(half, rows, p)
            return u, p, kept[rows, :]

        u, p, keep_first = lax.fori_loop(0, J, step, (fills[0], fills[1], fills[1]), unroll=16)
        enter = fills[0]
        for _ in range(SUB - 1):
            enter = shift_up(keep_first * (u + p * enter))

        if linked:

            @pl.when(turn == 3)
            def _():
                for i in (3, 2, 1):
                    reduce.plane(OUT, i)
                reduce.model(UPDOWN, 1)

            for k in (2, 1, 0):

                @pl.when(turn == k)
                def _():
                    reduce.plane(GATE, k + 1)

        @pl.loop(0, L // R)
        def _(i):
            rows = pl.ds(pl.multiple_of(i * R, R), R)
            carried = take(0, rows) + take(half, rows) * spread(enter)
            f = forget[m, rows, :]
            a = admit[m, rows, :]
            adm = a * recip(f + a)
            g = carried * (state[m, rows, :] - cand[m, rows, :]) * (kept[rows, :] * adm)
            dpre[rows, :hm] = (g * (1.0 - f)).astype(bf16)
            dpre[rows, hm : 2 * hm] = (g * (a - 1.0)).astype(bf16)
            dpre[rows, 2 * hm :] = (carried * adm).astype(bf16)
            keeps(m_next, rows)

        if linked:

            @pl.when(turn == 2)
            def _():
                for i in (3, 2, 1):
                    reduce.model(OUT, i)

            @pl.when(turn == 1)
            def _():
                reduce.model(GATE, 3)

            @pl.when(turn == 0)
            def _():
                reduce.model(GATE, 2)

        for k in range(3):
            stack(m, units[GATE][0], 3 * hm // BLK, k * hm // BLK, dot(n1t[...], dpre[:, k * hm : (k + 1) * hm]))
        for cols in column_halves:
            acc_b[:, cols] += dot(dpre[...], wg[m, cols, :], True)
        state_grads(m_next)
        if linked:
            for k in (3, 2, 1):

                @pl.when(turn == k)
                def _():
                    reduce.chip(GATE, k)
                    if k == 3:
                        reduce.turn(OUT, 3)
                        reduce.turn(OUT, 2)
                    else:
                        reduce.turn(GATE, k + 1)

    if linked:
        reduce.own(UPDOWN)
        reduce.own(OUT)
        reduce.model(GATE, 1)

    fetch_tok.wait()
    permute_in(cot, cot)
    def back_one(i, total):
        rows = pl.ds(pl.multiple_of(i * R, R), R)
        x = cot[rows, :].astype(f32)
        r = lax.rsqrt(jnp.mean(x * x, axis=-1, keepdims=True) + norm_eps)
        dn = acc_b[rows, :]
        q = dn * gain_one
        mixed[rows, :] += r * q - r * r * r * x * jnp.mean(q * x, axis=-1, keepdims=True)
        return total + jnp.sum(dn * x * r, axis=0, keepdims=True)

    gain_sum_one = lax.fori_loop(0, L // R, back_one, jnp.zeros((1, D), f32))

    permute_out(acc_a, n1)
    push_out = pltpu.make_async_copy(n1, block_out, local.at[0])
    push_out.start()

    place = lax.broadcasted_iota(jnp.int32, (SUB, hm), 0).astype(f32) * float(J)
    if linked:
        first = ((gather.me * parts + gather.m) * L + 1).astype(f32)
        token_total = float(L * parts * lax.axis_size("dp"))
    else:
        first = base[0]
        token_total = base[1]
    forget_sum = jnp.sum(tally[1] + tally[0] * (place + first), axis=0, keepdims=True) / token_total
    small[...] = jnp.zeros_like(small)
    small[0:1, :] = gain_sum_one
    small[1:2, :] = gain_sum_two
    small[2:3, :hm] = forget_sum
    if linked:
        flat = units[UPDOWN][1] // 2, units[GATE][0]
        count = owned.shape[0]
        flags = []
        for k in range(count):
            spot = slot_place[0, gather.me * count + k]
            flags.append(jnp.where((spot >= flat[0]) & (spot < flat[1]), 1.0, 0.0).astype(f32))

    if linked:
        tiny = SmallSum(net, gather, small, sum_a, sum_b, sum_c)
        tiny.send(0)
        reduce.own(GATE)
        reduce.slots_chip(slots, slot_place, pair)
        tiny.add(0)
        tiny.send(1)
        reduce.slots_plane(slots, pair, far)

    permute_out(mixed, acc_a)
    push_grad = pltpu.make_async_copy(acc_a, input_grad, local.at[2])
    push_grad.start()

    if linked:
        tiny.add(1)
        tiny.send(2)
        reduce.slots_end(slots, pair, far, owned)
        tiny.add(2)
        for k, flag in enumerate(flags):
            small[3 + k // 4 : 4 + k // 4, (k % 4) * BLK : (k % 4 + 1) * BLK] = jnp.full((1, BLK), flag, f32)
        net.drain()
    push_out.wait()
    push_grad.wait()


def compute(tokens, cotangent, gains, weights=None, base=None, master=None, owner=None):
    linked = weights is None
    parts = lax.axis_size("mp")
    hm, fm = H // parts, FF // parts
    stacked = (parts, D * (4 * hm + 2 * fm) // BLK**2, BLK, BLK)
    sds = jax.ShapeDtypeStruct
    vm, sm, hbm = (pl.BlockSpec(memory_space=k) for k in (pltpu.VMEM, pltpu.SMEM, pl.ANY))
    if linked:
        n = owner.shape[0]
        args = (tokens, cotangent, master, owner, gains)
        in_specs = [hbm, hbm, hbm, sm, vm]
        middle = sds((n // 8, BLK, BLK), f32)
        extra = [
            pltpu.VMEM((parts, D, 3 * hm), bf16),
            pltpu.VMEM((parts, hm, D), bf16),
            pltpu.VMEM((parts, D, fm), bf16),
            pltpu.VMEM((parts, fm, D), bf16),
            pltpu.VMEM(stacked, bf16),
            pltpu.VMEM((n, BLK, BLK), bf16),
            *[pltpu.VMEM((n, BLK, BLK), bf16) for _ in range(parts - 1)],
            pltpu.VMEM((n // 2, BLK, BLK), bf16),
            pltpu.VMEM((6, n // 16, BLK, BLK), bf16),
            pltpu.VMEM((parts, 8, D), f32),
            pltpu.VMEM((4, 8, D), f32),
            pltpu.VMEM((2, 8, D), f32),
            pltpu.VMEM((8, BLK), jnp.int32),
            pltpu.SMEM((8, BLK), jnp.int32),
            pltpu.SMEM((8, BLK), jnp.int32),
            pltpu.SemaphoreType.DMA((128,)),
            pltpu.SemaphoreType.DMA((128,)),
            pltpu.SemaphoreType.REGULAR,
        ]
        params = dict(collective_id=0, has_side_effects=True)
    else:
        args = (tokens, cotangent, base, *weights, gains)
        in_specs = [hbm, hbm, sm] + [vm] * 5
        middle = sds(stacked, bf16)
        extra = []
        params = {}
    return pl.pallas_call(
        functools.partial(compute_kernel, linked),
        out_shape=(sds((L, D), bf16), sds((L, D), f32), middle, sds((8, D), f32)),
        in_specs=in_specs,
        out_specs=[hbm, hbm, vm, vm],
        scratch_shapes=extra
        + [pltpu.VMEM(shape, bf16) for shape in ((L, D), (D, L)) * 3]
        + [pltpu.VMEM((parts, L, hm), f32)] * 3
        + [pltpu.VMEM((parts, L + SUB, hm), f32)]
        + [pltpu.VMEM((2 * hm // BLK, L, BLK), f32)]
        + [pltpu.VMEM((L, D), f32)] * 3
        + [
            pltpu.VMEM((L, 2 * fm), bf16),
            pltpu.VMEM((L, hm), f32),
            pltpu.VMEM((2, SUB, hm), f32),
            pltpu.VMEM((2, SUB, hm), f32),
            pltpu.SemaphoreType.DMA((3,)),
        ],
        compiler_params=pltpu.CompilerParams(vmem_limit_bytes=64 * 2**20 - 2**16, **params),
        name="block",
    )(*args)


def adam_update(first_old, second_old, gradient):
    first_new = beta_one * first_old + (1.0 - beta_one) * gradient
    second_new = beta_two * second_old + (1.0 - beta_two) * gradient * gradient
    first_hat = first_new / (1.0 - beta_one**STEP)
    second_hat = second_new / (1.0 - beta_two**STEP)
    return (first_new, second_new, first_hat / (jnp.sqrt(second_hat) + adam_eps))


def fine_dot(a, b, trans_b=False):
    a_high, b_high = a.astype(bf16), b.astype(bf16)
    a_low, b_low = (a - a_high.astype(f32)).astype(bf16), (b - b_high.astype(f32)).astype(bf16)
    return dot(a_high, b_high, trans_b) + (dot(a_high, b_low, trans_b) + dot(a_low, b_high, trans_b))


def update_kernel(token_total, passed, sums, gains, gain_moment_one, gain_moment_two, *refs):
    sources, refs = refs[:6], refs[6:]
    given, refs = refs[:passed], refs[passed:]
    results, refs = refs[:4], refs[4:]
    gain_first, gain_second, gains_new, forget_mean = refs[:4]
    copied, refs = refs[4 : 4 + passed], refs[4 + passed :]
    held, made, made_low, sem_in, sem_out, sem_pass = refs[:6]
    passage = refs[6:]
    count = held.shape[1]
    step = max(count // 2, 1)
    groups = [slice(first, first + step) for first in range(0, count, step)]
    enter = [pltpu.make_async_copy(src, via, sem_pass.at[0, k]) for k, (src, via) in enumerate(zip(given, passage))]
    leave = [pltpu.make_async_copy(via, dst, sem_pass.at[1, k]) for k, (via, dst) in enumerate(zip(passage, copied))]
    fetch = [
        [pltpu.make_async_copy(src.at[group], held.at[k, group], sem_in.at[g, k]) for k, src in enumerate(sources)]
        for g, group in enumerate(groups)
    ]
    for copy in fetch[0]:
        copy.start()
    for copy in enter:
        copy.start()
    for row in fetch[1:]:
        for copy in row:
            copy.start()
    first, second, direction = adam_update(gain_moment_one[...], gain_moment_two[...], sums[0:2, :])
    gain_first[...] = first
    gain_second[...] = second
    gains_new[...] = gains[...] - gain_rate * direction
    forget_mean[...] = jnp.sum(sums[2:3, :], axis=1, keepdims=True) * (1.0 / (H * (token_total + 1) / 2.0))
    push = []
    for g, group in enumerate(groups):
        blocks = range(group.start, group.stop)
        for copy in fetch[g]:
            copy.wait()
        if g == len(groups) - 1:
            for come, go in zip(enter, leave):
                come.wait()
                go.start()
        grads = []
        for s in blocks:
            grad = held[0, s]
            flag = sums[3 + s // 4 : 4 + s // 4, (s % 4) * BLK : (s % 4 + 1) * BLK]
            grads.append(jnp.where(flag > 0.5, grad.T, grad))
        values = [fine_dot(held[1, s].T, grad) for s, grad in zip(blocks, grads)]
        values = [fine_dot(value, held[2, s]) for s, value in zip(blocks, values)]
        for k, s in enumerate(blocks):
            first, second, values[k] = adam_update(held[3, s], held[4, s], values[k])
            made[0, s] = first
            made[1, s] = second
        values = [fine_dot(held[1, s], value) for s, value in zip(blocks, values)]
        values = [fine_dot(value, held[2, s], True) for s, value in zip(blocks, values)]
        for s, value in zip(blocks, values):
            fresh = held[5, s] - learn_rate * (value + weight_decay * held[5, s])
            made[2, s] = fresh
            made_low[s] = fresh.astype(bf16)
        for k, dst in enumerate(results):
            src = made.at[k, group] if k < 3 else made_low.at[group]
            copy = pltpu.make_async_copy(src, dst.at[group], sem_out.at[g, k])
            copy.start()
            push.append(copy)
    for copy in push + leave:
        copy.wait()


def update(token_total, small, large, passed):
    sds = jax.ShapeDtypeStruct
    blocks, gain = large[0].shape, small[1].shape
    vm, hbm = pl.BlockSpec(memory_space=pltpu.VMEM), pl.BlockSpec(memory_space=pl.ANY)
    return pl.pallas_call(
        functools.partial(update_kernel, token_total, len(passed)),
        out_shape=[sds(blocks, f32)] * 3
        + [sds(blocks, bf16)]
        + [sds(gain, f32)] * 3
        + [sds((1, 1), f32)]
        + [sds(v.shape, v.dtype) for v in passed],
        in_specs=[vm] * 4 + [hbm] * (len(large) + len(passed)),
        out_specs=[hbm] * 4 + [vm] * 4 + [hbm] * len(passed),
        scratch_shapes=[
            pltpu.VMEM((6, *blocks), f32),
            pltpu.VMEM((3, *blocks), f32),
            pltpu.VMEM(blocks, bf16),
            pltpu.SemaphoreType.DMA((2, 6)),
            pltpu.SemaphoreType.DMA((2, 4)),
            pltpu.SemaphoreType.DMA((2, len(passed))),
        ]
        + [pltpu.VMEM(v.shape, v.dtype) for v in passed],
        compiler_params=pltpu.CompilerParams(vmem_limit_bytes=56 * 2**20),
        name="update",
    )(*small, *large, *passed)


def on_device(
    tokens,
    cotangent,
    master,
    moment_one,
    moment_two,
    basis_left,
    basis_right,
    owner,
    gains,
    gain_moment_one,
    gain_moment_two,
):
    parts = lax.axis_size("mp")
    data_parts = lax.axis_size("dp")
    hm, fm = H // parts, FF // parts
    token_total = L * data_parts * parts
    row_tiles, cols, lows = D // BLK, (3 * hm + fm) // BLK, (hm + fm) // BLK
    if data_parts == 8 and parts == 4:
        block_out, input_grad, owned, sums = compute(tokens, cotangent, gains, master=master[0], owner=owner)
    else:
        number = jnp.arange(owner.shape[0], dtype=jnp.int32)
        ahead = (owner[None, :] < owner[:, None]) | ((owner[None, :] == owner[:, None]) & (number[None, :] < number[:, None]))
        block_rank = jnp.sum(ahead.astype(jnp.int32), axis=1)
        _, table = stack_places(hm, fm)
        table = jnp.asarray(table, jnp.int32)
        slot_place = jnp.sum(jnp.where(block_rank[None, :] == number[:, None], table[None, :], 0), axis=1)
        stored = lax.all_gather(master.astype(bf16), "dp", axis=1, tiled=True)
        stored = lax.all_gather(stored, "mp", axis=0, tiled=True)
        stack = stored[:, block_rank]
        upper = stack[:, : row_tiles * cols].reshape(parts, row_tiles, cols, BLK, BLK)
        upper = upper.transpose(0, 1, 3, 2, 4).reshape(parts, D, cols * BLK)
        lower = stack[:, row_tiles * cols :].reshape(parts, lows, row_tiles, BLK, BLK)
        lower = lower.transpose(0, 1, 3, 2, 4).reshape(parts, lows * BLK, D)
        weights = (upper[:, :, : 3 * hm], lower[:, :hm], upper[:, :, 3 * hm :], lower[:, hm:])
        first = ((lax.axis_index("dp") * parts + lax.axis_index("mp")) * L + 1).astype(f32)
        base = jnp.stack([first, jnp.asarray(token_total, f32)])
        block_out, input_grad, grads, sums = compute(tokens, cotangent, gains, weights=weights, base=base)
        owned = lax.psum_scatter(grads[:, slot_place].astype(f32), "dp", scatter_dimension=1, tiled=True)
        owned = lax.psum_scatter(owned, "mp", scatter_dimension=0, tiled=True)[0]
        sums = lax.psum(sums, ("dp", "mp"))
        count = master.shape[1]
        mine = lax.dynamic_slice_in_dim(slot_place, lax.axis_index("dp") * count, count)
        units, _ = stack_places(hm, fm)
        flags = ((mine >= units[UPDOWN][1] // 2) & (mine < units[GATE][0])).astype(f32)
        flags = jnp.pad(jnp.repeat(flags, BLK), (0, (8 - count) * BLK)).reshape(2, 4 * BLK)
        sums = jnp.concatenate([sums[:3], flags, sums[5:]])
    outs = update(
        token_total,
        (sums, gains, gain_moment_one, gain_moment_two),
        (owned, basis_left[0], basis_right[0], moment_one[0], moment_two[0], master[0]),
        (block_out, input_grad),
    )
    first_new, second_new, master_new, master_low, gain_first, gain_second, gains_new, forget_mean = outs[:8]
    block_out, input_grad = outs[8:]
    return (
        block_out,
        input_grad,
        first_new[None],
        second_new[None],
        master_new[None],
        master_low[None],
        gain_first,
        gain_second,
        gains_new,
        forget_mean[0, 0],
    )


def solution(mesh):
    rows, blocks = P(("dp", "mp"), None), P("mp", "dp", None, None)
    return jax.shard_map(
        on_device,
        mesh=mesh,
        in_specs=(rows, rows, blocks, blocks, blocks, blocks, blocks, P(), P(), P(), P()),
        out_specs=(rows, rows, blocks, blocks, blocks, blocks, P(), P(), P(), P()),
        check_vma=False,
    )
```

```python
import functools

import jax
import jax.numpy as jnp
from jax import lax
from jax.experimental import pallas as pl
from jax.experimental.pallas import tpu as pltpu
from jax.sharding import PartitionSpec as P

D = 512
H = 1024
FF = 2048
BLK = 128
STEP = 10
L = 1024

norm_eps = 1e-05
beta_one = 0.5
beta_two = 0.5
adam_eps = 1e-08
learn_rate = 0.02
gain_rate = 0.1
weight_decay = 0.1
highest = lax.Precision.HIGHEST

f32 = jnp.float32
bf16 = jnp.bfloat16
SUB = 8
J = L // SUB
R = 256


def dot(a, b, trans_b=False):
    dims = (((1,), (1,)), ((), ())) if trans_b else (((1,), (0,)), ((), ()))
    return lax.dot_general(a, b, dims, preferred_element_type=f32)


def recip(v):
    return pltpu.reciprocal(v, approx=True)


def sigmoid(v):
    return recip(1.0 + jnp.exp(-v))


def shift_down(v):
    rolled = pltpu.roll(v, 1, 0)
    row = lax.broadcasted_iota(jnp.int32, v.shape, 0)
    return jnp.where(row == 0, 0.0, rolled)


def shift_up(v):
    rolled = pltpu.roll(v, SUB - 1, 0)
    row = lax.broadcasted_iota(jnp.int32, v.shape, 0)
    return jnp.where(row == SUB - 1, 0.0, rolled)


def gelu_terms(x):
    a = jnp.abs(x)
    t = recip(1.0 + a * (0.3275911 * 0.7071067811865476))
    poly = t * (
        0.5 * 0.254829592
        + t
        * (
            0.5 * -0.284496736
            + t * (0.5 * 1.421413741 + t * (0.5 * -1.453152027 + t * (0.5 * 1.061405429)))
        )
    )
    e = jnp.exp(x * x * -0.5)
    tail = poly * e
    cdf = jnp.where(x < 0.0, tail, 1.0 - tail)
    return cdf, x * e * 0.3989422804014327


MESH = pl.DeviceIdType.MESH


class Copy:
    def __init__(self, net, make):
        self.net, self.make = net, make

    def start(self):
        self.net.open.append(self)
        self.make().start()
        return self

    def wait_recv(self):
        self.make().wait_recv()

    def wait_send(self):
        self.make().wait_send()


class Exchange:
    def __init__(self, send, recv):
        self.send, self.recv, self.known, self.used, self.open = send, recv, {}, 0, []

    def copy(self, parts, key=None):
        if key in self.known:
            return self.known[key]
        k = self.used
        self.used += 1

        def make():
            src, dst, device = parts()
            return pltpu.make_async_remote_copy(
                src_ref=src,
                dst_ref=dst,
                send_sem=self.send.at[k],
                recv_sem=self.recv.at[k],
                device_id=device,
                device_id_type=MESH,
            )

        copy = Copy(self, make)
        if key is not None:
            self.known[key] = copy
        return copy

    def start(self, parts):
        return self.copy(parts).start()

    def drain(self):
        for copy in self.open:
            copy.wait_send()
        self.open = []


class Gather:
    def __init__(self, net, fetch, master, slots, pool, weights, free):
        self.net, self.weights, self.free = net, weights, free
        self.held = [slots, *pool]
        d, m = lax.axis_index("dp"), lax.axis_index("mp")
        core, col, row = d % 2, (d // 2) % 2, d // 4
        self.me, self.m, self.side = d, m, core
        self.core = d + 1 - 2 * core
        self.plane = [d + 2 - 4 * col, d + 4 - 8 * row, d + 6 - 4 * col - 8 * row]
        self.order = [m, m + 1 - 2 * (m % 2), m + 2 - 4 * (m // 2), 3 - m]
        self.peers = [(e, m) for e in [self.core] + self.plane] + [(d, k) for k in self.order[1:]]
        barrier = pltpu.get_barrier_semaphore()
        for device in self.peers:
            pl.semaphore_signal(barrier, inc=1, device_id=device, device_id_type=MESH)
        self.n = master.shape[0]
        fetch.wait()
        for s in range(self.n):
            slots[d * self.n + s] = master[s].astype(bf16)
        pl.semaphore_wait(barrier, len(self.peers))

    def rows(self, i, e, first, count):
        return self.held[i].at[pl.ds(e * self.n + first, count)]

    def along(self, i, e):
        return self.net.copy(
            lambda: (self.rows(0, e, 0, self.n), self.rows(i, e, 0, self.n), (self.me, self.order[i])),
            ("along", i, e is self.me),
        )

    def within(self, key, i, e, first, count, to):
        return self.net.copy(
            lambda: (self.rows(i, e, first, count), self.rows(i, e, first, count), (to, self.m)), (key, i)
        )

    def first(self, i):
        (x, y, _), h = self.plane, self.n // 2
        if i == 1:
            jobs = ((0, self.n, x), (0, self.n, y))
        else:
            jobs = ((0, h, x), (h, h, y), (h, h, x), (0, h, y))
        return [self.within(("first", k), i, self.me, *job) for k, job in enumerate(jobs)]

    def last(self, i):
        x, y, z = self.plane
        if i == 1:
            return [self.along(1, z)]
        h = self.n // 2
        return [self.within("over y", i, x, 0, h, y), self.within("over x", i, y, h, h, x)]

    def inside(self, i):
        return [self.within(("inside", k), i, e, 0, self.n, self.core) for k, e in enumerate([self.me] + self.plane)]

    def along_start(self, i):
        self.along(i, self.me).start()

    def across_start(self):
        self.last(1)[0].start()

    def start(self, i):
        if i:
            self.along(i, self.me).wait_recv()
        for copy in self.first(i):
            copy.start()
        self.inside(i)[0].start()

    def forward(self, i):
        if i == 1:
            return
        for came, copy in zip(self.first(i), self.last(i)):
            came.wait_recv()
            copy.start()

    def pair(self, i):
        for came, copy in zip(self.first(i)[-2:], self.inside(i)[1:3]):
            came.wait_recv()
            copy.start()
        for came in self.last(i):
            came.wait_recv()
        self.inside(i)[3].start()

    def ready(self, i):
        for copy in self.inside(i):
            copy.wait_recv()

    def place(self, i, rank):
        wg, wo, wu, wd = self.weights
        row_tiles, gates = D // BLK, wg.shape[2] // BLK
        cols, outs = gates + wu.shape[2] // BLK, wo.shape[1] // BLK
        for b in range(row_tiles * cols + (wo.shape[1] + wd.shape[1]) // BLK * row_tiles):
            if b < row_tiles * cols:
                r, c = b // cols, b % cols
                ref = wg if c < gates else wu
                c -= 0 if c < gates else gates
            else:
                r, c = (b - row_tiles * cols) // row_tiles, (b - row_tiles * cols) % row_tiles
                ref = wo if r < outs else wd
                r -= 0 if r < outs else outs
            block = self.held[i][rank[0, b]]
            ref[self.order[i], r * BLK : (r + 1) * BLK, c * BLK : (c + 1) * BLK] = block

    def done(self):
        for device in self.peers:
            pl.semaphore_signal(self.free, inc=1, device_id=device, device_id_type=MESH)

    def all_done(self):
        pl.semaphore_wait(self.free, len(self.peers))


def stack_places(hm, fm):
    row_tiles, gates, ups, outs = D // BLK, 3 * hm // BLK, fm // BLK, hm // BLK
    cols = gates + ups
    first_down = row_tiles * ups
    first_out = 2 * first_down
    first_gate = first_out + row_tiles * outs
    table = []
    for b in range(row_tiles * (cols + outs + ups)):
        if b < row_tiles * cols:
            r, c = b // cols, b % cols
            table.append(first_gate + r * gates + c if c < gates else r * ups + c - gates)
        else:
            k = b - row_tiles * cols
            table.append(first_out + k if k < row_tiles * outs else first_down + k - row_tiles * outs)
    return ((0, first_out), (first_out, row_tiles * outs), (first_gate, row_tiles * gates)), table


UPDOWN, OUT, GATE = range(3)


class Reduce:
    def __init__(self, net, gather, grads, units, pool):
        self.net, self.g, self.grads, self.units, self.pool = net, gather, grads, units, pool
        self.half = grads.shape[1] // 2
        self.eighth = grads.shape[1] // 8

    def place(self, e):
        return (e % 2) * 4 + e // 2

    def inside(self, unit, i):
        g, (first, count) = self.g, self.units[unit]
        return self.net.copy(
            lambda: (
                self.grads.at[g.order[i], pl.ds(first + (1 - g.side) * (count // 2), count // 2)],
                self.pool[i - 1].at[pl.ds(first // 2, count // 2)],
                (g.core, g.m),
            ),
            ("chip", unit, i),
        )

    def chip(self, unit, i):
        self.inside(unit, i).start()

    def spot(self, unit, i, slot, first, count):
        base, total = self.units[unit]
        return self.pool[i - 1].at[pl.ds(self.half + slot * self.eighth + base // 8 + first, count)]

    def parts(self, unit, i):
        n = self.units[unit][1] // 8
        if i == 1:
            return ((0, n),)
        h = (n + i % 2) // 2 if n % 2 else n // 2
        return (0, h), (h, n - h)

    def share(self, unit, i, e, first, count):
        base, total = self.units[unit]
        return self.grads.at[self.g.order[i], pl.ds(base + self.place(e) * (total // 8) + first, count)]

    def over(self, unit, i, slot, part):
        x, y, z = self.g.plane
        e = (z, x, y)[slot]
        to = (x if part == self.parts(unit, i)[0] else y, x, y)[slot]
        return self.net.copy(
            lambda: (self.share(unit, i, e, *part), self.spot(unit, i, slot, *part), (to, self.g.m)),
            ("over", unit, i, slot, part),
        )

    def send(self, unit, i, slot, part):
        if part[1]:
            self.over(unit, i, slot, part).start()

    def take(self, unit, i, slot, part):
        self.over(unit, i, slot, part).wait_recv()
        return self.spot(unit, i, slot, *part)[...].astype(f32)

    def model_copy(self, unit, i):
        n = self.units[unit][1] // 8
        return self.net.copy(
            lambda: (self.share(unit, i, self.g.me, 0, n), self.spot(unit, i, 3, 0, n), (self.g.me, self.g.order[i])),
            ("model", unit, i),
        )

    def aside(self, unit):
        part = (0, self.units[unit][1] // 8)
        return self.net.copy(
            lambda: (
                self.share(unit, 1, self.g.plane[2], *part),
                self.spot(unit, 1, 0, *part),
                (self.g.me, self.g.order[1]),
            ),
            ("aside", unit),
        )

    def plane(self, unit, i):
        g, (first, count) = self.g, self.units[unit]
        x, y, z = g.plane
        self.inside(unit, i).wait_recv()
        m = g.order[i]
        start, came = first + g.side * (count // 2), self.pool[i - 1]

        @pl.loop(0, count // 2)
        def _(b):
            total = self.grads[m, start + b].astype(f32) + came[first // 2 + b].astype(f32)
            self.grads[m, start + b] = total.astype(bf16)

        if i == 1:
            (whole,) = self.parts(unit, i)
            self.send(unit, i, 1, whole)
            self.send(unit, i, 2, whole)
            self.aside(unit).start()
            return
        one, two = self.parts(unit, i)
        self.send(unit, i, 0, one)
        self.send(unit, i, 0, two)
        self.send(unit, i, 1, one)
        self.send(unit, i, 2, two)

    def turn(self, unit, i):
        if i == 1:
            return
        x, y, _ = self.g.plane
        for part, slot, e in zip(self.parts(unit, i), (2, 1), (y, x)):
            if part[1]:
                ref = self.share(unit, i, e, *part)
                ref[...] = (ref[...].astype(f32) + self.take(unit, i, 0, part)).astype(bf16)
                self.send(unit, i, slot, part)

    def model(self, unit, i):
        g, (first, count) = self.g, self.units[unit]
        n = count // 8
        for part in self.parts(unit, i):
            if part[1]:
                ref = self.share(unit, i, g.me, *part)
                total = ref[...].astype(f32) + self.take(unit, i, 1, part) + self.take(unit, i, 2, part)
                ref[...] = total.astype(bf16)
        self.model_copy(unit, i).start()

    def own(self, unit):
        g, (first, count) = self.g, self.units[unit]
        n = count // 8
        rows = pl.ds(first + self.place(g.me) * n, n)
        total = self.grads[g.m, rows].astype(f32)
        for i in (1, 2, 3):
            self.model_copy(unit, i).wait_recv()
            total += self.pool[i - 1][pl.ds(self.half + 3 * self.eighth + first // 8, n)].astype(f32)
        self.grads[g.m, rows] = total.astype(bf16)
        self.aside(unit).wait_recv()
        rows = pl.ds(first + self.place(g.plane[2]) * n, n)
        total = self.grads[g.m, rows].astype(f32) + self.spot(unit, 1, 0, 0, n)[...].astype(f32)
        self.grads[g.m, rows] = total.astype(bf16)

    def into_slots(self, out, slot_place, e):
        n = self.eighth
        for k in range(n):
            out[self.place(e) * n + k] = self.grads[self.g.m, slot_place[0, e * n + k]]

    def slots_chip(self, out, slot_place, pair):
        g, n = self.g, self.eighth
        self.last = []
        targets = (g.plane[2], g.plane[0], g.plane[1], g.me)
        for e in targets:
            other = e + 1 - 2 * g.side
            self.into_slots(out, slot_place, other)
            self.last.append(
                self.net.start(
                    lambda e=e, other=other: (
                        out.at[pl.ds(self.place(other) * n, n)],
                        pair.at[pl.ds((e // 2) * n, n)],
                        (g.core, g.m),
                    )
                )
            )
        for e in targets:
            self.into_slots(out, slot_place, e)

    def slots_plane(self, out, pair, far):
        g, n = self.g, out.shape[0] // 8
        h = n // 2
        x, y, z = g.plane
        wait = dict(zip("zxyo", self.last))

        def mine(e, first, count):
            return pl.ds((g.side * 4 + e // 2) * n + first, count)

        def join(e):
            rows = mine(e, 0, n)
            out[rows] = (out[rows].astype(f32) + pair[pl.ds((e // 2) * n, n)].astype(f32)).astype(bf16)

        def send(e, first, slot, to):
            return self.net.start(lambda: (out.at[mine(e, first, h)], far.at[slot], (to, g.m)))

        wait["z"].wait_recv()
        join(z)
        over_x = send(z, 0, 0, x)
        over_y = send(z, h, 1, y)
        wait["x"].wait_recv()
        join(x)
        self.ends = [send(x, 0, 2, x)]
        wait["y"].wait_recv()
        join(y)
        self.ends.append(send(y, h, 3, y))
        over_x.wait_recv()
        rows = mine(y, 0, h)
        out[rows] = (out[rows].astype(f32) + far[0].astype(f32)).astype(bf16)
        self.ends.append(send(y, 0, 4, y))
        over_y.wait_recv()
        rows = mine(x, h, h)
        out[rows] = (out[rows].astype(f32) + far[1].astype(f32)).astype(bf16)
        self.ends.append(send(x, h, 5, x))
        wait["o"].wait_recv()

    def slots_end(self, out, pair, far, owned):
        g, n = self.g, out.shape[0] // 8
        h = n // 2
        for copy in self.ends:
            copy.wait_recv()
        for first, slots in ((0, (2, 4)), (h, (3, 5))):
            total = out[pl.ds((g.side * 4 + g.me // 2) * n + first, h)].astype(f32)
            total += pair[pl.ds((g.me // 2) * n + first, h)].astype(f32)
            for k in slots:
                total += far[k].astype(f32)
            owned[first : first + h] = total


class SmallSum:
    def __init__(self, net, gather, values, along, across, inside):
        self.net, self.g, self.values = net, gather, values
        self.slots = (along, across, inside)
        self.peers = (
            [(gather.me, k) for k in gather.order[1:]],
            [(e, gather.m) for e in gather.plane],
            [(gather.core, gather.m)],
        )
        self.mine = (gather.m, gather.me // 2, gather.side)
        self.open = []

    def send(self, stage):
        slot = self.slots[stage]
        slot[self.mine[stage]] = self.values[...]
        ref = slot.at[self.mine[stage]]
        self.open = [self.net.start(lambda peer=peer: (ref, ref, peer)) for peer in self.peers[stage]]

    def add(self, stage):
        for copy in self.open:
            copy.wait_recv()
        slot = self.slots[stage]
        total = slot[0]
        for k in range(1, slot.shape[0]):
            total += slot[k]
        self.values[...] = total


def number_blocks(owner, table, vector, rank, slot_place, sem):
    lane = lax.broadcasted_iota(jnp.int32, vector.shape, 1)
    count = owner.shape[0]
    owners = jnp.zeros_like(lane)
    for b in range(count):
        owners = jnp.where(lane == b, owner[b], owners)
    ranks = jnp.zeros_like(lane)
    for b in range(count):
        ahead = (owner[b] < owners) | ((owner[b] == owners) & (lane > b))
        ranks += jnp.where(ahead, 1, 0)
    vector[...] = ranks
    copy = pltpu.make_async_copy(vector, rank, sem)
    copy.start()
    copy.wait()
    places = jnp.zeros_like(lane)
    for b in range(count):
        places = jnp.where(lane == rank[0, b], table[b], places)
    vector[...] = places
    copy = pltpu.make_async_copy(vector, slot_place, sem)
    copy.start()
    copy.wait()


def compute_kernel(linked, *refs):
    if linked:
        tokens, cotangent, master, owner, gains = refs[:5]
        block_out, input_grad, owned, small = refs[5:9]
        wg, wo, wu, wd, grads, slots, *pool, pair, far, sum_a, sum_b, sum_c, vector, rank, slot_place, send, recv, free = refs[9:29]
        scratch = refs[29:]
    else:
        tokens, cotangent, base, wg, wo, wu, wd, gains = refs[:8]
        block_out, input_grad, grads, small = refs[8:12]
        scratch = refs[12:]
    (n1, n1t, cot, cott, n2, n2t, forget, admit, cand, state, scan, acc_a, acc_b, mixed, mid, kept, fills, tally, local) = scratch
    dml, dmlt = n2, n2t
    parts, _, hm3 = wg.shape
    hm = hm3 // 3
    fm = wu.shape[2]
    units, table = stack_places(hm, fm)
    act, dup, dpre = mid.at[:, :fm], mid.at[:, fm:], mid.at[:, : 3 * hm]
    gain_one = gains[0:1, :]
    gain_two = gains[1:2, :]

    if linked:
        fetch_master = pltpu.make_async_copy(master, owned, local.at[2])
        fetch_master.start()
    fetch_cot = pltpu.make_async_copy(cotangent, cot, local.at[0])
    fetch_tok = pltpu.make_async_copy(tokens, n1, local.at[1])
    fetch_tok.start()
    fetch_cot.start()

    column_halves = (slice(0, D // 2), slice(D // 2, D))

    def stack(m, first, wide, left, value):
        for r in range(value.shape[0] // BLK):
            for c in range(value.shape[1] // BLK):
                grads[m, first + r * wide + left + c] = value[r * BLK : (r + 1) * BLK, c * BLK : (c + 1) * BLK].astype(bf16)

    def stack_turned(m, first, value):
        high = value.shape[0] // BLK
        for r in range(high):
            for c in range(value.shape[1] // BLK):
                grads[m, first + c * high + r] = value[r * BLK : (r + 1) * BLK, c * BLK : (c + 1) * BLK].astype(bf16)

    def permute_in(src, dst):
        for k in range(D // BLK):
            scan[k] = src[:, k * BLK : (k + 1) * BLK].astype(f32)

        @pl.loop(0, J // 2, unroll=4)
        def _(j):
            for k in range(D // BLK):
                lo = scan[k, pl.ds(2 * j, SUB, stride=J), :]
                hi = scan[k, pl.ds(2 * j + 1, SUB, stride=J), :]
                dst[pl.ds(pl.multiple_of(16 * j, 16), 16), k * BLK : (k + 1) * BLK] = jnp.concatenate([lo, hi], 0).astype(bf16)

    def permute_out(src, dst):
        @pl.loop(0, J, unroll=4)
        def _(j):
            rows = pl.ds(pl.multiple_of(j * SUB, SUB), SUB)
            for k in range(D // BLK):
                scan[k, pl.ds(j, SUB, stride=J), :] = src[rows, k * BLK : (k + 1) * BLK]

        for k in range(D // BLK):
            dst[:, k * BLK : (k + 1) * BLK] = scan[k].astype(dst.dtype)

    def put(first, rows, value):
        for k in range(hm // BLK):
            scan[first + k, rows, :] = value[:, k * BLK : (k + 1) * BLK]

    def take(first, rows):
        return jnp.concatenate([scan[first + k, rows, :] for k in range(hm // BLK)], 1)

    half = hm // BLK

    def spread(v):
        return jnp.broadcast_to(v[None], (R // SUB, SUB, hm)).reshape(R, hm)


    if linked:
        net = Exchange(send, recv)
        gather = Gather(net, fetch_master, owned, slots, pool, (wg, wo, wu, wd), free)
        gather.start(0)
        gather.along_start(1)
        gather.along_start(2)
        reduce = Reduce(net, gather, grads, units, pool)

    def of_turn(t):
        if not linked:
            return t
        high, low = gather.m // 2, gather.m % 2
        t_high, t_low = t // 2, t % 2
        return 2 * (high + t_high - 2 * high * t_high) + low + t_low - 2 * low * t_low

    fetch_tok.wait()
    permute_in(n1, n1)
    mixed[...] = n1[...].astype(f32)

    @pl.loop(0, L // R)
    def _(i):
        rows = pl.ds(pl.multiple_of(i * R, R), R)
        x = mixed[rows, :]
        r = lax.rsqrt(jnp.mean(x * x, axis=-1, keepdims=True) + norm_eps)
        n1[rows, :] = (x * r * gain_one).astype(bf16)

    n1t[...] = n1[...].T

    if linked:
        gather.forward(0)
        gather.along_start(3)
        number_blocks(owner, table, vector, rank, slot_place, local.at[2])
    fetch_cot.wait()
    permute_in(cot, cot)
    if linked:
        gather.start(1)
        gather.pair(0)
        gather.across_start()
        gather.start(2)
    cott[...] = cot[...].T

    fills[0] = jnp.zeros((SUB, hm), f32)
    fills[1] = jnp.ones((SUB, hm), f32)
    tally[0] = fills[0]
    tally[1] = fills[0]

    @pl.loop(0, parts)
    def _(turn):
        m = of_turn(turn)
        if linked:
            for k in range(parts):

                @pl.when(turn == k)
                def _():
                    if k > 1:
                        gather.pair(k)
                    gather.ready(k)
                    gather.place(k, rank)

        forget[m] = dot(n1[...], wg[m, :, :hm])
        admit[m] = dot(n1[...], wg[m, :, hm : 2 * hm])
        cand[m] = dot(n1[...], wg[m, :, 2 * hm :])

        if linked:

            @pl.when(turn == 2)
            def _():
                gather.forward(3)

        @pl.loop(0, L // R)
        def _(i):
            rows = pl.ds(pl.multiple_of(i * R, R), R)
            f = sigmoid(forget[m, rows, :])
            a = sigmoid(admit[m, rows, :])
            inv = recip(f + a)
            forget[m, rows, :] = f
            admit[m, rows, :] = a
            kept[rows, :] = f * inv
            put(0, rows, a * inv * cand[m, rows, :])

        def step(j, carry):
            s, p, k_sum, kj_sum = carry
            rows = pl.ds(pl.multiple_of(j * SUB, SUB), SUB)
            keep = kept[rows, :]
            s = keep * s + take(0, rows)
            p = keep * p
            put(0, rows, s)
            put(half, rows, p)
            return s, p, k_sum + keep, kj_sum + keep * j.astype(f32)

        s, p, k_sum, kj_sum = lax.fori_loop(0, J, step, (fills[0], fills[1], fills[0], fills[0]), unroll=16)
        tally[0] += k_sum
        tally[1] += kj_sum
        enter = fills[0]
        for _ in range(SUB - 1):
            enter = shift_down(s + p * enter)

        @pl.loop(0, L // R)
        def _(i):
            rows = pl.ds(pl.multiple_of(i * R, R), R)
            state[m, pl.ds(pl.multiple_of(i * R + SUB, SUB), R), :] = take(0, rows) + take(half, rows) * spread(enter)

        state[m, :SUB, :] = shift_down(state[m, L:, :])
        for cols in column_halves:
            mixed[:, cols] += dot(state[m, SUB:, :].astype(bf16), wo[m, :, cols])
        if linked:

            @pl.when(turn == 0)
            def _():
                gather.pair(1)
                gather.forward(2)
                gather.start(3)

    if linked:
        net.drain()
        gather.done()

    @pl.loop(0, L // R)
    def _(i):
        rows = pl.ds(pl.multiple_of(i * R, R), R)
        x = mixed[rows, :]
        r = lax.rsqrt(jnp.mean(x * x, axis=-1, keepdims=True) + norm_eps)
        n2[rows, :] = (x * r * gain_two).astype(bf16)
        acc_a[rows, :] = x
        acc_b[rows, :] = jnp.zeros_like(x)

    n2t[...] = n2[...].T

    @pl.loop(0, parts)
    def _(turn):
        m = of_turn((2 * (turn // 2 + turn % 2 - 2 * (turn // 2) * (turn % 2)) + turn // 2) if linked else turn)
        for first in range(0, fm, fm // 2):
            units_of = slice(first, first + fm // 2)
            up = dot(n2[...], wu[m, :, units_of])
            da = dot(cot[...], wd[m, units_of, :], True)
            cdf, xpdf = gelu_terms(up)
            act[:, units_of] = (up * cdf).astype(bf16)
            dup[:, units_of] = (da * (cdf + xpdf)).astype(bf16)
            if linked and first == 0:

                @pl.when(turn == 2)
                def _():
                    reduce.plane(UPDOWN, 2)

                @pl.when(turn == 3)
                def _():
                    reduce.plane(UPDOWN, 3)

        for cols in column_halves:
            acc_a[:, cols] += dot(act[...], wd[m, :, cols])
        for cols in column_halves:
            acc_b[:, cols] += dot(dup[...], wu[m, cols, :], True)
        for c in range(0, fm, fm // 2):
            part = slice(c, c + fm // 2)
            stack(m, 0, fm // BLK, c // BLK, dot(n2t[...], dup[:, part]))
        for c in range(0, fm, fm // 2):
            part = slice(c, c + fm // 2)
            stack_turned(m, units[UPDOWN][1] // 2 + c // BLK * (D // BLK), dot(cott[...], act[:, part]))
        if linked:

            @pl.when(turn == 1)
            def _():
                gather.all_done()
                reduce.chip(UPDOWN, 2)

            @pl.when(turn == 2)
            def _():
                reduce.chip(UPDOWN, 3)
                reduce.turn(UPDOWN, 2)

            @pl.when(turn == 3)
            def _():
                reduce.chip(UPDOWN, 1)
                reduce.turn(UPDOWN, 3)
                reduce.model(UPDOWN, 2)

    gain_sum_two = jnp.zeros((1, D), f32)

    def back_two(i, total):
        rows = pl.ds(pl.multiple_of(i * R, R), R)
        x = mixed[rows, :]
        r = lax.rsqrt(jnp.mean(x * x, axis=-1, keepdims=True) + norm_eps)
        dn = acc_b[rows, :]
        q = dn * gain_two
        d = cot[rows, :].astype(f32) + r * q - r * r * r * x * jnp.mean(q * x, axis=-1, keepdims=True)
        mixed[rows, :] = d
        dml[rows, :] = d.astype(bf16)
        acc_b[rows, :] = jnp.zeros_like(d)
        return total + jnp.sum(dn * x * r, axis=0, keepdims=True)

    gain_sum_two = lax.fori_loop(0, L // R, back_two, gain_sum_two)
    if linked:
        reduce.plane(UPDOWN, 1)
    dmlt[...] = dml[...].T
    fetch_tok = pltpu.make_async_copy(tokens, cot, local.at[1])
    fetch_tok.start()

    @pl.loop(0, parts)
    def _(m):
        stack_turned(m, units[OUT][0], dot(dmlt[...], state[m, SUB:, :].astype(bf16)))

    if linked:
        for i in (3, 2, 1):
            reduce.chip(OUT, i)
        reduce.model(UPDOWN, 3)

    def keeps(m, rows):
        f = forget[m, rows, :]
        kept[rows, :] = f * recip(f + admit[m, rows, :])

    def state_grads(m):
        put(0, slice(None), dot(dml[...], wo[m], True))

    state_grads(of_turn(parts - 1))

    @pl.loop(0, L // R)
    def _(i):
        keeps(of_turn(parts - 1), pl.ds(pl.multiple_of(i * R, R), R))

    @pl.loop(0, parts)
    def _(back_turn):
        turn = parts - 1 - back_turn
        m = of_turn(turn)
        m_next = of_turn((turn + parts - 1) % parts)

        def step(k, carry):
            u, p, keep_next = carry
            j = J - 1 - k
            rows = pl.ds(pl.multiple_of(j * SUB, SUB), SUB)
            u = take(0, rows) + keep_next * u
            p = keep_next * p
            put(0, rows, u)
            put(half, rows, p)
            return u, p, kept[rows, :]

        u, p, keep_first = lax.fori_loop(0, J, step, (fills[0], fills[1], fills[1]), unroll=16)
        enter = fills[0]
        for _ in range(SUB - 1):
            enter = shift_up(keep_first * (u + p * enter))

        if linked:

            @pl.when(turn == 3)
            def _():
                for i in (3, 2, 1):
                    reduce.plane(OUT, i)

            for k in (2, 1, 0):

                @pl.when(turn == k)
                def _():
                    reduce.plane(GATE, k + 1)
                    if k == 2:
                        reduce.turn(OUT, 3)
                        reduce.turn(OUT, 2)
                    else:
                        reduce.turn(GATE, k + 2)

        @pl.loop(0, L // R)
        def _(i):
            rows = pl.ds(pl.multiple_of(i * R, R), R)
            carried = take(0, rows) + take(half, rows) * spread(enter)
            f = forget[m, rows, :]
            a = admit[m, rows, :]
            adm = a * recip(f + a)
            g = carried * (state[m, rows, :] - cand[m, rows, :]) * (kept[rows, :] * adm)
            dpre[rows, :hm] = (g * (1.0 - f)).astype(bf16)
            dpre[rows, hm : 2 * hm] = (g * (a - 1.0)).astype(bf16)
            dpre[rows, 2 * hm :] = (carried * adm).astype(bf16)
            keeps(m_next, rows)

        for k in range(3):
            stack(m, units[GATE][0], 3 * hm // BLK, k * hm // BLK, dot(n1t[...], dpre[:, k * hm : (k + 1) * hm]))
        for cols in column_halves:
            acc_b[:, cols] += dot(dpre[...], wg[m, cols, :], True)
        state_grads(m_next)
        if linked:
            for k in (3, 2, 1):

                @pl.when(turn == k)
                def _():
                    reduce.chip(GATE, k)
                    if k == 3:
                        reduce.model(UPDOWN, 1)
                    if k == 2:
                        for i in (3, 2, 1):
                            reduce.model(OUT, i)
                    if k == 1:
                        reduce.model(GATE, 3)

    if linked:
        reduce.model(GATE, 2)
        reduce.own(UPDOWN)
        reduce.model(GATE, 1)
        reduce.own(OUT)

    fetch_tok.wait()
    permute_in(cot, cot)
    def back_one(i, total):
        rows = pl.ds(pl.multiple_of(i * R, R), R)
        x = cot[rows, :].astype(f32)
        r = lax.rsqrt(jnp.mean(x * x, axis=-1, keepdims=True) + norm_eps)
        dn = acc_b[rows, :]
        q = dn * gain_one
        mixed[rows, :] += r * q - r * r * r * x * jnp.mean(q * x, axis=-1, keepdims=True)
        return total + jnp.sum(dn * x * r, axis=0, keepdims=True)

    gain_sum_one = lax.fori_loop(0, L // R, back_one, jnp.zeros((1, D), f32))

    permute_out(acc_a, n1)
    push_out = pltpu.make_async_copy(n1, block_out, local.at[0])
    push_out.start()

    place = lax.broadcasted_iota(jnp.int32, (SUB, hm), 0).astype(f32) * float(J)
    if linked:
        first = ((gather.me * parts + gather.m) * L + 1).astype(f32)
        token_total = float(L * parts * lax.axis_size("dp"))
    else:
        first = base[0]
        token_total = base[1]
    forget_sum = jnp.sum(tally[1] + tally[0] * (place + first), axis=0, keepdims=True) / token_total
    small[...] = jnp.zeros_like(small)
    small[0:1, :] = gain_sum_one
    small[1:2, :] = gain_sum_two
    small[2:3, :hm] = forget_sum
    if linked:
        flat = units[UPDOWN][1] // 2, units[GATE][0]
        count = owned.shape[0]
        flags = []
        for k in range(count):
            spot = slot_place[0, gather.me * count + k]
            flags.append(jnp.where((spot >= flat[0]) & (spot < flat[1]), 1.0, 0.0).astype(f32))

    if linked:
        tiny = SmallSum(net, gather, small, sum_a, sum_b, sum_c)
        tiny.send(0)
        reduce.own(GATE)
        reduce.slots_chip(slots, slot_place, pair)
        tiny.add(0)
        tiny.send(1)
        reduce.slots_plane(slots, pair, far)

    permute_out(mixed, acc_a)
    push_grad = pltpu.make_async_copy(acc_a, input_grad, local.at[2])
    push_grad.start()

    if linked:
        tiny.add(1)
        tiny.send(2)
        reduce.slots_end(slots, pair, far, owned)
        tiny.add(2)
        for k, flag in enumerate(flags):
            small[3 + k // 4 : 4 + k // 4, (k % 4) * BLK : (k % 4 + 1) * BLK] = jnp.full((1, BLK), flag, f32)
        net.drain()
    push_out.wait()
    push_grad.wait()


def compute(tokens, cotangent, gains, weights=None, base=None, master=None, owner=None):
    linked = weights is None
    parts = lax.axis_size("mp")
    hm, fm = H // parts, FF // parts
    stacked = (parts, D * (4 * hm + 2 * fm) // BLK**2, BLK, BLK)
    sds = jax.ShapeDtypeStruct
    vm, sm, hbm = (pl.BlockSpec(memory_space=k) for k in (pltpu.VMEM, pltpu.SMEM, pl.ANY))
    if linked:
        n = owner.shape[0]
        args = (tokens, cotangent, master, owner, gains)
        in_specs = [hbm, hbm, hbm, sm, vm]
        middle = sds((n // 8, BLK, BLK), f32)
        extra = [
            pltpu.VMEM((parts, D, 3 * hm), bf16),
            pltpu.VMEM((parts, hm, D), bf16),
            pltpu.VMEM((parts, D, fm), bf16),
            pltpu.VMEM((parts, fm, D), bf16),
            pltpu.VMEM(stacked, bf16),
            pltpu.VMEM((n, BLK, BLK), bf16),
            *[pltpu.VMEM((n, BLK, BLK), bf16) for _ in range(parts - 1)],
            pltpu.VMEM((n // 2, BLK, BLK), bf16),
            pltpu.VMEM((6, n // 16, BLK, BLK), bf16),
            pltpu.VMEM((parts, 8, D), f32),
            pltpu.VMEM((4, 8, D), f32),
            pltpu.VMEM((2, 8, D), f32),
            pltpu.VMEM((8, BLK), jnp.int32),
            pltpu.SMEM((8, BLK), jnp.int32),
            pltpu.SMEM((8, BLK), jnp.int32),
            pltpu.SemaphoreType.DMA((128,)),
            pltpu.SemaphoreType.DMA((128,)),
            pltpu.SemaphoreType.REGULAR,
        ]
        params = dict(collective_id=0, has_side_effects=True)
    else:
        args = (tokens, cotangent, base, *weights, gains)
        in_specs = [hbm, hbm, sm] + [vm] * 5
        middle = sds(stacked, bf16)
        extra = []
        params = {}
    return pl.pallas_call(
        functools.partial(compute_kernel, linked),
        out_shape=(sds((L, D), bf16), sds((L, D), f32), middle, sds((8, D), f32)),
        in_specs=in_specs,
        out_specs=[hbm, hbm, vm, vm],
        scratch_shapes=extra
        + [pltpu.VMEM(shape, bf16) for shape in ((L, D), (D, L)) * 3]
        + [pltpu.VMEM((parts, L, hm), f32)] * 3
        + [pltpu.VMEM((parts, L + SUB, hm), f32)]
        + [pltpu.VMEM((2 * hm // BLK, L, BLK), f32)]
        + [pltpu.VMEM((L, D), f32)] * 3
        + [
            pltpu.VMEM((L, 2 * fm), bf16),
            pltpu.VMEM((L, hm), f32),
            pltpu.VMEM((2, SUB, hm), f32),
            pltpu.VMEM((2, SUB, hm), f32),
            pltpu.SemaphoreType.DMA((3,)),
        ],
        compiler_params=pltpu.CompilerParams(vmem_limit_bytes=64 * 2**20 - 2**16, **params),
        name="block",
    )(*args)


def adam_update(first_old, second_old, gradient):
    first_new = beta_one * first_old + (1.0 - beta_one) * gradient
    second_new = beta_two * second_old + (1.0 - beta_two) * gradient * gradient
    first_hat = first_new / (1.0 - beta_one**STEP)
    second_hat = second_new / (1.0 - beta_two**STEP)
    return (first_new, second_new, first_hat / (jnp.sqrt(second_hat) + adam_eps))


def fine_dot(a, b, trans_b=False):
    a_high, b_high = a.astype(bf16), b.astype(bf16)
    a_low, b_low = (a - a_high.astype(f32)).astype(bf16), (b - b_high.astype(f32)).astype(bf16)
    return dot(a_high, b_high, trans_b) + (dot(a_high, b_low, trans_b) + dot(a_low, b_high, trans_b))


def update_kernel(token_total, passed, sums, gains, gain_moment_one, gain_moment_two, *refs):
    sources, refs = refs[:6], refs[6:]
    given, refs = refs[:passed], refs[passed:]
    results, refs = refs[:4], refs[4:]
    gain_first, gain_second, gains_new, forget_mean = refs[:4]
    copied, refs = refs[4 : 4 + passed], refs[4 + passed :]
    held, made, made_low, sem_in, sem_out, sem_pass = refs[:6]
    passage = refs[6:]
    count = held.shape[1]
    step = max(count // 2, 1)
    groups = [slice(first, first + step) for first in range(0, count, step)]
    enter = [pltpu.make_async_copy(src, via, sem_pass.at[0, k]) for k, (src, via) in enumerate(zip(given, passage))]
    leave = [pltpu.make_async_copy(via, dst, sem_pass.at[1, k]) for k, (via, dst) in enumerate(zip(passage, copied))]
    fetch = [
        [pltpu.make_async_copy(src.at[group], held.at[k, group], sem_in.at[g, k]) for k, src in enumerate(sources)]
        for g, group in enumerate(groups)
    ]
    for copy in fetch[0]:
        copy.start()
    for copy in enter:
        copy.start()
    for row in fetch[1:]:
        for copy in row:
            copy.start()
    first, second, direction = adam_update(gain_moment_one[...], gain_moment_two[...], sums[0:2, :])
    gain_first[...] = first
    gain_second[...] = second
    gains_new[...] = gains[...] - gain_rate * direction
    forget_mean[...] = jnp.sum(sums[2:3, :], axis=1, keepdims=True) * (1.0 / (H * (token_total + 1) / 2.0))
    push = []
    for g, group in enumerate(groups):
        blocks = range(group.start, group.stop)
        for copy in fetch[g]:
            copy.wait()
        if g == len(groups) - 1:
            for come, go in zip(enter, leave):
                come.wait()
                go.start()
        grads = []
        for s in blocks:
            grad = held[0, s]
            flag = sums[3 + s // 4 : 4 + s // 4, (s % 4) * BLK : (s % 4 + 1) * BLK]
            grads.append(jnp.where(flag > 0.5, grad.T, grad))
        values = [fine_dot(held[1, s].T, grad) for s, grad in zip(blocks, grads)]
        values = [fine_dot(value, held[2, s]) for s, value in zip(blocks, values)]
        for k, s in enumerate(blocks):
            first, second, values[k] = adam_update(held[3, s], held[4, s], values[k])
            made[0, s] = first
            made[1, s] = second
        values = [fine_dot(held[1, s], value) for s, value in zip(blocks, values)]
        values = [fine_dot(value, held[2, s], True) for s, value in zip(blocks, values)]
        for s, value in zip(blocks, values):
            fresh = held[5, s] - learn_rate * (value + weight_decay * held[5, s])
            made[2, s] = fresh
            made_low[s] = fresh.astype(bf16)
        for k, dst in enumerate(results):
            src = made.at[k, group] if k < 3 else made_low.at[group]
            copy = pltpu.make_async_copy(src, dst.at[group], sem_out.at[g, k])
            copy.start()
            push.append(copy)
    for copy in push + leave:
        copy.wait()


def update(token_total, small, large, passed):
    sds = jax.ShapeDtypeStruct
    blocks, gain = large[0].shape, small[1].shape
    vm, hbm = pl.BlockSpec(memory_space=pltpu.VMEM), pl.BlockSpec(memory_space=pl.ANY)
    return pl.pallas_call(
        functools.partial(update_kernel, token_total, len(passed)),
        out_shape=[sds(blocks, f32)] * 3
        + [sds(blocks, bf16)]
        + [sds(gain, f32)] * 3
        + [sds((1, 1), f32)]
        + [sds(v.shape, v.dtype) for v in passed],
        in_specs=[vm] * 4 + [hbm] * (len(large) + len(passed)),
        out_specs=[hbm] * 4 + [vm] * 4 + [hbm] * len(passed),
        scratch_shapes=[
            pltpu.VMEM((6, *blocks), f32),
            pltpu.VMEM((3, *blocks), f32),
            pltpu.VMEM(blocks, bf16),
            pltpu.SemaphoreType.DMA((2, 6)),
            pltpu.SemaphoreType.DMA((2, 4)),
            pltpu.SemaphoreType.DMA((2, len(passed))),
        ]
        + [pltpu.VMEM(v.shape, v.dtype) for v in passed],
        compiler_params=pltpu.CompilerParams(vmem_limit_bytes=56 * 2**20),
        name="update",
    )(*small, *large, *passed)


def on_device(
    tokens,
    cotangent,
    master,
    moment_one,
    moment_two,
    basis_left,
    basis_right,
    owner,
    gains,
    gain_moment_one,
    gain_moment_two,
):
    parts = lax.axis_size("mp")
    data_parts = lax.axis_size("dp")
    hm, fm = H // parts, FF // parts
    token_total = L * data_parts * parts
    row_tiles, cols, lows = D // BLK, (3 * hm + fm) // BLK, (hm + fm) // BLK
    if data_parts == 8 and parts == 4:
        block_out, input_grad, owned, sums = compute(tokens, cotangent, gains, master=master[0], owner=owner)
    else:
        number = jnp.arange(owner.shape[0], dtype=jnp.int32)
        ahead = (owner[None, :] < owner[:, None]) | ((owner[None, :] == owner[:, None]) & (number[None, :] < number[:, None]))
        block_rank = jnp.sum(ahead.astype(jnp.int32), axis=1)
        _, table = stack_places(hm, fm)
        table = jnp.asarray(table, jnp.int32)
        slot_place = jnp.sum(jnp.where(block_rank[None, :] == number[:, None], table[None, :], 0), axis=1)
        stored = lax.all_gather(master.astype(bf16), "dp", axis=1, tiled=True)
        stored = lax.all_gather(stored, "mp", axis=0, tiled=True)
        stack = stored[:, block_rank]
        upper = stack[:, : row_tiles * cols].reshape(parts, row_tiles, cols, BLK, BLK)
        upper = upper.transpose(0, 1, 3, 2, 4).reshape(parts, D, cols * BLK)
        lower = stack[:, row_tiles * cols :].reshape(parts, lows, row_tiles, BLK, BLK)
        lower = lower.transpose(0, 1, 3, 2, 4).reshape(parts, lows * BLK, D)
        weights = (upper[:, :, : 3 * hm], lower[:, :hm], upper[:, :, 3 * hm :], lower[:, hm:])
        first = ((lax.axis_index("dp") * parts + lax.axis_index("mp")) * L + 1).astype(f32)
        base = jnp.stack([first, jnp.asarray(token_total, f32)])
        block_out, input_grad, grads, sums = compute(tokens, cotangent, gains, weights=weights, base=base)
        owned = lax.psum_scatter(grads[:, slot_place].astype(f32), "dp", scatter_dimension=1, tiled=True)
        owned = lax.psum_scatter(owned, "mp", scatter_dimension=0, tiled=True)[0]
        sums = lax.psum(sums, ("dp", "mp"))
        count = master.shape[1]
        mine = lax.dynamic_slice_in_dim(slot_place, lax.axis_index("dp") * count, count)
        units, _ = stack_places(hm, fm)
        flags = ((mine >= units[UPDOWN][1] // 2) & (mine < units[GATE][0])).astype(f32)
        flags = jnp.pad(jnp.repeat(flags, BLK), (0, (8 - count) * BLK)).reshape(2, 4 * BLK)
        sums = jnp.concatenate([sums[:3], flags, sums[5:]])
    outs = update(
        token_total,
        (sums, gains, gain_moment_one, gain_moment_two),
        (owned, basis_left[0], basis_right[0], moment_one[0], moment_two[0], master[0]),
        (block_out, input_grad),
    )
    first_new, second_new, master_new, master_low, gain_first, gain_second, gains_new, forget_mean = outs[:8]
    block_out, input_grad = outs[8:]
    return (
        block_out,
        input_grad,
        first_new[None],
        second_new[None],
        master_new[None],
        master_low[None],
        gain_first,
        gain_second,
        gains_new,
        forget_mean[0, 0],
    )


def solution(mesh):
    rows, blocks = P(("dp", "mp"), None), P("mp", "dp", None, None)
    return jax.shard_map(
        on_device,
        mesh=mesh,
        in_specs=(rows, rows, blocks, blocks, blocks, blocks, blocks, P(), P(), P(), P()),
        out_specs=(rows, rows, blocks, blocks, blocks, blocks, P(), P(), P(), P()),
        check_vma=False,
    )
```

```python
import functools

import jax
import jax.numpy as jnp
from jax import lax
from jax.experimental import pallas as pl
from jax.experimental.pallas import tpu as pltpu
from jax.sharding import PartitionSpec as P

D = 512
H = 1024
FF = 2048
BLK = 128
STEP = 10
L = 1024

norm_eps = 1e-05
beta_one = 0.5
beta_two = 0.5
adam_eps = 1e-08
learn_rate = 0.02
gain_rate = 0.1
weight_decay = 0.1
highest = lax.Precision.HIGHEST

f32 = jnp.float32
bf16 = jnp.bfloat16
SUB = 8
J = L // SUB
R = 256


def dot(a, b, trans_b=False):
    dims = (((1,), (1,)), ((), ())) if trans_b else (((1,), (0,)), ((), ()))
    return lax.dot_general(a, b, dims, preferred_element_type=f32)


def recip(v):
    return pltpu.reciprocal(v, approx=True)


def sigmoid(v):
    return recip(1.0 + jnp.exp(-v))


def shift_down(v):
    rolled = pltpu.roll(v, 1, 0)
    row = lax.broadcasted_iota(jnp.int32, v.shape, 0)
    return jnp.where(row == 0, 0.0, rolled)


def shift_up(v):
    rolled = pltpu.roll(v, SUB - 1, 0)
    row = lax.broadcasted_iota(jnp.int32, v.shape, 0)
    return jnp.where(row == SUB - 1, 0.0, rolled)


def gelu_terms(x):
    a = jnp.abs(x)
    t = recip(1.0 + a * (0.3275911 * 0.7071067811865476))
    poly = t * (
        0.5 * 0.254829592
        + t
        * (
            0.5 * -0.284496736
            + t * (0.5 * 1.421413741 + t * (0.5 * -1.453152027 + t * (0.5 * 1.061405429)))
        )
    )
    e = jnp.exp(x * x * -0.5)
    tail = poly * e
    cdf = jnp.where(x < 0.0, tail, 1.0 - tail)
    return cdf, x * e * 0.3989422804014327


MESH = pl.DeviceIdType.MESH


class Copy:
    def __init__(self, net, make):
        self.net, self.make = net, make

    def start(self):
        self.net.open.append(self)
        self.make().start()
        return self

    def wait_recv(self):
        self.make().wait_recv()

    def wait_send(self):
        self.make().wait_send()


class Exchange:
    def __init__(self, send, recv):
        self.send, self.recv, self.known, self.used, self.open = send, recv, {}, 0, []

    def copy(self, parts, key=None):
        if key in self.known:
            return self.known[key]
        k = self.used
        self.used += 1

        def make():
            src, dst, device = parts()
            return pltpu.make_async_remote_copy(
                src_ref=src,
                dst_ref=dst,
                send_sem=self.send.at[k],
                recv_sem=self.recv.at[k],
                device_id=device,
                device_id_type=MESH,
            )

        copy = Copy(self, make)
        if key is not None:
            self.known[key] = copy
        return copy

    def start(self, parts):
        return self.copy(parts).start()

    def drain(self):
        for copy in self.open:
            copy.wait_send()
        self.open = []


class Gather:
    def __init__(self, net, fetch, master, slots, pool, weights, free):
        self.net, self.weights, self.free = net, weights, free
        self.held = [slots, *pool]
        d, m = lax.axis_index("dp"), lax.axis_index("mp")
        core, col, row = d % 2, (d // 2) % 2, d // 4
        self.me, self.m, self.side = d, m, core
        self.core = d + 1 - 2 * core
        self.plane = [d + 2 - 4 * col, d + 4 - 8 * row, d + 6 - 4 * col - 8 * row]
        self.order = [m, m + 1 - 2 * (m % 2), m + 2 - 4 * (m // 2), 3 - m]
        self.peers = [(e, m) for e in [self.core] + self.plane] + [(d, k) for k in self.order[1:]]
        barrier = pltpu.get_barrier_semaphore()
        for device in self.peers:
            pl.semaphore_signal(barrier, inc=1, device_id=device, device_id_type=MESH)
        self.n = master.shape[0]
        fetch.wait()
        for s in range(self.n):
            slots[d * self.n + s] = master[s].astype(bf16)
        pl.semaphore_wait(barrier, len(self.peers))

    def rows(self, i, e, first, count):
        return self.held[i].at[pl.ds(e * self.n + first, count)]

    def along(self, i, e):
        return self.net.copy(
            lambda: (self.rows(0, e, 0, self.n), self.rows(i, e, 0, self.n), (self.me, self.order[i])),
            ("along", i, e is self.me),
        )

    def within(self, key, i, e, first, count, to):
        return self.net.copy(
            lambda: (self.rows(i, e, first, count), self.rows(i, e, first, count), (to, self.m)), (key, i)
        )

    def first(self, i):
        (x, y, _), h = self.plane, self.n // 2
        if i == 1:
            jobs = ((0, self.n, x), (0, self.n, y))
        else:
            jobs = ((0, h, x), (h, h, y), (h, h, x), (0, h, y))
        return [self.within(("first", k), i, self.me, *job) for k, job in enumerate(jobs)]

    def last(self, i):
        x, y, z = self.plane
        if i == 1:
            return [self.along(1, z)]
        h = self.n // 2
        return [self.within("over y", i, x, 0, h, y), self.within("over x", i, y, h, h, x)]

    def inside(self, i):
        return [self.within(("inside", k), i, e, 0, self.n, self.core) for k, e in enumerate([self.me] + self.plane)]

    def along_start(self, i):
        self.along(i, self.me).start()

    def across_start(self):
        self.last(1)[0].start()

    def start(self, i):
        if i:
            self.along(i, self.me).wait_recv()
        for copy in self.first(i):
            copy.start()
        self.inside(i)[0].start()

    def forward(self, i):
        if i == 1:
            return
        for came, copy in zip(self.first(i), self.last(i)):
            came.wait_recv()
            copy.start()

    def pair(self, i):
        for came, copy in zip(self.first(i)[-2:], self.inside(i)[1:3]):
            came.wait_recv()
            copy.start()
        for came in self.last(i):
            came.wait_recv()
        self.inside(i)[3].start()

    def ready(self, i):
        for copy in self.inside(i):
            copy.wait_recv()

    def place(self, i, rank):
        wg, wo, wu, wd = self.weights
        row_tiles, gates = D // BLK, wg.shape[2] // BLK
        cols, outs = gates + wu.shape[2] // BLK, wo.shape[1] // BLK
        for b in range(row_tiles * cols + (wo.shape[1] + wd.shape[1]) // BLK * row_tiles):
            if b < row_tiles * cols:
                r, c = b // cols, b % cols
                ref = wg if c < gates else wu
                c -= 0 if c < gates else gates
            else:
                r, c = (b - row_tiles * cols) // row_tiles, (b - row_tiles * cols) % row_tiles
                ref = wo if r < outs else wd
                r -= 0 if r < outs else outs
            block = self.held[i][rank[0, b]]
            ref[self.order[i], r * BLK : (r + 1) * BLK, c * BLK : (c + 1) * BLK] = block

    def done(self):
        for device in self.peers:
            pl.semaphore_signal(self.free, inc=1, device_id=device, device_id_type=MESH)

    def all_done(self):
        pl.semaphore_wait(self.free, len(self.peers))


def stack_places(hm, fm):
    row_tiles, gates, ups, outs = D // BLK, 3 * hm // BLK, fm // BLK, hm // BLK
    cols = gates + ups
    first_down = row_tiles * ups
    first_out = 2 * first_down
    first_gate = first_out + row_tiles * outs
    table = []
    for b in range(row_tiles * (cols + outs + ups)):
        if b < row_tiles * cols:
            r, c = b // cols, b % cols
            table.append(first_gate + r * gates + c if c < gates else r * ups + c - gates)
        else:
            k = b - row_tiles * cols
            table.append(first_out + k if k < row_tiles * outs else first_down + k - row_tiles * outs)
    return ((0, first_out), (first_out, row_tiles * outs), (first_gate, row_tiles * gates)), table


UPDOWN, OUT, GATE = range(3)
REST = 1


class Reduce:
    def __init__(self, net, gather, grads, units, pool):
        self.net, self.g, self.grads, self.pool = net, gather, grads, pool
        self.units = (units[UPDOWN], (units[OUT][0], units[OUT][1] + units[GATE][1]))
        self.half = grads.shape[1] // 2
        self.eighth = grads.shape[1] // 8

    def place(self, e):
        return (e % 2) * 4 + e // 2

    def inside(self, unit, i):
        g, (first, count) = self.g, self.units[unit]
        return self.net.copy(
            lambda: (
                self.grads.at[g.order[i], pl.ds(first + (1 - g.side) * (count // 2), count // 2)],
                self.pool[i - 1].at[pl.ds(first // 2, count // 2)],
                (g.core, g.m),
            ),
            ("chip", unit, i),
        )

    def chip(self, unit, i):
        self.inside(unit, i).start()

    def spot(self, unit, i, slot, first, count):
        base, total = self.units[unit]
        return self.pool[i - 1].at[pl.ds(self.half + slot * self.eighth + base // 8 + first, count)]

    def share(self, unit, i, e, first, count):
        base, total = self.units[unit]
        return self.grads.at[self.g.order[i], pl.ds(base + self.place(e) * (total // 8) + first, count)]

    def over(self, unit, i, k):
        n = self.units[unit][1] // 8
        e = self.g.plane[k]
        return self.net.copy(
            lambda: (self.share(unit, i, e, 0, n), self.spot(unit, i, k, 0, n), (e, self.g.m)), ("over", unit, i, k)
        )

    def model_copy(self, unit, i):
        n = self.units[unit][1] // 8
        return self.net.copy(
            lambda: (self.share(unit, i, self.g.me, 0, n), self.spot(unit, i, 3, 0, n), (self.g.me, self.g.order[i])),
            ("model", unit, i),
        )

    def aside(self, unit):
        part = (0, self.units[unit][1] // 8)
        return self.net.copy(
            lambda: (
                self.share(unit, 1, self.g.plane[2], *part),
                self.spot(unit, 1, 2, *part),
                (self.g.me, self.g.order[1]),
            ),
            ("aside", unit),
        )

    def plane(self, unit, i):
        g, (first, count) = self.g, self.units[unit]
        x, y, z = g.plane
        self.inside(unit, i).wait_recv()
        m = g.order[i]
        start, came = first + g.side * (count // 2), self.pool[i - 1]

        @pl.loop(0, count // 2, unroll=4)
        def _(b):
            total = self.grads[m, start + b].astype(f32) + came[first // 2 + b].astype(f32)
            self.grads[m, start + b] = total.astype(bf16)

        for k in range(2 if i == 1 else 3):
            self.over(unit, i, k).start()
        if i == 1:
            self.aside(unit).start()

    def model(self, unit, i):
        n = self.units[unit][1] // 8
        ref = self.share(unit, i, self.g.me, 0, n)
        total = ref[...].astype(f32)
        for k in range(2 if i == 1 else 3):
            self.over(unit, i, k).wait_recv()
            total += self.spot(unit, i, k, 0, n)[...].astype(f32)
        ref[...] = total.astype(bf16)
        self.model_copy(unit, i).start()

    def own(self, unit):
        g, (first, count) = self.g, self.units[unit]
        n = count // 8
        rows = pl.ds(first + self.place(g.me) * n, n)
        total = self.grads[g.m, rows].astype(f32)
        for i in (1, 2, 3):
            self.model_copy(unit, i).wait_recv()
            total += self.pool[i - 1][pl.ds(self.half + 3 * self.eighth + first // 8, n)].astype(f32)
        self.grads[g.m, rows] = total.astype(bf16)
        self.aside(unit).wait_recv()
        rows = pl.ds(first + self.place(g.plane[2]) * n, n)
        total = self.grads[g.m, rows].astype(f32) + self.spot(unit, 1, 2, 0, n)[...].astype(f32)
        self.grads[g.m, rows] = total.astype(bf16)

    def into_slots(self, out, slot_place, e):
        n = self.eighth
        for k in range(n):
            out[self.place(e) * n + k] = self.grads[self.g.m, slot_place[0, e * n + k]]

    def slots_chip(self, out, slot_place, pair):
        g, n = self.g, self.eighth
        self.last = []
        targets = (g.plane[2], g.plane[0], g.plane[1], g.me)
        for e in targets:
            other = e + 1 - 2 * g.side
            self.into_slots(out, slot_place, other)
            self.last.append(
                self.net.start(
                    lambda e=e, other=other: (
                        out.at[pl.ds(self.place(other) * n, n)],
                        pair.at[pl.ds((e // 2) * n, n)],
                        (g.core, g.m),
                    )
                )
            )
        for e in targets:
            self.into_slots(out, slot_place, e)

    def slots_plane(self, out, pair, far):
        g, n = self.g, out.shape[0] // 8
        h = n // 2
        x, y, z = g.plane
        wait = dict(zip("zxyo", self.last))

        def mine(e, first, count):
            return pl.ds((g.side * 4 + e // 2) * n + first, count)

        def join(e):
            rows = mine(e, 0, n)
            out[rows] = (out[rows].astype(f32) + pair[pl.ds((e // 2) * n, n)].astype(f32)).astype(bf16)

        def send(e, first, slot, to):
            return self.net.start(lambda: (out.at[mine(e, first, h)], far.at[slot], (to, g.m)))

        wait["z"].wait_recv()
        join(z)
        over_x = send(z, 0, 0, x)
        over_y = send(z, h, 1, y)
        wait["x"].wait_recv()
        join(x)
        self.ends = [send(x, 0, 2, x)]
        wait["y"].wait_recv()
        join(y)
        self.ends.append(send(y, h, 3, y))
        over_x.wait_recv()
        rows = mine(y, 0, h)
        out[rows] = (out[rows].astype(f32) + far[0].astype(f32)).astype(bf16)
        self.ends.append(send(y, 0, 4, y))
        over_y.wait_recv()
        rows = mine(x, h, h)
        out[rows] = (out[rows].astype(f32) + far[1].astype(f32)).astype(bf16)
        self.ends.append(send(x, h, 5, x))
        wait["o"].wait_recv()

    def slots_end(self, out, pair, far, owned):
        g, n = self.g, out.shape[0] // 8
        h = n // 2
        for copy in self.ends:
            copy.wait_recv()
        for first, slots in ((0, (2, 4)), (h, (3, 5))):
            total = out[pl.ds((g.side * 4 + g.me // 2) * n + first, h)].astype(f32)
            total += pair[pl.ds((g.me // 2) * n + first, h)].astype(f32)
            for k in slots:
                total += far[k].astype(f32)
            owned[first : first + h] = total


class SmallSum:
    def __init__(self, net, gather, values, along, across, inside):
        self.net, self.g, self.values = net, gather, values
        self.slots = (along, across, inside)
        self.peers = (
            [(gather.me, k) for k in gather.order[1:]],
            [(e, gather.m) for e in gather.plane],
            [(gather.core, gather.m)],
        )
        self.mine = (gather.m, gather.me // 2, gather.side)
        self.open = []

    def send(self, stage):
        slot = self.slots[stage]
        slot[self.mine[stage]] = self.values[...]
        ref = slot.at[self.mine[stage]]
        self.open = [self.net.start(lambda peer=peer: (ref, ref, peer)) for peer in self.peers[stage]]

    def add(self, stage):
        for copy in self.open:
            copy.wait_recv()
        slot = self.slots[stage]
        total = slot[0]
        for k in range(1, slot.shape[0]):
            total += slot[k]
        self.values[...] = total


def number_blocks(owner, table, vector, rank, slot_place, sem):
    lane = lax.broadcasted_iota(jnp.int32, vector.shape, 1)
    count = owner.shape[0]
    owners = jnp.zeros_like(lane)
    for b in range(count):
        owners = jnp.where(lane == b, owner[b], owners)
    ranks = jnp.zeros_like(lane)
    for b in range(count):
        ahead = (owner[b] < owners) | ((owner[b] == owners) & (lane > b))
        ranks += jnp.where(ahead, 1, 0)
    vector[...] = ranks
    copy = pltpu.make_async_copy(vector, rank, sem)
    copy.start()
    copy.wait()
    places = jnp.zeros_like(lane)
    for b in range(count):
        places = jnp.where(lane == rank[0, b], table[b], places)
    vector[...] = places
    copy = pltpu.make_async_copy(vector, slot_place, sem)
    copy.start()
    copy.wait()


def compute_kernel(linked, *refs):
    if linked:
        tokens, cotangent, master, owner, gains = refs[:5]
        block_out, input_grad, owned, small = refs[5:9]
        wg, wo, wu, wd, grads, slots, *pool, pair, far, sum_a, sum_b, sum_c, vector, rank, slot_place, send, recv, free = refs[9:29]
        scratch = refs[29:]
    else:
        tokens, cotangent, base, wg, wo, wu, wd, gains = refs[:8]
        block_out, input_grad, grads, small = refs[8:12]
        scratch = refs[12:]
    (n1, n1t, cot, cott, n2, n2t, forget, admit, cand, state, scan, acc_a, acc_b, mixed, mid, kept, fills, tally, local) = scratch
    dml, dmlt = n2, n2t
    parts, _, hm3 = wg.shape
    hm = hm3 // 3
    fm = wu.shape[2]
    units, table = stack_places(hm, fm)
    act, dup, dpre = mid.at[:, :fm], mid.at[:, fm:], mid.at[:, : 3 * hm]
    gain_one = gains[0:1, :]
    gain_two = gains[1:2, :]

    if linked:
        fetch_master = pltpu.make_async_copy(master, owned, local.at[2])
        fetch_master.start()
    fetch_cot = pltpu.make_async_copy(cotangent, cot, local.at[0])
    fetch_tok = pltpu.make_async_copy(tokens, n1, local.at[1])
    fetch_tok.start()
    fetch_cot.start()

    column_halves = (slice(0, D // 2), slice(D // 2, D))

    def stack(m, first, wide, left, value):
        for r in range(value.shape[0] // BLK):
            for c in range(value.shape[1] // BLK):
                grads[m, first + r * wide + left + c] = value[r * BLK : (r + 1) * BLK, c * BLK : (c + 1) * BLK].astype(bf16)

    def stack_turned(m, first, value):
        high = value.shape[0] // BLK
        for r in range(high):
            for c in range(value.shape[1] // BLK):
                grads[m, first + c * high + r] = value[r * BLK : (r + 1) * BLK, c * BLK : (c + 1) * BLK].astype(bf16)

    def permute_in(src, dst):
        for k in range(D // BLK):
            scan[k] = src[:, k * BLK : (k + 1) * BLK].astype(f32)

        @pl.loop(0, J // 2, unroll=4)
        def _(j):
            for k in range(D // BLK):
                lo = scan[k, pl.ds(2 * j, SUB, stride=J), :]
                hi = scan[k, pl.ds(2 * j + 1, SUB, stride=J), :]
                dst[pl.ds(pl.multiple_of(16 * j, 16), 16), k * BLK : (k + 1) * BLK] = jnp.concatenate([lo, hi], 0).astype(bf16)

    def permute_out(src, dst):
        @pl.loop(0, J, unroll=4)
        def _(j):
            rows = pl.ds(pl.multiple_of(j * SUB, SUB), SUB)
            for k in range(D // BLK):
                scan[k, pl.ds(j, SUB, stride=J), :] = src[rows, k * BLK : (k + 1) * BLK]

        for k in range(D // BLK):
            dst[:, k * BLK : (k + 1) * BLK] = scan[k].astype(dst.dtype)

    def put(first, rows, value):
        for k in range(hm // BLK):
            scan[first + k, rows, :] = value[:, k * BLK : (k + 1) * BLK]

    def take(first, rows):
        return jnp.concatenate([scan[first + k, rows, :] for k in range(hm // BLK)], 1)

    half = hm // BLK

    def spread(v):
        return jnp.broadcast_to(v[None], (R // SUB, SUB, hm)).reshape(R, hm)


    if linked:
        net = Exchange(send, recv)
        gather = Gather(net, fetch_master, owned, slots, pool, (wg, wo, wu, wd), free)
        gather.start(0)
        gather.along_start(1)
        gather.along_start(2)
        reduce = Reduce(net, gather, grads, units, pool)

    def of_turn(t):
        if not linked:
            return t
        high, low = gather.m // 2, gather.m % 2
        t_high, t_low = t // 2, t % 2
        return 2 * (high + t_high - 2 * high * t_high) + low + t_low - 2 * low * t_low

    fetch_tok.wait()
    permute_in(n1, n1)
    mixed[...] = n1[...].astype(f32)

    @pl.loop(0, L // R)
    def _(i):
        rows = pl.ds(pl.multiple_of(i * R, R), R)
        x = mixed[rows, :]
        r = lax.rsqrt(jnp.mean(x * x, axis=-1, keepdims=True) + norm_eps)
        n1[rows, :] = (x * r * gain_one).astype(bf16)

    n1t[...] = n1[...].T

    if linked:
        gather.forward(0)
        gather.along_start(3)
        number_blocks(owner, table, vector, rank, slot_place, local.at[2])
    fetch_cot.wait()
    permute_in(cot, cot)
    if linked:
        gather.start(1)
        gather.pair(0)
        gather.across_start()
        gather.start(2)
    cott[...] = cot[...].T

    fills[0] = jnp.zeros((SUB, hm), f32)
    fills[1] = jnp.ones((SUB, hm), f32)
    tally[0] = fills[0]
    tally[1] = fills[0]

    @pl.loop(0, parts)
    def _(turn):
        m = of_turn(turn)
        if linked:
            for k in range(parts):

                @pl.when(turn == k)
                def _():
                    if k > 1:
                        gather.pair(k)
                    gather.ready(k)
                    gather.place(k, rank)

        forget[m] = dot(n1[...], wg[m, :, :hm])
        admit[m] = dot(n1[...], wg[m, :, hm : 2 * hm])
        cand[m] = dot(n1[...], wg[m, :, 2 * hm :])

        if linked:

            @pl.when(turn == 2)
            def _():
                gather.forward(3)

        @pl.loop(0, L // R)
        def _(i):
            rows = pl.ds(pl.multiple_of(i * R, R), R)
            f = sigmoid(forget[m, rows, :])
            a = sigmoid(admit[m, rows, :])
            inv = recip(f + a)
            forget[m, rows, :] = f
            admit[m, rows, :] = a
            kept[rows, :] = f * inv
            put(0, rows, a * inv * cand[m, rows, :])

        def step(j, carry):
            s, p, k_sum, kj_sum = carry
            rows = pl.ds(pl.multiple_of(j * SUB, SUB), SUB)
            keep = kept[rows, :]
            s = keep * s + take(0, rows)
            p = keep * p
            put(0, rows, s)
            put(half, rows, p)
            return s, p, k_sum + keep, kj_sum + keep * j.astype(f32)

        s, p, k_sum, kj_sum = lax.fori_loop(0, J, step, (fills[0], fills[1], fills[0], fills[0]), unroll=16)
        tally[0] += k_sum
        tally[1] += kj_sum
        enter = fills[0]
        for _ in range(SUB - 1):
            enter = shift_down(s + p * enter)

        @pl.loop(0, L // R)
        def _(i):
            rows = pl.ds(pl.multiple_of(i * R, R), R)
            state[m, pl.ds(pl.multiple_of(i * R + SUB, SUB), R), :] = take(0, rows) + take(half, rows) * spread(enter)

        state[m, :SUB, :] = shift_down(state[m, L:, :])
        for cols in column_halves:
            mixed[:, cols] += dot(state[m, SUB:, :].astype(bf16), wo[m, :, cols])
        if linked:

            @pl.when(turn == 0)
            def _():
                gather.pair(1)
                gather.forward(2)
                gather.start(3)

    if linked:
        net.drain()
        gather.done()

    @pl.loop(0, L // R)
    def _(i):
        rows = pl.ds(pl.multiple_of(i * R, R), R)
        x = mixed[rows, :]
        r = lax.rsqrt(jnp.mean(x * x, axis=-1, keepdims=True) + norm_eps)
        n2[rows, :] = (x * r * gain_two).astype(bf16)
        acc_a[rows, :] = x
        acc_b[rows, :] = jnp.zeros_like(x)

    n2t[...] = n2[...].T

    @pl.loop(0, parts)
    def _(turn):
        m = of_turn((2 * (turn // 2 + turn % 2 - 2 * (turn // 2) * (turn % 2)) + turn // 2) if linked else turn)
        for first in range(0, fm, fm // 2):
            units_of = slice(first, first + fm // 2)
            up = dot(n2[...], wu[m, :, units_of])
            da = dot(cot[...], wd[m, units_of, :], True)
            cdf, xpdf = gelu_terms(up)
            act[:, units_of] = (up * cdf).astype(bf16)
            dup[:, units_of] = (da * (cdf + xpdf)).astype(bf16)
            if linked and first == 0:

                @pl.when(turn == 2)
                def _():
                    reduce.plane(UPDOWN, 2)

                @pl.when(turn == 3)
                def _():
                    reduce.plane(UPDOWN, 3)

        for cols in column_halves:
            acc_a[:, cols] += dot(act[...], wd[m, :, cols])
        for cols in column_halves:
            acc_b[:, cols] += dot(dup[...], wu[m, cols, :], True)
        for c in range(0, fm, fm // 2):
            part = slice(c, c + fm // 2)
            stack(m, 0, fm // BLK, c // BLK, dot(n2t[...], dup[:, part]))
        for c in range(0, fm, fm // 2):
            part = slice(c, c + fm // 2)
            stack_turned(m, units[UPDOWN][1] // 2 + c // BLK * (D // BLK), dot(cott[...], act[:, part]))
        if linked:

            @pl.when(turn == 1)
            def _():
                gather.all_done()
                reduce.chip(UPDOWN, 2)

            @pl.when(turn == 2)
            def _():
                reduce.chip(UPDOWN, 3)

            @pl.when(turn == 3)
            def _():
                reduce.chip(UPDOWN, 1)
                reduce.model(UPDOWN, 2)

    gain_sum_two = jnp.zeros((1, D), f32)

    def back_two(i, total):
        rows = pl.ds(pl.multiple_of(i * R, R), R)
        x = mixed[rows, :]
        r = lax.rsqrt(jnp.mean(x * x, axis=-1, keepdims=True) + norm_eps)
        dn = acc_b[rows, :]
        q = dn * gain_two
        d = cot[rows, :].astype(f32) + r * q - r * r * r * x * jnp.mean(q * x, axis=-1, keepdims=True)
        mixed[rows, :] = d
        dml[rows, :] = d.astype(bf16)
        acc_b[rows, :] = jnp.zeros_like(d)
        return total + jnp.sum(dn * x * r, axis=0, keepdims=True)

    gain_sum_two = lax.fori_loop(0, L // R, back_two, gain_sum_two)
    if linked:
        reduce.plane(UPDOWN, 1)
    dmlt[...] = dml[...].T
    fetch_tok = pltpu.make_async_copy(tokens, cot, local.at[1])
    fetch_tok.start()

    @pl.loop(0, parts)
    def _(m):
        stack_turned(m, units[OUT][0], dot(dmlt[...], state[m, SUB:, :].astype(bf16)))

    if linked:
        reduce.model(UPDOWN, 3)

    def keeps(m, rows):
        f = forget[m, rows, :]
        kept[rows, :] = f * recip(f + admit[m, rows, :])

    def state_grads(m):
        put(0, slice(None), dot(dml[...], wo[m], True))

    state_grads(of_turn(parts - 1))

    @pl.loop(0, L // R)
    def _(i):
        keeps(of_turn(parts - 1), pl.ds(pl.multiple_of(i * R, R), R))

    @pl.loop(0, parts)
    def _(back_turn):
        turn = parts - 1 - back_turn
        m = of_turn(turn)
        m_next = of_turn((turn + parts - 1) % parts)

        def step(k, carry):
            u, p, keep_next = carry
            j = J - 1 - k
            rows = pl.ds(pl.multiple_of(j * SUB, SUB), SUB)
            u = take(0, rows) + keep_next * u
            p = keep_next * p
            put(0, rows, u)
            put(half, rows, p)
            return u, p, kept[rows, :]

        u, p, keep_first = lax.fori_loop(0, J, step, (fills[0], fills[1], fills[1]), unroll=16)
        enter = fills[0]
        for _ in range(SUB - 1):
            enter = shift_up(keep_first * (u + p * enter))

        if linked:

            @pl.when(turn == 3)
            def _():
                reduce.model(UPDOWN, 1)

            for k in (2, 1, 0):

                @pl.when(turn == k)
                def _():
                    reduce.plane(REST, k + 1)

        @pl.loop(0, L // R)
        def _(i):
            rows = pl.ds(pl.multiple_of(i * R, R), R)
            carried = take(0, rows) + take(half, rows) * spread(enter)
            f = forget[m, rows, :]
            a = admit[m, rows, :]
            adm = a * recip(f + a)
            g = carried * (state[m, rows, :] - cand[m, rows, :]) * (kept[rows, :] * adm)
            dpre[rows, :hm] = (g * (1.0 - f)).astype(bf16)
            dpre[rows, hm : 2 * hm] = (g * (a - 1.0)).astype(bf16)
            dpre[rows, 2 * hm :] = (carried * adm).astype(bf16)
            keeps(m_next, rows)

        for k in range(3):
            stack(m, units[GATE][0], 3 * hm // BLK, k * hm // BLK, dot(n1t[...], dpre[:, k * hm : (k + 1) * hm]))
        for cols in column_halves:
            acc_b[:, cols] += dot(dpre[...], wg[m, cols, :], True)
        state_grads(m_next)
        if linked:
            for k in (3, 2, 1):

                @pl.when(turn == k)
                def _():
                    reduce.chip(REST, k)
                    if k == 1:
                        reduce.model(REST, 3)

    if linked:
        reduce.model(REST, 2)
        reduce.own(UPDOWN)
        reduce.model(REST, 1)

    fetch_tok.wait()
    permute_in(cot, cot)
    def back_one(i, total):
        rows = pl.ds(pl.multiple_of(i * R, R), R)
        x = cot[rows, :].astype(f32)
        r = lax.rsqrt(jnp.mean(x * x, axis=-1, keepdims=True) + norm_eps)
        dn = acc_b[rows, :]
        q = dn * gain_one
        mixed[rows, :] += r * q - r * r * r * x * jnp.mean(q * x, axis=-1, keepdims=True)
        return total + jnp.sum(dn * x * r, axis=0, keepdims=True)

    gain_sum_one = lax.fori_loop(0, L // R, back_one, jnp.zeros((1, D), f32))

    permute_out(acc_a, n1)
    push_out = pltpu.make_async_copy(n1, block_out, local.at[0])
    push_out.start()

    place = lax.broadcasted_iota(jnp.int32, (SUB, hm), 0).astype(f32) * float(J)
    if linked:
        first = ((gather.me * parts + gather.m) * L + 1).astype(f32)
        token_total = float(L * parts * lax.axis_size("dp"))
    else:
        first = base[0]
        token_total = base[1]
    forget_sum = jnp.sum(tally[1] + tally[0] * (place + first), axis=0, keepdims=True) / token_total
    small[...] = jnp.zeros_like(small)
    small[0:1, :] = gain_sum_one
    small[1:2, :] = gain_sum_two
    small[2:3, :hm] = forget_sum
    if linked:
        flat = units[UPDOWN][1] // 2, units[GATE][0]
        count = owned.shape[0]
        flags = []
        for k in range(count):
            spot = slot_place[0, gather.me * count + k]
            flags.append(jnp.where((spot >= flat[0]) & (spot < flat[1]), 1.0, 0.0).astype(f32))

    if linked:
        tiny = SmallSum(net, gather, small, sum_a, sum_b, sum_c)
        tiny.send(0)
        reduce.own(REST)
        reduce.slots_chip(slots, slot_place, pair)
        tiny.add(0)
        tiny.send(1)
        reduce.slots_plane(slots, pair, far)

    permute_out(mixed, acc_a)
    push_grad = pltpu.make_async_copy(acc_a, input_grad, local.at[2])
    push_grad.start()

    if linked:
        tiny.add(1)
        tiny.send(2)
        reduce.slots_end(slots, pair, far, owned)
        tiny.add(2)
        for k, flag in enumerate(flags):
            small[3 + k // 4 : 4 + k // 4, (k % 4) * BLK : (k % 4 + 1) * BLK] = jnp.full((1, BLK), flag, f32)
        net.drain()
    push_out.wait()
    push_grad.wait()


def compute(tokens, cotangent, gains, weights=None, base=None, master=None, owner=None):
    linked = weights is None
    parts = lax.axis_size("mp")
    hm, fm = H // parts, FF // parts
    stacked = (parts, D * (4 * hm + 2 * fm) // BLK**2, BLK, BLK)
    sds = jax.ShapeDtypeStruct
    vm, sm, hbm = (pl.BlockSpec(memory_space=k) for k in (pltpu.VMEM, pltpu.SMEM, pl.ANY))
    if linked:
        n = owner.shape[0]
        args = (tokens, cotangent, master, owner, gains)
        in_specs = [hbm, hbm, hbm, sm, vm]
        middle = sds((n // 8, BLK, BLK), f32)
        extra = [
            pltpu.VMEM((parts, D, 3 * hm), bf16),
            pltpu.VMEM((parts, hm, D), bf16),
            pltpu.VMEM((parts, D, fm), bf16),
            pltpu.VMEM((parts, fm, D), bf16),
            pltpu.VMEM(stacked, bf16),
            pltpu.VMEM((n, BLK, BLK), bf16),
            *[pltpu.VMEM((n, BLK, BLK), bf16) for _ in range(parts - 1)],
            pltpu.VMEM((n // 2, BLK, BLK), bf16),
            pltpu.VMEM((6, n // 16, BLK, BLK), bf16),
            pltpu.VMEM((parts, 8, D), f32),
            pltpu.VMEM((4, 8, D), f32),
            pltpu.VMEM((2, 8, D), f32),
            pltpu.VMEM((8, BLK), jnp.int32),
            pltpu.SMEM((8, BLK), jnp.int32),
            pltpu.SMEM((8, BLK), jnp.int32),
            pltpu.SemaphoreType.DMA((128,)),
            pltpu.SemaphoreType.DMA((128,)),
            pltpu.SemaphoreType.REGULAR,
        ]
        params = dict(collective_id=0, has_side_effects=True)
    else:
        args = (tokens, cotangent, base, *weights, gains)
        in_specs = [hbm, hbm, sm] + [vm] * 5
        middle = sds(stacked, bf16)
        extra = []
        params = {}
    return pl.pallas_call(
        functools.partial(compute_kernel, linked),
        out_shape=(sds((L, D), bf16), sds((L, D), f32), middle, sds((8, D), f32)),
        in_specs=in_specs,
        out_specs=[hbm, hbm, vm, vm],
        scratch_shapes=extra
        + [pltpu.VMEM(shape, bf16) for shape in ((L, D), (D, L)) * 3]
        + [pltpu.VMEM((parts, L, hm), f32)] * 3
        + [pltpu.VMEM((parts, L + SUB, hm), f32)]
        + [pltpu.VMEM((2 * hm // BLK, L, BLK), f32)]
        + [pltpu.VMEM((L, D), f32)] * 3
        + [
            pltpu.VMEM((L, 2 * fm), bf16),
            pltpu.VMEM((L, hm), f32),
            pltpu.VMEM((2, SUB, hm), f32),
            pltpu.VMEM((2, SUB, hm), f32),
            pltpu.SemaphoreType.DMA((3,)),
        ],
        compiler_params=pltpu.CompilerParams(vmem_limit_bytes=64 * 2**20 - 2**16, **params),
        name="block",
    )(*args)


def adam_update(first_old, second_old, gradient):
    first_new = beta_one * first_old + (1.0 - beta_one) * gradient
    second_new = beta_two * second_old + (1.0 - beta_two) * gradient * gradient
    first_hat = first_new / (1.0 - beta_one**STEP)
    second_hat = second_new / (1.0 - beta_two**STEP)
    return (first_new, second_new, first_hat / (jnp.sqrt(second_hat) + adam_eps))


def fine_dot(a, b, trans_b=False):
    a_high, b_high = a.astype(bf16), b.astype(bf16)
    a_low, b_low = (a - a_high.astype(f32)).astype(bf16), (b - b_high.astype(f32)).astype(bf16)
    return dot(a_high, b_high, trans_b) + (dot(a_high, b_low, trans_b) + dot(a_low, b_high, trans_b))


def update_kernel(token_total, passed, sums, gains, gain_moment_one, gain_moment_two, *refs):
    sources, refs = refs[:6], refs[6:]
    given, refs = refs[:passed], refs[passed:]
    results, refs = refs[:4], refs[4:]
    gain_first, gain_second, gains_new, forget_mean = refs[:4]
    copied, refs = refs[4 : 4 + passed], refs[4 + passed :]
    held, made, made_low, sem_in, sem_out, sem_pass = refs[:6]
    passage = refs[6:]
    count = held.shape[1]
    step = max(count // 2, 1)
    groups = [slice(first, first + step) for first in range(0, count, step)]
    enter = [pltpu.make_async_copy(src, via, sem_pass.at[0, k]) for k, (src, via) in enumerate(zip(given, passage))]
    leave = [pltpu.make_async_copy(via, dst, sem_pass.at[1, k]) for k, (via, dst) in enumerate(zip(passage, copied))]
    fetch = [
        [pltpu.make_async_copy(src.at[group], held.at[k, group], sem_in.at[g, k]) for k, src in enumerate(sources)]
        for g, group in enumerate(groups)
    ]
    for copy in fetch[0]:
        copy.start()
    for copy in enter:
        copy.start()
    for row in fetch[1:]:
        for copy in row:
            copy.start()
    first, second, direction = adam_update(gain_moment_one[...], gain_moment_two[...], sums[0:2, :])
    gain_first[...] = first
    gain_second[...] = second
    gains_new[...] = gains[...] - gain_rate * direction
    forget_mean[...] = jnp.sum(sums[2:3, :], axis=1, keepdims=True) * (1.0 / (H * (token_total + 1) / 2.0))
    push = []
    for g, group in enumerate(groups):
        blocks = range(group.start, group.stop)
        for copy in fetch[g]:
            copy.wait()
        if g == len(groups) - 1:
            for come, go in zip(enter, leave):
                come.wait()
                go.start()
        grads = []
        for s in blocks:
            grad = held[0, s]
            flag = sums[3 + s // 4 : 4 + s // 4, (s % 4) * BLK : (s % 4 + 1) * BLK]
            grads.append(jnp.where(flag > 0.5, grad.T, grad))
        values = [fine_dot(held[1, s].T, grad) for s, grad in zip(blocks, grads)]
        values = [fine_dot(value, held[2, s]) for s, value in zip(blocks, values)]
        for k, s in enumerate(blocks):
            first, second, values[k] = adam_update(held[3, s], held[4, s], values[k])
            made[0, s] = first
            made[1, s] = second
        values = [fine_dot(held[1, s], value) for s, value in zip(blocks, values)]
        values = [fine_dot(value, held[2, s], True) for s, value in zip(blocks, values)]
        for s, value in zip(blocks, values):
            fresh = held[5, s] - learn_rate * (value + weight_decay * held[5, s])
            made[2, s] = fresh
            made_low[s] = fresh.astype(bf16)
        for k, dst in enumerate(results):
            src = made.at[k, group] if k < 3 else made_low.at[group]
            copy = pltpu.make_async_copy(src, dst.at[group], sem_out.at[g, k])
            copy.start()
            push.append(copy)
    for copy in push + leave:
        copy.wait()


def update(token_total, small, large, passed):
    sds = jax.ShapeDtypeStruct
    blocks, gain = large[0].shape, small[1].shape
    vm, hbm = pl.BlockSpec(memory_space=pltpu.VMEM), pl.BlockSpec(memory_space=pl.ANY)
    return pl.pallas_call(
        functools.partial(update_kernel, token_total, len(passed)),
        out_shape=[sds(blocks, f32)] * 3
        + [sds(blocks, bf16)]
        + [sds(gain, f32)] * 3
        + [sds((1, 1), f32)]
        + [sds(v.shape, v.dtype) for v in passed],
        in_specs=[vm] * 4 + [hbm] * (len(large) + len(passed)),
        out_specs=[hbm] * 4 + [vm] * 4 + [hbm] * len(passed),
        scratch_shapes=[
            pltpu.VMEM((6, *blocks), f32),
            pltpu.VMEM((3, *blocks), f32),
            pltpu.VMEM(blocks, bf16),
            pltpu.SemaphoreType.DMA((2, 6)),
            pltpu.SemaphoreType.DMA((2, 4)),
            pltpu.SemaphoreType.DMA((2, len(passed))),
        ]
        + [pltpu.VMEM(v.shape, v.dtype) for v in passed],
        compiler_params=pltpu.CompilerParams(vmem_limit_bytes=56 * 2**20),
        name="update",
    )(*small, *large, *passed)


def on_device(
    tokens,
    cotangent,
    master,
    moment_one,
    moment_two,
    basis_left,
    basis_right,
    owner,
    gains,
    gain_moment_one,
    gain_moment_two,
):
    parts = lax.axis_size("mp")
    data_parts = lax.axis_size("dp")
    hm, fm = H // parts, FF // parts
    token_total = L * data_parts * parts
    row_tiles, cols, lows = D // BLK, (3 * hm + fm) // BLK, (hm + fm) // BLK
    if data_parts == 8 and parts == 4:
        block_out, input_grad, owned, sums = compute(tokens, cotangent, gains, master=master[0], owner=owner)
    else:
        number = jnp.arange(owner.shape[0], dtype=jnp.int32)
        ahead = (owner[None, :] < owner[:, None]) | ((owner[None, :] == owner[:, None]) & (number[None, :] < number[:, None]))
        block_rank = jnp.sum(ahead.astype(jnp.int32), axis=1)
        _, table = stack_places(hm, fm)
        table = jnp.asarray(table, jnp.int32)
        slot_place = jnp.sum(jnp.where(block_rank[None, :] == number[:, None], table[None, :], 0), axis=1)
        stored = lax.all_gather(master.astype(bf16), "dp", axis=1, tiled=True)
        stored = lax.all_gather(stored, "mp", axis=0, tiled=True)
        stack = stored[:, block_rank]
        upper = stack[:, : row_tiles * cols].reshape(parts, row_tiles, cols, BLK, BLK)
        upper = upper.transpose(0, 1, 3, 2, 4).reshape(parts, D, cols * BLK)
        lower = stack[:, row_tiles * cols :].reshape(parts, lows, row_tiles, BLK, BLK)
        lower = lower.transpose(0, 1, 3, 2, 4).reshape(parts, lows * BLK, D)
        weights = (upper[:, :, : 3 * hm], lower[:, :hm], upper[:, :, 3 * hm :], lower[:, hm:])
        first = ((lax.axis_index("dp") * parts + lax.axis_index("mp")) * L + 1).astype(f32)
        base = jnp.stack([first, jnp.asarray(token_total, f32)])
        block_out, input_grad, grads, sums = compute(tokens, cotangent, gains, weights=weights, base=base)
        owned = lax.psum_scatter(grads[:, slot_place].astype(f32), "dp", scatter_dimension=1, tiled=True)
        owned = lax.psum_scatter(owned, "mp", scatter_dimension=0, tiled=True)[0]
        sums = lax.psum(sums, ("dp", "mp"))
        count = master.shape[1]
        mine = lax.dynamic_slice_in_dim(slot_place, lax.axis_index("dp") * count, count)
        units, _ = stack_places(hm, fm)
        flags = ((mine >= units[UPDOWN][1] // 2) & (mine < units[GATE][0])).astype(f32)
        flags = jnp.pad(jnp.repeat(flags, BLK), (0, (8 - count) * BLK)).reshape(2, 4 * BLK)
        sums = jnp.concatenate([sums[:3], flags, sums[5:]])
    outs = update(
        token_total,
        (sums, gains, gain_moment_one, gain_moment_two),
        (owned, basis_left[0], basis_right[0], moment_one[0], moment_two[0], master[0]),
        (block_out, input_grad),
    )
    first_new, second_new, master_new, master_low, gain_first, gain_second, gains_new, forget_mean = outs[:8]
    block_out, input_grad = outs[8:]
    return (
        block_out,
        input_grad,
        first_new[None],
        second_new[None],
        master_new[None],
        master_low[None],
        gain_first,
        gain_second,
        gains_new,
        forget_mean[0, 0],
    )


def solution(mesh):
    rows, blocks = P(("dp", "mp"), None), P("mp", "dp", None, None)
    return jax.shard_map(
        on_device,
        mesh=mesh,
        in_specs=(rows, rows, blocks, blocks, blocks, blocks, blocks, P(), P(), P(), P()),
        out_specs=(rows, rows, blocks, blocks, blocks, blocks, P(), P(), P(), P()),
        check_vma=False,
    )
```

```python
import functools

import jax
import jax.numpy as jnp
from jax import lax
from jax.experimental import pallas as pl
from jax.experimental.pallas import tpu as pltpu
from jax.sharding import PartitionSpec as P

D = 512
H = 1024
FF = 2048
BLK = 128
STEP = 10
L = 1024

norm_eps = 1e-05
beta_one = 0.5
beta_two = 0.5
adam_eps = 1e-08
learn_rate = 0.02
gain_rate = 0.1
weight_decay = 0.1
highest = lax.Precision.HIGHEST

f32 = jnp.float32
bf16 = jnp.bfloat16
SUB = 8
J = L // SUB
R = 256


def dot(a, b, trans_b=False):
    dims = (((1,), (1,)), ((), ())) if trans_b else (((1,), (0,)), ((), ()))
    return lax.dot_general(a, b, dims, preferred_element_type=f32)


def recip(v):
    return pltpu.reciprocal(v, approx=True)


def sigmoid(v):
    return recip(1.0 + jnp.exp(-v))


def shift_down(v):
    rolled = pltpu.roll(v, 1, 0)
    row = lax.broadcasted_iota(jnp.int32, v.shape, 0)
    return jnp.where(row == 0, 0.0, rolled)


def shift_up(v):
    rolled = pltpu.roll(v, SUB - 1, 0)
    row = lax.broadcasted_iota(jnp.int32, v.shape, 0)
    return jnp.where(row == SUB - 1, 0.0, rolled)


def gelu_terms(x):
    a = jnp.abs(x)
    t = recip(1.0 + a * (0.3275911 * 0.7071067811865476))
    poly = t * (
        0.5 * 0.254829592
        + t
        * (
            0.5 * -0.284496736
            + t * (0.5 * 1.421413741 + t * (0.5 * -1.453152027 + t * (0.5 * 1.061405429)))
        )
    )
    e = jnp.exp(x * x * -0.5)
    tail = poly * e
    cdf = jnp.where(x < 0.0, tail, 1.0 - tail)
    return cdf, x * e * 0.3989422804014327


MESH = pl.DeviceIdType.MESH


class Copy:
    def __init__(self, net, make):
        self.net, self.make = net, make

    def start(self):
        self.net.open.append(self)
        self.make().start()
        return self

    def wait_recv(self):
        self.make().wait_recv()

    def wait_send(self):
        self.make().wait_send()


class Exchange:
    def __init__(self, send, recv):
        self.send, self.recv, self.known, self.used, self.open = send, recv, {}, 0, []

    def copy(self, parts, key=None):
        if key in self.known:
            return self.known[key]
        k = self.used
        self.used += 1

        def make():
            src, dst, device = parts()
            return pltpu.make_async_remote_copy(
                src_ref=src,
                dst_ref=dst,
                send_sem=self.send.at[k],
                recv_sem=self.recv.at[k],
                device_id=device,
                device_id_type=MESH,
            )

        copy = Copy(self, make)
        if key is not None:
            self.known[key] = copy
        return copy

    def start(self, parts):
        return self.copy(parts).start()

    def drain(self):
        for copy in self.open:
            copy.wait_send()
        self.open = []


class Gather:
    def __init__(self, net, fetch, master, slots, pool, weights, free):
        self.net, self.weights, self.free = net, weights, free
        self.held = [slots, *pool]
        d, m = lax.axis_index("dp"), lax.axis_index("mp")
        core, col, row = d % 2, (d // 2) % 2, d // 4
        self.me, self.m, self.side = d, m, core
        self.core = d + 1 - 2 * core
        self.plane = [d + 2 - 4 * col, d + 4 - 8 * row, d + 6 - 4 * col - 8 * row]
        self.order = [m, m + 1 - 2 * (m % 2), m + 2 - 4 * (m // 2), 3 - m]
        self.peers = [(e, m) for e in [self.core] + self.plane] + [(d, k) for k in self.order[1:]]
        barrier = pltpu.get_barrier_semaphore()
        for device in self.peers:
            pl.semaphore_signal(barrier, inc=1, device_id=device, device_id_type=MESH)
        self.n = master.shape[0]
        fetch.wait()
        for s in range(self.n):
            slots[d * self.n + s] = master[s].astype(bf16)
        pl.semaphore_wait(barrier, len(self.peers))

    def rows(self, i, e, first, count):
        return self.held[i].at[pl.ds(e * self.n + first, count)]

    def along(self, i, e):
        return self.net.copy(
            lambda: (self.rows(0, e, 0, self.n), self.rows(i, e, 0, self.n), (self.me, self.order[i])),
            ("along", i, e is self.me),
        )

    def within(self, key, i, e, first, count, to):
        return self.net.copy(
            lambda: (self.rows(i, e, first, count), self.rows(i, e, first, count), (to, self.m)), (key, i)
        )

    def first(self, i):
        (x, y, _), h = self.plane, self.n // 2
        if i == 1:
            jobs = ((0, self.n, x), (0, self.n, y))
        else:
            jobs = ((0, h, x), (h, h, y), (h, h, x), (0, h, y))
        return [self.within(("first", k), i, self.me, *job) for k, job in enumerate(jobs)]

    def last(self, i):
        x, y, z = self.plane
        if i == 1:
            return [self.along(1, z)]
        h = self.n // 2
        return [self.within("over y", i, x, 0, h, y), self.within("over x", i, y, h, h, x)]

    def inside(self, i):
        return [self.within(("inside", k), i, e, 0, self.n, self.core) for k, e in enumerate([self.me] + self.plane)]

    def along_start(self, i):
        self.along(i, self.me).start()

    def across_start(self):
        self.last(1)[0].start()

    def start(self, i):
        if i:
            self.along(i, self.me).wait_recv()
        for copy in self.first(i):
            copy.start()
        self.inside(i)[0].start()

    def forward(self, i):
        if i == 1:
            return
        for came, copy in zip(self.first(i), self.last(i)):
            came.wait_recv()
            copy.start()

    def pair(self, i):
        for came, copy in zip(self.first(i)[-2:], self.inside(i)[1:3]):
            came.wait_recv()
            copy.start()
        for came in self.last(i):
            came.wait_recv()
        self.inside(i)[3].start()

    def ready(self, i):
        for copy in self.inside(i):
            copy.wait_recv()

    def place(self, i, rank):
        wg, wo, wu, wd = self.weights
        row_tiles, gates = D // BLK, wg.shape[2] // BLK
        cols, outs = gates + wu.shape[2] // BLK, wo.shape[1] // BLK
        for b in range(row_tiles * cols + (wo.shape[1] + wd.shape[1]) // BLK * row_tiles):
            if b < row_tiles * cols:
                r, c = b // cols, b % cols
                ref = wg if c < gates else wu
                c -= 0 if c < gates else gates
            else:
                r, c = (b - row_tiles * cols) // row_tiles, (b - row_tiles * cols) % row_tiles
                ref = wo if r < outs else wd
                r -= 0 if r < outs else outs
            block = self.held[i][rank[0, b]]
            ref[self.order[i], r * BLK : (r + 1) * BLK, c * BLK : (c + 1) * BLK] = block

    def done(self):
        for device in self.peers:
            pl.semaphore_signal(self.free, inc=1, device_id=device, device_id_type=MESH)

    def all_done(self):
        pl.semaphore_wait(self.free, len(self.peers))


def stack_places(hm, fm):
    row_tiles, gates, ups, outs = D // BLK, 3 * hm // BLK, fm // BLK, hm // BLK
    cols = gates + ups
    first_down = row_tiles * ups
    first_out = 2 * first_down
    first_gate = first_out + row_tiles * outs
    table = []
    for b in range(row_tiles * (cols + outs + ups)):
        if b < row_tiles * cols:
            r, c = b // cols, b % cols
            table.append(first_gate + r * gates + c if c < gates else r * ups + c - gates)
        else:
            k = b - row_tiles * cols
            table.append(first_out + k if k < row_tiles * outs else first_down + k - row_tiles * outs)
    return ((0, first_out), (first_out, row_tiles * outs), (first_gate, row_tiles * gates)), table


UPDOWN, OUT, GATE = range(3)


class Reduce:
    def __init__(self, net, gather, grads, units, pool):
        self.net, self.g, self.grads, self.units, self.pool = net, gather, grads, units, pool
        self.half = grads.shape[1] // 2
        self.eighth = grads.shape[1] // 8

    def place(self, e):
        return (e % 2) * 4 + e // 2

    def inside(self, unit, i):
        g, (first, count) = self.g, self.units[unit]
        return self.net.copy(
            lambda: (
                self.grads.at[g.order[i], pl.ds(first + (1 - g.side) * (count // 2), count // 2)],
                self.pool[i - 1].at[pl.ds(first // 2, count // 2)],
                (g.core, g.m),
            ),
            ("chip", unit, i),
        )

    def chip(self, unit, i):
        self.inside(unit, i).start()

    def spot(self, unit, i, slot, first, count):
        base, total = self.units[unit]
        return self.pool[i - 1].at[pl.ds(self.half + slot * self.eighth + base // 8 + first, count)]

    def direct(self, unit, i):
        return i == 1 or unit == UPDOWN

    def parts(self, unit, i):
        n = self.units[unit][1] // 8
        if self.direct(unit, i):
            return ((0, n),)
        h = (n + i % 2) // 2 if n % 2 else n // 2
        return (0, h), (h, n - h)

    def share(self, unit, i, e, first, count):
        base, total = self.units[unit]
        return self.grads.at[self.g.order[i], pl.ds(base + self.place(e) * (total // 8) + first, count)]

    def over(self, unit, i, slot, part):
        x, y, z = self.g.plane
        e = (z, x, y)[slot]
        by = z if self.direct(unit, i) else x if part == self.parts(unit, i)[0] else y
        to = (by, x, y)[slot]
        return self.net.copy(
            lambda: (self.share(unit, i, e, *part), self.spot(unit, i, slot, *part), (to, self.g.m)),
            ("over", unit, i, slot, part),
        )

    def send(self, unit, i, slot, part):
        if part[1]:
            self.over(unit, i, slot, part).start()

    def take(self, unit, i, slot, part):
        self.over(unit, i, slot, part).wait_recv()
        return self.spot(unit, i, slot, *part)[...].astype(f32)

    def model_copy(self, unit, i):
        n = self.units[unit][1] // 8
        return self.net.copy(
            lambda: (self.share(unit, i, self.g.me, 0, n), self.spot(unit, i, 3, 0, n), (self.g.me, self.g.order[i])),
            ("model", unit, i),
        )

    def aside(self, unit):
        part = (0, self.units[unit][1] // 8)
        return self.net.copy(
            lambda: (
                self.share(unit, 1, self.g.plane[2], *part),
                self.spot(unit, 1, 0, *part),
                (self.g.me, self.g.order[1]),
            ),
            ("aside", unit),
        )

    def plane(self, unit, i):
        g, (first, count) = self.g, self.units[unit]
        x, y, z = g.plane
        self.inside(unit, i).wait_recv()
        m = g.order[i]
        start, came = first + g.side * (count // 2), self.pool[i - 1]

        @pl.loop(0, count // 2, unroll=4)
        def _(b):
            total = self.grads[m, start + b].astype(f32) + came[first // 2 + b].astype(f32)
            self.grads[m, start + b] = total.astype(bf16)

        if self.direct(unit, i):
            (whole,) = self.parts(unit, i)
            self.send(unit, i, 1, whole)
            self.send(unit, i, 2, whole)
            if i == 1:
                self.aside(unit).start()
            else:
                self.send(unit, i, 0, whole)
            return
        one, two = self.parts(unit, i)
        self.send(unit, i, 0, one)
        self.send(unit, i, 0, two)
        self.send(unit, i, 1, one)
        self.send(unit, i, 2, two)

    def turn(self, unit, i):
        if self.direct(unit, i):
            return
        x, y, _ = self.g.plane
        for part, slot, e in zip(self.parts(unit, i), (2, 1), (y, x)):
            if part[1]:
                ref = self.share(unit, i, e, *part)
                ref[...] = (ref[...].astype(f32) + self.take(unit, i, 0, part)).astype(bf16)
                self.send(unit, i, slot, part)

    def model(self, unit, i):
        g, (first, count) = self.g, self.units[unit]
        n = count // 8
        for part in self.parts(unit, i):
            if part[1]:
                ref = self.share(unit, i, g.me, *part)
                total = ref[...].astype(f32) + self.take(unit, i, 1, part) + self.take(unit, i, 2, part)
                if i > 1 and self.direct(unit, i):
                    total += self.take(unit, i, 0, part)
                ref[...] = total.astype(bf16)
        self.model_copy(unit, i).start()

    def own(self, unit):
        g, (first, count) = self.g, self.units[unit]
        n = count // 8
        rows = pl.ds(first + self.place(g.me) * n, n)
        total = self.grads[g.m, rows].astype(f32)
        for i in (1, 2, 3):
            self.model_copy(unit, i).wait_recv()
            total += self.pool[i - 1][pl.ds(self.half + 3 * self.eighth + first // 8, n)].astype(f32)
        self.grads[g.m, rows] = total.astype(bf16)
        self.aside(unit).wait_recv()
        rows = pl.ds(first + self.place(g.plane[2]) * n, n)
        total = self.grads[g.m, rows].astype(f32) + self.spot(unit, 1, 0, 0, n)[...].astype(f32)
        self.grads[g.m, rows] = total.astype(bf16)

    def into_slots(self, out, slot_place, e):
        n = self.eighth
        for k in range(n):
            out[self.place(e) * n + k] = self.grads[self.g.m, slot_place[0, e * n + k]]

    def slots_chip(self, out, slot_place, pair):
        g, n = self.g, self.eighth
        self.last = []
        targets = (g.plane[2], g.plane[0], g.plane[1], g.me)
        for e in targets:
            other = e + 1 - 2 * g.side
            self.into_slots(out, slot_place, other)
            self.last.append(
                self.net.start(
                    lambda e=e, other=other: (
                        out.at[pl.ds(self.place(other) * n, n)],
                        pair.at[pl.ds((e // 2) * n, n)],
                        (g.core, g.m),
                    )
                )
            )
        for e in targets:
            self.into_slots(out, slot_place, e)

    def slots_plane(self, out, pair, far):
        g, n = self.g, out.shape[0] // 8
        h = n // 2
        x, y, z = g.plane
        wait = dict(zip("zxyo", self.last))

        def mine(e, first, count):
            return pl.ds((g.side * 4 + e // 2) * n + first, count)

        def join(e):
            rows = mine(e, 0, n)
            out[rows] = (out[rows].astype(f32) + pair[pl.ds((e // 2) * n, n)].astype(f32)).astype(bf16)

        def send(e, first, slot, to):
            return self.net.start(lambda: (out.at[mine(e, first, h)], far.at[slot], (to, g.m)))

        wait["z"].wait_recv()
        join(z)
        over_x = send(z, 0, 0, x)
        over_y = send(z, h, 1, y)
        wait["x"].wait_recv()
        join(x)
        self.ends = [send(x, 0, 2, x)]
        wait["y"].wait_recv()
        join(y)
        self.ends.append(send(y, h, 3, y))
        over_x.wait_recv()
        rows = mine(y, 0, h)
        out[rows] = (out[rows].astype(f32) + far[0].astype(f32)).astype(bf16)
        self.ends.append(send(y, 0, 4, y))
        over_y.wait_recv()
        rows = mine(x, h, h)
        out[rows] = (out[rows].astype(f32) + far[1].astype(f32)).astype(bf16)
        self.ends.append(send(x, h, 5, x))
        wait["o"].wait_recv()

    def slots_end(self, out, pair, far, owned):
        g, n = self.g, out.shape[0] // 8
        h = n // 2
        for copy in self.ends:
            copy.wait_recv()
        for first, slots in ((0, (2, 4)), (h, (3, 5))):
            total = out[pl.ds((g.side * 4 + g.me // 2) * n + first, h)].astype(f32)
            total += pair[pl.ds((g.me // 2) * n + first, h)].astype(f32)
            for k in slots:
                total += far[k].astype(f32)
            owned[first : first + h] = total


class SmallSum:
    def __init__(self, net, gather, values, along, across, inside):
        self.net, self.g, self.values = net, gather, values
        self.slots = (along, across, inside)
        self.peers = (
            [(gather.me, k) for k in gather.order[1:]],
            [(e, gather.m) for e in gather.plane],
            [(gather.core, gather.m)],
        )
        self.mine = (gather.m, gather.me // 2, gather.side)
        self.open = []

    def send(self, stage):
        slot = self.slots[stage]
        slot[self.mine[stage]] = self.values[...]
        ref = slot.at[self.mine[stage]]
        self.open = [self.net.start(lambda peer=peer: (ref, ref, peer)) for peer in self.peers[stage]]

    def add(self, stage):
        for copy in self.open:
            copy.wait_recv()
        slot = self.slots[stage]
        total = slot[0]
        for k in range(1, slot.shape[0]):
            total += slot[k]
        self.values[...] = total


def number_blocks(owner, table, vector, rank, slot_place, sem):
    lane = lax.broadcasted_iota(jnp.int32, vector.shape, 1)
    count = owner.shape[0]
    owners = jnp.zeros_like(lane)
    for b in range(count):
        owners = jnp.where(lane == b, owner[b], owners)
    ranks = jnp.zeros_like(lane)
    for b in range(count):
        ahead = (owner[b] < owners) | ((owner[b] == owners) & (lane > b))
        ranks += jnp.where(ahead, 1, 0)
    vector[...] = ranks
    copy = pltpu.make_async_copy(vector, rank, sem)
    copy.start()
    copy.wait()
    places = jnp.zeros_like(lane)
    for b in range(count):
        places = jnp.where(lane == rank[0, b], table[b], places)
    vector[...] = places
    copy = pltpu.make_async_copy(vector, slot_place, sem)
    copy.start()
    copy.wait()


def compute_kernel(linked, *refs):
    if linked:
        tokens, cotangent, master, owner, gains = refs[:5]
        block_out, input_grad, owned, small = refs[5:9]
        wg, wo, wu, wd, grads, slots, *pool, pair, far, sum_a, sum_b, sum_c, vector, rank, slot_place, send, recv, free = refs[9:29]
        scratch = refs[29:]
    else:
        tokens, cotangent, base, wg, wo, wu, wd, gains = refs[:8]
        block_out, input_grad, grads, small = refs[8:12]
        scratch = refs[12:]
    (n1, n1t, cot, cott, n2, n2t, forget, admit, cand, state, scan, acc_a, acc_b, mixed, mid, kept, fills, tally, local) = scratch
    dml, dmlt = n2, n2t
    parts, _, hm3 = wg.shape
    hm = hm3 // 3
    fm = wu.shape[2]
    units, table = stack_places(hm, fm)
    act, dup, dpre = mid.at[:, :fm], mid.at[:, fm:], mid.at[:, : 3 * hm]
    gain_one = gains[0:1, :]
    gain_two = gains[1:2, :]

    if linked:
        fetch_master = pltpu.make_async_copy(master, owned, local.at[2])
        fetch_master.start()
    fetch_cot = pltpu.make_async_copy(cotangent, cot, local.at[0])
    fetch_tok = pltpu.make_async_copy(tokens, n1, local.at[1])
    fetch_tok.start()
    fetch_cot.start()

    column_halves = (slice(0, D // 2), slice(D // 2, D))

    def stack(m, first, wide, left, value):
        for r in range(value.shape[0] // BLK):
            for c in range(value.shape[1] // BLK):
                grads[m, first + r * wide + left + c] = value[r * BLK : (r + 1) * BLK, c * BLK : (c + 1) * BLK].astype(bf16)

    def stack_turned(m, first, value):
        high = value.shape[0] // BLK
        for r in range(high):
            for c in range(value.shape[1] // BLK):
                grads[m, first + c * high + r] = value[r * BLK : (r + 1) * BLK, c * BLK : (c + 1) * BLK].astype(bf16)

    def permute_in(src, dst):
        for k in range(D // BLK):
            scan[k] = src[:, k * BLK : (k + 1) * BLK].astype(f32)

        @pl.loop(0, J // 2, unroll=4)
        def _(j):
            for k in range(D // BLK):
                lo = scan[k, pl.ds(2 * j, SUB, stride=J), :]
                hi = scan[k, pl.ds(2 * j + 1, SUB, stride=J), :]
                dst[pl.ds(pl.multiple_of(16 * j, 16), 16), k * BLK : (k + 1) * BLK] = jnp.concatenate([lo, hi], 0).astype(bf16)

    def permute_out(src, dst):
        @pl.loop(0, J, unroll=4)
        def _(j):
            rows = pl.ds(pl.multiple_of(j * SUB, SUB), SUB)
            for k in range(D // BLK):
                scan[k, pl.ds(j, SUB, stride=J), :] = src[rows, k * BLK : (k + 1) * BLK]

        for k in range(D // BLK):
            dst[:, k * BLK : (k + 1) * BLK] = scan[k].astype(dst.dtype)

    def put(first, rows, value):
        for k in range(hm // BLK):
            scan[first + k, rows, :] = value[:, k * BLK : (k + 1) * BLK]

    def take(first, rows):
        return jnp.concatenate([scan[first + k, rows, :] for k in range(hm // BLK)], 1)

    half = hm // BLK

    def spread(v):
        return jnp.broadcast_to(v[None], (R // SUB, SUB, hm)).reshape(R, hm)


    if linked:
        net = Exchange(send, recv)
        gather = Gather(net, fetch_master, owned, slots, pool, (wg, wo, wu, wd), free)
        gather.start(0)
        gather.along_start(1)
        gather.along_start(2)
        reduce = Reduce(net, gather, grads, units, pool)

    def of_turn(t):
        if not linked:
            return t
        high, low = gather.m // 2, gather.m % 2
        t_high, t_low = t // 2, t % 2
        return 2 * (high + t_high - 2 * high * t_high) + low + t_low - 2 * low * t_low

    fetch_tok.wait()
    permute_in(n1, n1)
    mixed[...] = n1[...].astype(f32)

    @pl.loop(0, L // R)
    def _(i):
        rows = pl.ds(pl.multiple_of(i * R, R), R)
        x = mixed[rows, :]
        r = lax.rsqrt(jnp.mean(x * x, axis=-1, keepdims=True) + norm_eps)
        n1[rows, :] = (x * r * gain_one).astype(bf16)

    n1t[...] = n1[...].T

    if linked:
        gather.forward(0)
        gather.along_start(3)
        number_blocks(owner, table, vector, rank, slot_place, local.at[2])
    fetch_cot.wait()
    permute_in(cot, cot)
    if linked:
        gather.start(1)
        gather.pair(0)
        gather.across_start()
        gather.start(2)
    cott[...] = cot[...].T

    fills[0] = jnp.zeros((SUB, hm), f32)
    fills[1] = jnp.ones((SUB, hm), f32)
    tally[0] = fills[0]
    tally[1] = fills[0]

    @pl.loop(0, parts)
    def _(turn):
        m = of_turn(turn)
        if linked:
            for k in range(parts):

                @pl.when(turn == k)
                def _():
                    if k > 1:
                        gather.pair(k)
                    gather.ready(k)
                    gather.place(k, rank)

        forget[m] = dot(n1[...], wg[m, :, :hm])
        admit[m] = dot(n1[...], wg[m, :, hm : 2 * hm])
        cand[m] = dot(n1[...], wg[m, :, 2 * hm :])

        if linked:

            @pl.when(turn == 2)
            def _():
                gather.forward(3)

        @pl.loop(0, L // R)
        def _(i):
            rows = pl.ds(pl.multiple_of(i * R, R), R)
            f = sigmoid(forget[m, rows, :])
            a = sigmoid(admit[m, rows, :])
            inv = recip(f + a)
            forget[m, rows, :] = f
            admit[m, rows, :] = a
            kept[rows, :] = f * inv
            put(0, rows, a * inv * cand[m, rows, :])

        def step(j, carry):
            s, p, k_sum, kj_sum = carry
            rows = pl.ds(pl.multiple_of(j * SUB, SUB), SUB)
            keep = kept[rows, :]
            s = keep * s + take(0, rows)
            p = keep * p
            put(0, rows, s)
            put(half, rows, p)
            return s, p, k_sum + keep, kj_sum + keep * j.astype(f32)

        s, p, k_sum, kj_sum = lax.fori_loop(0, J, step, (fills[0], fills[1], fills[0], fills[0]), unroll=16)
        tally[0] += k_sum
        tally[1] += kj_sum
        enter = fills[0]
        for _ in range(SUB - 1):
            enter = shift_down(s + p * enter)

        @pl.loop(0, L // R)
        def _(i):
            rows = pl.ds(pl.multiple_of(i * R, R), R)
            state[m, pl.ds(pl.multiple_of(i * R + SUB, SUB), R), :] = take(0, rows) + take(half, rows) * spread(enter)

        state[m, :SUB, :] = shift_down(state[m, L:, :])
        for cols in column_halves:
            mixed[:, cols] += dot(state[m, SUB:, :].astype(bf16), wo[m, :, cols])
        if linked:

            @pl.when(turn == 0)
            def _():
                gather.pair(1)
                gather.forward(2)
                gather.start(3)

    if linked:
        net.drain()
        gather.done()

    @pl.loop(0, L // R)
    def _(i):
        rows = pl.ds(pl.multiple_of(i * R, R), R)
        x = mixed[rows, :]
        r = lax.rsqrt(jnp.mean(x * x, axis=-1, keepdims=True) + norm_eps)
        n2[rows, :] = (x * r * gain_two).astype(bf16)
        acc_a[rows, :] = x
        acc_b[rows, :] = jnp.zeros_like(x)

    n2t[...] = n2[...].T

    @pl.loop(0, parts)
    def _(turn):
        m = of_turn((2 * (turn // 2 + turn % 2 - 2 * (turn // 2) * (turn % 2)) + turn // 2) if linked else turn)
        for first in range(0, fm, fm // 2):
            units_of = slice(first, first + fm // 2)
            up = dot(n2[...], wu[m, :, units_of])
            da = dot(cot[...], wd[m, units_of, :], True)
            cdf, xpdf = gelu_terms(up)
            act[:, units_of] = (up * cdf).astype(bf16)
            dup[:, units_of] = (da * (cdf + xpdf)).astype(bf16)
            if linked and first == 0:

                @pl.when(turn == 2)
                def _():
                    reduce.plane(UPDOWN, 2)

                @pl.when(turn == 3)
                def _():
                    reduce.plane(UPDOWN, 3)

        for cols in column_halves:
            acc_a[:, cols] += dot(act[...], wd[m, :, cols])
        for cols in column_halves:
            acc_b[:, cols] += dot(dup[...], wu[m, cols, :], True)
        for c in range(0, fm, fm // 2):
            part = slice(c, c + fm // 2)
            stack(m, 0, fm // BLK, c // BLK, dot(n2t[...], dup[:, part]))
        for c in range(0, fm, fm // 2):
            part = slice(c, c + fm // 2)
            stack_turned(m, units[UPDOWN][1] // 2 + c // BLK * (D // BLK), dot(cott[...], act[:, part]))
        if linked:

            @pl.when(turn == 1)
            def _():
                gather.all_done()
                reduce.chip(UPDOWN, 2)

            @pl.when(turn == 2)
            def _():
                reduce.chip(UPDOWN, 3)
                reduce.turn(UPDOWN, 2)

            @pl.when(turn == 3)
            def _():
                reduce.chip(UPDOWN, 1)
                reduce.turn(UPDOWN, 3)
                reduce.model(UPDOWN, 2)

    gain_sum_two = jnp.zeros((1, D), f32)

    def back_two(i, total):
        rows = pl.ds(pl.multiple_of(i * R, R), R)
        x = mixed[rows, :]
        r = lax.rsqrt(jnp.mean(x * x, axis=-1, keepdims=True) + norm_eps)
        dn = acc_b[rows, :]
        q = dn * gain_two
        d = cot[rows, :].astype(f32) + r * q - r * r * r * x * jnp.mean(q * x, axis=-1, keepdims=True)
        mixed[rows, :] = d
        dml[rows, :] = d.astype(bf16)
        acc_b[rows, :] = jnp.zeros_like(d)
        return total + jnp.sum(dn * x * r, axis=0, keepdims=True)

    gain_sum_two = lax.fori_loop(0, L // R, back_two, gain_sum_two)
    if linked:
        reduce.plane(UPDOWN, 1)
    dmlt[...] = dml[...].T
    fetch_tok = pltpu.make_async_copy(tokens, cot, local.at[1])
    fetch_tok.start()

    @pl.loop(0, parts)
    def _(m):
        stack_turned(m, units[OUT][0], dot(dmlt[...], state[m, SUB:, :].astype(bf16)))

    if linked:
        for i in (3, 2, 1):
            reduce.chip(OUT, i)
        reduce.model(UPDOWN, 3)

    def keeps(m, rows):
        f = forget[m, rows, :]
        kept[rows, :] = f * recip(f + admit[m, rows, :])

    def state_grads(m):
        put(0, slice(None), dot(dml[...], wo[m], True))

    state_grads(of_turn(parts - 1))

    @pl.loop(0, L // R)
    def _(i):
        keeps(of_turn(parts - 1), pl.ds(pl.multiple_of(i * R, R), R))

    @pl.loop(0, parts)
    def _(back_turn):
        turn = parts - 1 - back_turn
        m = of_turn(turn)
        m_next = of_turn((turn + parts - 1) % parts)

        def step(k, carry):
            u, p, keep_next = carry
            j = J - 1 - k
            rows = pl.ds(pl.multiple_of(j * SUB, SUB), SUB)
            u = take(0, rows) + keep_next * u
            p = keep_next * p
            put(0, rows, u)
            put(half, rows, p)
            return u, p, kept[rows, :]

        u, p, keep_first = lax.fori_loop(0, J, step, (fills[0], fills[1], fills[1]), unroll=16)
        enter = fills[0]
        for _ in range(SUB - 1):
            enter = shift_up(keep_first * (u + p * enter))

        if linked:

            @pl.when(turn == 3)
            def _():
                for i in (3, 2, 1):
                    reduce.plane(OUT, i)

            for k in (2, 1, 0):

                @pl.when(turn == k)
                def _():
                    reduce.plane(GATE, k + 1)
                    if k == 2:
                        reduce.turn(OUT, 3)
                        reduce.turn(OUT, 2)
                    else:
                        reduce.turn(GATE, k + 2)

        @pl.loop(0, L // R)
        def _(i):
            rows = pl.ds(pl.multiple_of(i * R, R), R)
            carried = take(0, rows) + take(half, rows) * spread(enter)
            f = forget[m, rows, :]
            a = admit[m, rows, :]
            adm = a * recip(f + a)
            g = carried * (state[m, rows, :] - cand[m, rows, :]) * (kept[rows, :] * adm)
            dpre[rows, :hm] = (g * (1.0 - f)).astype(bf16)
            dpre[rows, hm : 2 * hm] = (g * (a - 1.0)).astype(bf16)
            dpre[rows, 2 * hm :] = (carried * adm).astype(bf16)
            keeps(m_next, rows)

        for k in range(3):
            stack(m, units[GATE][0], 3 * hm // BLK, k * hm // BLK, dot(n1t[...], dpre[:, k * hm : (k + 1) * hm]))
        for cols in column_halves:
            acc_b[:, cols] += dot(dpre[...], wg[m, cols, :], True)
        state_grads(m_next)
        if linked:
            for k in (3, 2, 1):

                @pl.when(turn == k)
                def _():
                    reduce.chip(GATE, k)
                    if k == 3:
                        reduce.model(UPDOWN, 1)
                    if k == 2:
                        for i in (3, 2, 1):
                            reduce.model(OUT, i)
                    if k == 1:
                        reduce.model(GATE, 3)

    if linked:
        reduce.model(GATE, 2)
        reduce.own(UPDOWN)
        reduce.model(GATE, 1)
        reduce.own(OUT)

    fetch_tok.wait()
    permute_in(cot, cot)
    def back_one(i, total):
        rows = pl.ds(pl.multiple_of(i * R, R), R)
        x = cot[rows, :].astype(f32)
        r = lax.rsqrt(jnp.mean(x * x, axis=-1, keepdims=True) + norm_eps)
        dn = acc_b[rows, :]
        q = dn * gain_one
        mixed[rows, :] += r * q - r * r * r * x * jnp.mean(q * x, axis=-1, keepdims=True)
        return total + jnp.sum(dn * x * r, axis=0, keepdims=True)

    gain_sum_one = lax.fori_loop(0, L // R, back_one, jnp.zeros((1, D), f32))

    permute_out(acc_a, n1)
    push_out = pltpu.make_async_copy(n1, block_out, local.at[0])
    push_out.start()

    place = lax.broadcasted_iota(jnp.int32, (SUB, hm), 0).astype(f32) * float(J)
    if linked:
        first = ((gather.me * parts + gather.m) * L + 1).astype(f32)
        token_total = float(L * parts * lax.axis_size("dp"))
    else:
        first = base[0]
        token_total = base[1]
    forget_sum = jnp.sum(tally[1] + tally[0] * (place + first), axis=0, keepdims=True) / token_total
    small[...] = jnp.zeros_like(small)
    small[0:1, :] = gain_sum_one
    small[1:2, :] = gain_sum_two
    small[2:3, :hm] = forget_sum
    if linked:
        flat = units[UPDOWN][1] // 2, units[GATE][0]
        count = owned.shape[0]
        flags = []
        for k in range(count):
            spot = slot_place[0, gather.me * count + k]
            flags.append(jnp.where((spot >= flat[0]) & (spot < flat[1]), 1.0, 0.0).astype(f32))

    if linked:
        tiny = SmallSum(net, gather, small, sum_a, sum_b, sum_c)
        tiny.send(0)
        reduce.own(GATE)
        reduce.slots_chip(slots, slot_place, pair)
        tiny.add(0)
        tiny.send(1)
        reduce.slots_plane(slots, pair, far)

    permute_out(mixed, acc_a)
    push_grad = pltpu.make_async_copy(acc_a, input_grad, local.at[2])
    push_grad.start()

    if linked:
        tiny.add(1)
        tiny.send(2)
        reduce.slots_end(slots, pair, far, owned)
        tiny.add(2)
        for k, flag in enumerate(flags):
            small[3 + k // 4 : 4 + k // 4, (k % 4) * BLK : (k % 4 + 1) * BLK] = jnp.full((1, BLK), flag, f32)
        net.drain()
    push_out.wait()
    push_grad.wait()


def compute(tokens, cotangent, gains, weights=None, base=None, master=None, owner=None):
    linked = weights is None
    parts = lax.axis_size("mp")
    hm, fm = H // parts, FF // parts
    stacked = (parts, D * (4 * hm + 2 * fm) // BLK**2, BLK, BLK)
    sds = jax.ShapeDtypeStruct
    vm, sm, hbm = (pl.BlockSpec(memory_space=k) for k in (pltpu.VMEM, pltpu.SMEM, pl.ANY))
    if linked:
        n = owner.shape[0]
        args = (tokens, cotangent, master, owner, gains)
        in_specs = [hbm, hbm, hbm, sm, vm]
        middle = sds((n // 8, BLK, BLK), f32)
        extra = [
            pltpu.VMEM((parts, D, 3 * hm), bf16),
            pltpu.VMEM((parts, hm, D), bf16),
            pltpu.VMEM((parts, D, fm), bf16),
            pltpu.VMEM((parts, fm, D), bf16),
            pltpu.VMEM(stacked, bf16),
            pltpu.VMEM((n, BLK, BLK), bf16),
            *[pltpu.VMEM((n, BLK, BLK), bf16) for _ in range(parts - 1)],
            pltpu.VMEM((n // 2, BLK, BLK), bf16),
            pltpu.VMEM((6, n // 16, BLK, BLK), bf16),
            pltpu.VMEM((parts, 8, D), f32),
            pltpu.VMEM((4, 8, D), f32),
            pltpu.VMEM((2, 8, D), f32),
            pltpu.VMEM((8, BLK), jnp.int32),
            pltpu.SMEM((8, BLK), jnp.int32),
            pltpu.SMEM((8, BLK), jnp.int32),
            pltpu.SemaphoreType.DMA((128,)),
            pltpu.SemaphoreType.DMA((128,)),
            pltpu.SemaphoreType.REGULAR,
        ]
        params = dict(collective_id=0, has_side_effects=True)
    else:
        args = (tokens, cotangent, base, *weights, gains)
        in_specs = [hbm, hbm, sm] + [vm] * 5
        middle = sds(stacked, bf16)
        extra = []
        params = {}
    return pl.pallas_call(
        functools.partial(compute_kernel, linked),
        out_shape=(sds((L, D), bf16), sds((L, D), f32), middle, sds((8, D), f32)),
        in_specs=in_specs,
        out_specs=[hbm, hbm, vm, vm],
        scratch_shapes=extra
        + [pltpu.VMEM(shape, bf16) for shape in ((L, D), (D, L)) * 3]
        + [pltpu.VMEM((parts, L, hm), f32)] * 3
        + [pltpu.VMEM((parts, L + SUB, hm), f32)]
        + [pltpu.VMEM((2 * hm // BLK, L, BLK), f32)]
        + [pltpu.VMEM((L, D), f32)] * 3
        + [
            pltpu.VMEM((L, 2 * fm), bf16),
            pltpu.VMEM((L, hm), f32),
            pltpu.VMEM((2, SUB, hm), f32),
            pltpu.VMEM((2, SUB, hm), f32),
            pltpu.SemaphoreType.DMA((3,)),
        ],
        compiler_params=pltpu.CompilerParams(vmem_limit_bytes=64 * 2**20 - 2**16, **params),
        name="block",
    )(*args)


def adam_update(first_old, second_old, gradient):
    first_new = beta_one * first_old + (1.0 - beta_one) * gradient
    second_new = beta_two * second_old + (1.0 - beta_two) * gradient * gradient
    first_hat = first_new / (1.0 - beta_one**STEP)
    second_hat = second_new / (1.0 - beta_two**STEP)
    return (first_new, second_new, first_hat / (jnp.sqrt(second_hat) + adam_eps))


def fine_dot(a, b, trans_b=False):
    a_high, b_high = a.astype(bf16), b.astype(bf16)
    a_low, b_low = (a - a_high.astype(f32)).astype(bf16), (b - b_high.astype(f32)).astype(bf16)
    return dot(a_high, b_high, trans_b) + (dot(a_high, b_low, trans_b) + dot(a_low, b_high, trans_b))


def update_kernel(token_total, passed, sums, gains, gain_moment_one, gain_moment_two, *refs):
    sources, refs = refs[:6], refs[6:]
    given, refs = refs[:passed], refs[passed:]
    results, refs = refs[:4], refs[4:]
    gain_first, gain_second, gains_new, forget_mean = refs[:4]
    copied, refs = refs[4 : 4 + passed], refs[4 + passed :]
    held, made, made_low, sem_in, sem_out, sem_pass = refs[:6]
    passage = refs[6:]
    count = held.shape[1]
    step = max(count // 2, 1)
    groups = [slice(first, first + step) for first in range(0, count, step)]
    enter = [pltpu.make_async_copy(src, via, sem_pass.at[0, k]) for k, (src, via) in enumerate(zip(given, passage))]
    leave = [pltpu.make_async_copy(via, dst, sem_pass.at[1, k]) for k, (via, dst) in enumerate(zip(passage, copied))]
    fetch = [
        [pltpu.make_async_copy(src.at[group], held.at[k, group], sem_in.at[g, k]) for k, src in enumerate(sources)]
        for g, group in enumerate(groups)
    ]
    for copy in fetch[0]:
        copy.start()
    for copy in enter:
        copy.start()
    for row in fetch[1:]:
        for copy in row:
            copy.start()
    first, second, direction = adam_update(gain_moment_one[...], gain_moment_two[...], sums[0:2, :])
    gain_first[...] = first
    gain_second[...] = second
    gains_new[...] = gains[...] - gain_rate * direction
    forget_mean[...] = jnp.sum(sums[2:3, :], axis=1, keepdims=True) * (1.0 / (H * (token_total + 1) / 2.0))
    push = []
    for g, group in enumerate(groups):
        blocks = range(group.start, group.stop)
        for copy in fetch[g]:
            copy.wait()
        if g == len(groups) - 1:
            for come, go in zip(enter, leave):
                come.wait()
                go.start()
        grads = []
        for s in blocks:
            grad = held[0, s]
            flag = sums[3 + s // 4 : 4 + s // 4, (s % 4) * BLK : (s % 4 + 1) * BLK]
            grads.append(jnp.where(flag > 0.5, grad.T, grad))
        values = [fine_dot(held[1, s].T, grad) for s, grad in zip(blocks, grads)]
        values = [fine_dot(value, held[2, s]) for s, value in zip(blocks, values)]
        for k, s in enumerate(blocks):
            first, second, values[k] = adam_update(held[3, s], held[4, s], values[k])
            made[0, s] = first
            made[1, s] = second
        values = [fine_dot(held[1, s], value) for s, value in zip(blocks, values)]
        values = [fine_dot(value, held[2, s], True) for s, value in zip(blocks, values)]
        for s, value in zip(blocks, values):
            fresh = held[5, s] - learn_rate * (value + weight_decay * held[5, s])
            made[2, s] = fresh
            made_low[s] = fresh.astype(bf16)
        for k, dst in enumerate(results):
            src = made.at[k, group] if k < 3 else made_low.at[group]
            copy = pltpu.make_async_copy(src, dst.at[group], sem_out.at[g, k])
            copy.start()
            push.append(copy)
    for copy in push + leave:
        copy.wait()


def update(token_total, small, large, passed):
    sds = jax.ShapeDtypeStruct
    blocks, gain = large[0].shape, small[1].shape
    vm, hbm = pl.BlockSpec(memory_space=pltpu.VMEM), pl.BlockSpec(memory_space=pl.ANY)
    return pl.pallas_call(
        functools.partial(update_kernel, token_total, len(passed)),
        out_shape=[sds(blocks, f32)] * 3
        + [sds(blocks, bf16)]
        + [sds(gain, f32)] * 3
        + [sds((1, 1), f32)]
        + [sds(v.shape, v.dtype) for v in passed],
        in_specs=[vm] * 4 + [hbm] * (len(large) + len(passed)),
        out_specs=[hbm] * 4 + [vm] * 4 + [hbm] * len(passed),
        scratch_shapes=[
            pltpu.VMEM((6, *blocks), f32),
            pltpu.VMEM((3, *blocks), f32),
            pltpu.VMEM(blocks, bf16),
            pltpu.SemaphoreType.DMA((2, 6)),
            pltpu.SemaphoreType.DMA((2, 4)),
            pltpu.SemaphoreType.DMA((2, len(passed))),
        ]
        + [pltpu.VMEM(v.shape, v.dtype) for v in passed],
        compiler_params=pltpu.CompilerParams(vmem_limit_bytes=56 * 2**20),
        name="update",
    )(*small, *large, *passed)


def on_device(
    tokens,
    cotangent,
    master,
    moment_one,
    moment_two,
    basis_left,
    basis_right,
    owner,
    gains,
    gain_moment_one,
    gain_moment_two,
):
    parts = lax.axis_size("mp")
    data_parts = lax.axis_size("dp")
    hm, fm = H // parts, FF // parts
    token_total = L * data_parts * parts
    row_tiles, cols, lows = D // BLK, (3 * hm + fm) // BLK, (hm + fm) // BLK
    if data_parts == 8 and parts == 4:
        block_out, input_grad, owned, sums = compute(tokens, cotangent, gains, master=master[0], owner=owner)
    else:
        number = jnp.arange(owner.shape[0], dtype=jnp.int32)
        ahead = (owner[None, :] < owner[:, None]) | ((owner[None, :] == owner[:, None]) & (number[None, :] < number[:, None]))
        block_rank = jnp.sum(ahead.astype(jnp.int32), axis=1)
        _, table = stack_places(hm, fm)
        table = jnp.asarray(table, jnp.int32)
        slot_place = jnp.sum(jnp.where(block_rank[None, :] == number[:, None], table[None, :], 0), axis=1)
        stored = lax.all_gather(master.astype(bf16), "dp", axis=1, tiled=True)
        stored = lax.all_gather(stored, "mp", axis=0, tiled=True)
        stack = stored[:, block_rank]
        upper = stack[:, : row_tiles * cols].reshape(parts, row_tiles, cols, BLK, BLK)
        upper = upper.transpose(0, 1, 3, 2, 4).reshape(parts, D, cols * BLK)
        lower = stack[:, row_tiles * cols :].reshape(parts, lows, row_tiles, BLK, BLK)
        lower = lower.transpose(0, 1, 3, 2, 4).reshape(parts, lows * BLK, D)
        weights = (upper[:, :, : 3 * hm], lower[:, :hm], upper[:, :, 3 * hm :], lower[:, hm:])
        first = ((lax.axis_index("dp") * parts + lax.axis_index("mp")) * L + 1).astype(f32)
        base = jnp.stack([first, jnp.asarray(token_total, f32)])
        block_out, input_grad, grads, sums = compute(tokens, cotangent, gains, weights=weights, base=base)
        owned = lax.psum_scatter(grads[:, slot_place].astype(f32), "dp", scatter_dimension=1, tiled=True)
        owned = lax.psum_scatter(owned, "mp", scatter_dimension=0, tiled=True)[0]
        sums = lax.psum(sums, ("dp", "mp"))
        count = master.shape[1]
        mine = lax.dynamic_slice_in_dim(slot_place, lax.axis_index("dp") * count, count)
        units, _ = stack_places(hm, fm)
        flags = ((mine >= units[UPDOWN][1] // 2) & (mine < units[GATE][0])).astype(f32)
        flags = jnp.pad(jnp.repeat(flags, BLK), (0, (8 - count) * BLK)).reshape(2, 4 * BLK)
        sums = jnp.concatenate([sums[:3], flags, sums[5:]])
    outs = update(
        token_total,
        (sums, gains, gain_moment_one, gain_moment_two),
        (owned, basis_left[0], basis_right[0], moment_one[0], moment_two[0], master[0]),
        (block_out, input_grad),
    )
    first_new, second_new, master_new, master_low, gain_first, gain_second, gains_new, forget_mean = outs[:8]
    block_out, input_grad = outs[8:]
    return (
        block_out,
        input_grad,
        first_new[None],
        second_new[None],
        master_new[None],
        master_low[None],
        gain_first,
        gain_second,
        gains_new,
        forget_mean[0, 0],
    )


def solution(mesh):
    rows, blocks = P(("dp", "mp"), None), P("mp", "dp", None, None)
    return jax.shard_map(
        on_device,
        mesh=mesh,
        in_specs=(rows, rows, blocks, blocks, blocks, blocks, blocks, P(), P(), P(), P()),
        out_specs=(rows, rows, blocks, blocks, blocks, blocks, P(), P(), P(), P()),
        check_vma=False,
    )
```

```python
import functools

import jax
import jax.numpy as jnp
from jax import lax
from jax.experimental import pallas as pl
from jax.experimental.pallas import tpu as pltpu
from jax.sharding import PartitionSpec as P

D = 512
H = 1024
FF = 2048
BLK = 128
STEP = 10
L = 1024

norm_eps = 1e-05
beta_one = 0.5
beta_two = 0.5
adam_eps = 1e-08
learn_rate = 0.02
gain_rate = 0.1
weight_decay = 0.1
highest = lax.Precision.HIGHEST

f32 = jnp.float32
bf16 = jnp.bfloat16
SUB = 8
J = L // SUB
R = 256


def dot(a, b, trans_b=False):
    dims = (((1,), (1,)), ((), ())) if trans_b else (((1,), (0,)), ((), ()))
    return lax.dot_general(a, b, dims, preferred_element_type=f32)


def recip(v):
    return pltpu.reciprocal(v, approx=True)


def sigmoid(v):
    return recip(1.0 + jnp.exp(-v))


def shift_down(v):
    rolled = pltpu.roll(v, 1, 0)
    row = lax.broadcasted_iota(jnp.int32, v.shape, 0)
    return jnp.where(row == 0, 0.0, rolled)


def shift_up(v):
    rolled = pltpu.roll(v, SUB - 1, 0)
    row = lax.broadcasted_iota(jnp.int32, v.shape, 0)
    return jnp.where(row == SUB - 1, 0.0, rolled)


def gelu_terms(x):
    a = jnp.abs(x)
    t = recip(1.0 + a * (0.3275911 * 0.7071067811865476))
    poly = t * (
        0.5 * 0.254829592
        + t
        * (
            0.5 * -0.284496736
            + t * (0.5 * 1.421413741 + t * (0.5 * -1.453152027 + t * (0.5 * 1.061405429)))
        )
    )
    e = jnp.exp(x * x * -0.5)
    tail = poly * e
    cdf = jnp.where(x < 0.0, tail, 1.0 - tail)
    return cdf, x * e * 0.3989422804014327


MESH = pl.DeviceIdType.MESH


class Copy:
    def __init__(self, net, make):
        self.net, self.make = net, make

    def start(self):
        self.net.open.append(self)
        self.make().start()
        return self

    def wait_recv(self):
        self.make().wait_recv()

    def wait_send(self):
        self.make().wait_send()


class Exchange:
    def __init__(self, send, recv):
        self.send, self.recv, self.known, self.used, self.open = send, recv, {}, 0, []

    def copy(self, parts, key=None):
        if key in self.known:
            return self.known[key]
        k = self.used
        self.used += 1

        def make():
            src, dst, device = parts()
            return pltpu.make_async_remote_copy(
                src_ref=src,
                dst_ref=dst,
                send_sem=self.send.at[k],
                recv_sem=self.recv.at[k],
                device_id=device,
                device_id_type=MESH,
            )

        copy = Copy(self, make)
        if key is not None:
            self.known[key] = copy
        return copy

    def start(self, parts):
        return self.copy(parts).start()

    def drain(self):
        for copy in self.open:
            copy.wait_send()
        self.open = []


class Gather:
    def __init__(self, net, fetch, master, slots, pool, weights, free):
        self.net, self.weights, self.free = net, weights, free
        self.held = [slots, *pool]
        d, m = lax.axis_index("dp"), lax.axis_index("mp")
        core, col, row = d % 2, (d // 2) % 2, d // 4
        self.me, self.m, self.side = d, m, core
        self.core = d + 1 - 2 * core
        self.plane = [d + 2 - 4 * col, d + 4 - 8 * row, d + 6 - 4 * col - 8 * row]
        self.order = [m, m + 1 - 2 * (m % 2), m + 2 - 4 * (m // 2), 3 - m]
        self.peers = [(e, m) for e in [self.core] + self.plane] + [(d, k) for k in self.order[1:]]
        barrier = pltpu.get_barrier_semaphore()
        for device in self.peers:
            pl.semaphore_signal(barrier, inc=1, device_id=device, device_id_type=MESH)
        self.n = master.shape[0]
        fetch.wait()
        for s in range(self.n):
            slots[d * self.n + s] = master[s].astype(bf16)
        pl.semaphore_wait(barrier, len(self.peers))

    def rows(self, i, e, first, count):
        return self.held[i].at[pl.ds(e * self.n + first, count)]

    def along(self, i, e):
        return self.net.copy(
            lambda: (self.rows(0, e, 0, self.n), self.rows(i, e, 0, self.n), (self.me, self.order[i])),
            ("along", i, e is self.me),
        )

    def within(self, key, i, e, first, count, to):
        return self.net.copy(
            lambda: (self.rows(i, e, first, count), self.rows(i, e, first, count), (to, self.m)), (key, i)
        )

    def first(self, i):
        (x, y, _), h = self.plane, self.n // 2
        if i == 1:
            jobs = ((0, self.n, x), (0, self.n, y))
        else:
            jobs = ((0, h, x), (h, h, y), (h, h, x), (0, h, y))
        return [self.within(("first", k), i, self.me, *job) for k, job in enumerate(jobs)]

    def last(self, i):
        x, y, z = self.plane
        if i == 1:
            return [self.along(1, z)]
        h = self.n // 2
        return [self.within("over y", i, x, 0, h, y), self.within("over x", i, y, h, h, x)]

    def inside(self, i):
        return [self.within(("inside", k), i, e, 0, self.n, self.core) for k, e in enumerate([self.me] + self.plane)]

    def along_start(self, i):
        self.along(i, self.me).start()

    def across_start(self):
        self.last(1)[0].start()

    def start(self, i):
        if i:
            self.along(i, self.me).wait_recv()
        for copy in self.first(i):
            copy.start()
        self.inside(i)[0].start()

    def forward(self, i):
        if i == 1:
            return
        for came, copy in zip(self.first(i), self.last(i)):
            came.wait_recv()
            copy.start()

    def pair(self, i):
        for came, copy in zip(self.first(i)[-2:], self.inside(i)[1:3]):
            came.wait_recv()
            copy.start()
        for came in self.last(i):
            came.wait_recv()
        self.inside(i)[3].start()

    def ready(self, i):
        for copy in self.inside(i):
            copy.wait_recv()

    def place(self, i, rank):
        wg, wo, wu, wd = self.weights
        row_tiles, gates = D // BLK, wg.shape[2] // BLK
        cols, outs = gates + wu.shape[2] // BLK, wo.shape[1] // BLK
        for b in range(row_tiles * cols + (wo.shape[1] + wd.shape[1]) // BLK * row_tiles):
            if b < row_tiles * cols:
                r, c = b // cols, b % cols
                ref = wg if c < gates else wu
                c -= 0 if c < gates else gates
            else:
                r, c = (b - row_tiles * cols) // row_tiles, (b - row_tiles * cols) % row_tiles
                ref = wo if r < outs else wd
                r -= 0 if r < outs else outs
            block = self.held[i][rank[0, b]]
            ref[self.order[i], r * BLK : (r + 1) * BLK, c * BLK : (c + 1) * BLK] = block

    def done(self):
        for device in self.peers:
            pl.semaphore_signal(self.free, inc=1, device_id=device, device_id_type=MESH)

    def all_done(self):
        pl.semaphore_wait(self.free, len(self.peers))


def stack_places(hm, fm):
    row_tiles, gates, ups, outs = D // BLK, 3 * hm // BLK, fm // BLK, hm // BLK
    cols = gates + ups
    first_down = row_tiles * ups
    first_out = 2 * first_down
    first_gate = first_out + row_tiles * outs
    table = []
    for b in range(row_tiles * (cols + outs + ups)):
        if b < row_tiles * cols:
            r, c = b // cols, b % cols
            table.append(first_gate + r * gates + c if c < gates else r * ups + c - gates)
        else:
            k = b - row_tiles * cols
            table.append(first_out + k if k < row_tiles * outs else first_down + k - row_tiles * outs)
    return ((0, first_out), (first_out, row_tiles * outs), (first_gate, row_tiles * gates)), table


UPDOWN, OUT, GATE = range(3)


class Reduce:
    def __init__(self, net, gather, grads, units, pool):
        self.net, self.g, self.grads, self.units, self.pool = net, gather, grads, units, pool
        self.half = grads.shape[1] // 2
        self.eighth = grads.shape[1] // 8

    def place(self, e):
        return (e % 2) * 4 + e // 2

    def inside(self, unit, i):
        g, (first, count) = self.g, self.units[unit]
        return self.net.copy(
            lambda: (
                self.grads.at[g.order[i], pl.ds(first + (1 - g.side) * (count // 2), count // 2)],
                self.pool[i - 1].at[pl.ds(first // 2, count // 2)],
                (g.core, g.m),
            ),
            ("chip", unit, i),
        )

    def chip(self, unit, i):
        self.inside(unit, i).start()

    def spot(self, unit, i, slot, first, count):
        base, total = self.units[unit]
        return self.pool[i - 1].at[pl.ds(self.half + slot * self.eighth + base // 8 + first, count)]

    def parts(self, unit, i):
        n = self.units[unit][1] // 8
        if i == 1:
            return ((0, n),)
        h = (n + i % 2) // 2 if n % 2 else n // 2
        return (0, h), (h, n - h)

    def share(self, unit, i, e, first, count):
        base, total = self.units[unit]
        return self.grads.at[self.g.order[i], pl.ds(base + self.place(e) * (total // 8) + first, count)]

    def over(self, unit, i, slot, part):
        x, y, z = self.g.plane
        e = (z, x, y)[slot]
        to = (x if part == self.parts(unit, i)[0] else y, x, y)[slot]
        return self.net.copy(
            lambda: (self.share(unit, i, e, *part), self.spot(unit, i, slot, *part), (to, self.g.m)),
            ("over", unit, i, slot, part),
        )

    def send(self, unit, i, slot, part):
        if part[1]:
            self.over(unit, i, slot, part).start()

    def take(self, unit, i, slot, part):
        self.over(unit, i, slot, part).wait_recv()
        return self.spot(unit, i, slot, *part)[...].astype(f32)

    def model_copy(self, unit, i):
        n = self.units[unit][1] // 8
        return self.net.copy(
            lambda: (self.share(unit, i, self.g.me, 0, n), self.spot(unit, i, 3, 0, n), (self.g.me, self.g.order[i])),
            ("model", unit, i),
        )

    def aside(self, unit):
        part = (0, self.units[unit][1] // 8)
        return self.net.copy(
            lambda: (
                self.share(unit, 1, self.g.plane[2], *part),
                self.spot(unit, 1, 0, *part),
                (self.g.me, self.g.order[1]),
            ),
            ("aside", unit),
        )

    def plane(self, unit, i):
        g, (first, count) = self.g, self.units[unit]
        x, y, z = g.plane
        self.inside(unit, i).wait_recv()
        m = g.order[i]
        start, came = first + g.side * (count // 2), self.pool[i - 1]

        @pl.loop(0, count // 2, unroll=4)
        def _(b):
            total = self.grads[m, start + b].astype(f32) + came[first // 2 + b].astype(f32)
            self.grads[m, start + b] = total.astype(bf16)

        if i == 1:
            (whole,) = self.parts(unit, i)
            self.send(unit, i, 1, whole)
            self.send(unit, i, 2, whole)
            self.aside(unit).start()
            return
        one, two = self.parts(unit, i)
        self.send(unit, i, 0, one)
        self.send(unit, i, 0, two)
        self.send(unit, i, 1, one)
        self.send(unit, i, 2, two)

    def turn(self, unit, i):
        if i == 1:
            return
        x, y, _ = self.g.plane
        for part, slot, e in zip(self.parts(unit, i), (2, 1), (y, x)):
            if part[1]:
                ref = self.share(unit, i, e, *part)
                ref[...] = (ref[...].astype(f32) + self.take(unit, i, 0, part)).astype(bf16)
                self.send(unit, i, slot, part)

    def model(self, unit, i):
        g, (first, count) = self.g, self.units[unit]
        n = count // 8
        for part in self.parts(unit, i):
            if part[1]:
                ref = self.share(unit, i, g.me, *part)
                total = ref[...].astype(f32) + self.take(unit, i, 1, part) + self.take(unit, i, 2, part)
                ref[...] = total.astype(bf16)
        self.model_copy(unit, i).start()

    def own(self, unit):
        g, (first, count) = self.g, self.units[unit]
        n = count // 8
        rows = pl.ds(first + self.place(g.me) * n, n)
        total = self.grads[g.m, rows].astype(f32)
        for i in (1, 2, 3):
            self.model_copy(unit, i).wait_recv()
            total += self.pool[i - 1][pl.ds(self.half + 3 * self.eighth + first // 8, n)].astype(f32)
        self.grads[g.m, rows] = total.astype(bf16)
        self.aside(unit).wait_recv()
        rows = pl.ds(first + self.place(g.plane[2]) * n, n)
        total = self.grads[g.m, rows].astype(f32) + self.spot(unit, 1, 0, 0, n)[...].astype(f32)
        self.grads[g.m, rows] = total.astype(bf16)

    def into_slots(self, out, slot_place, e):
        n = self.eighth
        for k in range(n):
            out[self.place(e) * n + k] = self.grads[self.g.m, slot_place[0, e * n + k]]

    def slots_chip(self, out, slot_place, pair):
        g, n = self.g, self.eighth
        self.last = []
        targets = (g.plane[2], g.plane[0], g.plane[1], g.me)
        for e in targets:
            other = e + 1 - 2 * g.side
            self.into_slots(out, slot_place, other)
            self.last.append(
                self.net.start(
                    lambda e=e, other=other: (
                        out.at[pl.ds(self.place(other) * n, n)],
                        pair.at[pl.ds((e // 2) * n, n)],
                        (g.core, g.m),
                    )
                )
            )
        for e in targets:
            self.into_slots(out, slot_place, e)

    def slots_plane(self, out, pair, far, meanwhile):
        g, n = self.g, out.shape[0] // 8
        h = n // 2
        x, y, z = g.plane
        wait = dict(zip("zxyo", self.last))

        def mine(e, first, count):
            return pl.ds((g.side * 4 + e // 2) * n + first, count)

        def join(e):
            rows = mine(e, 0, n)
            out[rows] = (out[rows].astype(f32) + pair[pl.ds((e // 2) * n, n)].astype(f32)).astype(bf16)

        def send(e, first, slot, to):
            return self.net.start(lambda: (out.at[mine(e, first, h)], far.at[slot], (to, g.m)))

        wait["z"].wait_recv()
        join(z)
        over_x = send(z, 0, 0, x)
        over_y = send(z, h, 1, y)
        wait["x"].wait_recv()
        join(x)
        self.ends = [send(x, 0, 2, x)]
        wait["y"].wait_recv()
        join(y)
        self.ends.append(send(y, h, 3, y))
        meanwhile()
        over_x.wait_recv()
        rows = mine(y, 0, h)
        out[rows] = (out[rows].astype(f32) + far[0].astype(f32)).astype(bf16)
        self.ends.append(send(y, 0, 4, y))
        over_y.wait_recv()
        rows = mine(x, h, h)
        out[rows] = (out[rows].astype(f32) + far[1].astype(f32)).astype(bf16)
        self.ends.append(send(x, h, 5, x))
        wait["o"].wait_recv()

    def slots_end(self, out, pair, far, owned):
        g, n = self.g, out.shape[0] // 8
        h = n // 2
        for copy in self.ends:
            copy.wait_recv()
        for first, slots in ((0, (2, 4)), (h, (3, 5))):
            total = out[pl.ds((g.side * 4 + g.me // 2) * n + first, h)].astype(f32)
            total += pair[pl.ds((g.me // 2) * n + first, h)].astype(f32)
            for k in slots:
                total += far[k].astype(f32)
            owned[first : first + h] = total


class SmallSum:
    def __init__(self, net, gather, values, along, across, inside):
        self.net, self.g, self.values = net, gather, values
        self.slots = (along, across, inside)
        self.peers = (
            [(gather.me, k) for k in gather.order[1:]],
            [(e, gather.m) for e in gather.plane],
            [(gather.core, gather.m)],
        )
        self.mine = (gather.m, gather.me // 2, gather.side)
        self.open = []

    def send(self, stage):
        slot = self.slots[stage]
        slot[self.mine[stage]] = self.values[...]
        ref = slot.at[self.mine[stage]]
        self.open = [self.net.start(lambda peer=peer: (ref, ref, peer)) for peer in self.peers[stage]]

    def add(self, stage):
        for copy in self.open:
            copy.wait_recv()
        slot = self.slots[stage]
        total = slot[0]
        for k in range(1, slot.shape[0]):
            total += slot[k]
        self.values[...] = total


def number_blocks(owner, table, vector, rank, slot_place, sem):
    lane = lax.broadcasted_iota(jnp.int32, vector.shape, 1)
    count = owner.shape[0]
    owners = jnp.zeros_like(lane)
    for b in range(count):
        owners = jnp.where(lane == b, owner[b], owners)
    ranks = jnp.zeros_like(lane)
    for b in range(count):
        ahead = (owner[b] < owners) | ((owner[b] == owners) & (lane > b))
        ranks += jnp.where(ahead, 1, 0)
    vector[...] = ranks
    copy = pltpu.make_async_copy(vector, rank, sem)
    copy.start()
    copy.wait()
    places = jnp.zeros_like(lane)
    for b in range(count):
        places = jnp.where(lane == rank[0, b], table[b], places)
    vector[...] = places
    copy = pltpu.make_async_copy(vector, slot_place, sem)
    copy.start()
    copy.wait()


def compute_kernel(linked, *refs):
    if linked:
        tokens, cotangent, master, owner, gains = refs[:5]
        block_out, input_grad, owned, small = refs[5:9]
        wg, wo, wu, wd, grads, slots, *pool, pair, far, sum_a, sum_b, sum_c, vector, rank, slot_place, send, recv, free = refs[9:29]
        scratch = refs[29:]
    else:
        tokens, cotangent, base, wg, wo, wu, wd, gains = refs[:8]
        block_out, input_grad, grads, small = refs[8:12]
        scratch = refs[12:]
    (n1, n1t, cot, cott, n2, n2t, forget, admit, cand, state, scan, acc_a, acc_b, mixed, mid, kept, fills, tally, local) = scratch
    dml, dmlt = n2, n2t
    parts, _, hm3 = wg.shape
    hm = hm3 // 3
    fm = wu.shape[2]
    units, table = stack_places(hm, fm)
    act, dup, dpre = mid.at[:, :fm], mid.at[:, fm:], mid.at[:, : 3 * hm]
    gain_one = gains[0:1, :]
    gain_two = gains[1:2, :]

    if linked:
        fetch_master = pltpu.make_async_copy(master, owned, local.at[2])
        fetch_master.start()
    fetch_cot = pltpu.make_async_copy(cotangent, cot, local.at[0])
    fetch_tok = pltpu.make_async_copy(tokens, n1, local.at[1])
    fetch_tok.start()
    fetch_cot.start()

    column_halves = (slice(0, D // 2), slice(D // 2, D))

    def stack(m, first, wide, left, value):
        for r in range(value.shape[0] // BLK):
            for c in range(value.shape[1] // BLK):
                grads[m, first + r * wide + left + c] = value[r * BLK : (r + 1) * BLK, c * BLK : (c + 1) * BLK].astype(bf16)

    def stack_turned(m, first, value):
        high = value.shape[0] // BLK
        for r in range(high):
            for c in range(value.shape[1] // BLK):
                grads[m, first + c * high + r] = value[r * BLK : (r + 1) * BLK, c * BLK : (c + 1) * BLK].astype(bf16)

    def permute_in(src, dst):
        for k in range(D // BLK):
            scan[k] = src[:, k * BLK : (k + 1) * BLK].astype(f32)

        @pl.loop(0, J // 2, unroll=4)
        def _(j):
            for k in range(D // BLK):
                lo = scan[k, pl.ds(2 * j, SUB, stride=J), :]
                hi = scan[k, pl.ds(2 * j + 1, SUB, stride=J), :]
                dst[pl.ds(pl.multiple_of(16 * j, 16), 16), k * BLK : (k + 1) * BLK] = jnp.concatenate([lo, hi], 0).astype(bf16)

    def permute_out(src, dst):
        @pl.loop(0, J, unroll=4)
        def _(j):
            rows = pl.ds(pl.multiple_of(j * SUB, SUB), SUB)
            for k in range(D // BLK):
                scan[k, pl.ds(j, SUB, stride=J), :] = src[rows, k * BLK : (k + 1) * BLK]

        for k in range(D // BLK):
            dst[:, k * BLK : (k + 1) * BLK] = scan[k].astype(dst.dtype)

    def put(first, rows, value):
        for k in range(hm // BLK):
            scan[first + k, rows, :] = value[:, k * BLK : (k + 1) * BLK]

    def take(first, rows):
        return jnp.concatenate([scan[first + k, rows, :] for k in range(hm // BLK)], 1)

    half = hm // BLK

    def spread(v):
        return jnp.broadcast_to(v[None], (R // SUB, SUB, hm)).reshape(R, hm)


    if linked:
        net = Exchange(send, recv)
        gather = Gather(net, fetch_master, owned, slots, pool, (wg, wo, wu, wd), free)
        gather.start(0)
        gather.along_start(1)
        gather.along_start(2)
        reduce = Reduce(net, gather, grads, units, pool)

    def of_turn(t):
        if not linked:
            return t
        high, low = gather.m // 2, gather.m % 2
        t_high, t_low = t // 2, t % 2
        return 2 * (high + t_high - 2 * high * t_high) + low + t_low - 2 * low * t_low

    fetch_tok.wait()
    permute_in(n1, n1)
    mixed[...] = n1[...].astype(f32)

    @pl.loop(0, L // R)
    def _(i):
        rows = pl.ds(pl.multiple_of(i * R, R), R)
        x = mixed[rows, :]
        r = lax.rsqrt(jnp.mean(x * x, axis=-1, keepdims=True) + norm_eps)
        n1[rows, :] = (x * r * gain_one).astype(bf16)

    n1t[...] = n1[...].T

    if linked:
        gather.forward(0)
        gather.along_start(3)
        number_blocks(owner, table, vector, rank, slot_place, local.at[2])
    fetch_cot.wait()
    permute_in(cot, cot)
    if linked:
        gather.start(1)
        gather.pair(0)
        gather.across_start()
        gather.start(2)
    cott[...] = cot[...].T

    fills[0] = jnp.zeros((SUB, hm), f32)
    fills[1] = jnp.ones((SUB, hm), f32)
    tally[0] = fills[0]
    tally[1] = fills[0]

    @pl.loop(0, parts)
    def _(turn):
        m = of_turn(turn)
        if linked:
            for k in range(parts):

                @pl.when(turn == k)
                def _():
                    if k > 1:
                        gather.pair(k)
                    gather.ready(k)
                    gather.place(k, rank)

        forget[m] = dot(n1[...], wg[m, :, :hm])
        admit[m] = dot(n1[...], wg[m, :, hm : 2 * hm])
        cand[m] = dot(n1[...], wg[m, :, 2 * hm :])

        if linked:

            @pl.when(turn == 2)
            def _():
                gather.forward(3)

        @pl.loop(0, L // R)
        def _(i):
            rows = pl.ds(pl.multiple_of(i * R, R), R)
            f = sigmoid(forget[m, rows, :])
            a = sigmoid(admit[m, rows, :])
            inv = recip(f + a)
            forget[m, rows, :] = f
            admit[m, rows, :] = a
            kept[rows, :] = f * inv
            put(0, rows, a * inv * cand[m, rows, :])

        def step(j, carry):
            s, p, k_sum, kj_sum = carry
            rows = pl.ds(pl.multiple_of(j * SUB, SUB), SUB)
            keep = kept[rows, :]
            s = keep * s + take(0, rows)
            p = keep * p
            put(0, rows, s)
            put(half, rows, p)
            return s, p, k_sum + keep, kj_sum + keep * j.astype(f32)

        s, p, k_sum, kj_sum = lax.fori_loop(0, J, step, (fills[0], fills[1], fills[0], fills[0]), unroll=16)
        tally[0] += k_sum
        tally[1] += kj_sum
        enter = fills[0]
        for _ in range(SUB - 1):
            enter = shift_down(s + p * enter)

        @pl.loop(0, L // R)
        def _(i):
            rows = pl.ds(pl.multiple_of(i * R, R), R)
            state[m, pl.ds(pl.multiple_of(i * R + SUB, SUB), R), :] = take(0, rows) + take(half, rows) * spread(enter)

        state[m, :SUB, :] = shift_down(state[m, L:, :])
        for cols in column_halves:
            mixed[:, cols] += dot(state[m, SUB:, :].astype(bf16), wo[m, :, cols])
        if linked:

            @pl.when(turn == 0)
            def _():
                gather.pair(1)
                gather.forward(2)
                gather.start(3)

    if linked:
        net.drain()
        gather.done()

    @pl.loop(0, L // R)
    def _(i):
        rows = pl.ds(pl.multiple_of(i * R, R), R)
        x = mixed[rows, :]
        r = lax.rsqrt(jnp.mean(x * x, axis=-1, keepdims=True) + norm_eps)
        n2[rows, :] = (x * r * gain_two).astype(bf16)
        acc_a[rows, :] = x
        acc_b[rows, :] = jnp.zeros_like(x)

    n2t[...] = n2[...].T

    @pl.loop(0, parts)
    def _(turn):
        m = of_turn((2 * (turn // 2 + turn % 2 - 2 * (turn // 2) * (turn % 2)) + turn // 2) if linked else turn)
        for first in range(0, fm, fm // 2):
            units_of = slice(first, first + fm // 2)
            up = dot(n2[...], wu[m, :, units_of])
            da = dot(cot[...], wd[m, units_of, :], True)
            cdf, xpdf = gelu_terms(up)
            act[:, units_of] = (up * cdf).astype(bf16)
            dup[:, units_of] = (da * (cdf + xpdf)).astype(bf16)
            if linked and first == 0:

                @pl.when(turn == 2)
                def _():
                    reduce.plane(UPDOWN, 2)

                @pl.when(turn == 3)
                def _():
                    reduce.plane(UPDOWN, 3)
                    reduce.model(UPDOWN, 2)

        for cols in column_halves:
            acc_a[:, cols] += dot(act[...], wd[m, :, cols])
        for cols in column_halves:
            acc_b[:, cols] += dot(dup[...], wu[m, cols, :], True)
        for c in range(0, fm, fm // 2):
            part = slice(c, c + fm // 2)
            stack(m, 0, fm // BLK, c // BLK, dot(n2t[...], dup[:, part]))
        for c in range(0, fm, fm // 2):
            part = slice(c, c + fm // 2)
            stack_turned(m, units[UPDOWN][1] // 2 + c // BLK * (D // BLK), dot(cott[...], act[:, part]))
        if linked:

            @pl.when(turn == 1)
            def _():
                gather.all_done()
                reduce.chip(UPDOWN, 2)

            @pl.when(turn == 2)
            def _():
                reduce.chip(UPDOWN, 3)
                reduce.turn(UPDOWN, 2)

            @pl.when(turn == 3)
            def _():
                reduce.chip(UPDOWN, 1)
                reduce.turn(UPDOWN, 3)

    gain_sum_two = jnp.zeros((1, D), f32)

    def back_two(i, total):
        rows = pl.ds(pl.multiple_of(i * R, R), R)
        x = mixed[rows, :]
        r = lax.rsqrt(jnp.mean(x * x, axis=-1, keepdims=True) + norm_eps)
        dn = acc_b[rows, :]
        q = dn * gain_two
        d = cot[rows, :].astype(f32) + r * q - r * r * r * x * jnp.mean(q * x, axis=-1, keepdims=True)
        mixed[rows, :] = d
        dml[rows, :] = d.astype(bf16)
        acc_b[rows, :] = jnp.zeros_like(d)
        return total + jnp.sum(dn * x * r, axis=0, keepdims=True)

    gain_sum_two = lax.fori_loop(0, L // R, back_two, gain_sum_two)
    if linked:
        reduce.plane(UPDOWN, 1)
        reduce.model(UPDOWN, 3)
    dmlt[...] = dml[...].T
    fetch_tok = pltpu.make_async_copy(tokens, cot, local.at[1])
    fetch_tok.start()

    @pl.loop(0, parts)
    def _(m):
        stack_turned(m, units[OUT][0], dot(dmlt[...], state[m, SUB:, :].astype(bf16)))

    if linked:
        for i in (3, 2, 1):
            reduce.chip(OUT, i)

    def keeps(m, rows):
        f = forget[m, rows, :]
        kept[rows, :] = f * recip(f + admit[m, rows, :])

    def state_grads(m):
        put(0, slice(None), dot(dml[...], wo[m], True))

    state_grads(of_turn(parts - 1))

    @pl.loop(0, L // R)
    def _(i):
        keeps(of_turn(parts - 1), pl.ds(pl.multiple_of(i * R, R), R))

    @pl.loop(0, parts)
    def _(back_turn):
        turn = parts - 1 - back_turn
        m = of_turn(turn)
        m_next = of_turn((turn + parts - 1) % parts)

        def step(k, carry):
            u, p, keep_next = carry
            j = J - 1 - k
            rows = pl.ds(pl.multiple_of(j * SUB, SUB), SUB)
            u = take(0, rows) + keep_next * u
            p = keep_next * p
            put(0, rows, u)
            put(half, rows, p)
            return u, p, kept[rows, :]

        u, p, keep_first = lax.fori_loop(0, J, step, (fills[0], fills[1], fills[1]), unroll=16)
        enter = fills[0]
        for _ in range(SUB - 1):
            enter = shift_up(keep_first * (u + p * enter))

        if linked:

            @pl.when(turn == 3)
            def _():
                for i in (3, 2, 1):
                    reduce.plane(OUT, i)
                reduce.model(UPDOWN, 1)

            for k in (2, 1, 0):

                @pl.when(turn == k)
                def _():
                    reduce.plane(GATE, k + 1)

        @pl.loop(0, L // R)
        def _(i):
            rows = pl.ds(pl.multiple_of(i * R, R), R)
            carried = take(0, rows) + take(half, rows) * spread(enter)
            f = forget[m, rows, :]
            a = admit[m, rows, :]
            adm = a * recip(f + a)
            g = carried * (state[m, rows, :] - cand[m, rows, :]) * (kept[rows, :] * adm)
            dpre[rows, :hm] = (g * (1.0 - f)).astype(bf16)
            dpre[rows, hm : 2 * hm] = (g * (a - 1.0)).astype(bf16)
            dpre[rows, 2 * hm :] = (carried * adm).astype(bf16)
            keeps(m_next, rows)

        if linked:

            @pl.when(turn == 2)
            def _():
                for i in (3, 2, 1):
                    reduce.model(OUT, i)

            @pl.when(turn == 1)
            def _():
                reduce.model(GATE, 3)

            @pl.when(turn == 0)
            def _():
                reduce.model(GATE, 2)

        for k in range(3):
            stack(m, units[GATE][0], 3 * hm // BLK, k * hm // BLK, dot(n1t[...], dpre[:, k * hm : (k + 1) * hm]))
        for cols in column_halves:
            acc_b[:, cols] += dot(dpre[...], wg[m, cols, :], True)
        state_grads(m_next)
        if linked:
            for k in (3, 2, 1):

                @pl.when(turn == k)
                def _():
                    reduce.chip(GATE, k)
                    if k == 3:
                        reduce.turn(OUT, 3)
                        reduce.turn(OUT, 2)
                    else:
                        reduce.turn(GATE, k + 1)

    if linked:
        reduce.own(UPDOWN)
        reduce.model(GATE, 1)
        reduce.own(OUT)

    fetch_tok.wait()
    permute_in(cot, cot)
    def back_one(i, total):
        rows = pl.ds(pl.multiple_of(i * R, R), R)
        x = cot[rows, :].astype(f32)
        r = lax.rsqrt(jnp.mean(x * x, axis=-1, keepdims=True) + norm_eps)
        dn = acc_b[rows, :]
        q = dn * gain_one
        mixed[rows, :] += r * q - r * r * r * x * jnp.mean(q * x, axis=-1, keepdims=True)
        return total + jnp.sum(dn * x * r, axis=0, keepdims=True)

    gain_sum_one = lax.fori_loop(0, L // R, back_one, jnp.zeros((1, D), f32))

    push_out = pltpu.make_async_copy(n1, block_out, local.at[0])

    def finish_block_out():
        permute_out(acc_a, n1)
        push_out.start()

    place = lax.broadcasted_iota(jnp.int32, (SUB, hm), 0).astype(f32) * float(J)
    if linked:
        first = ((gather.me * parts + gather.m) * L + 1).astype(f32)
        token_total = float(L * parts * lax.axis_size("dp"))
    else:
        first = base[0]
        token_total = base[1]
    forget_sum = jnp.sum(tally[1] + tally[0] * (place + first), axis=0, keepdims=True) / token_total
    small[...] = jnp.zeros_like(small)
    small[0:1, :] = gain_sum_one
    small[1:2, :] = gain_sum_two
    small[2:3, :hm] = forget_sum
    if linked:
        flat = units[UPDOWN][1] // 2, units[GATE][0]
        count = owned.shape[0]
        flags = []
        for k in range(count):
            spot = slot_place[0, gather.me * count + k]
            flags.append(jnp.where((spot >= flat[0]) & (spot < flat[1]), 1.0, 0.0).astype(f32))

    if linked:
        tiny = SmallSum(net, gather, small, sum_a, sum_b, sum_c)
        tiny.send(0)
        reduce.own(GATE)
        reduce.slots_chip(slots, slot_place, pair)
        tiny.add(0)
        tiny.send(1)
        reduce.slots_plane(slots, pair, far, finish_block_out)
    else:
        finish_block_out()

    permute_out(mixed, acc_a)
    push_grad = pltpu.make_async_copy(acc_a, input_grad, local.at[2])
    push_grad.start()

    if linked:
        tiny.add(1)
        tiny.send(2)
        reduce.slots_end(slots, pair, far, owned)
        tiny.add(2)
        for k, flag in enumerate(flags):
            small[3 + k // 4 : 4 + k // 4, (k % 4) * BLK : (k % 4 + 1) * BLK] = jnp.full((1, BLK), flag, f32)
        net.drain()
    push_out.wait()
    push_grad.wait()


def compute(tokens, cotangent, gains, weights=None, base=None, master=None, owner=None):
    linked = weights is None
    parts = lax.axis_size("mp")
    hm, fm = H // parts, FF // parts
    stacked = (parts, D * (4 * hm + 2 * fm) // BLK**2, BLK, BLK)
    sds = jax.ShapeDtypeStruct
    vm, sm, hbm = (pl.BlockSpec(memory_space=k) for k in (pltpu.VMEM, pltpu.SMEM, pl.ANY))
    if linked:
        n = owner.shape[0]
        args = (tokens, cotangent, master, owner, gains)
        in_specs = [hbm, hbm, hbm, sm, vm]
        middle = sds((n // 8, BLK, BLK), f32)
        extra = [
            pltpu.VMEM((parts, D, 3 * hm), bf16),
            pltpu.VMEM((parts, hm, D), bf16),
            pltpu.VMEM((parts, D, fm), bf16),
            pltpu.VMEM((parts, fm, D), bf16),
            pltpu.VMEM(stacked, bf16),
            pltpu.VMEM((n, BLK, BLK), bf16),
            *[pltpu.VMEM((n, BLK, BLK), bf16) for _ in range(parts - 1)],
            pltpu.VMEM((n // 2, BLK, BLK), bf16),
            pltpu.VMEM((6, n // 16, BLK, BLK), bf16),
            pltpu.VMEM((parts, 8, D), f32),
            pltpu.VMEM((4, 8, D), f32),
            pltpu.VMEM((2, 8, D), f32),
            pltpu.VMEM((8, BLK), jnp.int32),
            pltpu.SMEM((8, BLK), jnp.int32),
            pltpu.SMEM((8, BLK), jnp.int32),
            pltpu.SemaphoreType.DMA((128,)),
            pltpu.SemaphoreType.DMA((128,)),
            pltpu.SemaphoreType.REGULAR,
        ]
        params = dict(collective_id=0, has_side_effects=True)
    else:
        args = (tokens, cotangent, base, *weights, gains)
        in_specs = [hbm, hbm, sm] + [vm] * 5
        middle = sds(stacked, bf16)
        extra = []
        params = {}
    return pl.pallas_call(
        functools.partial(compute_kernel, linked),
        out_shape=(sds((L, D), bf16), sds((L, D), f32), middle, sds((8, D), f32)),
        in_specs=in_specs,
        out_specs=[hbm, hbm, vm, vm],
        scratch_shapes=extra
        + [pltpu.VMEM(shape, bf16) for shape in ((L, D), (D, L)) * 3]
        + [pltpu.VMEM((parts, L, hm), f32)] * 3
        + [pltpu.VMEM((parts, L + SUB, hm), f32)]
        + [pltpu.VMEM((2 * hm // BLK, L, BLK), f32)]
        + [pltpu.VMEM((L, D), f32)] * 3
        + [
            pltpu.VMEM((L, 2 * fm), bf16),
            pltpu.VMEM((L, hm), f32),
            pltpu.VMEM((2, SUB, hm), f32),
            pltpu.VMEM((2, SUB, hm), f32),
            pltpu.SemaphoreType.DMA((3,)),
        ],
        compiler_params=pltpu.CompilerParams(vmem_limit_bytes=64 * 2**20 - 2**16, **params),
        name="block",
    )(*args)


def adam_update(first_old, second_old, gradient):
    first_new = beta_one * first_old + (1.0 - beta_one) * gradient
    second_new = beta_two * second_old + (1.0 - beta_two) * gradient * gradient
    first_hat = first_new / (1.0 - beta_one**STEP)
    second_hat = second_new / (1.0 - beta_two**STEP)
    return (first_new, second_new, first_hat / (jnp.sqrt(second_hat) + adam_eps))


def fine_dot(a, b, trans_b=False):
    a_high, b_high = a.astype(bf16), b.astype(bf16)
    a_low, b_low = (a - a_high.astype(f32)).astype(bf16), (b - b_high.astype(f32)).astype(bf16)
    return dot(a_high, b_high, trans_b) + (dot(a_high, b_low, trans_b) + dot(a_low, b_high, trans_b))


def update_kernel(token_total, passed, sums, gains, gain_moment_one, gain_moment_two, *refs):
    sources, refs = refs[:6], refs[6:]
    given, refs = refs[:passed], refs[passed:]
    results, refs = refs[:4], refs[4:]
    gain_first, gain_second, gains_new, forget_mean = refs[:4]
    copied, refs = refs[4 : 4 + passed], refs[4 + passed :]
    held, made, made_low, sem_in, sem_out, sem_pass = refs[:6]
    passage = refs[6:]
    count = held.shape[1]
    step = max(count // 2, 1)
    groups = [slice(first, first + step) for first in range(0, count, step)]
    enter = [pltpu.make_async_copy(src, via, sem_pass.at[0, k]) for k, (src, via) in enumerate(zip(given, passage))]
    leave = [pltpu.make_async_copy(via, dst, sem_pass.at[1, k]) for k, (via, dst) in enumerate(zip(passage, copied))]
    fetch = [
        [pltpu.make_async_copy(src.at[group], held.at[k, group], sem_in.at[g, k]) for k, src in enumerate(sources)]
        for g, group in enumerate(groups)
    ]
    for copy in fetch[0]:
        copy.start()
    for copy in enter:
        copy.start()
    for row in fetch[1:]:
        for copy in row:
            copy.start()
    first, second, direction = adam_update(gain_moment_one[...], gain_moment_two[...], sums[0:2, :])
    gain_first[...] = first
    gain_second[...] = second
    gains_new[...] = gains[...] - gain_rate * direction
    forget_mean[...] = jnp.sum(sums[2:3, :], axis=1, keepdims=True) * (1.0 / (H * (token_total + 1) / 2.0))
    push = []
    for g, group in enumerate(groups):
        blocks = range(group.start, group.stop)
        for copy in fetch[g]:
            copy.wait()
        if g == len(groups) - 1:
            for come, go in zip(enter, leave):
                come.wait()
                go.start()
        grads = []
        for s in blocks:
            grad = held[0, s]
            flag = sums[3 + s // 4 : 4 + s // 4, (s % 4) * BLK : (s % 4 + 1) * BLK]
            grads.append(jnp.where(flag > 0.5, grad.T, grad))
        values = [fine_dot(held[1, s].T, grad) for s, grad in zip(blocks, grads)]
        values = [fine_dot(value, held[2, s]) for s, value in zip(blocks, values)]
        for k, s in enumerate(blocks):
            first, second, values[k] = adam_update(held[3, s], held[4, s], values[k])
            made[0, s] = first
            made[1, s] = second
        values = [fine_dot(held[1, s], value) for s, value in zip(blocks, values)]
        values = [fine_dot(value, held[2, s], True) for s, value in zip(blocks, values)]
        for s, value in zip(blocks, values):
            fresh = held[5, s] - learn_rate * (value + weight_decay * held[5, s])
            made[2, s] = fresh
            made_low[s] = fresh.astype(bf16)
        for k, dst in enumerate(results):
            src = made.at[k, group] if k < 3 else made_low.at[group]
            copy = pltpu.make_async_copy(src, dst.at[group], sem_out.at[g, k])
            copy.start()
            push.append(copy)
    for copy in push + leave:
        copy.wait()


def update(token_total, small, large, passed):
    sds = jax.ShapeDtypeStruct
    blocks, gain = large[0].shape, small[1].shape
    vm, hbm = pl.BlockSpec(memory_space=pltpu.VMEM), pl.BlockSpec(memory_space=pl.ANY)
    return pl.pallas_call(
        functools.partial(update_kernel, token_total, len(passed)),
        out_shape=[sds(blocks, f32)] * 3
        + [sds(blocks, bf16)]
        + [sds(gain, f32)] * 3
        + [sds((1, 1), f32)]
        + [sds(v.shape, v.dtype) for v in passed],
        in_specs=[vm] * 4 + [hbm] * (len(large) + len(passed)),
        out_specs=[hbm] * 4 + [vm] * 4 + [hbm] * len(passed),
        scratch_shapes=[
            pltpu.VMEM((6, *blocks), f32),
            pltpu.VMEM((3, *blocks), f32),
            pltpu.VMEM(blocks, bf16),
            pltpu.SemaphoreType.DMA((2, 6)),
            pltpu.SemaphoreType.DMA((2, 4)),
            pltpu.SemaphoreType.DMA((2, len(passed))),
        ]
        + [pltpu.VMEM(v.shape, v.dtype) for v in passed],
        compiler_params=pltpu.CompilerParams(vmem_limit_bytes=56 * 2**20),
        name="update",
    )(*small, *large, *passed)


def on_device(
    tokens,
    cotangent,
    master,
    moment_one,
    moment_two,
    basis_left,
    basis_right,
    owner,
    gains,
    gain_moment_one,
    gain_moment_two,
):
    parts = lax.axis_size("mp")
    data_parts = lax.axis_size("dp")
    hm, fm = H // parts, FF // parts
    token_total = L * data_parts * parts
    row_tiles, cols, lows = D // BLK, (3 * hm + fm) // BLK, (hm + fm) // BLK
    if data_parts == 8 and parts == 4:
        block_out, input_grad, owned, sums = compute(tokens, cotangent, gains, master=master[0], owner=owner)
    else:
        number = jnp.arange(owner.shape[0], dtype=jnp.int32)
        ahead = (owner[None, :] < owner[:, None]) | ((owner[None, :] == owner[:, None]) & (number[None, :] < number[:, None]))
        block_rank = jnp.sum(ahead.astype(jnp.int32), axis=1)
        _, table = stack_places(hm, fm)
        table = jnp.asarray(table, jnp.int32)
        slot_place = jnp.sum(jnp.where(block_rank[None, :] == number[:, None], table[None, :], 0), axis=1)
        stored = lax.all_gather(master.astype(bf16), "dp", axis=1, tiled=True)
        stored = lax.all_gather(stored, "mp", axis=0, tiled=True)
        stack = stored[:, block_rank]
        upper = stack[:, : row_tiles * cols].reshape(parts, row_tiles, cols, BLK, BLK)
        upper = upper.transpose(0, 1, 3, 2, 4).reshape(parts, D, cols * BLK)
        lower = stack[:, row_tiles * cols :].reshape(parts, lows, row_tiles, BLK, BLK)
        lower = lower.transpose(0, 1, 3, 2, 4).reshape(parts, lows * BLK, D)
        weights = (upper[:, :, : 3 * hm], lower[:, :hm], upper[:, :, 3 * hm :], lower[:, hm:])
        first = ((lax.axis_index("dp") * parts + lax.axis_index("mp")) * L + 1).astype(f32)
        base = jnp.stack([first, jnp.asarray(token_total, f32)])
        block_out, input_grad, grads, sums = compute(tokens, cotangent, gains, weights=weights, base=base)
        owned = lax.psum_scatter(grads[:, slot_place].astype(f32), "dp", scatter_dimension=1, tiled=True)
        owned = lax.psum_scatter(owned, "mp", scatter_dimension=0, tiled=True)[0]
        sums = lax.psum(sums, ("dp", "mp"))
        count = master.shape[1]
        mine = lax.dynamic_slice_in_dim(slot_place, lax.axis_index("dp") * count, count)
        units, _ = stack_places(hm, fm)
        flags = ((mine >= units[UPDOWN][1] // 2) & (mine < units[GATE][0])).astype(f32)
        flags = jnp.pad(jnp.repeat(flags, BLK), (0, (8 - count) * BLK)).reshape(2, 4 * BLK)
        sums = jnp.concatenate([sums[:3], flags, sums[5:]])
    outs = update(
        token_total,
        (sums, gains, gain_moment_one, gain_moment_two),
        (owned, basis_left[0], basis_right[0], moment_one[0], moment_two[0], master[0]),
        (block_out, input_grad),
    )
    first_new, second_new, master_new, master_low, gain_first, gain_second, gains_new, forget_mean = outs[:8]
    block_out, input_grad = outs[8:]
    return (
        block_out,
        input_grad,
        first_new[None],
        second_new[None],
        master_new[None],
        master_low[None],
        gain_first,
        gain_second,
        gains_new,
        forget_mean[0, 0],
    )


def solution(mesh):
    rows, blocks = P(("dp", "mp"), None), P("mp", "dp", None, None)
    return jax.shard_map(
        on_device,
        mesh=mesh,
        in_specs=(rows, rows, blocks, blocks, blocks, blocks, blocks, P(), P(), P(), P()),
        out_specs=(rows, rows, blocks, blocks, blocks, blocks, P(), P(), P(), P()),
        check_vma=False,
    )
```
